32 devices in a mesh: slab: 4 (over x, core), dom: 8 (over z, y).
Axes of the slice: x: 2, y: 2, z: 4, core: 2. Of those that a mesh axis runs over, the one named last changes fastest.
Arguments:
- coords: float32 [3, 4, 8, 512], P(None, 'slab', 'dom'), may hold values from -6 to 6
- velocity: float32 [3, 4, 8, 512], P(None, 'slab', 'dom'), may hold values from -6 to 6
- charge: float32 [4, 8, 512], P('slab', 'dom'), may hold values from -1 to 1
- inv_mass: float32 [4, 8, 512], P('slab', 'dom'), may hold values from 0.0625 to 1
- tile_block: int32 [4, 8, 64], P('slab', 'dom'), may hold values from 0 to 3
- tile_atoms: int32 [4, 8, 64, 128], P('slab', 'dom'), may hold values from 0 to 2047
- active_tile_count: int32 [4, 8], P('slab', 'dom'), may hold values from 1 to 64
- bond_atoms: int32 [2, 4, 8, 256], P(None, 'slab', 'dom'), may hold values from 0 to 511, as said below
- cross_atoms: int32 [2, 4, 8, 128], P(None, 'slab', 'dom'), may hold values from 0 to 255
- cross_side: int32 [4, 8, 128], P('slab', 'dom'), may hold values from 0 to 3
- cross_count: int32 [4, 8], P('slab', 'dom'), may hold values from 1 to 128
Outputs:
- coords_out: float32 [3, 4, 8, 512], P(None, 'slab', 'dom')
- velocity_out: float32 [3, 4, 8, 512], P(None, 'slab', 'dom')
The draws below stay inside these ranges and needn't reach their ends.
Inputs may be any that keep to these rules, and one draw needn't show every extreme that they name: `bond_atoms`: each bond joins two different atoms of the domain that holds it. `cross_atoms`: row 0 is an atom of the owning domain, row 1 an atom of the neighbour named by cross_side; both are among the first 256 atoms of their domains. `cross_side`: codes 0 to 3 name the in-slab neighbours at offsets +1, -1, +2, -2 along dom, cyclically. `cross_count`: slots below the count are live. `active_tile_count`: tiles below the count are live. `tile_atoms`: entries index the domain's halo list as in the first step.
All inputs are finite; a program needn't handle non-finite values.
Results may differ from the reference program's by a relative error of at most 0.0003.
Values sent between devices are 32-bit elements; how exact they have to be, the bound alone decides.
No kernel may reach another device: no remote copies, remote signals or barrier semaphores. Data moves between devices by JAX's collectives and lax.ppermute only.
A program may use at most 64 MiB of HBM per device.

```python
import math
import jax
import jax.numpy as jnp
from jax import lax

ATOMS_DEV = 512
TILE = 128
ORDER = 4
CROSS_CAP = 128
SHELL = 256
TILES_DEV = 64
BONDS_DEV = 256
N_SLAB = 4
N_DOM = 8


def chain_order(device_key):
    return jax.random.permutation(device_key, ATOMS_DEV)


def draw_bond_atoms(key, part):
    device_keys = jax.random.split(jax.random.fold_in(key, 17), N_SLAB * N_DOM)
    orders = jax.vmap(chain_order)(device_keys).astype(jnp.int32)
    bond_left = orders[:, :BONDS_DEV]
    bond_partner_right = orders[:, 1:BONDS_DEV + 1]
    return jnp.stack([bond_left, bond_partner_right]).reshape(2, N_SLAB, N_DOM, BONDS_DEV)


def place_ends(values, key, low, high):
    shape = values.shape
    index_at = [jax.random.randint(jax.random.fold_in(key, axis), (), 0, shape[axis]) for axis in range(len(shape))]
    values = values.at[tuple(index_at)].set(low)
    longest = shape.index(max(shape))
    index_at[longest] = (index_at[longest] + 1) % shape[longest]
    return values.at[tuple(index_at)].set(high)


def shard_levels(own_key, shape, cuts, low, top_value):
    level = 1.0
    for axis_at, shards_of in cuts:
        heights = jax.random.uniform(jax.random.fold_in(jax.random.fold_in(own_key, 6), axis_at), (shards_of,), jnp.float32, low / len(cuts), top_value / len(cuts))
        level = level * jnp.repeat(jnp.exp(heights), shape[axis_at] // shards_of).reshape((-1,) + (1,) * (len(shape) - 1 - axis_at))
    return level


def bell_draw(stream_key, dims, deviation, limit, cuts=(), kind=jnp.bfloat16):
    result = jax.random.normal(stream_key, dims, jnp.float32) * deviation
    if len(cuts) > 0:
        result = shard_levels(stream_key, dims, cuts, -0.22, 0.18) * result
    return jnp.clip(result, min=-limit, max=limit).astype(kind)


def setup_inputs(seed: int = 0) -> dict:
    splits = jax.random.split(jax.random.key(seed), 12)
    return {
        "coords": bell_draw(splits[0], (3, N_SLAB, N_DOM, ATOMS_DEV), 1.0, 6.0, ((1, 4), (2, 8)), jnp.float32),
        "velocity": bell_draw(splits[1], (3, N_SLAB, N_DOM, ATOMS_DEV), 1.0, 6.0, ((1, 4), (2, 8)), jnp.float32),
        "charge": jnp.clip(jax.random.uniform(splits[2], (N_SLAB, N_DOM, ATOMS_DEV), jnp.float32, -1.0, 1.0) * shard_levels(splits[2], (N_SLAB, N_DOM, ATOMS_DEV), ((0, 4), (1, 8)), -0.4, 0.0), -1.0, 1.0),
        "inv_mass": jnp.clip(jnp.exp(math.log(1.0) - 2.7725887 * jax.random.uniform(splits[3], (N_SLAB, N_DOM, ATOMS_DEV), jnp.float32) ** shard_levels(splits[3], (N_SLAB, N_DOM, ATOMS_DEV), ((0, 4), (1, 8)), -0.2, 0.2)), 0.0625, 1.0),
        "tile_block": place_ends(jax.random.randint(splits[4], (N_SLAB, N_DOM, TILES_DEV), 0, ATOMS_DEV // TILE), jax.random.fold_in(splits[4], 1), 0, (ATOMS_DEV // TILE) - 1).astype(jnp.int32),
        "tile_atoms": place_ends(jax.random.randint(splits[5], (N_SLAB, N_DOM, TILES_DEV, TILE), 0, ATOMS_DEV + 6 * SHELL), jax.random.fold_in(splits[5], 1), 0, (ATOMS_DEV + 6 * SHELL) - 1).astype(jnp.int32),
        "active_tile_count": place_ends(jax.random.randint(splits[6], (N_SLAB, N_DOM), 1, TILES_DEV + 1), jax.random.fold_in(splits[6], 1), 1, TILES_DEV).astype(jnp.int32),
        "bond_atoms": draw_bond_atoms(jax.random.fold_in(splits[11], 71), 0),
        "cross_atoms": place_ends(jax.random.randint(splits[8], (2, N_SLAB, N_DOM, CROSS_CAP), 0, SHELL), jax.random.fold_in(splits[8], 1), 0, SHELL - 1).astype(jnp.int32),
        "cross_side": place_ends(jax.random.randint(splits[9], (N_SLAB, N_DOM, CROSS_CAP), 0, 4), jax.random.fold_in(splits[9], 1), 0, 3).astype(jnp.int32),
        "cross_count": place_ends(jax.random.randint(splits[10], (N_SLAB, N_DOM), 1, CROSS_CAP + 1), jax.random.fold_in(splits[10], 1), 1, CROSS_CAP).astype(jnp.int32),
    }


time_step = 0.1
cutoff_sq = 16.0
force_scale = 4.0
length_floor = 0.25

def tile_force(own_data, halo_data, block_index, atom_ids, tile_index, live_count):
    near_data = lax.dynamic_slice_in_dim(own_data, block_index * TILE, TILE, 1)
    far_data = jnp.take(halo_data, atom_ids, axis=1)
    offset_vec = near_data[:3, :, None] - far_data[:3, None, :]
    dist_sq = lax.optimization_barrier(jnp.sum(offset_vec * offset_vec, axis=0))
    inverse = 1.0 / (dist_sq + 1.0)
    switch = jnp.maximum(1.0 - dist_sq / cutoff_sq, 0.0) ** 2
    strength = force_scale * (2.0 * inverse ** 3 - near_data[3][:, None] * far_data[3][None, :] * inverse ** 2) * switch
    forces = lax.optimization_barrier(jnp.sum(strength[None] * offset_vec, axis=2))
    return forces * (tile_index < live_count).astype(jnp.float32)

def block_sum(tile_wise_values, block_ids, atom_count):
    pick_entries = (block_ids[:, None] == jnp.arange(atom_count // TILE, dtype=jnp.int32)[None, :]).astype(jnp.float32)
    accumulated_sum = jnp.einsum('mz,max->azx', pick_entries, tile_wise_values, precision=lax.Precision.HIGHEST)
    return accumulated_sum.reshape(3, atom_count)

def geometry(atom_first, atom_second, mass_first, mass_second):
    offset_vec = atom_first - atom_second
    length = jnp.sqrt(lax.optimization_barrier(jnp.sum(offset_vec * offset_vec, axis=0)) + length_floor)
    return (offset_vec / length, lax.rsqrt(mass_first + mass_second))

def project_bond(direction, bond_scale, atom_first, atom_second):
    return bond_scale * lax.optimization_barrier(jnp.sum(direction * (atom_first - atom_second), axis=0))

def reference(coords, velocity, charge, inv_mass, tile_block, tile_atoms, active_tile_count, bond_atoms, cross_atoms, cross_side, cross_count):
    slab_count, domains, atom_count = (coords.shape[1], coords.shape[2], coords.shape[3])
    devices = slab_count * domains
    shell_size = atom_count // 2
    row_width = max(2, domains // 8)
    strides = (1, -1, row_width, -row_width)
    own_data = jnp.concatenate([coords, charge[None], inv_mass[None]], axis=0)
    outer_rim = own_data[..., :shell_size]
    pieces = [own_data] + [jnp.roll(outer_rim, -stride, axis=2) for stride in strides]
    pieces = pieces + [jnp.roll(outer_rim, 1, axis=1), jnp.roll(outer_rim, -1, axis=1)]
    halo_data = jnp.concatenate(pieces, axis=3)
    own_flat = jnp.moveaxis(own_data.reshape(5, devices, atom_count), 1, 0)
    halo_flat = jnp.moveaxis(halo_data.reshape(5, devices, -1), 1, 0)

    def device_forces(packed):
        own_one, halo_one, block_ids, atom_ids, live_count = packed
        tile_ids = jnp.arange(block_ids.shape[0], dtype=jnp.int32)
        tile_wise_values = jax.vmap(tile_force, in_axes=(None, None, 0, 0, 0, None))(own_one, halo_one, block_ids, atom_ids, tile_ids, live_count)
        return block_sum(tile_wise_values, block_ids, atom_count)
    forces = lax.map(device_forces, (own_flat, halo_flat, tile_block.reshape(devices, -1), tile_atoms.reshape(devices, -1, TILE), active_tile_count.reshape(devices)))
    forces = jnp.moveaxis(forces, 0, 1).reshape(3, slab_count, domains, atom_count)
    velocity_half = velocity + time_step * forces * inv_mass[None]
    displace = time_step * velocity_half
    updated_positions = coords + displace
    total_atoms = devices * atom_count
    flat_coords = coords.reshape(3, total_atoms)
    flattened_masses = inv_mass.reshape(total_atoms)
    flat_displace = displace.reshape(3, total_atoms)
    device_ids = jnp.arange(devices, dtype=jnp.int32)
    offset_base = (device_ids * atom_count)[:, None]
    bond_left = (bond_atoms[0].reshape(devices, -1) + offset_base).reshape(-1)
    bond_partner_right = (bond_atoms[1].reshape(devices, -1) + offset_base).reshape(-1)
    stride_table = jnp.array(strides, dtype=jnp.int32)
    side_code = cross_side.reshape(devices, -1)
    dom_index = (device_ids % domains)[:, None]
    layer_slab_number = (device_ids // domains)[:, None]
    other_device = layer_slab_number * domains + (dom_index + stride_table[side_code]) % domains
    cross_first = (cross_atoms[0].reshape(devices, -1) + offset_base).reshape(-1)
    cross_second = (other_device * atom_count + cross_atoms[1].reshape(devices, -1)).reshape(-1)
    slot_ids = jnp.arange(side_code.shape[1], dtype=jnp.int32)[None, :]
    cross_flag = (slot_ids < cross_count.reshape(devices, 1)).astype(jnp.float32).reshape(-1)
    atom_first = jnp.concatenate([bond_left, cross_first])
    atom_second = jnp.concatenate([bond_partner_right, cross_second])
    live_mask = jnp.concatenate([jnp.ones(bond_left.shape, jnp.float32), cross_flag])
    direction, bond_scale = geometry(flat_coords[:, atom_first], flat_coords[:, atom_second], flattened_masses[atom_first], flattened_masses[atom_second])
    residue = project_bond(direction, bond_scale, flat_displace[:, atom_first], flat_displace[:, atom_second]) * live_mask

    def collect(values):
        pushed = direction * (bond_scale * values)
        totals = jnp.zeros((3, total_atoms), jnp.float32).at[:, atom_first].add(pushed).at[:, atom_second].add(-pushed)
        return flattened_masses * totals
    accumulated_sum = residue
    for expansion in range(ORDER):
        spread_now = collect(residue)
        residue = residue - project_bond(direction, bond_scale, spread_now[:, atom_first], spread_now[:, atom_second]) * live_mask
        accumulated_sum = accumulated_sum + residue
    correction = collect(accumulated_sum).reshape(3, slab_count, domains, atom_count)
    return (updated_positions - correction, velocity_half - correction / time_step)
```

```python
import functools

import jax
import jax.numpy as jnp
from jax import lax
from jax.experimental import pallas as pl
from jax.experimental.pallas import tpu as pltpu
from jax.sharding import PartitionSpec as P

TILE = 128
ORDER = 4
LANES = 128
SUBLANES = 8

time_step = 0.1
cutoff_sq = 16.0
force_scale = 4.0
length_floor = 0.25

VMEM_LIMIT = 48 * 1024 * 1024


def passed_along(array, axis, by):
    length = lax.axis_size(axis)
    return lax.ppermute(array, axis, [(i, (i + by) % length) for i in range(length)])


def strides_of(domains):
    row_width = max(2, domains // 8)
    return (1, -1, row_width, -row_width)


def round_up(count, step):
    return -(-count // step) * step


class Rows:
    def __init__(self, atoms, bonds, slots):
        self.atom_rows = atoms // LANES
        self.shell_rows = atoms // 2 // LANES
        self.bond_rows = bonds // LANES
        self.slot_rows = slots // LANES
        at = 0
        self.coords = []
        for _ in range(3):
            self.coords.append(at)
            at += self.atom_rows
        self.charge = at
        at += self.atom_rows
        self.mass = at
        at += self.atom_rows
        self.bond_first = at
        at += self.bond_rows
        self.bond_second = at
        at += self.bond_rows
        self.cross_first = at
        at += self.slot_rows
        self.cross_second = at
        at += self.slot_rows
        self.side = at
        at += self.slot_rows
        self.live = at
        at += self.slot_rows
        self.used = at
        self.count = round_up(at, SUBLANES)
        self.disp_used = 3 * self.atom_rows
        self.disp_count = round_up(self.disp_used, SUBLANES)


def take_lanes(table, lanes):
    return jnp.take_along_axis(table, lanes, axis=1, mode="promise_in_bounds")


def pick(tables, index):
    lanes = index & (LANES - 1)
    chunk = index >> 7
    result = take_lanes(tables[0], lanes)
    for k in range(1, len(tables)):
        result = jnp.where(chunk == k, take_lanes(tables[k], lanes), result)
    return result


def rsqrt(value):
    guess = lax.rsqrt(value)
    return guess * (1.5 - 0.5 * value * guess * guess)


def pack_kernel(
    rows, copies, count_ref, coords_ref, charge_ref, mass_ref, bonds_ref, cross_ref, side_ref, out_ref, rim_ref
):
    def put(row, value):
        for part in range(value.shape[1] // LANES):
            piece = value[:, part * LANES : (part + 1) * LANES]
            for copy in range(copies):
                out_ref[pl.ds(copy * rows.count + row + part, 1), :] = piece

    shell = rows.shell_rows * LANES
    fields = [coords_ref[c, 0] for c in range(3)] + [charge_ref[0]]
    for c in range(4):
        at = rows.coords[c] if c < 3 else rows.charge
        put(at, fields[c])
        for part in range(rows.shell_rows):
            rim_ref[pl.ds(c * rows.shell_rows + part, 1), :] = fields[c][:, part * LANES : (part + 1) * LANES]
    put(rows.mass, mass_ref[0])
    put(rows.bond_first, bonds_ref[0, 0].astype(jnp.float32))
    put(rows.bond_second, bonds_ref[1, 0].astype(jnp.float32))
    put(rows.cross_first, cross_ref[0, 0].astype(jnp.float32))
    put(rows.cross_second, cross_ref[1, 0].astype(jnp.float32))
    side = side_ref[0]
    put(rows.side, side.astype(jnp.float32))
    slot = lax.broadcasted_iota(jnp.int32, side.shape, 1)
    put(rows.live, jnp.where(slot < count_ref[0, 0], 1.0, 0.0))
    if rows.count > rows.used:
        for copy in range(copies):
            out_ref[pl.ds(copy * rows.count + rows.used, rows.count - rows.used), :] = jnp.zeros(
                (rows.count - rows.used, LANES), jnp.float32
            )


def force_kernel(
    rows,
    copies,
    holders,
    here_ref,
    live_ref,
    block_ref,
    around_ref,
    below_ref,
    above_ref,
    velocity_ref,
    atoms_ref,
    out_ref,
    table_ref,
    far_ref,
    own_ref,
    sum_ref,
):
    atom_rows, shell_rows = rows.atom_rows, rows.shell_rows
    tiles = atoms_ref.shape[2]
    me = here_ref[0]
    starts = [rows.coords[0], rows.coords[1], rows.coords[2], rows.charge]
    entry_rows = atom_rows + 6 * shell_rows
    blocks = around_ref.shape[0] // rows.count
    shrink = 1.0 / 4.0

    def broadcast(row):
        return jnp.broadcast_to(row, (SUBLANES, LANES))

    for c in range(4):
        factor = shrink if c < 3 else 1.0
        at = 0
        for part in range(atom_rows):
            table_ref[c, at] = broadcast(around_ref[pl.ds(me * rows.count + starts[c] + part, 1), :] * factor)
            at += 1
        for neighbour in range(4):
            base = lax.rem(me + holders[neighbour], blocks) * rows.count + starts[c]
            for part in range(shell_rows):
                table_ref[c, at] = broadcast(around_ref[pl.ds(base + part, 1), :] * factor)
                at += 1
        for slab_ref in (below_ref, above_ref):
            for part in range(shell_rows):
                table_ref[c, at] = broadcast(slab_ref[pl.ds(c * shell_rows + part, 1), :] * factor)
                at += 1

    for group in range(tiles // SUBLANES):
        index = atoms_ref[0, 0, pl.ds(group * SUBLANES, SUBLANES), :]
        lanes = index & (LANES - 1)
        chunk = index >> 7
        values = [take_lanes(table_ref[c, 0], lanes) for c in range(4)]
        for k in range(1, entry_rows):
            here = chunk == k
            values = [jnp.where(here, take_lanes(table_ref[c, k], lanes), values[c]) for c in range(4)]
        for c in range(4):
            far_ref[c, pl.ds(group * SUBLANES, SUBLANES), :] = values[c]

    down = lax.broadcasted_iota(jnp.int32, (SUBLANES, LANES), 0)
    zero = jnp.zeros((SUBLANES, LANES), jnp.float32)
    for part in range(atom_rows):
        for group in range(LANES // SUBLANES):
            at = part * LANES + group * SUBLANES
            for c in range(4):
                value = take_lanes(table_ref[c, part], down + group * SUBLANES)
                own_ref[c, pl.ds(at, SUBLANES), :] = value if c < 3 else value * 8.0
            for c in range(3):
                sum_ref[c, pl.ds(at, SUBLANES), :] = zero

    def add_tile(tile, _):
        base = block_ref[0, 0, tile] * TILE
        far = [broadcast(far_ref[c, pl.ds(tile, 1), :]) for c in range(4)]
        for group in range(TILE // SUBLANES):
            at = pl.ds(pl.multiple_of(base + group * SUBLANES, SUBLANES), SUBLANES)
            gap = [own_ref[c, at, :] - far[c] for c in range(3)]
            square = gap[0] * gap[0] + gap[1] * gap[1] + gap[2] * gap[2]
            shifted = square + 1.0 / cutoff_sq
            inverse = pl.reciprocal(shifted, approx=True)
            inverse = inverse * (2.0 - shifted * inverse)
            switch = jnp.maximum(1.0 - square, 0.0)
            weight = inverse * switch
            strength = (inverse - own_ref[3, at, :] * far[3]) * (weight * weight)
            for c in range(3):
                sum_ref[c, at, :] = sum_ref[c, at, :] + strength * gap[c]
        return 0

    lax.fori_loop(0, live_ref[0, 0], add_tile, 0)

    scale = time_step * time_step * force_scale * 4.0 / 2048.0
    for c in range(3):
        speed = velocity_ref[c, 0]
        for part in range(atom_rows):
            total = jnp.sum(sum_ref[c, pl.ds(part * LANES, LANES), :].T, axis=0, keepdims=True)
            mass = around_ref[pl.ds(me * rows.count + rows.mass + part, 1), :]
            moved = time_step * speed[:, part * LANES : (part + 1) * LANES] + scale * total * mass
            for copy in range(copies):
                out_ref[pl.ds(copy * rows.disp_count + c * atom_rows + part, 1), :] = moved
    if rows.disp_count > rows.disp_used:
        for copy in range(copies):
            out_ref[pl.ds(copy * rows.disp_count + rows.disp_used, rows.disp_count - rows.disp_used), :] = jnp.zeros(
                (rows.disp_count - rows.disp_used, LANES), jnp.float32
            )


def bond_kernel(rows, domains, strides, around_ref, weight_ref, inner_ref, cross_ref, key_ref):
    atom_rows, shell_rows = rows.atom_rows, rows.shell_rows

    def load(row):
        return around_ref[pl.ds(row, domains, stride=rows.count), :]

    def index(row):
        return load(row).astype(jnp.int32)

    fields = [[load(at + part) for part in range(atom_rows)] for at in rows.coords + [rows.mass]]

    def weights(first, second, row):
        gap = [first[c] - second[c] for c in range(3)]
        length_sq = gap[0] * gap[0] + gap[1] * gap[1] + gap[2] * gap[2] + length_floor
        scale = rsqrt(length_sq) * rsqrt(first[3] + second[3])
        return [gap[c] * scale for c in range(3)]

    at = 0
    for part in range(rows.bond_rows):
        first = index(rows.bond_first + part)
        second = index(rows.bond_second + part)
        values = weights([pick(f, first) for f in fields], [pick(f, second) for f in fields], at)
        for c in range(3):
            weight_ref[pl.ds((at * 3 + c) * domains, domains), :] = values[c]
        at += 1
    for part in range(rows.slot_rows):
        first = index(rows.cross_first + part)
        second = index(rows.cross_second + part)
        side = load(rows.side + part)
        live = load(rows.live + part)
        other = [jnp.zeros((domains, LANES), jnp.float32) for _ in range(4)]
        for code, stride in enumerate(strides):
            seen = pltpu.roll(second, stride % domains, 0)
            for f in range(4):
                value = pltpu.roll(pick(fields[f][:shell_rows], seen), -stride % domains, 0)
                other[f] = jnp.where(side == code, value, other[f])
            key = jnp.where(side == code, load(rows.cross_second + part), -1.0)
            key_ref[pl.ds((part * 4 + code) * domains, domains), :] = key
        values = weights([pick(f[:shell_rows], first) for f in fields], other, at)
        for c in range(3):
            weight_ref[pl.ds((at * 3 + c) * domains, domains), :] = values[c] * live
        at += 1

    down = lax.broadcasted_iota(jnp.int32, (SUBLANES, LANES), 0)
    across = lax.broadcasted_iota(jnp.int32, (SUBLANES, LANES), 1).astype(jnp.float32)
    pair = 2 * SUBLANES

    def column(row, group):
        return take_lanes(jnp.broadcast_to(row, (SUBLANES, LANES)), down + group * SUBLANES)

    def one_hot(values, part):
        return jnp.where(values == across + float(part * LANES), 1.0, 0.0)

    def build(domain, _):
        for part in range(rows.bond_rows):
            first = around_ref[pl.ds(domain * rows.count + rows.bond_first + part, 1), :]
            second = around_ref[pl.ds(domain * rows.count + rows.bond_second + part, 1), :]
            for step in range(LANES // pair):
                ends = [(column(first, 2 * step + h), column(second, 2 * step + h)) for h in range(2)]
                at = pl.multiple_of((domain * rows.bond_rows + part) * LANES + step * pair, pair)
                for block in range(atom_rows):
                    halves = [one_hot(a, block) - one_hot(b, block) for a, b in ends]
                    inner_ref[pl.ds(at, pair), block * LANES : (block + 1) * LANES] = jnp.concatenate(
                        halves, axis=0
                    ).astype(jnp.bfloat16)
        for part in range(rows.slot_rows):
            for code in range(5):
                if code == 0:
                    row = around_ref[pl.ds(domain * rows.count + rows.cross_first + part, 1), :]
                else:
                    owner = lax.rem(domain + (-strides[code - 1]) % domains, domains)
                    row = key_ref[pl.ds((part * 4 + code - 1) * domains + owner, 1), :]
                sign = 1.0 if code == 0 else -1.0
                for step in range(LANES // pair):
                    ends = [column(row, 2 * step + h) for h in range(2)]
                    at = pl.multiple_of(((domain * rows.slot_rows + part) * 5 + code) * LANES + step * pair, pair)
                    for block in range(shell_rows):
                        halves = [sign * one_hot(a, block) for a in ends]
                        cross_ref[pl.ds(at, pair), block * LANES : (block + 1) * LANES] = jnp.concatenate(
                            halves, axis=0
                        ).astype(jnp.bfloat16)
        return 0

    lax.fori_loop(0, domains, build, 0)


def solve_kernel(
    rows,
    domains,
    strides,
    here_ref,
    around_ref,
    moves_ref,
    weight_ref,
    inner_ref,
    cross_ref,
    coords_out_ref,
    velocity_out_ref,
    push_ref,
    field_ref,
):
    atom_rows, shell_rows = rows.atom_rows, rows.shell_rows
    bond_rows, slot_rows = rows.bond_rows, rows.slot_rows
    me = here_ref[0]

    def load(row):
        return around_ref[pl.ds(row, domains, stride=rows.count), :]

    def index(row):
        return load(row).astype(jnp.int32)

    inner_first = [index(rows.bond_first + p) for p in range(bond_rows)]
    inner_second = [index(rows.bond_second + p) for p in range(bond_rows)]
    cross_first = [index(rows.cross_first + p) for p in range(slot_rows)]
    cross_second = [index(rows.cross_second + p) for p in range(slot_rows)]
    sides = [load(rows.side + p) for p in range(slot_rows)]
    masses = [load(rows.mass + p) for p in range(atom_rows)]

    def weight(at, c):
        return weight_ref[pl.ds((at * 3 + c) * domains, domains), :]

    def project(fields):
        result = []
        for part in range(bond_rows):
            total = 0.0
            for c in range(3):
                ends = pick(fields[c], inner_first[part]) - pick(fields[c], inner_second[part])
                total = total + weight(part, c) * ends
            result.append(total)
        for part in range(slot_rows):
            seen = [pltpu.roll(cross_second[part], stride % domains, 0) for stride in strides]
            total = 0.0
            for c in range(3):
                shell = fields[c][:shell_rows]
                other = 0.0
                for code, stride in enumerate(strides):
                    value = pltpu.roll(pick(shell, seen[code]), -stride % domains, 0)
                    other = jnp.where(sides[part] == code, value, other)
                total = total + weight(bond_rows + part, c) * (pick(shell, cross_first[part]) - other)
            result.append(total)
        return result

    def put_pushes(values):
        for at, value in enumerate(values):
            for c in range(3):
                pushed = weight(at, c) * value
                high = pushed.astype(jnp.bfloat16).astype(jnp.float32)
                push_ref[at, pl.ds(c * domains, domains), :] = high
                push_ref[at, pl.ds((3 + c) * domains, domains), :] = pushed - high

    def pushes_of(at, domain):
        return push_ref[at, pl.ds(domain, SUBLANES, stride=domains), :].astype(jnp.bfloat16)

    def totals(domain, owners):
        inner = jnp.concatenate([pushes_of(p, domain) for p in range(bond_rows)], axis=1)
        at = domain * bond_rows * LANES
        if not isinstance(at, int):
            at = pl.multiple_of(at, LANES)
        inner_sum = jnp.dot(inner, inner_ref[pl.ds(at, bond_rows * LANES), :], preferred_element_type=jnp.float32)
        pieces = []
        for part in range(slot_rows):
            pieces.extend(pushes_of(bond_rows + part, owner) for owner in [domain] + owners)
        cross = jnp.concatenate(pieces, axis=1)
        at = domain * slot_rows * 5 * LANES
        if not isinstance(at, int):
            at = pl.multiple_of(at, LANES)
        cross_sum = jnp.dot(
            cross, cross_ref[pl.ds(at, slot_rows * 5 * LANES), :], preferred_element_type=jnp.float32
        )
        shell = shell_rows * LANES
        return [
            inner_sum[:, p * LANES : (p + 1) * LANES]
            + (cross_sum[:, p * LANES : (p + 1) * LANES] if p < shell_rows else 0.0)
            for p in range(atom_rows)
        ]

    def spread(values):
        put_pushes(values)
        for domain in range(domains):
            sums = totals(domain, [(domain - stride) % domains for stride in strides])
            for part in range(atom_rows):
                field_ref[part, pl.ds(domain, SUBLANES, stride=domains), :] = sums[part]
        return [
            [
                masses[part]
                * (
                    field_ref[part, pl.ds(c * domains, domains), :]
                    + field_ref[part, pl.ds((3 + c) * domains, domains), :]
                )
                for part in range(atom_rows)
            ]
            for c in range(3)
        ]

    moves = [
        [moves_ref[pl.ds(c * atom_rows + p, domains, stride=rows.disp_count), :] for p in range(atom_rows)]
        for c in range(3)
    ]
    push_ref[...] = jnp.zeros(push_ref.shape, jnp.float32)
    residue = project(moves)

    def expand(_, carry):
        residue, summed = carry
        change = project(spread(residue))
        residue = [now - step for now, step in zip(residue, change)]
        return residue, [a + b for a, b in zip(summed, residue)]

    residue, summed = lax.fori_loop(0, ORDER, expand, (residue, residue))
    put_pushes(summed)
    sums = totals(me, [lax.rem(me + (-stride) % domains, domains) for stride in strides])
    for part in range(atom_rows):
        lanes = slice(part * LANES, (part + 1) * LANES)
        mass = around_ref[pl.ds(me * rows.count + rows.mass + part, 1), :]
        for c in range(3):
            correction = mass * (sums[part][c : c + 1, :] + sums[part][3 + c : 4 + c, :])
            move = moves_ref[pl.ds(me * rows.disp_count + c * atom_rows + part, 1), :] - correction
            start = around_ref[pl.ds(me * rows.count + rows.coords[c] + part, 1), :]
            coords_out_ref[c, 0, :, lanes] = start + move
            velocity_out_ref[c, 0, :, lanes] = move * (1.0 / time_step)


def vmem(count):
    return [pl.BlockSpec(memory_space=pltpu.VMEM)] * count


def smem(count):
    return [pl.BlockSpec(memory_space=pltpu.SMEM)] * count


def params():
    return pltpu.CompilerParams(vmem_limit_bytes=VMEM_LIMIT)


def cost(flops, moved):
    return pl.CostEstimate(flops=flops, bytes_accessed=moved, transcendentals=0)


def shards(
    coords,
    velocity,
    charge,
    inv_mass,
    tile_block,
    tile_atoms,
    active_tile_count,
    bond_atoms,
    cross_atoms,
    cross_side,
    cross_count,
):
    atoms = coords.shape[-1]
    tiles = tile_atoms.shape[2]
    domains = lax.axis_size("dom")
    strides = strides_of(domains)
    rows = Rows(atoms, bond_atoms.shape[-1], cross_side.shape[-1])
    whole_slab = domains == SUBLANES
    copies = domains if whole_slab else 1
    f32 = jnp.float32

    packed, rim = pl.pallas_call(
        functools.partial(pack_kernel, rows, copies),
        out_shape=(
            jax.ShapeDtypeStruct((copies * rows.count, LANES), f32),
            jax.ShapeDtypeStruct((4 * rows.shell_rows, LANES), f32),
        ),
        in_specs=smem(1) + vmem(6),
        out_specs=tuple(vmem(2)),
        compiler_params=params(),
        name="pack",
    )(cross_count, coords, charge, inv_mass, bond_atoms, cross_atoms, cross_side)

    below = passed_along(rim, "slab", 1)
    above = passed_along(rim, "slab", -1)
    if whole_slab:
        around = lax.all_to_all(packed, "dom", 0, 0, tiled=True)
        here = lax.axis_index("dom").reshape(1)
        holders = [stride % domains for stride in strides]
    else:
        around = jnp.concatenate([packed] + [passed_along(packed, "dom", -stride) for stride in strides], axis=0)
        here = jnp.zeros(1, jnp.int32)
        holders = [1, 2, 3, 4]

    entry_rows = rows.atom_rows + 6 * rows.shell_rows
    moves = pl.pallas_call(
        functools.partial(force_kernel, rows, copies, holders),
        out_shape=jax.ShapeDtypeStruct((copies * rows.disp_count, LANES), f32),
        in_specs=smem(3) + vmem(5),
        out_specs=vmem(1)[0],
        scratch_shapes=[
            pltpu.VMEM((4, entry_rows, SUBLANES, LANES), f32),
            pltpu.VMEM((4, tiles, LANES), f32),
            pltpu.VMEM((4, atoms, LANES), f32),
            pltpu.VMEM((3, atoms, LANES), f32),
        ],
        compiler_params=params(),
        cost_estimate=cost(30 * tiles * TILE * TILE, 4 * around.size),
        name="force",
    )(here, active_tile_count, tile_block, around, below, above, velocity, tile_atoms)

    if not whole_slab:
        return by_exchange(rows, strides, around, moves, cross_count)

    constraint_rows = rows.bond_rows + rows.slot_rows
    weight, inner, cross = pl.pallas_call(
        functools.partial(bond_kernel, rows, domains, strides),
        out_shape=(
            jax.ShapeDtypeStruct((constraint_rows * 3 * domains, LANES), f32),
            jax.ShapeDtypeStruct((domains * rows.bond_rows * LANES, atoms), jnp.bfloat16),
            jax.ShapeDtypeStruct((domains * rows.slot_rows * 5 * LANES, atoms // 2), jnp.bfloat16),
        ),
        in_specs=vmem(1),
        out_specs=tuple(vmem(3)),
        scratch_shapes=[pltpu.VMEM((rows.slot_rows * 4 * domains, LANES), f32)],
        compiler_params=params(),
        cost_estimate=cost(8 * domains * (rows.bond_rows * LANES * atoms + rows.slot_rows * 5 * LANES * atoms // 2), 4 * around.size),
        name="bonds",
    )(around)

    every_move = lax.all_to_all(moves, "dom", 0, 0, tiled=True)

    return pl.pallas_call(
        functools.partial(solve_kernel, rows, domains, strides),
        out_shape=(
            jax.ShapeDtypeStruct(coords.shape, f32),
            jax.ShapeDtypeStruct(coords.shape, f32),
        ),
        in_specs=smem(1) + vmem(5),
        out_specs=tuple(vmem(2)),
        scratch_shapes=[
            pltpu.VMEM((constraint_rows, SUBLANES * domains, LANES), f32),
            pltpu.VMEM((rows.atom_rows, SUBLANES * domains, LANES), f32),
        ],
        compiler_params=params(),
        name="solve",
    )(here, around, every_move, weight, inner, cross)


def by_exchange(rows, strides, around, moves, cross_count):
    atom_count = rows.atom_rows * LANES
    shell = rows.shell_rows * LANES
    inside = around.reshape(5, rows.count, LANES)

    def flat(at, count):
        return inside[0, at : at + count].reshape(-1)

    def neighbours(at):
        return inside[1:, at : at + rows.shell_rows].reshape(-1)

    coords = jnp.stack([flat(at, rows.atom_rows) for at in rows.coords])
    inv_mass = flat(rows.mass, rows.atom_rows)
    displace = moves[: rows.disp_used].reshape(3, atom_count)
    left = flat(rows.bond_first, rows.bond_rows).astype(jnp.int32)
    right = flat(rows.bond_second, rows.bond_rows).astype(jnp.int32)
    cross_left = flat(rows.cross_first, rows.slot_rows).astype(jnp.int32)
    cross_right = flat(rows.cross_second, rows.slot_rows).astype(jnp.int32)
    side = flat(rows.side, rows.slot_rows).astype(jnp.int32)
    flag = flat(rows.live, rows.slot_rows)
    cross_index = side * shell + cross_right
    far_coords = jnp.stack([neighbours(at) for at in rows.coords])
    far_mass = neighbours(rows.mass)

    def weights(first, second, mass_first, mass_second):
        gap = first - second
        length = jnp.sqrt(jnp.sum(gap * gap, axis=0) + length_floor)
        return gap / length * lax.rsqrt(mass_first + mass_second)

    inner = weights(coords[:, left], coords[:, right], inv_mass[left], inv_mass[right])
    cross = flag * weights(
        coords[:, cross_left], far_coords[:, cross_index], inv_mass[cross_left], far_mass[cross_index]
    )

    def project(field):
        rim = field[:, :shell]
        far = jnp.concatenate([passed_along(rim, "dom", -stride) for stride in strides], axis=1)
        return (
            jnp.sum(inner * (field[:, left] - field[:, right]), axis=0),
            jnp.sum(cross * (field[:, cross_left] - far[:, cross_index]), axis=0),
        )

    def spread(values):
        pushed = inner * values[0]
        pushed_cross = cross * values[1]
        totals = jnp.zeros((3, atom_count), jnp.float32).at[:, left].add(pushed).at[:, right].add(-pushed)
        totals = totals.at[:, cross_left].add(pushed_cross)
        outward = jnp.zeros((3, 4 * shell), jnp.float32).at[:, cross_index].add(-pushed_cross)
        for code, stride in enumerate(strides):
            totals = totals.at[:, :shell].add(
                passed_along(outward[:, code * shell : (code + 1) * shell], "dom", stride)
            )
        return inv_mass * totals

    residue = project(displace)
    summed = residue
    for _ in range(ORDER):
        change = project(spread(residue))
        residue = tuple(now - step for now, step in zip(residue, change))
        summed = tuple(a + b for a, b in zip(summed, residue))
    move = displace - spread(summed)
    return (
        (coords + move).reshape(3, 1, 1, atom_count),
        (move * (1.0 / time_step)).reshape(3, 1, 1, atom_count),
    )


def solution(mesh):
    return jax.shard_map(
        shards,
        mesh=mesh,
        in_specs=(
            P(None, "slab", "dom", None),
            P(None, "slab", "dom", None),
            P("slab", "dom", None),
            P("slab", "dom", None),
            P("slab", "dom", None),
            P("slab", "dom", None, None),
            P("slab", "dom"),
            P(None, "slab", "dom", None),
            P(None, "slab", "dom", None),
            P("slab", "dom", None),
            P("slab", "dom"),
        ),
        out_specs=(P(None, "slab", "dom", None), P(None, "slab", "dom", None)),
        check_vma=False,
    )
```

```python
import functools

import jax
import jax.numpy as jnp
from jax import lax
from jax.experimental import pallas as pl
from jax.experimental.pallas import tpu as pltpu
from jax.sharding import PartitionSpec as P

TILE = 128
ORDER = 4
LANES = 128
SUBLANES = 8

time_step = 0.1
cutoff_sq = 16.0
force_scale = 4.0
length_floor = 0.25


def passed_along(array, axis, by):
    length = lax.axis_size(axis)
    return lax.ppermute(array, axis, [(i, (i + by) % length) for i in range(length)])


def strides_of(domains):
    row_width = max(2, domains // 8)
    return (1, -1, row_width, -row_width)


def round_up(count, step):
    return -(-count // step) * step


class Rows:
    def __init__(self, atoms, bonds, slots):
        self.atom_rows = atoms // LANES
        self.shell_rows = atoms // 2 // LANES
        self.bond_rows = bonds // LANES
        self.slot_rows = slots // LANES
        at = 0
        self.coords = []
        for _ in range(3):
            self.coords.append(at)
            at += self.atom_rows
        self.charge = at
        at += self.atom_rows
        self.mass = at
        at += self.atom_rows
        self.bond_first = at
        at += self.bond_rows
        self.bond_second = at
        at += self.bond_rows
        self.cross_first = at
        at += self.slot_rows
        self.cross_second = at
        at += self.slot_rows
        self.side = at
        at += self.slot_rows
        self.live = at
        at += self.slot_rows
        self.used = at
        self.count = round_up(at, SUBLANES)
        self.disp_used = 3 * self.atom_rows
        self.disp_count = round_up(self.disp_used, SUBLANES)


def take_lanes(table, lanes):
    return jnp.take_along_axis(table, lanes, axis=1, mode="promise_in_bounds")


def pick(tables, index):
    lanes = index & (LANES - 1)
    chunk = index >> 7
    result = take_lanes(tables[0], lanes)
    for k in range(1, len(tables)):
        result = jnp.where(chunk == k, take_lanes(tables[k], lanes), result)
    return result


def rsqrt(value):
    guess = lax.rsqrt(value)
    return guess * (1.5 - 0.5 * value * guess * guess)


def fetched(sources, targets, sem_ref):
    copies = [pltpu.make_async_copy(s, t, sem_ref.at[n]) for n, (s, t) in enumerate(zip(sources, targets))]
    for copy in copies:
        copy.start()
    return copies


def pack_kernel(rows, copies, count_ref, *refs):
    sources, (out_ref, rim_ref), targets, sem_ref = refs[:6], refs[6:8], refs[8:14], refs[14]
    for copy in fetched(sources, targets, sem_ref):
        copy.wait()
    coords_ref, charge_ref, mass_ref, bonds_ref, cross_ref, side_ref = targets

    def put(row, value):
        for part in range(value.shape[1] // LANES):
            piece = value[:, part * LANES : (part + 1) * LANES]
            for copy in range(copies):
                out_ref[pl.ds(copy * rows.count + row + part, 1), :] = piece

    shell = rows.shell_rows * LANES
    fields = [coords_ref[c, 0] for c in range(3)] + [charge_ref[0]]
    for c in range(4):
        at = rows.coords[c] if c < 3 else rows.charge
        put(at, fields[c])
        for part in range(rows.shell_rows):
            rim_ref[pl.ds(c * rows.shell_rows + part, 1), :] = fields[c][:, part * LANES : (part + 1) * LANES]
    put(rows.mass, mass_ref[0])
    put(rows.bond_first, bonds_ref[0, 0].astype(jnp.float32))
    put(rows.bond_second, bonds_ref[1, 0].astype(jnp.float32))
    put(rows.cross_first, cross_ref[0, 0].astype(jnp.float32))
    put(rows.cross_second, cross_ref[1, 0].astype(jnp.float32))
    side = side_ref[0]
    put(rows.side, side.astype(jnp.float32))
    slot = lax.broadcasted_iota(jnp.int32, side.shape, 1)
    put(rows.live, jnp.where(slot < count_ref[0, 0], 1.0, 0.0))
    if rows.count > rows.used:
        for copy in range(copies):
            out_ref[pl.ds(copy * rows.count + rows.used, rows.count - rows.used), :] = jnp.zeros(
                (rows.count - rows.used, LANES), jnp.float32
            )


SHRINK = 1.0 / 4.0


def own_kernel(
    rows, coords_hbm, charge_hbm, velocity_hbm, atoms_hbm, own_ref, far_ref, index_ref, speed_ref, coords_ref, charge_ref, velocity_ref, sem_ref
):
    atom_rows = rows.atom_rows
    copies = fetched(
        (coords_hbm, charge_hbm, atoms_hbm.at[0, 0], velocity_hbm),
        (coords_ref, charge_ref, index_ref, velocity_ref),
        sem_ref,
    )
    down = lax.broadcasted_iota(jnp.int32, (SUBLANES, LANES), 0)
    copies[0].wait()
    copies[1].wait()

    def lanes_of(part):
        return slice(part * LANES, (part + 1) * LANES)

    table = []
    for c in range(4):
        field = coords_ref[c, 0] * SHRINK if c < 3 else charge_ref[0]
        table.append(
            [jnp.broadcast_to(field[:, lanes_of(part)], (SUBLANES, LANES)) for part in range(atom_rows)]
        )
    for part in range(atom_rows):
        for group in range(LANES // SUBLANES):
            at = part * LANES + group * SUBLANES
            for c in range(4):
                value = take_lanes(table[c][part], down + group * SUBLANES)
                own_ref[c, pl.ds(at, SUBLANES), :] = value if c < 3 else value * 8.0
    copies[2].wait()
    for group in range(index_ref.shape[0] // SUBLANES):
        at = pl.ds(group * SUBLANES, SUBLANES)
        index = index_ref[at, :]
        for c in range(4):
            far_ref[c, at, :] = pick(table[c], index)
    copies[3].wait()
    for c in range(3):
        for part in range(atom_rows):
            speed_ref[pl.ds(c * atom_rows + part, 1), :] = velocity_ref[c, 0, :, lanes_of(part)]


def force_kernel(
    rows,
    copies,
    holders,
    here_ref,
    live_ref,
    block_hbm,
    around_ref,
    below_ref,
    above_ref,
    own_ref,
    near_ref,
    index_ref,
    speed_ref,
    out_ref,
    table_ref,
    far_ref,
    sum_ref,
    block_ref,
    sem_ref,
):
    atom_rows, shell_rows = rows.atom_rows, rows.shell_rows
    tiles = index_ref.shape[0]
    block_copy = pltpu.make_async_copy(block_hbm, block_ref, sem_ref)
    block_copy.start()
    me = here_ref[0]
    starts = [rows.coords[0], rows.coords[1], rows.coords[2], rows.charge]
    entry_rows = 6 * shell_rows
    blocks = around_ref.shape[0] // rows.count

    def broadcast(row):
        return jnp.broadcast_to(row, (SUBLANES, LANES))

    for c in range(4):
        factor = SHRINK if c < 3 else 1.0
        at = 0
        for neighbour in range(4):
            base = lax.rem(me + holders[neighbour], blocks) * rows.count + starts[c]
            for part in range(shell_rows):
                table_ref[c, at] = broadcast(around_ref[pl.ds(base + part, 1), :] * factor)
                at += 1
        for slab_ref in (below_ref, above_ref):
            for part in range(shell_rows):
                table_ref[c, at] = broadcast(slab_ref[pl.ds(c * shell_rows + part, 1), :] * factor)
                at += 1

    for group in range(tiles // SUBLANES):
        at = pl.ds(group * SUBLANES, SUBLANES)
        index = index_ref[at, :]
        lanes = index & (LANES - 1)
        chunk = index >> 7
        values = [near_ref[c, at, :] for c in range(4)]
        for k in range(entry_rows):
            here = chunk == atom_rows + k
            values = [jnp.where(here, take_lanes(table_ref[c, k], lanes), values[c]) for c in range(4)]
        for c in range(4):
            far_ref[c, at, :] = values[c]

    sum_ref[...] = jnp.zeros(sum_ref.shape, jnp.float32)
    block_copy.wait()

    def add_tile(tile, _):
        base = block_ref[0, 0, tile] * TILE
        far = [broadcast(far_ref[c, pl.ds(tile, 1), :]) for c in range(4)]
        for group in range(TILE // SUBLANES):
            at = pl.ds(pl.multiple_of(base + group * SUBLANES, SUBLANES), SUBLANES)
            gap = [own_ref[c, at, :] - far[c] for c in range(3)]
            square = gap[0] * gap[0] + gap[1] * gap[1] + gap[2] * gap[2]
            shifted = square + 1.0 / cutoff_sq
            inverse = pl.reciprocal(shifted, approx=True)
            inverse = inverse * (2.0 - shifted * inverse)
            switch = jnp.maximum(1.0 - square, 0.0)
            weight = inverse * switch
            strength = (inverse - own_ref[3, at, :] * far[3]) * (weight * weight)
            for c in range(3):
                sum_ref[c, at, :] = sum_ref[c, at, :] + strength * gap[c]
        return 0

    lax.fori_loop(0, live_ref[0, 0], add_tile, 0)

    scale = time_step * time_step * force_scale * 4.0 / 2048.0
    for c in range(3):
        for part in range(atom_rows):
            total = jnp.sum(sum_ref[c, pl.ds(part * LANES, LANES), :].T, axis=0, keepdims=True)
            mass = around_ref[pl.ds(me * rows.count + rows.mass + part, 1), :]
            moved = time_step * speed_ref[pl.ds(c * atom_rows + part, 1), :] + scale * total * mass
            for copy in range(copies):
                out_ref[pl.ds(copy * rows.disp_count + c * atom_rows + part, 1), :] = moved
    if rows.disp_count > rows.disp_used:
        for copy in range(copies):
            out_ref[pl.ds(copy * rows.disp_count + rows.disp_used, rows.disp_count - rows.disp_used), :] = jnp.zeros(
                (rows.disp_count - rows.disp_used, LANES), jnp.float32
            )


def bond_kernel(rows, domains, strides, around_ref, weight_ref, inner_ref, cross_ref, key_ref):
    atom_rows, shell_rows = rows.atom_rows, rows.shell_rows

    def load(row):
        return around_ref[pl.ds(row, domains, stride=rows.count), :]

    def index(row):
        return load(row).astype(jnp.int32)

    fields = [[load(at + part) for part in range(atom_rows)] for at in rows.coords + [rows.mass]]

    def weights(first, second, row):
        gap = [first[c] - second[c] for c in range(3)]
        length_sq = gap[0] * gap[0] + gap[1] * gap[1] + gap[2] * gap[2] + length_floor
        scale = rsqrt(length_sq) * rsqrt(first[3] + second[3])
        return [gap[c] * scale for c in range(3)]

    at = 0
    for part in range(rows.bond_rows):
        first = index(rows.bond_first + part)
        second = index(rows.bond_second + part)
        values = weights([pick(f, first) for f in fields], [pick(f, second) for f in fields], at)
        for c in range(3):
            weight_ref[pl.ds((at * 3 + c) * domains, domains), :] = values[c]
        at += 1
    for part in range(rows.slot_rows):
        first = index(rows.cross_first + part)
        second = index(rows.cross_second + part)
        side = load(rows.side + part)
        live = load(rows.live + part)
        other = [jnp.zeros((domains, LANES), jnp.float32) for _ in range(4)]
        for code, stride in enumerate(strides):
            seen = pltpu.roll(second, stride % domains, 0)
            for f in range(4):
                value = pltpu.roll(pick(fields[f][:shell_rows], seen), -stride % domains, 0)
                other[f] = jnp.where(side == code, value, other[f])
            key = jnp.where(side == code, load(rows.cross_second + part), -1.0)
            key_ref[pl.ds((part * 4 + code) * domains, domains), :] = key
        values = weights([pick(f[:shell_rows], first) for f in fields], other, at)
        for c in range(3):
            weight_ref[pl.ds((at * 3 + c) * domains, domains), :] = values[c] * live
        at += 1

    down = lax.broadcasted_iota(jnp.int32, (SUBLANES, LANES), 0)
    across = lax.broadcasted_iota(jnp.int32, (SUBLANES, LANES), 1).astype(jnp.float32)
    pair = 2 * SUBLANES

    def column(row, group):
        return take_lanes(jnp.broadcast_to(row, (SUBLANES, LANES)), down + group * SUBLANES)

    def one_hot(values, part):
        return jnp.where(values == across + float(part * LANES), 1.0, 0.0)

    def build(domain, _):
        for part in range(rows.bond_rows):
            first = around_ref[pl.ds(domain * rows.count + rows.bond_first + part, 1), :]
            second = around_ref[pl.ds(domain * rows.count + rows.bond_second + part, 1), :]
            for step in range(LANES // pair):
                ends = [(column(first, 2 * step + h), column(second, 2 * step + h)) for h in range(2)]
                at = pl.multiple_of((domain * rows.bond_rows + part) * LANES + step * pair, pair)
                for block in range(atom_rows):
                    halves = [one_hot(a, block) - one_hot(b, block) for a, b in ends]
                    inner_ref[pl.ds(at, pair), block * LANES : (block + 1) * LANES] = jnp.concatenate(
                        halves, axis=0
                    ).astype(jnp.bfloat16)
        for part in range(rows.slot_rows):
            for code in range(5):
                if code == 0:
                    row = around_ref[pl.ds(domain * rows.count + rows.cross_first + part, 1), :]
                else:
                    owner = lax.rem(domain + (-strides[code - 1]) % domains, domains)
                    row = key_ref[pl.ds((part * 4 + code - 1) * domains + owner, 1), :]
                sign = 1.0 if code == 0 else -1.0
                for step in range(LANES // pair):
                    ends = [column(row, 2 * step + h) for h in range(2)]
                    at = pl.multiple_of(((domain * rows.slot_rows + part) * 5 + code) * LANES + step * pair, pair)
                    for block in range(shell_rows):
                        halves = [sign * one_hot(a, block) for a in ends]
                        cross_ref[pl.ds(at, pair), block * LANES : (block + 1) * LANES] = jnp.concatenate(
                            halves, axis=0
                        ).astype(jnp.bfloat16)
        return 0

    lax.fori_loop(0, domains, build, 0)


def solve_kernel(
    rows,
    domains,
    strides,
    here_ref,
    around_ref,
    moves_ref,
    weight_ref,
    inner_ref,
    cross_ref,
    coords_out_ref,
    velocity_out_ref,
    push_ref,
    field_ref,
):
    atom_rows, shell_rows = rows.atom_rows, rows.shell_rows
    bond_rows, slot_rows = rows.bond_rows, rows.slot_rows
    me = here_ref[0]

    def load(row):
        return around_ref[pl.ds(row, domains, stride=rows.count), :]

    def index(row):
        return load(row).astype(jnp.int32)

    inner_first = [index(rows.bond_first + p) for p in range(bond_rows)]
    inner_second = [index(rows.bond_second + p) for p in range(bond_rows)]
    cross_first = [index(rows.cross_first + p) for p in range(slot_rows)]
    cross_second = [index(rows.cross_second + p) for p in range(slot_rows)]
    sides = [load(rows.side + p) for p in range(slot_rows)]
    masses = [load(rows.mass + p) for p in range(atom_rows)]

    def weight(at, c):
        return weight_ref[pl.ds((at * 3 + c) * domains, domains), :]

    def project(fields):
        result = []
        for part in range(bond_rows):
            total = 0.0
            for c in range(3):
                ends = pick(fields[c], inner_first[part]) - pick(fields[c], inner_second[part])
                total = total + weight(part, c) * ends
            result.append(total)
        for part in range(slot_rows):
            seen = [pltpu.roll(cross_second[part], stride % domains, 0) for stride in strides]
            total = 0.0
            for c in range(3):
                shell = fields[c][:shell_rows]
                other = 0.0
                for code, stride in enumerate(strides):
                    value = pltpu.roll(pick(shell, seen[code]), -stride % domains, 0)
                    other = jnp.where(sides[part] == code, value, other)
                total = total + weight(bond_rows + part, c) * (pick(shell, cross_first[part]) - other)
            result.append(total)
        return result

    def put_pushes(values):
        for at, value in enumerate(values):
            for c in range(3):
                pushed = weight(at, c) * value
                high = pushed.astype(jnp.bfloat16).astype(jnp.float32)
                push_ref[at, pl.ds(c * domains, domains), :] = high
                push_ref[at, pl.ds((3 + c) * domains, domains), :] = pushed - high

    def pushes_of(at, domain):
        return push_ref[at, pl.ds(domain, SUBLANES, stride=domains), :].astype(jnp.bfloat16)

    def totals(domain, owners):
        inner = jnp.concatenate([pushes_of(p, domain) for p in range(bond_rows)], axis=1)
        at = domain * bond_rows * LANES
        if not isinstance(at, int):
            at = pl.multiple_of(at, LANES)
        inner_sum = jnp.dot(inner, inner_ref[pl.ds(at, bond_rows * LANES), :], preferred_element_type=jnp.float32)
        pieces = []
        for part in range(slot_rows):
            pieces.extend(pushes_of(bond_rows + part, owner) for owner in [domain] + owners)
        cross = jnp.concatenate(pieces, axis=1)
        at = domain * slot_rows * 5 * LANES
        if not isinstance(at, int):
            at = pl.multiple_of(at, LANES)
        cross_sum = jnp.dot(
            cross, cross_ref[pl.ds(at, slot_rows * 5 * LANES), :], preferred_element_type=jnp.float32
        )
        shell = shell_rows * LANES
        return [
            inner_sum[:, p * LANES : (p + 1) * LANES]
            + (cross_sum[:, p * LANES : (p + 1) * LANES] if p < shell_rows else 0.0)
            for p in range(atom_rows)
        ]

    def spread(values):
        put_pushes(values)
        for domain in range(domains):
            sums = totals(domain, [(domain - stride) % domains for stride in strides])
            for part in range(atom_rows):
                field_ref[part, pl.ds(domain, SUBLANES, stride=domains), :] = sums[part]
        return [
            [
                masses[part]
                * (
                    field_ref[part, pl.ds(c * domains, domains), :]
                    + field_ref[part, pl.ds((3 + c) * domains, domains), :]
                )
                for part in range(atom_rows)
            ]
            for c in range(3)
        ]

    moves = [
        [moves_ref[pl.ds(c * atom_rows + p, domains, stride=rows.disp_count), :] for p in range(atom_rows)]
        for c in range(3)
    ]
    push_ref[...] = jnp.zeros(push_ref.shape, jnp.float32)
    residue = project(moves)

    def expand(_, carry):
        residue, summed = carry
        change = project(spread(residue))
        residue = [now - step for now, step in zip(residue, change)]
        return residue, [a + b for a, b in zip(summed, residue)]

    residue, summed = lax.fori_loop(0, ORDER, expand, (residue, residue))
    put_pushes(summed)
    sums = totals(me, [lax.rem(me + (-stride) % domains, domains) for stride in strides])
    for part in range(atom_rows):
        lanes = slice(part * LANES, (part + 1) * LANES)
        mass = around_ref[pl.ds(me * rows.count + rows.mass + part, 1), :]
        for c in range(3):
            correction = mass * (sums[part][c : c + 1, :] + sums[part][3 + c : 4 + c, :])
            move = moves_ref[pl.ds(me * rows.disp_count + c * atom_rows + part, 1), :] - correction
            start = around_ref[pl.ds(me * rows.count + rows.coords[c] + part, 1), :]
            coords_out_ref[c, 0, :, lanes] = start + move
            velocity_out_ref[c, 0, :, lanes] = move * (1.0 / time_step)


def vmem(count):
    return [pl.BlockSpec(memory_space=pltpu.VMEM)] * count


def smem(count):
    return [pl.BlockSpec(memory_space=pltpu.SMEM)] * count


def hbm(count):
    return [pl.BlockSpec(memory_space=pltpu.HBM)] * count


def in_hbm(arrays):
    return [pltpu.with_memory_space_constraint(a, pltpu.HBM) for a in arrays]


def params(mebibytes):
    return pltpu.CompilerParams(vmem_limit_bytes=mebibytes * 1024 * 1024)


def cost(flops, moved):
    return pl.CostEstimate(flops=flops, bytes_accessed=moved, transcendentals=0)


def room_for(arrays):
    return [pltpu.VMEM(a.shape, a.dtype) for a in arrays]


def shards(
    coords,
    velocity,
    charge,
    inv_mass,
    tile_block,
    tile_atoms,
    active_tile_count,
    bond_atoms,
    cross_atoms,
    cross_side,
    cross_count,
):
    atoms = coords.shape[-1]
    tiles = tile_atoms.shape[2]
    domains = lax.axis_size("dom")
    strides = strides_of(domains)
    rows = Rows(atoms, bond_atoms.shape[-1], cross_side.shape[-1])
    whole_slab = domains == SUBLANES
    copies = domains if whole_slab else 1
    f32 = jnp.float32

    sent = (coords, charge, inv_mass, bond_atoms, cross_atoms, cross_side)
    packed, rim = pl.pallas_call(
        functools.partial(pack_kernel, rows, copies),
        out_shape=(
            jax.ShapeDtypeStruct((copies * rows.count, LANES), f32),
            jax.ShapeDtypeStruct((4 * rows.shell_rows, LANES), f32),
        ),
        in_specs=smem(1) + hbm(len(sent)),
        out_specs=tuple(vmem(2)),
        scratch_shapes=room_for(sent) + [pltpu.SemaphoreType.DMA((len(sent),))],
        compiler_params=params(4),
        name="pack",
    )(cross_count, *in_hbm(sent))

    alone = (coords, charge, velocity, tile_atoms)
    own, near, index, speed = pl.pallas_call(
        functools.partial(own_kernel, rows),
        out_shape=(
            jax.ShapeDtypeStruct((4, atoms, LANES), f32),
            jax.ShapeDtypeStruct((4, tiles, TILE), f32),
            jax.ShapeDtypeStruct((tiles, TILE), jnp.int32),
            jax.ShapeDtypeStruct((rows.disp_used, LANES), f32),
        ),
        in_specs=hbm(len(alone)),
        out_specs=tuple(vmem(4)),
        scratch_shapes=room_for(alone[:3]) + [pltpu.SemaphoreType.DMA((len(alone),))],
        compiler_params=params(4),
        cost_estimate=cost(64 * atoms * LANES, 16 * atoms * LANES),
        name="own",
    )(*in_hbm(alone))

    below = passed_along(rim, "slab", 1)
    above = passed_along(rim, "slab", -1)
    if whole_slab:
        around = lax.all_to_all(packed, "dom", 0, 0, tiled=True)
        here = lax.axis_index("dom").reshape(1)
        holders = [stride % domains for stride in strides]
    else:
        around = jnp.concatenate([packed] + [passed_along(packed, "dom", -stride) for stride in strides], axis=0)
        here = jnp.zeros(1, jnp.int32)
        holders = [1, 2, 3, 4]

    moves = pl.pallas_call(
        functools.partial(force_kernel, rows, copies, holders),
        out_shape=jax.ShapeDtypeStruct((copies * rows.disp_count, LANES), f32),
        in_specs=smem(2) + hbm(1) + vmem(7),
        out_specs=vmem(1)[0],
        scratch_shapes=[
            pltpu.VMEM((4, 6 * rows.shell_rows, SUBLANES, LANES), f32),
            pltpu.VMEM((4, tiles, LANES), f32),
            pltpu.VMEM((3, atoms, LANES), f32),
            pltpu.SMEM(tile_block.shape, jnp.int32),
            pltpu.SemaphoreType.DMA(()),
        ],
        compiler_params=params(8),
        cost_estimate=cost(30 * tiles * TILE * TILE, 4 * around.size),
        name="force",
    )(here, active_tile_count, *in_hbm([tile_block]), around, below, above, own, near, index, speed)

    if not whole_slab:
        return by_exchange(rows, strides, around, moves, cross_count)

    constraint_rows = rows.bond_rows + rows.slot_rows
    weight, inner, cross = pl.pallas_call(
        functools.partial(bond_kernel, rows, domains, strides),
        out_shape=(
            jax.ShapeDtypeStruct((constraint_rows * 3 * domains, LANES), f32),
            jax.ShapeDtypeStruct((domains * rows.bond_rows * LANES, atoms), jnp.bfloat16),
            jax.ShapeDtypeStruct((domains * rows.slot_rows * 5 * LANES, atoms // 2), jnp.bfloat16),
        ),
        in_specs=vmem(1),
        out_specs=tuple(vmem(3)),
        scratch_shapes=[pltpu.VMEM((rows.slot_rows * 4 * domains, LANES), f32)],
        compiler_params=params(16),
        cost_estimate=cost(8 * domains * (rows.bond_rows * LANES * atoms + rows.slot_rows * 5 * LANES * atoms // 2), 4 * around.size),
        name="bonds",
    )(around)

    every_move = lax.all_to_all(moves, "dom", 0, 0, tiled=True)

    return pl.pallas_call(
        functools.partial(solve_kernel, rows, domains, strides),
        out_shape=(
            jax.ShapeDtypeStruct(coords.shape, f32),
            jax.ShapeDtypeStruct(coords.shape, f32),
        ),
        in_specs=smem(1) + vmem(5),
        out_specs=tuple(vmem(2)),
        scratch_shapes=[
            pltpu.VMEM((constraint_rows, SUBLANES * domains, LANES), f32),
            pltpu.VMEM((rows.atom_rows, SUBLANES * domains, LANES), f32),
        ],
        compiler_params=params(16),
        name="solve",
    )(here, around, every_move, weight, inner, cross)


def by_exchange(rows, strides, around, moves, cross_count):
    atom_count = rows.atom_rows * LANES
    shell = rows.shell_rows * LANES
    inside = around.reshape(5, rows.count, LANES)

    def flat(at, count):
        return inside[0, at : at + count].reshape(-1)

    def neighbours(at):
        return inside[1:, at : at + rows.shell_rows].reshape(-1)

    coords = jnp.stack([flat(at, rows.atom_rows) for at in rows.coords])
    inv_mass = flat(rows.mass, rows.atom_rows)
    displace = moves[: rows.disp_used].reshape(3, atom_count)
    left = flat(rows.bond_first, rows.bond_rows).astype(jnp.int32)
    right = flat(rows.bond_second, rows.bond_rows).astype(jnp.int32)
    cross_left = flat(rows.cross_first, rows.slot_rows).astype(jnp.int32)
    cross_right = flat(rows.cross_second, rows.slot_rows).astype(jnp.int32)
    side = flat(rows.side, rows.slot_rows).astype(jnp.int32)
    flag = flat(rows.live, rows.slot_rows)
    cross_index = side * shell + cross_right
    far_coords = jnp.stack([neighbours(at) for at in rows.coords])
    far_mass = neighbours(rows.mass)

    def weights(first, second, mass_first, mass_second):
        gap = first - second
        length = jnp.sqrt(jnp.sum(gap * gap, axis=0) + length_floor)
        return gap / length * lax.rsqrt(mass_first + mass_second)

    inner = weights(coords[:, left], coords[:, right], inv_mass[left], inv_mass[right])
    cross = flag * weights(
        coords[:, cross_left], far_coords[:, cross_index], inv_mass[cross_left], far_mass[cross_index]
    )

    def project(field):
        rim = field[:, :shell]
        far = jnp.concatenate([passed_along(rim, "dom", -stride) for stride in strides], axis=1)
        return (
            jnp.sum(inner * (field[:, left] - field[:, right]), axis=0),
            jnp.sum(cross * (field[:, cross_left] - far[:, cross_index]), axis=0),
        )

    def spread(values):
        pushed = inner * values[0]
        pushed_cross = cross * values[1]
        totals = jnp.zeros((3, atom_count), jnp.float32).at[:, left].add(pushed).at[:, right].add(-pushed)
        totals = totals.at[:, cross_left].add(pushed_cross)
        outward = jnp.zeros((3, 4 * shell), jnp.float32).at[:, cross_index].add(-pushed_cross)
        for code, stride in enumerate(strides):
            totals = totals.at[:, :shell].add(
                passed_along(outward[:, code * shell : (code + 1) * shell], "dom", stride)
            )
        return inv_mass * totals

    residue = project(displace)
    summed = residue
    for _ in range(ORDER):
        change = project(spread(residue))
        residue = tuple(now - step for now, step in zip(residue, change))
        summed = tuple(a + b for a, b in zip(summed, residue))
    move = displace - spread(summed)
    return (
        (coords + move).reshape(3, 1, 1, atom_count),
        (move * (1.0 / time_step)).reshape(3, 1, 1, atom_count),
    )


def solution(mesh):
    return jax.shard_map(
        shards,
        mesh=mesh,
        in_specs=(
            P(None, "slab", "dom", None),
            P(None, "slab", "dom", None),
            P("slab", "dom", None),
            P("slab", "dom", None),
            P("slab", "dom", None),
            P("slab", "dom", None, None),
            P("slab", "dom"),
            P(None, "slab", "dom", None),
            P(None, "slab", "dom", None),
            P("slab", "dom", None),
            P("slab", "dom"),
        ),
        out_specs=(P(None, "slab", "dom", None), P(None, "slab", "dom", None)),
        check_vma=False,
    )
```

```python
import functools

import jax
import jax.numpy as jnp
from jax import lax
from jax.experimental import pallas as pl
from jax.experimental.pallas import tpu as pltpu
from jax.sharding import PartitionSpec as P

TILE = 128
ORDER = 4
LANES = 128
SUBLANES = 8

time_step = 0.1
cutoff_sq = 16.0
force_scale = 4.0
length_floor = 0.25


def passed_along(array, axis, by):
    length = lax.axis_size(axis)
    return lax.ppermute(array, axis, [(i, (i + by) % length) for i in range(length)])


def strides_of(domains):
    row_width = max(2, domains // 8)
    return (1, -1, row_width, -row_width)


def round_up(count, step):
    return -(-count // step) * step


class Rows:
    def __init__(self, atoms, bonds, slots):
        self.atom_rows = atoms // LANES
        self.shell_rows = atoms // 2 // LANES
        self.bond_rows = bonds // LANES
        self.slot_rows = slots // LANES
        at = 0
        self.coords = []
        for _ in range(3):
            self.coords.append(at)
            at += self.atom_rows
        self.mass = at
        at += self.atom_rows
        self.bond_first = at
        at += self.bond_rows
        self.bond_second = at
        at += self.bond_rows
        self.cross_first = at
        at += self.slot_rows
        self.cross_second = at
        at += self.slot_rows
        self.side = at
        at += self.slot_rows
        self.live = at
        at += self.slot_rows
        self.used = at
        self.count = round_up(at, SUBLANES)
        self.rim = 4 * self.shell_rows
        self.disp_used = 3 * self.atom_rows
        self.disp_count = round_up(self.disp_used, SUBLANES)


def take_lanes(table, lanes):
    return jnp.take_along_axis(table, lanes, axis=1, mode="promise_in_bounds")


def pick(tables, index):
    lanes = index & (LANES - 1)
    chunk = index >> 7
    result = take_lanes(tables[0], lanes)
    for k in range(1, len(tables)):
        result = jnp.where(chunk == k, take_lanes(tables[k], lanes), result)
    return result


def rsqrt(value):
    guess = lax.rsqrt(value)
    return guess * (1.5 - 0.5 * value * guess * guess)


def fetched(sources, targets, sem_ref):
    copies = [pltpu.make_async_copy(s, t, sem_ref.at[n]) for n, (s, t) in enumerate(zip(sources, targets))]
    for copy in copies:
        copy.start()
    return copies


def pack_kernel(rows, copies, count_ref, *refs):
    sources, (rim_ref, spread_ref, out_ref), targets, sem_ref = refs[:6], refs[6:9], refs[9:15], refs[15]
    for copy in fetched(sources, targets, sem_ref):
        copy.wait()
    coords_ref, charge_ref, mass_ref, bonds_ref, cross_ref, side_ref = targets

    def put(row, value):
        for part in range(value.shape[1] // LANES):
            out_ref[pl.ds(row + part, 1), :] = value[:, part * LANES : (part + 1) * LANES]

    fields = [coords_ref[c, 0] for c in range(3)] + [charge_ref[0]]
    for c in range(4):
        for part in range(rows.shell_rows):
            piece = fields[c][:, part * LANES : (part + 1) * LANES]
            rim_ref[pl.ds(c * rows.shell_rows + part, 1), :] = piece
            for copy in range(copies):
                spread_ref[pl.ds(copy * rows.rim + c * rows.shell_rows + part, 1), :] = piece
    for c in range(3):
        put(rows.coords[c], fields[c])
    put(rows.mass, mass_ref[0])
    put(rows.bond_first, bonds_ref[0, 0].astype(jnp.float32))
    put(rows.bond_second, bonds_ref[1, 0].astype(jnp.float32))
    put(rows.cross_first, cross_ref[0, 0].astype(jnp.float32))
    put(rows.cross_second, cross_ref[1, 0].astype(jnp.float32))
    side = side_ref[0]
    put(rows.side, side.astype(jnp.float32))
    slot = lax.broadcasted_iota(jnp.int32, side.shape, 1)
    put(rows.live, jnp.where(slot < count_ref[0, 0], 1.0, 0.0))
    if rows.count > rows.used:
        out_ref[rows.used :, :] = jnp.zeros((rows.count - rows.used, LANES), jnp.float32)


SHRINK = 1.0 / 4.0


def own_kernel(
    rows, coords_hbm, charge_hbm, velocity_hbm, atoms_hbm, own_ref, far_ref, index_ref, speed_ref, coords_ref, charge_ref, velocity_ref, sem_ref
):
    atom_rows = rows.atom_rows
    copies = fetched(
        (coords_hbm, charge_hbm, atoms_hbm.at[0, 0], velocity_hbm),
        (coords_ref, charge_ref, index_ref, velocity_ref),
        sem_ref,
    )
    down = lax.broadcasted_iota(jnp.int32, (SUBLANES, LANES), 0)
    copies[0].wait()
    copies[1].wait()

    def lanes_of(part):
        return slice(part * LANES, (part + 1) * LANES)

    table = []
    for c in range(4):
        field = coords_ref[c, 0] * SHRINK if c < 3 else charge_ref[0]
        table.append(
            [jnp.broadcast_to(field[:, lanes_of(part)], (SUBLANES, LANES)) for part in range(atom_rows)]
        )
    for part in range(atom_rows):
        for group in range(LANES // SUBLANES):
            at = part * LANES + group * SUBLANES
            for c in range(4):
                value = take_lanes(table[c][part], down + group * SUBLANES)
                own_ref[c, pl.ds(at, SUBLANES), :] = value if c < 3 else value * 8.0
    copies[2].wait()
    for group in range(index_ref.shape[0] // SUBLANES):
        at = pl.ds(group * SUBLANES, SUBLANES)
        index = index_ref[at, :]
        for c in range(4):
            far_ref[c, at, :] = pick(table[c], index)
    copies[3].wait()
    for c in range(3):
        for part in range(atom_rows):
            speed_ref[pl.ds(c * atom_rows + part, 1), :] = velocity_ref[c, 0, :, lanes_of(part)]


def force_kernel(
    rows,
    copies,
    holders,
    here_ref,
    live_ref,
    block_hbm,
    rims_ref,
    below_ref,
    above_ref,
    static_ref,
    own_ref,
    near_ref,
    index_ref,
    speed_ref,
    out_ref,
    table_ref,
    far_ref,
    sum_ref,
    block_ref,
    sem_ref,
):
    atom_rows, shell_rows = rows.atom_rows, rows.shell_rows
    tiles = index_ref.shape[0]
    block_copy = pltpu.make_async_copy(block_hbm, block_ref, sem_ref)
    block_copy.start()
    me = here_ref[0]
    entry_rows = 6 * shell_rows
    blocks = rims_ref.shape[0] // rows.rim

    def broadcast(row):
        return jnp.broadcast_to(row, (SUBLANES, LANES))

    for c in range(4):
        factor = SHRINK if c < 3 else 1.0
        at = 0
        for neighbour in range(4):
            base = lax.rem(me + holders[neighbour], blocks) * rows.rim + c * shell_rows
            for part in range(shell_rows):
                table_ref[c, at] = broadcast(rims_ref[pl.ds(base + part, 1), :] * factor)
                at += 1
        for slab_ref in (below_ref, above_ref):
            for part in range(shell_rows):
                table_ref[c, at] = broadcast(slab_ref[pl.ds(c * shell_rows + part, 1), :] * factor)
                at += 1

    for group in range(tiles // SUBLANES):
        at = pl.ds(group * SUBLANES, SUBLANES)
        index = index_ref[at, :]
        lanes = index & (LANES - 1)
        chunk = index >> 7
        values = [near_ref[c, at, :] for c in range(4)]
        for k in range(entry_rows):
            here = chunk == atom_rows + k
            values = [jnp.where(here, take_lanes(table_ref[c, k], lanes), values[c]) for c in range(4)]
        for c in range(4):
            far_ref[c, at, :] = values[c]

    sum_ref[...] = jnp.zeros(sum_ref.shape, jnp.float32)
    block_copy.wait()

    def add_tile(tile, _):
        base = block_ref[0, 0, tile] * TILE
        far = [broadcast(far_ref[c, pl.ds(tile, 1), :]) for c in range(4)]
        for group in range(TILE // SUBLANES):
            at = pl.ds(pl.multiple_of(base + group * SUBLANES, SUBLANES), SUBLANES)
            gap = [own_ref[c, at, :] - far[c] for c in range(3)]
            square = gap[0] * gap[0] + gap[1] * gap[1] + gap[2] * gap[2]
            shifted = square + 1.0 / cutoff_sq
            inverse = pl.reciprocal(shifted, approx=True)
            inverse = inverse * (2.0 - shifted * inverse)
            switch = jnp.maximum(1.0 - square, 0.0)
            weight = inverse * switch
            strength = (inverse - own_ref[3, at, :] * far[3]) * (weight * weight)
            for c in range(3):
                sum_ref[c, at, :] = sum_ref[c, at, :] + strength * gap[c]
        return 0

    lax.fori_loop(0, live_ref[0, 0], add_tile, 0)

    scale = time_step * time_step * force_scale * 4.0 / 2048.0
    for c in range(3):
        for part in range(atom_rows):
            total = jnp.sum(sum_ref[c, pl.ds(part * LANES, LANES), :].T, axis=0, keepdims=True)
            mass = static_ref[pl.ds(rows.mass + part, 1), :]
            moved = time_step * speed_ref[pl.ds(c * atom_rows + part, 1), :] + scale * total * mass
            for copy in range(copies):
                out_ref[pl.ds(copy * rows.disp_count + c * atom_rows + part, 1), :] = moved
    if rows.disp_count > rows.disp_used:
        for copy in range(copies):
            out_ref[pl.ds(copy * rows.disp_count + rows.disp_used, rows.disp_count - rows.disp_used), :] = jnp.zeros(
                (rows.disp_count - rows.disp_used, LANES), jnp.float32
            )


def bond_kernel(rows, domains, strides, around_ref, weight_ref, inner_ref, cross_ref, key_ref):
    atom_rows, shell_rows = rows.atom_rows, rows.shell_rows

    def load(row):
        return around_ref[pl.ds(row, domains, stride=rows.count), :]

    def index(row):
        return load(row).astype(jnp.int32)

    fields = [[load(at + part) for part in range(atom_rows)] for at in rows.coords + [rows.mass]]

    def weights(first, second, row):
        gap = [first[c] - second[c] for c in range(3)]
        length_sq = gap[0] * gap[0] + gap[1] * gap[1] + gap[2] * gap[2] + length_floor
        scale = rsqrt(length_sq) * rsqrt(first[3] + second[3])
        return [gap[c] * scale for c in range(3)]

    at = 0
    for part in range(rows.bond_rows):
        first = index(rows.bond_first + part)
        second = index(rows.bond_second + part)
        values = weights([pick(f, first) for f in fields], [pick(f, second) for f in fields], at)
        for c in range(3):
            weight_ref[pl.ds((at * 3 + c) * domains, domains), :] = values[c]
        at += 1
    for part in range(rows.slot_rows):
        first = index(rows.cross_first + part)
        second = index(rows.cross_second + part)
        side = load(rows.side + part)
        live = load(rows.live + part)
        other = [jnp.zeros((domains, LANES), jnp.float32) for _ in range(4)]
        for code, stride in enumerate(strides):
            seen = pltpu.roll(second, stride % domains, 0)
            for f in range(4):
                value = pltpu.roll(pick(fields[f][:shell_rows], seen), -stride % domains, 0)
                other[f] = jnp.where(side == code, value, other[f])
            key = jnp.where(side == code, load(rows.cross_second + part), -1.0)
            key_ref[pl.ds((part * 4 + code) * domains, domains), :] = key
        values = weights([pick(f[:shell_rows], first) for f in fields], other, at)
        for c in range(3):
            weight_ref[pl.ds((at * 3 + c) * domains, domains), :] = values[c] * live
        at += 1

    down = lax.broadcasted_iota(jnp.int32, (SUBLANES, LANES), 0)
    across = lax.broadcasted_iota(jnp.int32, (SUBLANES, LANES), 1).astype(jnp.float32)
    pair = 2 * SUBLANES

    def column(row, group):
        return take_lanes(jnp.broadcast_to(row, (SUBLANES, LANES)), down + group * SUBLANES)

    def one_hot(values, part):
        return jnp.where(values == across + float(part * LANES), 1.0, 0.0)

    def build(domain, _):
        for part in range(rows.bond_rows):
            first = around_ref[pl.ds(domain * rows.count + rows.bond_first + part, 1), :]
            second = around_ref[pl.ds(domain * rows.count + rows.bond_second + part, 1), :]
            for step in range(LANES // pair):
                ends = [(column(first, 2 * step + h), column(second, 2 * step + h)) for h in range(2)]
                at = pl.multiple_of((domain * rows.bond_rows + part) * LANES + step * pair, pair)
                for block in range(atom_rows):
                    halves = [one_hot(a, block) - one_hot(b, block) for a, b in ends]
                    inner_ref[pl.ds(at, pair), block * LANES : (block + 1) * LANES] = jnp.concatenate(
                        halves, axis=0
                    ).astype(jnp.bfloat16)
        for part in range(rows.slot_rows):
            for code in range(5):
                if code == 0:
                    row = around_ref[pl.ds(domain * rows.count + rows.cross_first + part, 1), :]
                else:
                    owner = lax.rem(domain + (-strides[code - 1]) % domains, domains)
                    row = key_ref[pl.ds((part * 4 + code - 1) * domains + owner, 1), :]
                sign = 1.0 if code == 0 else -1.0
                for step in range(LANES // pair):
                    ends = [column(row, 2 * step + h) for h in range(2)]
                    at = pl.multiple_of(((domain * rows.slot_rows + part) * 5 + code) * LANES + step * pair, pair)
                    for block in range(shell_rows):
                        halves = [sign * one_hot(a, block) for a in ends]
                        cross_ref[pl.ds(at, pair), block * LANES : (block + 1) * LANES] = jnp.concatenate(
                            halves, axis=0
                        ).astype(jnp.bfloat16)
        return 0

    lax.fori_loop(0, domains, build, 0)


def solve_kernel(
    rows,
    domains,
    strides,
    here_ref,
    around_ref,
    moves_ref,
    weight_ref,
    inner_ref,
    cross_ref,
    coords_out_ref,
    velocity_out_ref,
    push_ref,
    field_ref,
):
    atom_rows, shell_rows = rows.atom_rows, rows.shell_rows
    bond_rows, slot_rows = rows.bond_rows, rows.slot_rows
    me = here_ref[0]

    def load(row):
        return around_ref[pl.ds(row, domains, stride=rows.count), :]

    def index(row):
        return load(row).astype(jnp.int32)

    inner_first = [index(rows.bond_first + p) for p in range(bond_rows)]
    inner_second = [index(rows.bond_second + p) for p in range(bond_rows)]
    cross_first = [index(rows.cross_first + p) for p in range(slot_rows)]
    cross_second = [index(rows.cross_second + p) for p in range(slot_rows)]
    sides = [load(rows.side + p) for p in range(slot_rows)]
    masses = [load(rows.mass + p) for p in range(atom_rows)]

    def weight(at, c):
        return weight_ref[pl.ds((at * 3 + c) * domains, domains), :]

    def project(fields):
        result = []
        for part in range(bond_rows):
            total = 0.0
            for c in range(3):
                ends = pick(fields[c], inner_first[part]) - pick(fields[c], inner_second[part])
                total = total + weight(part, c) * ends
            result.append(total)
        for part in range(slot_rows):
            seen = [pltpu.roll(cross_second[part], stride % domains, 0) for stride in strides]
            total = 0.0
            for c in range(3):
                shell = fields[c][:shell_rows]
                other = 0.0
                for code, stride in enumerate(strides):
                    value = pltpu.roll(pick(shell, seen[code]), -stride % domains, 0)
                    other = jnp.where(sides[part] == code, value, other)
                total = total + weight(bond_rows + part, c) * (pick(shell, cross_first[part]) - other)
            result.append(total)
        return result

    def put_pushes(values):
        for at, value in enumerate(values):
            for c in range(3):
                pushed = weight(at, c) * value
                high = pushed.astype(jnp.bfloat16).astype(jnp.float32)
                push_ref[at, pl.ds(c * domains, domains), :] = high
                push_ref[at, pl.ds((3 + c) * domains, domains), :] = pushed - high

    def pushes_of(at, domain):
        return push_ref[at, pl.ds(domain, SUBLANES, stride=domains), :].astype(jnp.bfloat16)

    def totals(domain, owners):
        inner = jnp.concatenate([pushes_of(p, domain) for p in range(bond_rows)], axis=1)
        at = domain * bond_rows * LANES
        if not isinstance(at, int):
            at = pl.multiple_of(at, LANES)
        inner_sum = jnp.dot(inner, inner_ref[pl.ds(at, bond_rows * LANES), :], preferred_element_type=jnp.float32)
        pieces = []
        for part in range(slot_rows):
            pieces.extend(pushes_of(bond_rows + part, owner) for owner in [domain] + owners)
        cross = jnp.concatenate(pieces, axis=1)
        at = domain * slot_rows * 5 * LANES
        if not isinstance(at, int):
            at = pl.multiple_of(at, LANES)
        cross_sum = jnp.dot(
            cross, cross_ref[pl.ds(at, slot_rows * 5 * LANES), :], preferred_element_type=jnp.float32
        )
        shell = shell_rows * LANES
        return [
            inner_sum[:, p * LANES : (p + 1) * LANES]
            + (cross_sum[:, p * LANES : (p + 1) * LANES] if p < shell_rows else 0.0)
            for p in range(atom_rows)
        ]

    def spread(values):
        put_pushes(values)
        for domain in range(domains):
            sums = totals(domain, [(domain - stride) % domains for stride in strides])
            for part in range(atom_rows):
                field_ref[part, pl.ds(domain, SUBLANES, stride=domains), :] = sums[part]
        return [
            [
                masses[part]
                * (
                    field_ref[part, pl.ds(c * domains, domains), :]
                    + field_ref[part, pl.ds((3 + c) * domains, domains), :]
                )
                for part in range(atom_rows)
            ]
            for c in range(3)
        ]

    moves = [
        [moves_ref[pl.ds(c * atom_rows + p, domains, stride=rows.disp_count), :] for p in range(atom_rows)]
        for c in range(3)
    ]
    push_ref[...] = jnp.zeros(push_ref.shape, jnp.float32)
    residue = project(moves)

    def expand(_, carry):
        residue, summed = carry
        change = project(spread(residue))
        residue = [now - step for now, step in zip(residue, change)]
        return residue, [a + b for a, b in zip(summed, residue)]

    residue, summed = lax.fori_loop(0, ORDER, expand, (residue, residue))
    put_pushes(summed)
    sums = totals(me, [lax.rem(me + (-stride) % domains, domains) for stride in strides])
    for part in range(atom_rows):
        lanes = slice(part * LANES, (part + 1) * LANES)
        mass = around_ref[pl.ds(me * rows.count + rows.mass + part, 1), :]
        for c in range(3):
            correction = mass * (sums[part][c : c + 1, :] + sums[part][3 + c : 4 + c, :])
            move = moves_ref[pl.ds(me * rows.disp_count + c * atom_rows + part, 1), :] - correction
            start = around_ref[pl.ds(me * rows.count + rows.coords[c] + part, 1), :]
            coords_out_ref[c, 0, :, lanes] = start + move
            velocity_out_ref[c, 0, :, lanes] = move * (1.0 / time_step)


def vmem(count):
    return [pl.BlockSpec(memory_space=pltpu.VMEM)] * count


def smem(count):
    return [pl.BlockSpec(memory_space=pltpu.SMEM)] * count


def hbm(count):
    return [pl.BlockSpec(memory_space=pltpu.HBM)] * count


def in_hbm(arrays):
    return [pltpu.with_memory_space_constraint(a, pltpu.HBM) for a in arrays]


def params(mebibytes):
    return pltpu.CompilerParams(vmem_limit_bytes=mebibytes * 1024 * 1024)


def cost(flops, moved):
    return pl.CostEstimate(flops=flops, bytes_accessed=moved, transcendentals=0)


def room_for(arrays):
    return [pltpu.VMEM(a.shape, a.dtype) for a in arrays]


def shards(
    coords,
    velocity,
    charge,
    inv_mass,
    tile_block,
    tile_atoms,
    active_tile_count,
    bond_atoms,
    cross_atoms,
    cross_side,
    cross_count,
):
    atoms = coords.shape[-1]
    tiles = tile_atoms.shape[2]
    domains = lax.axis_size("dom")
    strides = strides_of(domains)
    rows = Rows(atoms, bond_atoms.shape[-1], cross_side.shape[-1])
    whole_slab = domains == SUBLANES
    copies = domains if whole_slab else 1
    f32 = jnp.float32

    sent = (coords, charge, inv_mass, bond_atoms, cross_atoms, cross_side)
    rim, rims, static = pl.pallas_call(
        functools.partial(pack_kernel, rows, copies),
        out_shape=(
            jax.ShapeDtypeStruct((rows.rim, LANES), f32),
            jax.ShapeDtypeStruct((copies * rows.rim, LANES), f32),
            jax.ShapeDtypeStruct((rows.count, LANES), f32),
        ),
        in_specs=smem(1) + hbm(len(sent)),
        out_specs=tuple(vmem(3)),
        scratch_shapes=room_for(sent) + [pltpu.SemaphoreType.DMA((len(sent),))],
        compiler_params=params(4),
        name="pack",
    )(cross_count, *in_hbm(sent))

    alone = (coords, charge, velocity, tile_atoms)
    own, near, index, speed = pl.pallas_call(
        functools.partial(own_kernel, rows),
        out_shape=(
            jax.ShapeDtypeStruct((4, atoms, LANES), f32),
            jax.ShapeDtypeStruct((4, tiles, TILE), f32),
            jax.ShapeDtypeStruct((tiles, TILE), jnp.int32),
            jax.ShapeDtypeStruct((rows.disp_used, LANES), f32),
        ),
        in_specs=hbm(len(alone)),
        out_specs=tuple(vmem(4)),
        scratch_shapes=room_for(alone[:3]) + [pltpu.SemaphoreType.DMA((len(alone),))],
        compiler_params=params(4),
        cost_estimate=cost(64 * atoms * LANES, 16 * atoms * LANES),
        name="own",
    )(*in_hbm(alone))

    below = passed_along(rim, "slab", 1)
    above = passed_along(rim, "slab", -1)
    if whole_slab:
        rims = lax.all_to_all(rims, "dom", 0, 0, tiled=True)
        here = lax.axis_index("dom").reshape(1)
        holders = [stride % domains for stride in strides]
    else:
        rims = jnp.concatenate([passed_along(rim, "dom", -stride) for stride in strides], axis=0)
        here = jnp.zeros(1, jnp.int32)
        holders = [0, 1, 2, 3]

    moves = pl.pallas_call(
        functools.partial(force_kernel, rows, copies, holders),
        out_shape=jax.ShapeDtypeStruct((copies * rows.disp_count, LANES), f32),
        in_specs=smem(2) + hbm(1) + vmem(8),
        out_specs=vmem(1)[0],
        scratch_shapes=[
            pltpu.VMEM((4, 6 * rows.shell_rows, SUBLANES, LANES), f32),
            pltpu.VMEM((4, tiles, LANES), f32),
            pltpu.VMEM((3, atoms, LANES), f32),
            pltpu.SMEM(tile_block.shape, jnp.int32),
            pltpu.SemaphoreType.DMA(()),
        ],
        compiler_params=params(4),
        cost_estimate=cost(30 * tiles * TILE * TILE, 4 * own.size),
        name="force",
    )(here, active_tile_count, *in_hbm([tile_block]), rims, below, above, static, own, near, index, speed)

    if not whole_slab:
        around = jnp.concatenate([static] + [passed_along(static, "dom", -stride) for stride in strides], axis=0)
        return by_exchange(rows, strides, around, moves)

    around = lax.all_gather(static, "dom", tiled=True)

    constraint_rows = rows.bond_rows + rows.slot_rows
    weight, inner, cross = pl.pallas_call(
        functools.partial(bond_kernel, rows, domains, strides),
        out_shape=(
            jax.ShapeDtypeStruct((constraint_rows * 3 * domains, LANES), f32),
            jax.ShapeDtypeStruct((domains * rows.bond_rows * LANES, atoms), jnp.bfloat16),
            jax.ShapeDtypeStruct((domains * rows.slot_rows * 5 * LANES, atoms // 2), jnp.bfloat16),
        ),
        in_specs=vmem(1),
        out_specs=tuple(vmem(3)),
        scratch_shapes=[pltpu.VMEM((rows.slot_rows * 4 * domains, LANES), f32)],
        compiler_params=params(8),
        cost_estimate=cost(8 * domains * (rows.bond_rows * LANES * atoms + rows.slot_rows * 5 * LANES * atoms // 2), 4 * around.size),
        name="bonds",
    )(around)

    every_move = lax.all_to_all(moves, "dom", 0, 0, tiled=True)

    return pl.pallas_call(
        functools.partial(solve_kernel, rows, domains, strides),
        out_shape=(
            jax.ShapeDtypeStruct(coords.shape, f32),
            jax.ShapeDtypeStruct(coords.shape, f32),
        ),
        in_specs=smem(1) + vmem(5),
        out_specs=tuple(vmem(2)),
        scratch_shapes=[
            pltpu.VMEM((constraint_rows, SUBLANES * domains, LANES), f32),
            pltpu.VMEM((rows.atom_rows, SUBLANES * domains, LANES), f32),
        ],
        compiler_params=params(8),
        name="solve",
    )(here, around, every_move, weight, inner, cross)


def by_exchange(rows, strides, around, moves):
    atom_count = rows.atom_rows * LANES
    shell = rows.shell_rows * LANES
    inside = around.reshape(5, rows.count, LANES)

    def flat(at, count):
        return inside[0, at : at + count].reshape(-1)

    def neighbours(at):
        return inside[1:, at : at + rows.shell_rows].reshape(-1)

    coords = jnp.stack([flat(at, rows.atom_rows) for at in rows.coords])
    inv_mass = flat(rows.mass, rows.atom_rows)
    displace = moves[: rows.disp_used].reshape(3, atom_count)
    left = flat(rows.bond_first, rows.bond_rows).astype(jnp.int32)
    right = flat(rows.bond_second, rows.bond_rows).astype(jnp.int32)
    cross_left = flat(rows.cross_first, rows.slot_rows).astype(jnp.int32)
    cross_right = flat(rows.cross_second, rows.slot_rows).astype(jnp.int32)
    side = flat(rows.side, rows.slot_rows).astype(jnp.int32)
    flag = flat(rows.live, rows.slot_rows)
    cross_index = side * shell + cross_right
    far_coords = jnp.stack([neighbours(at) for at in rows.coords])
    far_mass = neighbours(rows.mass)

    def weights(first, second, mass_first, mass_second):
        gap = first - second
        length = jnp.sqrt(jnp.sum(gap * gap, axis=0) + length_floor)
        return gap / length * lax.rsqrt(mass_first + mass_second)

    inner = weights(coords[:, left], coords[:, right], inv_mass[left], inv_mass[right])
    cross = flag * weights(
        coords[:, cross_left], far_coords[:, cross_index], inv_mass[cross_left], far_mass[cross_index]
    )

    def project(field):
        rim = field[:, :shell]
        far = jnp.concatenate([passed_along(rim, "dom", -stride) for stride in strides], axis=1)
        return (
            jnp.sum(inner * (field[:, left] - field[:, right]), axis=0),
            jnp.sum(cross * (field[:, cross_left] - far[:, cross_index]), axis=0),
        )

    def spread(values):
        pushed = inner * values[0]
        pushed_cross = cross * values[1]
        totals = jnp.zeros((3, atom_count), jnp.float32).at[:, left].add(pushed).at[:, right].add(-pushed)
        totals = totals.at[:, cross_left].add(pushed_cross)
        outward = jnp.zeros((3, 4 * shell), jnp.float32).at[:, cross_index].add(-pushed_cross)
        for code, stride in enumerate(strides):
            totals = totals.at[:, :shell].add(
                passed_along(outward[:, code * shell : (code + 1) * shell], "dom", stride)
            )
        return inv_mass * totals

    residue = project(displace)
    summed = residue
    for _ in range(ORDER):
        change = project(spread(residue))
        residue = tuple(now - step for now, step in zip(residue, change))
        summed = tuple(a + b for a, b in zip(summed, residue))
    move = displace - spread(summed)
    return (
        (coords + move).reshape(3, 1, 1, atom_count),
        (move * (1.0 / time_step)).reshape(3, 1, 1, atom_count),
    )


def solution(mesh):
    return jax.shard_map(
        shards,
        mesh=mesh,
        in_specs=(
            P(None, "slab", "dom", None),
            P(None, "slab", "dom", None),
            P("slab", "dom", None),
            P("slab", "dom", None),
            P("slab", "dom", None),
            P("slab", "dom", None, None),
            P("slab", "dom"),
            P(None, "slab", "dom", None),
            P(None, "slab", "dom", None),
            P("slab", "dom", None),
            P("slab", "dom"),
        ),
        out_specs=(P(None, "slab", "dom", None), P(None, "slab", "dom", None)),
        check_vma=False,
    )
```

```python
import functools

import jax
import jax.numpy as jnp
from jax import lax
from jax.experimental import pallas as pl
from jax.experimental.pallas import tpu as pltpu
from jax.sharding import PartitionSpec as P

TILE = 128
ORDER = 4
LANES = 128
SUBLANES = 8

time_step = 0.1
cutoff_sq = 16.0
force_scale = 4.0
length_floor = 0.25


def passed_along(array, axis, by):
    length = lax.axis_size(axis)
    return lax.ppermute(array, axis, [(i, (i + by) % length) for i in range(length)])


def strides_of(domains):
    row_width = max(2, domains // 8)
    return (1, -1, row_width, -row_width)


def round_up(count, step):
    return -(-count // step) * step


class Rows:
    def __init__(self, atoms, bonds, slots):
        self.atom_rows = atoms // LANES
        self.shell_rows = atoms // 2 // LANES
        self.bond_rows = bonds // LANES
        self.slot_rows = slots // LANES
        at = 0
        self.coords = []
        for _ in range(3):
            self.coords.append(at)
            at += self.atom_rows
        self.charge = at
        at += self.atom_rows
        self.mass = at
        at += self.atom_rows
        self.bond_first = at
        at += self.bond_rows
        self.bond_second = at
        at += self.bond_rows
        self.cross_first = at
        at += self.slot_rows
        self.cross_second = at
        at += self.slot_rows
        self.side = at
        at += self.slot_rows
        self.live = at
        at += self.slot_rows
        self.used = at
        self.count = round_up(at, SUBLANES)
        self.disp_used = 3 * self.atom_rows
        self.disp_count = round_up(self.disp_used, SUBLANES)


def take_lanes(table, lanes):
    return jnp.take_along_axis(table, lanes, axis=1, mode="promise_in_bounds")


def pick(tables, index):
    lanes = index & (LANES - 1)
    chunk = index >> 7
    result = take_lanes(tables[0], lanes)
    for k in range(1, len(tables)):
        result = jnp.where(chunk == k, take_lanes(tables[k], lanes), result)
    return result


def rsqrt(value):
    guess = lax.rsqrt(value)
    return guess * (1.5 - 0.5 * value * guess * guess)


def fetched(sources, targets, sem_ref):
    copies = [pltpu.make_async_copy(s, t, sem_ref.at[n]) for n, (s, t) in enumerate(zip(sources, targets))]
    for copy in copies:
        copy.start()
    return copies


def pack_kernel(rows, copies, count_ref, *refs):
    sources, (out_ref, rim_ref), targets, sem_ref = refs[:6], refs[6:8], refs[8:14], refs[14]
    for copy in fetched(sources, targets, sem_ref):
        copy.wait()
    coords_ref, charge_ref, mass_ref, bonds_ref, cross_ref, side_ref = targets

    def put(row, value):
        for part in range(value.shape[1] // LANES):
            piece = value[:, part * LANES : (part + 1) * LANES]
            for copy in range(copies):
                out_ref[pl.ds(copy * rows.count + row + part, 1), :] = piece

    shell = rows.shell_rows * LANES
    fields = [coords_ref[c, 0] for c in range(3)] + [charge_ref[0]]
    for c in range(4):
        at = rows.coords[c] if c < 3 else rows.charge
        put(at, fields[c])
        for part in range(rows.shell_rows):
            rim_ref[pl.ds(c * rows.shell_rows + part, 1), :] = fields[c][:, part * LANES : (part + 1) * LANES]
    put(rows.mass, mass_ref[0])
    put(rows.bond_first, bonds_ref[0, 0].astype(jnp.float32))
    put(rows.bond_second, bonds_ref[1, 0].astype(jnp.float32))
    put(rows.cross_first, cross_ref[0, 0].astype(jnp.float32))
    put(rows.cross_second, cross_ref[1, 0].astype(jnp.float32))
    side = side_ref[0]
    put(rows.side, side.astype(jnp.float32))
    slot = lax.broadcasted_iota(jnp.int32, side.shape, 1)
    put(rows.live, jnp.where(slot < count_ref[0, 0], 1.0, 0.0))
    if rows.count > rows.used:
        for copy in range(copies):
            out_ref[pl.ds(copy * rows.count + rows.used, rows.count - rows.used), :] = jnp.zeros(
                (rows.count - rows.used, LANES), jnp.float32
            )


SHRINK = 1.0 / 4.0


def own_kernel(
    rows, coords_hbm, charge_hbm, velocity_hbm, atoms_hbm, own_ref, far_ref, index_ref, speed_ref, coords_ref, charge_ref, velocity_ref, sem_ref
):
    atom_rows = rows.atom_rows
    copies = fetched(
        (coords_hbm, charge_hbm, atoms_hbm.at[0, 0], velocity_hbm),
        (coords_ref, charge_ref, index_ref, velocity_ref),
        sem_ref,
    )
    down = lax.broadcasted_iota(jnp.int32, (SUBLANES, LANES), 0)
    copies[0].wait()
    copies[1].wait()

    def lanes_of(part):
        return slice(part * LANES, (part + 1) * LANES)

    table = []
    for c in range(4):
        field = coords_ref[c, 0] * SHRINK if c < 3 else charge_ref[0]
        table.append(
            [jnp.broadcast_to(field[:, lanes_of(part)], (SUBLANES, LANES)) for part in range(atom_rows)]
        )
    for part in range(atom_rows):
        for group in range(LANES // SUBLANES):
            at = part * LANES + group * SUBLANES
            for c in range(4):
                value = take_lanes(table[c][part], down + group * SUBLANES)
                own_ref[c, pl.ds(at, SUBLANES), :] = value if c < 3 else value * 8.0
    copies[2].wait()
    for group in range(index_ref.shape[0] // SUBLANES):
        at = pl.ds(group * SUBLANES, SUBLANES)
        index = index_ref[at, :]
        for c in range(4):
            far_ref[c, at, :] = pick(table[c], index)
    copies[3].wait()
    for c in range(3):
        for part in range(atom_rows):
            speed_ref[pl.ds(c * atom_rows + part, 1), :] = velocity_ref[c, 0, :, lanes_of(part)]


def force_kernel(
    rows,
    copies,
    holders,
    here_ref,
    live_ref,
    block_hbm,
    around_ref,
    below_ref,
    above_ref,
    own_ref,
    near_ref,
    index_ref,
    speed_ref,
    out_ref,
    table_ref,
    far_ref,
    sum_ref,
    block_ref,
    sem_ref,
):
    atom_rows, shell_rows = rows.atom_rows, rows.shell_rows
    tiles = index_ref.shape[0]
    block_copy = pltpu.make_async_copy(block_hbm, block_ref, sem_ref)
    block_copy.start()
    me = here_ref[0]
    starts = [rows.coords[0], rows.coords[1], rows.coords[2], rows.charge]
    entry_rows = 6 * shell_rows
    blocks = around_ref.shape[0] // rows.count

    def broadcast(row):
        return jnp.broadcast_to(row, (SUBLANES, LANES))

    for c in range(4):
        factor = SHRINK if c < 3 else 1.0
        at = 0
        for neighbour in range(4):
            base = lax.rem(me + holders[neighbour], blocks) * rows.count + starts[c]
            for part in range(shell_rows):
                table_ref[c, at] = broadcast(around_ref[pl.ds(base + part, 1), :] * factor)
                at += 1
        for slab_ref in (below_ref, above_ref):
            for part in range(shell_rows):
                table_ref[c, at] = broadcast(slab_ref[pl.ds(c * shell_rows + part, 1), :] * factor)
                at += 1

    for group in range(tiles // SUBLANES):
        at = pl.ds(group * SUBLANES, SUBLANES)
        index = index_ref[at, :]
        lanes = index & (LANES - 1)
        chunk = index >> 7
        values = [near_ref[c, at, :] for c in range(4)]
        for k in range(entry_rows):
            here = chunk == atom_rows + k
            values = [jnp.where(here, take_lanes(table_ref[c, k], lanes), values[c]) for c in range(4)]
        for c in range(4):
            far_ref[c, at, :] = values[c]

    sum_ref[...] = jnp.zeros(sum_ref.shape, jnp.float32)
    block_copy.wait()

    def add_tile(tile, _):
        base = block_ref[0, 0, tile] * TILE
        far = [broadcast(far_ref[c, pl.ds(tile, 1), :]) for c in range(4)]
        for group in range(TILE // SUBLANES):
            at = pl.ds(pl.multiple_of(base + group * SUBLANES, SUBLANES), SUBLANES)
            gap = [own_ref[c, at, :] - far[c] for c in range(3)]
            square = gap[0] * gap[0] + gap[1] * gap[1] + gap[2] * gap[2]
            shifted = square + 1.0 / cutoff_sq
            inverse = pl.reciprocal(shifted, approx=True)
            inverse = inverse * (2.0 - shifted * inverse)
            switch = jnp.maximum(1.0 - square, 0.0)
            weight = inverse * switch
            strength = (inverse - own_ref[3, at, :] * far[3]) * (weight * weight)
            for c in range(3):
                sum_ref[c, at, :] = sum_ref[c, at, :] + strength * gap[c]
        return 0

    lax.fori_loop(0, live_ref[0, 0], add_tile, 0)

    scale = time_step * time_step * force_scale * 4.0 / 2048.0
    for c in range(3):
        for part in range(atom_rows):
            total = jnp.sum(sum_ref[c, pl.ds(part * LANES, LANES), :].T, axis=0, keepdims=True)
            mass = around_ref[pl.ds(me * rows.count + rows.mass + part, 1), :]
            moved = time_step * speed_ref[pl.ds(c * atom_rows + part, 1), :] + scale * total * mass
            for copy in range(copies):
                out_ref[pl.ds(copy * rows.disp_count + c * atom_rows + part, 1), :] = moved
    if rows.disp_count > rows.disp_used:
        for copy in range(copies):
            out_ref[pl.ds(copy * rows.disp_count + rows.disp_used, rows.disp_count - rows.disp_used), :] = jnp.zeros(
                (rows.disp_count - rows.disp_used, LANES), jnp.float32
            )


def inner_copy(rows, source, target, sems, domain):
    at = pl.ds(domain * rows.bond_rows * LANES, rows.bond_rows * LANES)
    return pltpu.make_async_copy(source.at[at], target.at[at], sems.at[domain])


def bond_kernel(rows, domains, strides, around_ref, weight_ref, inner_hbm, cross_ref, key_ref, inner_ref, sem_ref):
    atom_rows, shell_rows = rows.atom_rows, rows.shell_rows

    def load(row):
        return around_ref[pl.ds(row, domains, stride=rows.count), :]

    def index(row):
        return load(row).astype(jnp.int32)

    fields = [[load(at + part) for part in range(atom_rows)] for at in rows.coords + [rows.mass]]

    def weights(first, second, row):
        gap = [first[c] - second[c] for c in range(3)]
        length_sq = gap[0] * gap[0] + gap[1] * gap[1] + gap[2] * gap[2] + length_floor
        scale = rsqrt(length_sq) * rsqrt(first[3] + second[3])
        return [gap[c] * scale for c in range(3)]

    at = 0
    for part in range(rows.bond_rows):
        first = index(rows.bond_first + part)
        second = index(rows.bond_second + part)
        values = weights([pick(f, first) for f in fields], [pick(f, second) for f in fields], at)
        for c in range(3):
            weight_ref[pl.ds((at * 3 + c) * domains, domains), :] = values[c]
        at += 1
    for part in range(rows.slot_rows):
        first = index(rows.cross_first + part)
        second = index(rows.cross_second + part)
        side = load(rows.side + part)
        live = load(rows.live + part)
        other = [jnp.zeros((domains, LANES), jnp.float32) for _ in range(4)]
        for code, stride in enumerate(strides):
            seen = pltpu.roll(second, stride % domains, 0)
            for f in range(4):
                value = pltpu.roll(pick(fields[f][:shell_rows], seen), -stride % domains, 0)
                other[f] = jnp.where(side == code, value, other[f])
            key = jnp.where(side == code, load(rows.cross_second + part), -1.0)
            key_ref[pl.ds((part * 4 + code) * domains, domains), :] = key
        values = weights([pick(f[:shell_rows], first) for f in fields], other, at)
        for c in range(3):
            weight_ref[pl.ds((at * 3 + c) * domains, domains), :] = values[c] * live
        at += 1

    down = lax.broadcasted_iota(jnp.int32, (SUBLANES, LANES), 0)
    across = lax.broadcasted_iota(jnp.int32, (SUBLANES, LANES), 1).astype(jnp.float32)
    pair = 2 * SUBLANES

    def column(row, group):
        return take_lanes(jnp.broadcast_to(row, (SUBLANES, LANES)), down + group * SUBLANES)

    def put(target_ref, at, columns, signs, blocks):
        for block in range(blocks):
            lanes = across + float(block * LANES)
            halves = []
            for ends in columns:
                value = 0.0
                for end, sign in zip(ends, signs):
                    value = jnp.where(end == lanes, sign, value)
                halves.append(value)
            target_ref[pl.ds(at, pair), block * LANES : (block + 1) * LANES] = jnp.concatenate(
                halves, axis=0
            ).astype(jnp.bfloat16)

    def build(domain, _):
        for part in range(rows.bond_rows):
            first = around_ref[pl.ds(domain * rows.count + rows.bond_first + part, 1), :]
            second = around_ref[pl.ds(domain * rows.count + rows.bond_second + part, 1), :]
            start = pl.multiple_of((domain * rows.bond_rows + part) * LANES, LANES)
            for step in range(LANES // pair):
                columns = [(column(first, 2 * step + h), column(second, 2 * step + h)) for h in range(2)]
                put(inner_ref, start + step * pair, columns, (1.0, -1.0), atom_rows)
        inner_copy(rows, inner_ref, inner_hbm, sem_ref, domain).start()
        for part in range(rows.slot_rows):
            for code in range(5):
                if code == 0:
                    row = around_ref[pl.ds(domain * rows.count + rows.cross_first + part, 1), :]
                else:
                    owner = lax.rem(domain + (-strides[code - 1]) % domains, domains)
                    row = key_ref[pl.ds((part * 4 + code - 1) * domains + owner, 1), :]
                sign = 1.0 if code == 0 else -1.0
                start = pl.multiple_of(((domain * rows.slot_rows + part) * 5 + code) * LANES, LANES)
                for step in range(LANES // pair):
                    columns = [(column(row, 2 * step + h),) for h in range(2)]
                    put(cross_ref, start + step * pair, columns, (sign,), shell_rows)
        return 0

    lax.fori_loop(0, domains, build, 0)
    for domain in range(domains):
        inner_copy(rows, inner_ref, inner_hbm, sem_ref, domain).wait()


def solve_kernel(
    rows,
    domains,
    strides,
    here_ref,
    around_ref,
    moves_ref,
    weight_ref,
    inner_hbm,
    cross_ref,
    coords_out_ref,
    velocity_out_ref,
    push_ref,
    field_ref,
    inner_ref,
    sem_ref,
):
    atom_rows, shell_rows = rows.atom_rows, rows.shell_rows
    bond_rows, slot_rows = rows.bond_rows, rows.slot_rows
    me = here_ref[0]
    copies = [inner_copy(rows, inner_hbm, inner_ref, sem_ref, domain) for domain in range(domains)]
    for copy in copies:
        copy.start()

    def load(row):
        return around_ref[pl.ds(row, domains, stride=rows.count), :]

    def index(row):
        return load(row).astype(jnp.int32)

    inner_first = [index(rows.bond_first + p) for p in range(bond_rows)]
    inner_second = [index(rows.bond_second + p) for p in range(bond_rows)]
    cross_first = [index(rows.cross_first + p) for p in range(slot_rows)]
    cross_second = [index(rows.cross_second + p) for p in range(slot_rows)]
    sides = [load(rows.side + p) for p in range(slot_rows)]
    masses = [load(rows.mass + p) for p in range(atom_rows)]

    def weight(at, c):
        return weight_ref[pl.ds((at * 3 + c) * domains, domains), :]

    def project(fields):
        result = []
        for part in range(bond_rows):
            total = 0.0
            for c in range(3):
                ends = pick(fields[c], inner_first[part]) - pick(fields[c], inner_second[part])
                total = total + weight(part, c) * ends
            result.append(total)
        for part in range(slot_rows):
            seen = [pltpu.roll(cross_second[part], stride % domains, 0) for stride in strides]
            total = 0.0
            for c in range(3):
                shell = fields[c][:shell_rows]
                other = 0.0
                for code, stride in enumerate(strides):
                    value = pltpu.roll(pick(shell, seen[code]), -stride % domains, 0)
                    other = jnp.where(sides[part] == code, value, other)
                total = total + weight(bond_rows + part, c) * (pick(shell, cross_first[part]) - other)
            result.append(total)
        return result

    def put_pushes(values):
        for at, value in enumerate(values):
            for c in range(3):
                pushed = weight(at, c) * value
                high = pushed.astype(jnp.bfloat16).astype(jnp.float32)
                push_ref[at, pl.ds(c * domains, domains), :] = high
                push_ref[at, pl.ds((3 + c) * domains, domains), :] = pushed - high

    def pushes_of(at, domain):
        return push_ref[at, pl.ds(domain, SUBLANES, stride=domains), :].astype(jnp.bfloat16)

    def totals(domain, owners):
        inner = jnp.concatenate([pushes_of(p, domain) for p in range(bond_rows)], axis=1)
        at = domain * bond_rows * LANES
        if not isinstance(at, int):
            at = pl.multiple_of(at, LANES)
        inner_sum = jnp.dot(inner, inner_ref[pl.ds(at, bond_rows * LANES), :], preferred_element_type=jnp.float32)
        pieces = []
        for part in range(slot_rows):
            pieces.extend(pushes_of(bond_rows + part, owner) for owner in [domain] + owners)
        cross = jnp.concatenate(pieces, axis=1)
        at = domain * slot_rows * 5 * LANES
        if not isinstance(at, int):
            at = pl.multiple_of(at, LANES)
        cross_sum = jnp.dot(
            cross, cross_ref[pl.ds(at, slot_rows * 5 * LANES), :], preferred_element_type=jnp.float32
        )
        shell = shell_rows * LANES
        return [
            inner_sum[:, p * LANES : (p + 1) * LANES]
            + (cross_sum[:, p * LANES : (p + 1) * LANES] if p < shell_rows else 0.0)
            for p in range(atom_rows)
        ]

    def spread(values, first=False):
        put_pushes(values)
        for domain in range(domains):
            if first:
                copies[domain].wait()
            sums = totals(domain, [(domain - stride) % domains for stride in strides])
            for part in range(atom_rows):
                field_ref[part, pl.ds(domain, SUBLANES, stride=domains), :] = sums[part]
        return [
            [
                masses[part]
                * (
                    field_ref[part, pl.ds(c * domains, domains), :]
                    + field_ref[part, pl.ds((3 + c) * domains, domains), :]
                )
                for part in range(atom_rows)
            ]
            for c in range(3)
        ]

    moves = [
        [moves_ref[pl.ds(c * atom_rows + p, domains, stride=rows.disp_count), :] for p in range(atom_rows)]
        for c in range(3)
    ]
    push_ref[...] = jnp.zeros(push_ref.shape, jnp.float32)
    residue = project(moves)

    def expand(_, carry, first=False):
        residue, summed = carry
        change = project(spread(residue, first))
        residue = [now - step for now, step in zip(residue, change)]
        return residue, [a + b for a, b in zip(summed, residue)]

    residue, summed = lax.fori_loop(1, ORDER, expand, expand(0, (residue, residue), first=True))
    put_pushes(summed)
    sums = totals(me, [lax.rem(me + (-stride) % domains, domains) for stride in strides])
    for part in range(atom_rows):
        lanes = slice(part * LANES, (part + 1) * LANES)
        mass = around_ref[pl.ds(me * rows.count + rows.mass + part, 1), :]
        for c in range(3):
            correction = mass * (sums[part][c : c + 1, :] + sums[part][3 + c : 4 + c, :])
            move = moves_ref[pl.ds(me * rows.disp_count + c * atom_rows + part, 1), :] - correction
            start = around_ref[pl.ds(me * rows.count + rows.coords[c] + part, 1), :]
            coords_out_ref[c, 0, :, lanes] = start + move
            velocity_out_ref[c, 0, :, lanes] = move * (1.0 / time_step)


def vmem(count):
    return [pl.BlockSpec(memory_space=pltpu.VMEM)] * count


def smem(count):
    return [pl.BlockSpec(memory_space=pltpu.SMEM)] * count


def hbm(count):
    return [pl.BlockSpec(memory_space=pltpu.HBM)] * count


def in_hbm(arrays):
    return [pltpu.with_memory_space_constraint(a, pltpu.HBM) for a in arrays]


def params(mebibytes):
    return pltpu.CompilerParams(vmem_limit_bytes=mebibytes * 1024 * 1024)


def cost(flops, moved):
    return pl.CostEstimate(flops=flops, bytes_accessed=moved, transcendentals=0)


def room_for(arrays):
    return [pltpu.VMEM(a.shape, a.dtype) for a in arrays]


def shards(
    coords,
    velocity,
    charge,
    inv_mass,
    tile_block,
    tile_atoms,
    active_tile_count,
    bond_atoms,
    cross_atoms,
    cross_side,
    cross_count,
):
    atoms = coords.shape[-1]
    tiles = tile_atoms.shape[2]
    domains = lax.axis_size("dom")
    strides = strides_of(domains)
    rows = Rows(atoms, bond_atoms.shape[-1], cross_side.shape[-1])
    whole_slab = domains == SUBLANES
    copies = domains if whole_slab else 1
    f32 = jnp.float32

    sent = (coords, charge, inv_mass, bond_atoms, cross_atoms, cross_side)
    packed, rim = pl.pallas_call(
        functools.partial(pack_kernel, rows, copies),
        out_shape=(
            jax.ShapeDtypeStruct((copies * rows.count, LANES), f32),
            jax.ShapeDtypeStruct((4 * rows.shell_rows, LANES), f32),
        ),
        in_specs=smem(1) + hbm(len(sent)),
        out_specs=tuple(vmem(2)),
        scratch_shapes=room_for(sent) + [pltpu.SemaphoreType.DMA((len(sent),))],
        compiler_params=params(4),
        name="pack",
    )(cross_count, *in_hbm(sent))

    alone = (coords, charge, velocity, tile_atoms)
    own, near, index, speed = pl.pallas_call(
        functools.partial(own_kernel, rows),
        out_shape=(
            jax.ShapeDtypeStruct((4, atoms, LANES), f32),
            jax.ShapeDtypeStruct((4, tiles, TILE), f32),
            jax.ShapeDtypeStruct((tiles, TILE), jnp.int32),
            jax.ShapeDtypeStruct((rows.disp_used, LANES), f32),
        ),
        in_specs=hbm(len(alone)),
        out_specs=tuple(vmem(4)),
        scratch_shapes=room_for(alone[:3]) + [pltpu.SemaphoreType.DMA((len(alone),))],
        compiler_params=params(4),
        cost_estimate=cost(64 * atoms * LANES, 16 * atoms * LANES),
        name="own",
    )(*in_hbm(alone))

    below = passed_along(rim, "slab", 1)
    above = passed_along(rim, "slab", -1)
    if whole_slab:
        around = lax.all_to_all(packed, "dom", 0, 0, tiled=True)
        here = lax.axis_index("dom").reshape(1)
        holders = [stride % domains for stride in strides]
    else:
        around = jnp.concatenate([packed] + [passed_along(packed, "dom", -stride) for stride in strides], axis=0)
        here = jnp.zeros(1, jnp.int32)
        holders = [1, 2, 3, 4]

    moves = pl.pallas_call(
        functools.partial(force_kernel, rows, copies, holders),
        out_shape=jax.ShapeDtypeStruct((copies * rows.disp_count, LANES), f32),
        in_specs=smem(2) + hbm(1) + vmem(7),
        out_specs=vmem(1)[0],
        scratch_shapes=[
            pltpu.VMEM((4, 6 * rows.shell_rows, SUBLANES, LANES), f32),
            pltpu.VMEM((4, tiles, LANES), f32),
            pltpu.VMEM((3, atoms, LANES), f32),
            pltpu.SMEM(tile_block.shape, jnp.int32),
            pltpu.SemaphoreType.DMA(()),
        ],
        compiler_params=params(8),
        cost_estimate=cost(30 * tiles * TILE * TILE, 4 * around.size),
        name="force",
    )(here, active_tile_count, *in_hbm([tile_block]), around, below, above, own, near, index, speed)

    if not whole_slab:
        return by_exchange(rows, strides, around, moves, cross_count)

    constraint_rows = rows.bond_rows + rows.slot_rows
    weight, inner, cross = pl.pallas_call(
        functools.partial(bond_kernel, rows, domains, strides),
        out_shape=(
            jax.ShapeDtypeStruct((constraint_rows * 3 * domains, LANES), f32),
            pltpu.HBM((domains * rows.bond_rows * LANES, atoms), jnp.bfloat16),
            jax.ShapeDtypeStruct((domains * rows.slot_rows * 5 * LANES, atoms // 2), jnp.bfloat16),
        ),
        in_specs=vmem(1),
        out_specs=tuple(vmem(1) + hbm(1) + vmem(1)),
        scratch_shapes=[
            pltpu.VMEM((rows.slot_rows * 4 * domains, LANES), f32),
            pltpu.VMEM((domains * rows.bond_rows * LANES, atoms), jnp.bfloat16),
            pltpu.SemaphoreType.DMA((domains,)),
        ],
        compiler_params=params(16),
        cost_estimate=cost(8 * domains * (rows.bond_rows * LANES * atoms + rows.slot_rows * 5 * LANES * atoms // 2), 4 * around.size),
        name="bonds",
    )(around)

    every_move = lax.all_to_all(moves, "dom", 0, 0, tiled=True)

    return pl.pallas_call(
        functools.partial(solve_kernel, rows, domains, strides),
        out_shape=(
            jax.ShapeDtypeStruct(coords.shape, f32),
            jax.ShapeDtypeStruct(coords.shape, f32),
        ),
        in_specs=smem(1) + vmem(3) + hbm(1) + vmem(1),
        out_specs=tuple(vmem(2)),
        scratch_shapes=[
            pltpu.VMEM((constraint_rows, SUBLANES * domains, LANES), f32),
            pltpu.VMEM((rows.atom_rows, SUBLANES * domains, LANES), f32),
            pltpu.VMEM(inner.shape, inner.dtype),
            pltpu.SemaphoreType.DMA((domains,)),
        ],
        compiler_params=params(16),
        name="solve",
    )(here, around, every_move, weight, *in_hbm([inner]), cross)


def by_exchange(rows, strides, around, moves, cross_count):
    atom_count = rows.atom_rows * LANES
    shell = rows.shell_rows * LANES
    inside = around.reshape(5, rows.count, LANES)

    def flat(at, count):
        return inside[0, at : at + count].reshape(-1)

    def neighbours(at):
        return inside[1:, at : at + rows.shell_rows].reshape(-1)

    coords = jnp.stack([flat(at, rows.atom_rows) for at in rows.coords])
    inv_mass = flat(rows.mass, rows.atom_rows)
    displace = moves[: rows.disp_used].reshape(3, atom_count)
    left = flat(rows.bond_first, rows.bond_rows).astype(jnp.int32)
    right = flat(rows.bond_second, rows.bond_rows).astype(jnp.int32)
    cross_left = flat(rows.cross_first, rows.slot_rows).astype(jnp.int32)
    cross_right = flat(rows.cross_second, rows.slot_rows).astype(jnp.int32)
    side = flat(rows.side, rows.slot_rows).astype(jnp.int32)
    flag = flat(rows.live, rows.slot_rows)
    cross_index = side * shell + cross_right
    far_coords = jnp.stack([neighbours(at) for at in rows.coords])
    far_mass = neighbours(rows.mass)

    def weights(first, second, mass_first, mass_second):
        gap = first - second
        length = jnp.sqrt(jnp.sum(gap * gap, axis=0) + length_floor)
        return gap / length * lax.rsqrt(mass_first + mass_second)

    inner = weights(coords[:, left], coords[:, right], inv_mass[left], inv_mass[right])
    cross = flag * weights(
        coords[:, cross_left], far_coords[:, cross_index], inv_mass[cross_left], far_mass[cross_index]
    )

    def project(field):
        rim = field[:, :shell]
        far = jnp.concatenate([passed_along(rim, "dom", -stride) for stride in strides], axis=1)
        return (
            jnp.sum(inner * (field[:, left] - field[:, right]), axis=0),
            jnp.sum(cross * (field[:, cross_left] - far[:, cross_index]), axis=0),
        )

    def spread(values):
        pushed = inner * values[0]
        pushed_cross = cross * values[1]
        totals = jnp.zeros((3, atom_count), jnp.float32).at[:, left].add(pushed).at[:, right].add(-pushed)
        totals = totals.at[:, cross_left].add(pushed_cross)
        outward = jnp.zeros((3, 4 * shell), jnp.float32).at[:, cross_index].add(-pushed_cross)
        for code, stride in enumerate(strides):
            totals = totals.at[:, :shell].add(
                passed_along(outward[:, code * shell : (code + 1) * shell], "dom", stride)
            )
        return inv_mass * totals

    residue = project(displace)
    summed = residue
    for _ in range(ORDER):
        change = project(spread(residue))
        residue = tuple(now - step for now, step in zip(residue, change))
        summed = tuple(a + b for a, b in zip(summed, residue))
    move = displace - spread(summed)
    return (
        (coords + move).reshape(3, 1, 1, atom_count),
        (move * (1.0 / time_step)).reshape(3, 1, 1, atom_count),
    )


def solution(mesh):
    return jax.shard_map(
        shards,
        mesh=mesh,
        in_specs=(
            P(None, "slab", "dom", None),
            P(None, "slab", "dom", None),
            P("slab", "dom", None),
            P("slab", "dom", None),
            P("slab", "dom", None),
            P("slab", "dom", None, None),
            P("slab", "dom"),
            P(None, "slab", "dom", None),
            P(None, "slab", "dom", None),
            P("slab", "dom", None),
            P("slab", "dom"),
        ),
        out_specs=(P(None, "slab", "dom", None), P(None, "slab", "dom", None)),
        check_vma=False,
    )
```

```python
import functools

import jax
import jax.numpy as jnp
from jax import lax
from jax.experimental import pallas as pl
from jax.experimental.pallas import tpu as pltpu
from jax.sharding import PartitionSpec as P

TILE = 128
ORDER = 4
LANES = 128
SUBLANES = 8

time_step = 0.1
cutoff_sq = 16.0
force_scale = 4.0
length_floor = 0.25


def passed_along(array, axis, by):
    length = lax.axis_size(axis)
    return lax.ppermute(array, axis, [(i, (i + by) % length) for i in range(length)])


def from_slab(block):
    length = lax.axis_size("dom")
    step = length // 2
    while step:
        other = lax.ppermute(block, "dom", [(i, i ^ step) for i in range(length)])
        block = jnp.concatenate([block, other], axis=0)
        step //= 2
    return block


def place_of(index, me, domains):
    far = index ^ me
    place, step, bit = 0, 1, domains // 2
    while bit:
        place = place + jnp.where((far & bit) != 0, step, 0)
        step *= 2
        bit //= 2
    return place


def in_order(source_ref, target_ref, me, domains):
    count = source_ref.shape[0] // domains
    for index in range(domains):
        start = pl.multiple_of(place_of(index, me, domains) * count, SUBLANES)
        target_ref[pl.ds(index * count, count), :] = source_ref[pl.ds(start, count), :]


def strides_of(domains):
    row_width = max(2, domains // 8)
    return (1, -1, row_width, -row_width)


def round_up(count, step):
    return -(-count // step) * step


class Rows:
    def __init__(self, atoms, bonds, slots):
        self.atom_rows = atoms // LANES
        self.shell_rows = atoms // 2 // LANES
        self.bond_rows = bonds // LANES
        self.slot_rows = slots // LANES
        at = 0
        self.coords = []
        for _ in range(3):
            self.coords.append(at)
            at += self.atom_rows
        self.charge = at
        at += self.atom_rows
        self.mass = at
        at += self.atom_rows
        self.bond_first = at
        at += self.bond_rows
        self.bond_second = at
        at += self.bond_rows
        self.cross_first = at
        at += self.slot_rows
        self.cross_second = at
        at += self.slot_rows
        self.side = at
        at += self.slot_rows
        self.live = at
        at += self.slot_rows
        self.used = at
        self.count = round_up(at, SUBLANES)
        self.shell_terms = (self.bond_rows + 5 * self.slot_rows) * LANES
        self.matrix = self.shell_terms + self.bond_rows * LANES
        self.inner_at = (0, self.shell_terms)
        self.cross_at = self.bond_rows * LANES
        self.disp_used = 3 * self.atom_rows
        self.disp_count = round_up(self.disp_used, SUBLANES)


def take_lanes(table, lanes):
    return jnp.take_along_axis(table, lanes, axis=1, mode="promise_in_bounds")


def pick(tables, index):
    lanes = index & (LANES - 1)
    chunk = index >> 7
    result = take_lanes(tables[0], lanes)
    for k in range(1, len(tables)):
        result = jnp.where(chunk == k, take_lanes(tables[k], lanes), result)
    return result


def rsqrt(value):
    guess = lax.rsqrt(value)
    return guess * (1.5 - 0.5 * value * guess * guess)


def fetched(sources, targets, sem_ref):
    copies = [pltpu.make_async_copy(s, t, sem_ref.at[n]) for n, (s, t) in enumerate(zip(sources, targets))]
    for copy in copies:
        copy.start()
    return copies


def pack_kernel(rows, copies, count_ref, *refs):
    sources, (out_ref, rim_ref), targets, sem_ref = refs[:6], refs[6:8], refs[8:14], refs[14]
    for copy in fetched(sources, targets, sem_ref):
        copy.wait()
    coords_ref, charge_ref, mass_ref, bonds_ref, cross_ref, side_ref = targets

    def put(row, value):
        for part in range(value.shape[1] // LANES):
            piece = value[:, part * LANES : (part + 1) * LANES]
            for copy in range(copies):
                out_ref[pl.ds(copy * rows.count + row + part, 1), :] = piece

    shell = rows.shell_rows * LANES
    fields = [coords_ref[c, 0] for c in range(3)] + [charge_ref[0]]
    for c in range(4):
        at = rows.coords[c] if c < 3 else rows.charge
        put(at, fields[c])
        for part in range(rows.shell_rows):
            rim_ref[pl.ds(c * rows.shell_rows + part, 1), :] = fields[c][:, part * LANES : (part + 1) * LANES]
    put(rows.mass, mass_ref[0])
    put(rows.bond_first, bonds_ref[0, 0].astype(jnp.float32))
    put(rows.bond_second, bonds_ref[1, 0].astype(jnp.float32))
    put(rows.cross_first, cross_ref[0, 0].astype(jnp.float32))
    put(rows.cross_second, cross_ref[1, 0].astype(jnp.float32))
    side = side_ref[0]
    put(rows.side, side.astype(jnp.float32))
    slot = lax.broadcasted_iota(jnp.int32, side.shape, 1)
    put(rows.live, jnp.where(slot < count_ref[0, 0], 1.0, 0.0))
    if rows.count > rows.used:
        for copy in range(copies):
            out_ref[pl.ds(copy * rows.count + rows.used, rows.count - rows.used), :] = jnp.zeros(
                (rows.count - rows.used, LANES), jnp.float32
            )


SHRINK = 1.0 / 4.0


def own_kernel(
    rows, coords_hbm, charge_hbm, velocity_hbm, atoms_hbm, own_ref, far_ref, index_ref, speed_ref, coords_ref, charge_ref, velocity_ref, sem_ref
):
    atom_rows = rows.atom_rows
    copies = fetched(
        (coords_hbm, charge_hbm, atoms_hbm.at[0, 0], velocity_hbm),
        (coords_ref, charge_ref, index_ref, velocity_ref),
        sem_ref,
    )
    down = lax.broadcasted_iota(jnp.int32, (SUBLANES, LANES), 0)
    copies[0].wait()
    copies[1].wait()

    def lanes_of(part):
        return slice(part * LANES, (part + 1) * LANES)

    table = []
    for c in range(4):
        field = coords_ref[c, 0] * SHRINK if c < 3 else charge_ref[0]
        table.append(
            [jnp.broadcast_to(field[:, lanes_of(part)], (SUBLANES, LANES)) for part in range(atom_rows)]
        )
    for part in range(atom_rows):
        for group in range(LANES // SUBLANES):
            at = part * LANES + group * SUBLANES
            for c in range(4):
                value = take_lanes(table[c][part], down + group * SUBLANES)
                own_ref[c, pl.ds(at, SUBLANES), :] = value if c < 3 else value * 8.0
    copies[2].wait()
    for group in range(index_ref.shape[0] // SUBLANES):
        at = pl.ds(group * SUBLANES, SUBLANES)
        index = index_ref[at, :]
        for c in range(4):
            far_ref[c, at, :] = pick(table[c], index)
    copies[3].wait()
    for c in range(3):
        for part in range(atom_rows):
            speed_ref[pl.ds(c * atom_rows + part, 1), :] = velocity_ref[c, 0, :, lanes_of(part)]


def force_kernel(
    rows,
    copies,
    holder,
    here_ref,
    live_ref,
    block_hbm,
    around_ref,
    below_ref,
    above_ref,
    own_ref,
    near_ref,
    index_ref,
    speed_ref,
    out_ref,
    table_ref,
    far_ref,
    sum_ref,
    block_ref,
    sem_ref,
):
    atom_rows, shell_rows = rows.atom_rows, rows.shell_rows
    tiles = index_ref.shape[0]
    block_copy = pltpu.make_async_copy(block_hbm, block_ref, sem_ref)
    block_copy.start()
    me = here_ref[0]
    starts = [rows.coords[0], rows.coords[1], rows.coords[2], rows.charge]
    entry_rows = 6 * shell_rows

    def broadcast(row):
        return jnp.broadcast_to(row, (SUBLANES, LANES))

    for c in range(4):
        factor = SHRINK if c < 3 else 1.0
        at = 0
        for neighbour in range(4):
            base = holder(me, neighbour) * rows.count + starts[c]
            for part in range(shell_rows):
                table_ref[c, at] = broadcast(around_ref[pl.ds(base + part, 1), :] * factor)
                at += 1
        for slab_ref in (below_ref, above_ref):
            for part in range(shell_rows):
                table_ref[c, at] = broadcast(slab_ref[pl.ds(c * shell_rows + part, 1), :] * factor)
                at += 1

    for group in range(tiles // SUBLANES):
        at = pl.ds(group * SUBLANES, SUBLANES)
        index = index_ref[at, :]
        lanes = index & (LANES - 1)
        chunk = index >> 7
        values = [near_ref[c, at, :] for c in range(4)]
        for k in range(entry_rows):
            here = chunk == atom_rows + k
            values = [jnp.where(here, take_lanes(table_ref[c, k], lanes), values[c]) for c in range(4)]
        for c in range(4):
            far_ref[c, at, :] = values[c]

    sum_ref[...] = jnp.zeros(sum_ref.shape, jnp.float32)
    block_copy.wait()

    def add_tile(tile, _):
        base = block_ref[0, 0, tile] * TILE
        far = [broadcast(far_ref[c, pl.ds(tile, 1), :]) for c in range(4)]
        for group in range(TILE // SUBLANES):
            at = pl.ds(pl.multiple_of(base + group * SUBLANES, SUBLANES), SUBLANES)
            gap = [own_ref[c, at, :] - far[c] for c in range(3)]
            square = gap[0] * gap[0] + gap[1] * gap[1] + gap[2] * gap[2]
            shifted = square + 1.0 / cutoff_sq
            inverse = pl.reciprocal(shifted, approx=True)
            inverse = inverse * (2.0 - shifted * inverse)
            switch = jnp.maximum(1.0 - square, 0.0)
            weight = inverse * switch
            strength = (inverse - own_ref[3, at, :] * far[3]) * (weight * weight)
            for c in range(3):
                sum_ref[c, at, :] = sum_ref[c, at, :] + strength * gap[c]
        return 0

    lax.fori_loop(0, live_ref[0, 0], add_tile, 0)

    scale = time_step * time_step * force_scale * 4.0 / 2048.0
    for c in range(3):
        for part in range(atom_rows):
            total = jnp.sum(sum_ref[c, pl.ds(part * LANES, LANES), :].T, axis=0, keepdims=True)
            mass = around_ref[pl.ds(rows.mass + part, 1), :]
            moved = time_step * speed_ref[pl.ds(c * atom_rows + part, 1), :] + scale * total * mass
            for copy in range(copies):
                out_ref[pl.ds(copy * rows.disp_count + c * atom_rows + part, 1), :] = moved
    if rows.disp_count > rows.disp_used:
        for copy in range(copies):
            out_ref[pl.ds(copy * rows.disp_count + rows.disp_used, rows.disp_count - rows.disp_used), :] = jnp.zeros(
                (rows.disp_count - rows.disp_used, LANES), jnp.float32
            )


def bond_kernel(rows, domains, strides, here_ref, blocks_ref, around_ref, weight_ref, matrix_ref, key_ref):
    in_order(blocks_ref, around_ref, here_ref[0], domains)
    atom_rows, shell_rows = rows.atom_rows, rows.shell_rows

    def load(row):
        return around_ref[pl.ds(row, domains, stride=rows.count), :]

    def index(row):
        return load(row).astype(jnp.int32)

    fields = [[load(at + part) for part in range(atom_rows)] for at in rows.coords + [rows.mass]]

    def weights(first, second, row):
        gap = [first[c] - second[c] for c in range(3)]
        length_sq = gap[0] * gap[0] + gap[1] * gap[1] + gap[2] * gap[2] + length_floor
        scale = rsqrt(length_sq) * rsqrt(first[3] + second[3])
        return [gap[c] * scale for c in range(3)]

    at = 0
    for part in range(rows.bond_rows):
        first = index(rows.bond_first + part)
        second = index(rows.bond_second + part)
        values = weights([pick(f, first) for f in fields], [pick(f, second) for f in fields], at)
        for c in range(3):
            weight_ref[pl.ds((at * 3 + c) * domains, domains), :] = values[c]
        at += 1
    for part in range(rows.slot_rows):
        first = index(rows.cross_first + part)
        second = index(rows.cross_second + part)
        side = load(rows.side + part)
        live = load(rows.live + part)
        other = [jnp.zeros((domains, LANES), jnp.float32) for _ in range(4)]
        for code, stride in enumerate(strides):
            seen = pltpu.roll(second, stride % domains, 0)
            for f in range(4):
                value = pltpu.roll(pick(fields[f][:shell_rows], seen), -stride % domains, 0)
                other[f] = jnp.where(side == code, value, other[f])
            key = jnp.where(side == code, load(rows.cross_second + part), -1.0)
            key_ref[pl.ds((part * 4 + code) * domains, domains), :] = key
        values = weights([pick(f[:shell_rows], first) for f in fields], other, at)
        for c in range(3):
            weight_ref[pl.ds((at * 3 + c) * domains, domains), :] = values[c] * live
        at += 1

    down = lax.broadcasted_iota(jnp.int32, (SUBLANES, LANES), 0)
    across = lax.broadcasted_iota(jnp.int32, (SUBLANES, LANES), 1).astype(jnp.float32)
    pair = 2 * SUBLANES

    def column(row, group):
        return take_lanes(jnp.broadcast_to(row, (SUBLANES, LANES)), down + group * SUBLANES)

    def put(at, columns, signs, half):
        for block in range(shell_rows):
            lanes = across + float((half * shell_rows + block) * LANES)
            halves = []
            for ends in columns:
                value = 0.0
                for end, sign in zip(ends, signs):
                    value = jnp.where(end == lanes, sign, value)
                halves.append(value)
            matrix_ref[pl.ds(at, pair), block * LANES : (block + 1) * LANES] = jnp.concatenate(
                halves, axis=0
            ).astype(jnp.bfloat16)

    def build(domain, _):
        start = pl.multiple_of(domain * rows.matrix, LANES)
        for part in range(rows.bond_rows):
            first = around_ref[pl.ds(domain * rows.count + rows.bond_first + part, 1), :]
            second = around_ref[pl.ds(domain * rows.count + rows.bond_second + part, 1), :]
            for step in range(LANES // pair):
                columns = [(column(first, 2 * step + h), column(second, 2 * step + h)) for h in range(2)]
                for half in range(2):
                    put(start + rows.inner_at[half] + part * LANES + step * pair, columns, (1.0, -1.0), half)
        for part in range(rows.slot_rows):
            for code in range(5):
                if code == 0:
                    row = around_ref[pl.ds(domain * rows.count + rows.cross_first + part, 1), :]
                else:
                    owner = lax.rem(domain + (-strides[code - 1]) % domains, domains)
                    row = key_ref[pl.ds((part * 4 + code - 1) * domains + owner, 1), :]
                sign = 1.0 if code == 0 else -1.0
                for step in range(LANES // pair):
                    columns = [(column(row, 2 * step + h),) for h in range(2)]
                    put(start + rows.cross_at + (part * 5 + code) * LANES + step * pair, columns, (sign,), 0)
        return 0

    lax.fori_loop(0, domains, build, 0)


def solve_kernel(
    rows,
    domains,
    strides,
    here_ref,
    around_ref,
    blocks_ref,
    weight_ref,
    matrix_ref,
    coords_out_ref,
    velocity_out_ref,
    moves_ref,
    push_ref,
    field_ref,
):
    atom_rows, shell_rows = rows.atom_rows, rows.shell_rows
    bond_rows, slot_rows = rows.bond_rows, rows.slot_rows
    me = here_ref[0]
    in_order(blocks_ref, moves_ref, me, domains)

    def load(row):
        return around_ref[pl.ds(row, domains, stride=rows.count), :]

    def index(row):
        return load(row).astype(jnp.int32)

    inner_first = [index(rows.bond_first + p) for p in range(bond_rows)]
    inner_second = [index(rows.bond_second + p) for p in range(bond_rows)]
    cross_first = [index(rows.cross_first + p) for p in range(slot_rows)]
    cross_second = [index(rows.cross_second + p) for p in range(slot_rows)]
    sides = [load(rows.side + p) for p in range(slot_rows)]
    masses = [load(rows.mass + p) for p in range(atom_rows)]

    def weight(at, c):
        return weight_ref[pl.ds((at * 3 + c) * domains, domains), :]

    def project(fields):
        result = []
        for part in range(bond_rows):
            total = 0.0
            for c in range(3):
                ends = pick(fields[c], inner_first[part]) - pick(fields[c], inner_second[part])
                total = total + weight(part, c) * ends
            result.append(total)
        for part in range(slot_rows):
            seen = [pltpu.roll(cross_second[part], stride % domains, 0) for stride in strides]
            total = 0.0
            for c in range(3):
                shell = fields[c][:shell_rows]
                other = 0.0
                for code, stride in enumerate(strides):
                    value = pltpu.roll(pick(shell, seen[code]), -stride % domains, 0)
                    other = jnp.where(sides[part] == code, value, other)
                total = total + weight(bond_rows + part, c) * (pick(shell, cross_first[part]) - other)
            result.append(total)
        return result

    def put_pushes(values):
        for at, value in enumerate(values):
            for c in range(3):
                pushed = weight(at, c) * value
                high = pushed.astype(jnp.bfloat16).astype(jnp.float32)
                push_ref[at, pl.ds(c * domains, domains), :] = high
                push_ref[at, pl.ds((3 + c) * domains, domains), :] = pushed - high

    def pushes_of(at, domain):
        return push_ref[at, pl.ds(domain, SUBLANES, stride=domains), :].astype(jnp.bfloat16)

    def totals(domain, owners):
        inner = [pushes_of(p, domain) for p in range(bond_rows)]
        cross = []
        for part in range(slot_rows):
            cross.extend(pushes_of(bond_rows + part, owner) for owner in [domain] + owners)
        start = domain * rows.matrix
        if not isinstance(start, int):
            start = pl.multiple_of(start, LANES)
        shell_sum = jnp.dot(
            jnp.concatenate(inner + cross, axis=1),
            matrix_ref[pl.ds(start, rows.shell_terms), :],
            preferred_element_type=jnp.float32,
        )
        other_sum = jnp.dot(
            jnp.concatenate(inner, axis=1),
            matrix_ref[pl.ds(start + rows.shell_terms, bond_rows * LANES), :],
            preferred_element_type=jnp.float32,
        )
        return [
            half[:, p * LANES : (p + 1) * LANES] for half in (shell_sum, other_sum) for p in range(shell_rows)
        ]

    def spread(values):
        put_pushes(values)
        for domain in range(domains):
            sums = totals(domain, [(domain - stride) % domains for stride in strides])
            for part in range(atom_rows):
                field_ref[part, pl.ds(domain, SUBLANES, stride=domains), :] = sums[part]
        return [
            [
                masses[part]
                * (
                    field_ref[part, pl.ds(c * domains, domains), :]
                    + field_ref[part, pl.ds((3 + c) * domains, domains), :]
                )
                for part in range(atom_rows)
            ]
            for c in range(3)
        ]

    moves = [
        [moves_ref[pl.ds(c * atom_rows + p, domains, stride=rows.disp_count), :] for p in range(atom_rows)]
        for c in range(3)
    ]
    push_ref[...] = jnp.zeros(push_ref.shape, jnp.float32)
    residue = project(moves)

    def expand(_, carry):
        residue, summed = carry
        change = project(spread(residue))
        residue = [now - step for now, step in zip(residue, change)]
        return residue, [a + b for a, b in zip(summed, residue)]

    residue, summed = lax.fori_loop(0, ORDER, expand, (residue, residue))
    put_pushes(summed)
    sums = totals(me, [lax.rem(me + (-stride) % domains, domains) for stride in strides])
    for part in range(atom_rows):
        lanes = slice(part * LANES, (part + 1) * LANES)
        mass = around_ref[pl.ds(me * rows.count + rows.mass + part, 1), :]
        for c in range(3):
            correction = mass * (sums[part][c : c + 1, :] + sums[part][3 + c : 4 + c, :])
            move = moves_ref[pl.ds(me * rows.disp_count + c * atom_rows + part, 1), :] - correction
            start = around_ref[pl.ds(me * rows.count + rows.coords[c] + part, 1), :]
            coords_out_ref[c, 0, :, lanes] = start + move
            velocity_out_ref[c, 0, :, lanes] = move * (1.0 / time_step)


def vmem(count):
    return [pl.BlockSpec(memory_space=pltpu.VMEM)] * count


def smem(count):
    return [pl.BlockSpec(memory_space=pltpu.SMEM)] * count


def hbm(count):
    return [pl.BlockSpec(memory_space=pltpu.HBM)] * count


def in_hbm(arrays):
    return [pltpu.with_memory_space_constraint(a, pltpu.HBM) for a in arrays]


def params(mebibytes):
    return pltpu.CompilerParams(vmem_limit_bytes=mebibytes * 1024 * 1024)


def cost(flops, moved):
    return pl.CostEstimate(flops=flops, bytes_accessed=moved, transcendentals=0)


def room_for(arrays):
    return [pltpu.VMEM(a.shape, a.dtype) for a in arrays]


def shards(
    coords,
    velocity,
    charge,
    inv_mass,
    tile_block,
    tile_atoms,
    active_tile_count,
    bond_atoms,
    cross_atoms,
    cross_side,
    cross_count,
):
    atoms = coords.shape[-1]
    tiles = tile_atoms.shape[2]
    domains = lax.axis_size("dom")
    strides = strides_of(domains)
    rows = Rows(atoms, bond_atoms.shape[-1], cross_side.shape[-1])
    whole_slab = domains == SUBLANES
    copies = 1
    f32 = jnp.float32

    sent = (coords, charge, inv_mass, bond_atoms, cross_atoms, cross_side)
    packed, rim = pl.pallas_call(
        functools.partial(pack_kernel, rows, copies),
        out_shape=(
            jax.ShapeDtypeStruct((copies * rows.count, LANES), f32),
            jax.ShapeDtypeStruct((4 * rows.shell_rows, LANES), f32),
        ),
        in_specs=smem(1) + hbm(len(sent)),
        out_specs=tuple(vmem(2)),
        scratch_shapes=room_for(sent) + [pltpu.SemaphoreType.DMA((len(sent),))],
        compiler_params=params(4),
        name="pack",
    )(cross_count, *in_hbm(sent))

    alone = (coords, charge, velocity, tile_atoms)
    own, near, index, speed = pl.pallas_call(
        functools.partial(own_kernel, rows),
        out_shape=(
            jax.ShapeDtypeStruct((4, atoms, LANES), f32),
            jax.ShapeDtypeStruct((4, tiles, TILE), f32),
            jax.ShapeDtypeStruct((tiles, TILE), jnp.int32),
            jax.ShapeDtypeStruct((rows.disp_used, LANES), f32),
        ),
        in_specs=hbm(len(alone)),
        out_specs=tuple(vmem(4)),
        scratch_shapes=room_for(alone[:3]) + [pltpu.SemaphoreType.DMA((len(alone),))],
        compiler_params=params(4),
        cost_estimate=cost(64 * atoms * LANES, 16 * atoms * LANES),
        name="own",
    )(*in_hbm(alone))

    below = passed_along(rim, "slab", 1)
    above = passed_along(rim, "slab", -1)
    if whole_slab:
        around = from_slab(packed)
        here = lax.axis_index("dom").reshape(1)

        def holder(me, neighbour):
            return place_of(lax.rem(me + strides[neighbour] % domains, domains), me, domains)

    else:
        around = jnp.concatenate([packed] + [passed_along(packed, "dom", -stride) for stride in strides], axis=0)
        here = jnp.zeros(1, jnp.int32)

        def holder(me, neighbour):
            return neighbour + 1


    moves = pl.pallas_call(
        functools.partial(force_kernel, rows, copies, holder),
        out_shape=jax.ShapeDtypeStruct((copies * rows.disp_count, LANES), f32),
        in_specs=smem(2) + hbm(1) + vmem(7),
        out_specs=vmem(1)[0],
        scratch_shapes=[
            pltpu.VMEM((4, 6 * rows.shell_rows, SUBLANES, LANES), f32),
            pltpu.VMEM((4, tiles, LANES), f32),
            pltpu.VMEM((3, atoms, LANES), f32),
            pltpu.SMEM(tile_block.shape, jnp.int32),
            pltpu.SemaphoreType.DMA(()),
        ],
        compiler_params=params(8),
        cost_estimate=cost(30 * tiles * TILE * TILE, 4 * around.size),
        name="force",
    )(here, active_tile_count, *in_hbm([tile_block]), around, below, above, own, near, index, speed)

    if not whole_slab:
        return by_exchange(rows, strides, around, moves, cross_count)

    constraint_rows = rows.bond_rows + rows.slot_rows
    ordered, weight, matrix = pl.pallas_call(
        functools.partial(bond_kernel, rows, domains, strides),
        out_shape=(
            jax.ShapeDtypeStruct(around.shape, f32),
            jax.ShapeDtypeStruct((constraint_rows * 3 * domains, LANES), f32),
            jax.ShapeDtypeStruct((domains * rows.matrix, atoms // 2), jnp.bfloat16),
        ),
        in_specs=smem(1) + vmem(1),
        out_specs=tuple(vmem(3)),
        scratch_shapes=[pltpu.VMEM((rows.slot_rows * 4 * domains, LANES), f32)],
        compiler_params=params(16),
        cost_estimate=cost(8 * domains * rows.matrix * atoms // 2, 4 * around.size),
        name="bonds",
    )(here, around)

    every_move = from_slab(moves)

    return pl.pallas_call(
        functools.partial(solve_kernel, rows, domains, strides),
        out_shape=(
            jax.ShapeDtypeStruct(coords.shape, f32),
            jax.ShapeDtypeStruct(coords.shape, f32),
        ),
        in_specs=smem(1) + vmem(4),
        out_specs=tuple(vmem(2)),
        scratch_shapes=[
            pltpu.VMEM(every_move.shape, f32),
            pltpu.VMEM((constraint_rows, SUBLANES * domains, LANES), f32),
            pltpu.VMEM((rows.atom_rows, SUBLANES * domains, LANES), f32),
        ],
        compiler_params=params(16),
        name="solve",
    )(here, ordered, every_move, weight, matrix)


def by_exchange(rows, strides, around, moves, cross_count):
    atom_count = rows.atom_rows * LANES
    shell = rows.shell_rows * LANES
    inside = around.reshape(5, rows.count, LANES)

    def flat(at, count):
        return inside[0, at : at + count].reshape(-1)

    def neighbours(at):
        return inside[1:, at : at + rows.shell_rows].reshape(-1)

    coords = jnp.stack([flat(at, rows.atom_rows) for at in rows.coords])
    inv_mass = flat(rows.mass, rows.atom_rows)
    displace = moves[: rows.disp_used].reshape(3, atom_count)
    left = flat(rows.bond_first, rows.bond_rows).astype(jnp.int32)
    right = flat(rows.bond_second, rows.bond_rows).astype(jnp.int32)
    cross_left = flat(rows.cross_first, rows.slot_rows).astype(jnp.int32)
    cross_right = flat(rows.cross_second, rows.slot_rows).astype(jnp.int32)
    side = flat(rows.side, rows.slot_rows).astype(jnp.int32)
    flag = flat(rows.live, rows.slot_rows)
    cross_index = side * shell + cross_right
    far_coords = jnp.stack([neighbours(at) for at in rows.coords])
    far_mass = neighbours(rows.mass)

    def weights(first, second, mass_first, mass_second):
        gap = first - second
        length = jnp.sqrt(jnp.sum(gap * gap, axis=0) + length_floor)
        return gap / length * lax.rsqrt(mass_first + mass_second)

    inner = weights(coords[:, left], coords[:, right], inv_mass[left], inv_mass[right])
    cross = flag * weights(
        coords[:, cross_left], far_coords[:, cross_index], inv_mass[cross_left], far_mass[cross_index]
    )

    def project(field):
        rim = field[:, :shell]
        far = jnp.concatenate([passed_along(rim, "dom", -stride) for stride in strides], axis=1)
        return (
            jnp.sum(inner * (field[:, left] - field[:, right]), axis=0),
            jnp.sum(cross * (field[:, cross_left] - far[:, cross_index]), axis=0),
        )

    def spread(values):
        pushed = inner * values[0]
        pushed_cross = cross * values[1]
        totals = jnp.zeros((3, atom_count), jnp.float32).at[:, left].add(pushed).at[:, right].add(-pushed)
        totals = totals.at[:, cross_left].add(pushed_cross)
        outward = jnp.zeros((3, 4 * shell), jnp.float32).at[:, cross_index].add(-pushed_cross)
        for code, stride in enumerate(strides):
            totals = totals.at[:, :shell].add(
                passed_along(outward[:, code * shell : (code + 1) * shell], "dom", stride)
            )
        return inv_mass * totals

    residue = project(displace)
    summed = residue
    for _ in range(ORDER):
        change = project(spread(residue))
        residue = tuple(now - step for now, step in zip(residue, change))
        summed = tuple(a + b for a, b in zip(summed, residue))
    move = displace - spread(summed)
    return (
        (coords + move).reshape(3, 1, 1, atom_count),
        (move * (1.0 / time_step)).reshape(3, 1, 1, atom_count),
    )


def solution(mesh):
    return jax.shard_map(
        shards,
        mesh=mesh,
        in_specs=(
            P(None, "slab", "dom", None),
            P(None, "slab", "dom", None),
            P("slab", "dom", None),
            P("slab", "dom", None),
            P("slab", "dom", None),
            P("slab", "dom", None, None),
            P("slab", "dom"),
            P(None, "slab", "dom", None),
            P(None, "slab", "dom", None),
            P("slab", "dom", None),
            P("slab", "dom"),
        ),
        out_specs=(P(None, "slab", "dom", None), P(None, "slab", "dom", None)),
        check_vma=False,
    )
```

```python
import functools

import jax
import jax.numpy as jnp
from jax import lax
from jax.experimental import pallas as pl
from jax.experimental.pallas import tpu as pltpu
from jax.sharding import PartitionSpec as P

TILE = 128
ORDER = 4
LANES = 128
SUBLANES = 8

time_step = 0.1
cutoff_sq = 16.0
force_scale = 4.0
length_floor = 0.25


def passed_along(array, axis, by):
    length = lax.axis_size(axis)
    return lax.ppermute(array, axis, [(i, (i + by) % length) for i in range(length)])


def strides_of(domains):
    row_width = max(2, domains // 8)
    return (1, -1, row_width, -row_width)


def round_up(count, step):
    return -(-count // step) * step


class Rows:
    def __init__(self, atoms, bonds, slots):
        self.atom_rows = atoms // LANES
        self.shell_rows = atoms // 2 // LANES
        self.bond_rows = bonds // LANES
        self.slot_rows = slots // LANES
        at = 0
        self.coords = []
        for _ in range(3):
            self.coords.append(at)
            at += self.atom_rows
        self.mass = at
        at += self.atom_rows
        self.bond_first = at
        at += self.bond_rows
        self.bond_second = at
        at += self.bond_rows
        self.cross_first = at
        at += self.slot_rows
        self.cross_second = at
        at += self.slot_rows
        self.side = at
        at += self.slot_rows
        self.live = at
        at += self.slot_rows
        self.used = at
        self.count = round_up(at, SUBLANES)
        self.rim = 4 * self.shell_rows
        self.shell_terms = (self.bond_rows + 5 * self.slot_rows) * LANES
        self.matrix = self.shell_terms + self.bond_rows * LANES
        self.inner_at = (0, self.shell_terms)
        self.cross_at = self.bond_rows * LANES
        self.disp_used = 3 * self.atom_rows
        self.disp_count = round_up(self.disp_used, SUBLANES)


def take_lanes(table, lanes):
    return jnp.take_along_axis(table, lanes, axis=1, mode="promise_in_bounds")


def pick(tables, index):
    lanes = index & (LANES - 1)
    chunk = index >> 7
    result = take_lanes(tables[0], lanes)
    for k in range(1, len(tables)):
        result = jnp.where(chunk == k, take_lanes(tables[k], lanes), result)
    return result


def rsqrt(value):
    guess = lax.rsqrt(value)
    return guess * (1.5 - 0.5 * value * guess * guess)


def fetched(sources, targets, sem_ref):
    copies = [pltpu.make_async_copy(s, t, sem_ref.at[n]) for n, (s, t) in enumerate(zip(sources, targets))]
    for copy in copies:
        copy.start()
    return copies


def pack_kernel(rows, copies, count_ref, *refs):
    sources, (rim_ref, out_ref), targets, sem_ref = refs[:6], refs[6:8], refs[8:14], refs[14]
    for copy in fetched(sources, targets, sem_ref):
        copy.wait()
    coords_ref, charge_ref, mass_ref, bonds_ref, cross_ref, side_ref = targets

    def put(row, value):
        for part in range(value.shape[1] // LANES):
            piece = value[:, part * LANES : (part + 1) * LANES]
            for copy in range(copies):
                out_ref[pl.ds(copy * rows.count + row + part, 1), :] = piece

    fields = [coords_ref[c, 0] for c in range(3)] + [charge_ref[0]]
    for c in range(4):
        for part in range(rows.shell_rows):
            rim_ref[pl.ds(c * rows.shell_rows + part, 1), :] = fields[c][:, part * LANES : (part + 1) * LANES]
    for c in range(3):
        put(rows.coords[c], fields[c])
    put(rows.mass, mass_ref[0])
    put(rows.bond_first, bonds_ref[0, 0].astype(jnp.float32))
    put(rows.bond_second, bonds_ref[1, 0].astype(jnp.float32))
    put(rows.cross_first, cross_ref[0, 0].astype(jnp.float32))
    put(rows.cross_second, cross_ref[1, 0].astype(jnp.float32))
    side = side_ref[0]
    put(rows.side, side.astype(jnp.float32))
    slot = lax.broadcasted_iota(jnp.int32, side.shape, 1)
    put(rows.live, jnp.where(slot < count_ref[0, 0], 1.0, 0.0))
    for row in range(rows.used, rows.count):
        put(row, jnp.zeros((1, LANES), jnp.float32))


SHRINK = 1.0 / 4.0


def own_kernel(
    rows,
    coords_hbm,
    charge_hbm,
    velocity_hbm,
    mass_hbm,
    atoms_hbm,
    own_ref,
    far_ref,
    index_ref,
    motion_ref,
    coords_ref,
    charge_ref,
    velocity_ref,
    mass_ref,
    sem_ref,
):
    atom_rows = rows.atom_rows
    copies = fetched(
        (coords_hbm, charge_hbm, atoms_hbm.at[0, 0], velocity_hbm, mass_hbm),
        (coords_ref, charge_ref, index_ref, velocity_ref, mass_ref),
        sem_ref,
    )
    down = lax.broadcasted_iota(jnp.int32, (SUBLANES, LANES), 0)
    copies[0].wait()
    copies[1].wait()

    def lanes_of(part):
        return slice(part * LANES, (part + 1) * LANES)

    table = []
    for c in range(4):
        field = coords_ref[c, 0] * SHRINK if c < 3 else charge_ref[0]
        table.append(
            [jnp.broadcast_to(field[:, lanes_of(part)], (SUBLANES, LANES)) for part in range(atom_rows)]
        )
    for part in range(atom_rows):
        for group in range(LANES // SUBLANES):
            at = part * LANES + group * SUBLANES
            for c in range(4):
                value = take_lanes(table[c][part], down + group * SUBLANES)
                own_ref[c, pl.ds(at, SUBLANES), :] = value if c < 3 else value * 8.0
    copies[2].wait()
    for group in range(index_ref.shape[0] // SUBLANES):
        at = pl.ds(group * SUBLANES, SUBLANES)
        index = index_ref[at, :]
        for c in range(4):
            far_ref[c, at, :] = pick(table[c], index)
    copies[3].wait()
    copies[4].wait()
    for c in range(4):
        field = velocity_ref[c, 0] if c < 3 else mass_ref[0]
        for part in range(atom_rows):
            motion_ref[pl.ds(c * atom_rows + part, 1), :] = field[:, lanes_of(part)]


def force_kernel(
    rows,
    copies,
    live_ref,
    block_hbm,
    rims_ref,
    below_ref,
    above_ref,
    own_ref,
    near_ref,
    index_ref,
    motion_ref,
    out_ref,
    table_ref,
    far_ref,
    sum_ref,
    block_ref,
    sem_ref,
):
    atom_rows, shell_rows = rows.atom_rows, rows.shell_rows
    tiles = index_ref.shape[0]
    block_copy = pltpu.make_async_copy(block_hbm, block_ref, sem_ref)
    block_copy.start()
    entry_rows = 6 * shell_rows

    def broadcast(row):
        return jnp.broadcast_to(row, (SUBLANES, LANES))

    for c in range(4):
        factor = SHRINK if c < 3 else 1.0
        at = 0
        for neighbour in range(4):
            for part in range(shell_rows):
                row = neighbour * rows.rim + c * shell_rows + part
                table_ref[c, at] = broadcast(rims_ref[pl.ds(row, 1), :] * factor)
                at += 1
        for slab_ref in (below_ref, above_ref):
            for part in range(shell_rows):
                table_ref[c, at] = broadcast(slab_ref[pl.ds(c * shell_rows + part, 1), :] * factor)
                at += 1

    for group in range(tiles // SUBLANES):
        at = pl.ds(group * SUBLANES, SUBLANES)
        index = index_ref[at, :]
        lanes = index & (LANES - 1)
        chunk = index >> 7
        values = [near_ref[c, at, :] for c in range(4)]
        for k in range(entry_rows):
            here = chunk == atom_rows + k
            values = [jnp.where(here, take_lanes(table_ref[c, k], lanes), values[c]) for c in range(4)]
        for c in range(4):
            far_ref[c, at, :] = values[c]

    sum_ref[...] = jnp.zeros(sum_ref.shape, jnp.float32)
    block_copy.wait()

    def add_tile(tile, _):
        base = block_ref[0, 0, tile] * TILE
        far = [broadcast(far_ref[c, pl.ds(tile, 1), :]) for c in range(4)]
        for group in range(TILE // SUBLANES):
            at = pl.ds(pl.multiple_of(base + group * SUBLANES, SUBLANES), SUBLANES)
            gap = [own_ref[c, at, :] - far[c] for c in range(3)]
            square = gap[0] * gap[0] + gap[1] * gap[1] + gap[2] * gap[2]
            shifted = square + 1.0 / cutoff_sq
            inverse = pl.reciprocal(shifted, approx=True)
            inverse = inverse * (2.0 - shifted * inverse)
            switch = jnp.maximum(1.0 - square, 0.0)
            weight = inverse * switch
            strength = (inverse - own_ref[3, at, :] * far[3]) * (weight * weight)
            for c in range(3):
                sum_ref[c, at, :] = sum_ref[c, at, :] + strength * gap[c]
        return 0

    lax.fori_loop(0, live_ref[0, 0], add_tile, 0)

    scale = time_step * time_step * force_scale * 4.0 / 2048.0
    for c in range(3):
        for part in range(atom_rows):
            total = jnp.sum(sum_ref[c, pl.ds(part * LANES, LANES), :].T, axis=0, keepdims=True)
            mass = motion_ref[pl.ds(3 * atom_rows + part, 1), :]
            moved = time_step * motion_ref[pl.ds(c * atom_rows + part, 1), :] + scale * total * mass
            for copy in range(copies):
                out_ref[pl.ds(copy * rows.disp_count + c * atom_rows + part, 1), :] = moved
    if rows.disp_count > rows.disp_used:
        for copy in range(copies):
            out_ref[pl.ds(copy * rows.disp_count + rows.disp_used, rows.disp_count - rows.disp_used), :] = jnp.zeros(
                (rows.disp_count - rows.disp_used, LANES), jnp.float32
            )


def bond_kernel(rows, domains, strides, around_ref, weight_ref, matrix_ref, key_ref):
    atom_rows, shell_rows = rows.atom_rows, rows.shell_rows

    def load(row):
        return around_ref[pl.ds(row, domains, stride=rows.count), :]

    def index(row):
        return load(row).astype(jnp.int32)

    fields = [[load(at + part) for part in range(atom_rows)] for at in rows.coords + [rows.mass]]

    def weights(first, second, row):
        gap = [first[c] - second[c] for c in range(3)]
        length_sq = gap[0] * gap[0] + gap[1] * gap[1] + gap[2] * gap[2] + length_floor
        scale = rsqrt(length_sq) * rsqrt(first[3] + second[3])
        return [gap[c] * scale for c in range(3)]

    at = 0
    for part in range(rows.bond_rows):
        first = index(rows.bond_first + part)
        second = index(rows.bond_second + part)
        values = weights([pick(f, first) for f in fields], [pick(f, second) for f in fields], at)
        for c in range(3):
            weight_ref[pl.ds((at * 3 + c) * domains, domains), :] = values[c]
        at += 1
    for part in range(rows.slot_rows):
        first = index(rows.cross_first + part)
        second = index(rows.cross_second + part)
        side = load(rows.side + part)
        live = load(rows.live + part)
        other = [jnp.zeros((domains, LANES), jnp.float32) for _ in range(4)]
        for code, stride in enumerate(strides):
            seen = pltpu.roll(second, stride % domains, 0)
            for f in range(4):
                value = pltpu.roll(pick(fields[f][:shell_rows], seen), -stride % domains, 0)
                other[f] = jnp.where(side == code, value, other[f])
            key = jnp.where(side == code, load(rows.cross_second + part), -1.0)
            key_ref[pl.ds((part * 4 + code) * domains, domains), :] = key
        values = weights([pick(f[:shell_rows], first) for f in fields], other, at)
        for c in range(3):
            weight_ref[pl.ds((at * 3 + c) * domains, domains), :] = values[c] * live
        at += 1

    down = lax.broadcasted_iota(jnp.int32, (SUBLANES, LANES), 0)
    across = lax.broadcasted_iota(jnp.int32, (SUBLANES, LANES), 1).astype(jnp.float32)
    group_rows = 4 * SUBLANES

    def column(row, group):
        return take_lanes(jnp.broadcast_to(row, (SUBLANES, LANES)), down + group * SUBLANES)

    def put(at, columns, signs, half):
        for block in range(shell_rows):
            lanes = across + float((half * shell_rows + block) * LANES)
            halves = []
            for ends in columns:
                value = 0.0
                for end, sign in zip(ends, signs):
                    value = jnp.where(end == lanes, sign, value)
                halves.append(value)
            matrix_ref[pl.ds(at, group_rows), block * LANES : (block + 1) * LANES] = jnp.concatenate(
                halves, axis=0
            ).astype(matrix_ref.dtype)

    def build(domain, _):
        start = pl.multiple_of(domain * rows.matrix, LANES)
        for part in range(rows.bond_rows):
            first = around_ref[pl.ds(domain * rows.count + rows.bond_first + part, 1), :]
            second = around_ref[pl.ds(domain * rows.count + rows.bond_second + part, 1), :]
            for step in range(LANES // group_rows):
                columns = [(column(first, 4 * step + h), column(second, 4 * step + h)) for h in range(4)]
                for half in range(2):
                    put(start + rows.inner_at[half] + part * LANES + step * group_rows, columns, (1.0, -1.0), half)
        for part in range(rows.slot_rows):
            for code in range(5):
                if code == 0:
                    row = around_ref[pl.ds(domain * rows.count + rows.cross_first + part, 1), :]
                else:
                    owner = lax.rem(domain + (-strides[code - 1]) % domains, domains)
                    row = key_ref[pl.ds((part * 4 + code - 1) * domains + owner, 1), :]
                sign = 1.0 if code == 0 else -1.0
                for step in range(LANES // group_rows):
                    columns = [(column(row, 4 * step + h),) for h in range(4)]
                    put(start + rows.cross_at + (part * 5 + code) * LANES + step * group_rows, columns, (sign,), 0)
        return 0

    lax.fori_loop(0, domains, build, 0)


def solve_kernel(
    rows,
    domains,
    strides,
    here_ref,
    around_ref,
    moves_ref,
    weight_ref,
    signs_ref,
    coords_out_ref,
    velocity_out_ref,
    push_ref,
    field_ref,
    matrix_ref,
):
    atom_rows, shell_rows = rows.atom_rows, rows.shell_rows
    bond_rows, slot_rows = rows.bond_rows, rows.slot_rows
    me = here_ref[0]

    def widen(domain, _):
        at = pl.ds(pl.multiple_of(domain * rows.matrix, LANES), rows.matrix)
        matrix_ref[at, :] = signs_ref[at, :].astype(matrix_ref.dtype)
        return 0

    lax.fori_loop(0, domains, widen, 0)

    def load(row):
        return around_ref[pl.ds(row, domains, stride=rows.count), :]

    def index(row):
        return load(row).astype(jnp.int32)

    inner_first = [index(rows.bond_first + p) for p in range(bond_rows)]
    inner_second = [index(rows.bond_second + p) for p in range(bond_rows)]
    cross_first = [index(rows.cross_first + p) for p in range(slot_rows)]
    cross_second = [index(rows.cross_second + p) for p in range(slot_rows)]
    sides = [load(rows.side + p) for p in range(slot_rows)]
    masses = [load(rows.mass + p) for p in range(atom_rows)]

    def weight(at, c):
        return weight_ref[pl.ds((at * 3 + c) * domains, domains), :]

    def project(fields):
        result = []
        for part in range(bond_rows):
            total = 0.0
            for c in range(3):
                ends = pick(fields[c], inner_first[part]) - pick(fields[c], inner_second[part])
                total = total + weight(part, c) * ends
            result.append(total)
        for part in range(slot_rows):
            seen = [pltpu.roll(cross_second[part], stride % domains, 0) for stride in strides]
            total = 0.0
            for c in range(3):
                shell = fields[c][:shell_rows]
                other = 0.0
                for code, stride in enumerate(strides):
                    value = pltpu.roll(pick(shell, seen[code]), -stride % domains, 0)
                    other = jnp.where(sides[part] == code, value, other)
                total = total + weight(bond_rows + part, c) * (pick(shell, cross_first[part]) - other)
            result.append(total)
        return result

    def put_pushes(values):
        for at, value in enumerate(values):
            for c in range(3):
                pushed = weight(at, c) * value
                high = pushed.astype(jnp.bfloat16).astype(jnp.float32)
                push_ref[at, pl.ds(c * domains, domains), :] = high
                push_ref[at, pl.ds((3 + c) * domains, domains), :] = pushed - high

    def pushes_of(at, domain):
        return push_ref[at, pl.ds(domain, SUBLANES, stride=domains), :].astype(jnp.bfloat16)

    def totals(domain, owners):
        inner = [pushes_of(p, domain) for p in range(bond_rows)]
        cross = []
        for part in range(slot_rows):
            cross.extend(pushes_of(bond_rows + part, owner) for owner in [domain] + owners)
        start = domain * rows.matrix
        if not isinstance(start, int):
            start = pl.multiple_of(start, LANES)
        shell_sum = jnp.dot(
            jnp.concatenate(inner + cross, axis=1),
            matrix_ref[pl.ds(start, rows.shell_terms), :],
            preferred_element_type=jnp.float32,
        )
        other_sum = jnp.dot(
            jnp.concatenate(inner, axis=1),
            matrix_ref[pl.ds(start + rows.shell_terms, bond_rows * LANES), :],
            preferred_element_type=jnp.float32,
        )
        return [
            half[:, p * LANES : (p + 1) * LANES] for half in (shell_sum, other_sum) for p in range(shell_rows)
        ]

    def spread(values):
        put_pushes(values)
        for domain in range(domains):
            sums = totals(domain, [(domain - stride) % domains for stride in strides])
            for part in range(atom_rows):
                field_ref[part, pl.ds(domain, SUBLANES, stride=domains), :] = sums[part]
        return [
            [
                masses[part]
                * (
                    field_ref[part, pl.ds(c * domains, domains), :]
                    + field_ref[part, pl.ds((3 + c) * domains, domains), :]
                )
                for part in range(atom_rows)
            ]
            for c in range(3)
        ]

    moves = [
        [moves_ref[pl.ds(c * atom_rows + p, domains, stride=rows.disp_count), :] for p in range(atom_rows)]
        for c in range(3)
    ]
    push_ref[...] = jnp.zeros(push_ref.shape, jnp.float32)
    residue = project(moves)

    def expand(_, carry):
        residue, summed = carry
        change = project(spread(residue))
        residue = [now - step for now, step in zip(residue, change)]
        return residue, [a + b for a, b in zip(summed, residue)]

    residue, summed = lax.fori_loop(0, ORDER, expand, (residue, residue))
    put_pushes(summed)
    sums = totals(me, [lax.rem(me + (-stride) % domains, domains) for stride in strides])
    for part in range(atom_rows):
        lanes = slice(part * LANES, (part + 1) * LANES)
        mass = around_ref[pl.ds(me * rows.count + rows.mass + part, 1), :]
        for c in range(3):
            correction = mass * (sums[part][c : c + 1, :] + sums[part][3 + c : 4 + c, :])
            move = moves_ref[pl.ds(me * rows.disp_count + c * atom_rows + part, 1), :] - correction
            start = around_ref[pl.ds(me * rows.count + rows.coords[c] + part, 1), :]
            coords_out_ref[c, 0, :, lanes] = start + move
            velocity_out_ref[c, 0, :, lanes] = move * (1.0 / time_step)


def vmem(count):
    return [pl.BlockSpec(memory_space=pltpu.VMEM)] * count


def smem(count):
    return [pl.BlockSpec(memory_space=pltpu.SMEM)] * count


def hbm(count):
    return [pl.BlockSpec(memory_space=pltpu.HBM)] * count


def in_hbm(arrays):
    return [pltpu.with_memory_space_constraint(a, pltpu.HBM) for a in arrays]


def params(mebibytes):
    return pltpu.CompilerParams(vmem_limit_bytes=mebibytes * 1024 * 1024)


def cost(flops, moved):
    return pl.CostEstimate(flops=flops, bytes_accessed=moved, transcendentals=0)


def room_for(arrays):
    return [pltpu.VMEM(a.shape, a.dtype) for a in arrays]


def shards(
    coords,
    velocity,
    charge,
    inv_mass,
    tile_block,
    tile_atoms,
    active_tile_count,
    bond_atoms,
    cross_atoms,
    cross_side,
    cross_count,
):
    atoms = coords.shape[-1]
    tiles = tile_atoms.shape[2]
    domains = lax.axis_size("dom")
    strides = strides_of(domains)
    rows = Rows(atoms, bond_atoms.shape[-1], cross_side.shape[-1])
    whole_slab = domains == SUBLANES
    copies = domains if whole_slab else 1
    f32 = jnp.float32

    sent = (coords, charge, inv_mass, bond_atoms, cross_atoms, cross_side)
    rim, static = pl.pallas_call(
        functools.partial(pack_kernel, rows, copies),
        out_shape=(
            jax.ShapeDtypeStruct((rows.rim, LANES), f32),
            jax.ShapeDtypeStruct((copies * rows.count, LANES), f32),
        ),
        in_specs=smem(1) + hbm(len(sent)),
        out_specs=tuple(vmem(2)),
        scratch_shapes=room_for(sent) + [pltpu.SemaphoreType.DMA((len(sent),))],
        compiler_params=params(4),
        name="pack",
    )(cross_count, *in_hbm(sent))

    if whole_slab:
        around = lax.all_to_all(static, "dom", 0, 0, tiled=True)
        here = lax.axis_index("dom").reshape(1)
    else:
        around = jnp.concatenate([static] + [passed_along(static, "dom", -stride) for stride in strides], axis=0)
    rims = jnp.concatenate([passed_along(rim, "dom", -stride) for stride in strides], axis=0)
    below = passed_along(rim, "slab", 1)
    above = passed_along(rim, "slab", -1)

    alone = (coords, charge, velocity, inv_mass, tile_atoms)
    own, near, index, motion = pl.pallas_call(
        functools.partial(own_kernel, rows),
        out_shape=(
            jax.ShapeDtypeStruct((4, atoms, LANES), f32),
            jax.ShapeDtypeStruct((4, tiles, TILE), f32),
            jax.ShapeDtypeStruct((tiles, TILE), jnp.int32),
            jax.ShapeDtypeStruct((4 * rows.atom_rows, LANES), f32),
        ),
        in_specs=hbm(len(alone)),
        out_specs=tuple(vmem(4)),
        scratch_shapes=room_for(alone[:4]) + [pltpu.SemaphoreType.DMA((len(alone),))],
        compiler_params=params(4),
        cost_estimate=cost(64 * atoms * LANES, 16 * atoms * LANES),
        name="own",
    )(*in_hbm(alone))

    moves = pl.pallas_call(
        functools.partial(force_kernel, rows, copies),
        out_shape=jax.ShapeDtypeStruct((copies * rows.disp_count, LANES), f32),
        in_specs=smem(1) + hbm(1) + vmem(7),
        out_specs=vmem(1)[0],
        scratch_shapes=[
            pltpu.VMEM((4, 6 * rows.shell_rows, SUBLANES, LANES), f32),
            pltpu.VMEM((4, tiles, LANES), f32),
            pltpu.VMEM((3, atoms, LANES), f32),
            pltpu.SMEM(tile_block.shape, jnp.int32),
            pltpu.SemaphoreType.DMA(()),
        ],
        compiler_params=params(4),
        cost_estimate=cost(30 * tiles * TILE * TILE, 4 * own.size),
        name="force",
    )(active_tile_count, *in_hbm([tile_block]), rims, below, above, own, near, index, motion)

    if not whole_slab:
        return by_exchange(rows, strides, around, moves)

    constraint_rows = rows.bond_rows + rows.slot_rows
    weight, matrix = pl.pallas_call(
        functools.partial(bond_kernel, rows, domains, strides),
        out_shape=(
            jax.ShapeDtypeStruct((constraint_rows * 3 * domains, LANES), f32),
            jax.ShapeDtypeStruct((domains * rows.matrix, atoms // 2), jnp.float8_e4m3fn),
        ),
        in_specs=vmem(1),
        out_specs=tuple(vmem(2)),
        scratch_shapes=[pltpu.VMEM((rows.slot_rows * 4 * domains, LANES), f32)],
        compiler_params=params(16),
        cost_estimate=cost(8 * domains * rows.matrix * atoms // 2, 4 * around.size),
        name="bonds",
    )(around)

    every_move = lax.all_to_all(moves, "dom", 0, 0, tiled=True)

    return pl.pallas_call(
        functools.partial(solve_kernel, rows, domains, strides),
        out_shape=(
            jax.ShapeDtypeStruct(coords.shape, f32),
            jax.ShapeDtypeStruct(coords.shape, f32),
        ),
        in_specs=smem(1) + vmem(4),
        out_specs=tuple(vmem(2)),
        scratch_shapes=[
            pltpu.VMEM((constraint_rows, SUBLANES * domains, LANES), f32),
            pltpu.VMEM((rows.atom_rows, SUBLANES * domains, LANES), f32),
            pltpu.VMEM(matrix.shape, jnp.bfloat16),
        ],
        compiler_params=params(16),
        name="solve",
    )(here, around, every_move, weight, matrix)


def by_exchange(rows, strides, around, moves):
    atom_count = rows.atom_rows * LANES
    shell = rows.shell_rows * LANES
    inside = around.reshape(5, rows.count, LANES)

    def flat(at, count):
        return inside[0, at : at + count].reshape(-1)

    def neighbours(at):
        return inside[1:, at : at + rows.shell_rows].reshape(-1)

    coords = jnp.stack([flat(at, rows.atom_rows) for at in rows.coords])
    inv_mass = flat(rows.mass, rows.atom_rows)
    displace = moves[: rows.disp_used].reshape(3, atom_count)
    left = flat(rows.bond_first, rows.bond_rows).astype(jnp.int32)
    right = flat(rows.bond_second, rows.bond_rows).astype(jnp.int32)
    cross_left = flat(rows.cross_first, rows.slot_rows).astype(jnp.int32)
    cross_right = flat(rows.cross_second, rows.slot_rows).astype(jnp.int32)
    side = flat(rows.side, rows.slot_rows).astype(jnp.int32)
    flag = flat(rows.live, rows.slot_rows)
    cross_index = side * shell + cross_right
    far_coords = jnp.stack([neighbours(at) for at in rows.coords])
    far_mass = neighbours(rows.mass)

    def weights(first, second, mass_first, mass_second):
        gap = first - second
        length = jnp.sqrt(jnp.sum(gap * gap, axis=0) + length_floor)
        return gap / length * lax.rsqrt(mass_first + mass_second)

    inner = weights(coords[:, left], coords[:, right], inv_mass[left], inv_mass[right])
    cross = flag * weights(
        coords[:, cross_left], far_coords[:, cross_index], inv_mass[cross_left], far_mass[cross_index]
    )

    def project(field):
        rim = field[:, :shell]
        far = jnp.concatenate([passed_along(rim, "dom", -stride) for stride in strides], axis=1)
        return (
            jnp.sum(inner * (field[:, left] - field[:, right]), axis=0),
            jnp.sum(cross * (field[:, cross_left] - far[:, cross_index]), axis=0),
        )

    def spread(values):
        pushed = inner * values[0]
        pushed_cross = cross * values[1]
        totals = jnp.zeros((3, atom_count), jnp.float32).at[:, left].add(pushed).at[:, right].add(-pushed)
        totals = totals.at[:, cross_left].add(pushed_cross)
        outward = jnp.zeros((3, 4 * shell), jnp.float32).at[:, cross_index].add(-pushed_cross)
        for code, stride in enumerate(strides):
            totals = totals.at[:, :shell].add(
                passed_along(outward[:, code * shell : (code + 1) * shell], "dom", stride)
            )
        return inv_mass * totals

    residue = project(displace)
    summed = residue
    for _ in range(ORDER):
        change = project(spread(residue))
        residue = tuple(now - step for now, step in zip(residue, change))
        summed = tuple(a + b for a, b in zip(summed, residue))
    move = displace - spread(summed)
    return (
        (coords + move).reshape(3, 1, 1, atom_count),
        (move * (1.0 / time_step)).reshape(3, 1, 1, atom_count),
    )


def solution(mesh):
    return jax.shard_map(
        shards,
        mesh=mesh,
        in_specs=(
            P(None, "slab", "dom", None),
            P(None, "slab", "dom", None),
            P("slab", "dom", None),
            P("slab", "dom", None),
            P("slab", "dom", None),
            P("slab", "dom", None, None),
            P("slab", "dom"),
            P(None, "slab", "dom", None),
            P(None, "slab", "dom", None),
            P("slab", "dom", None),
            P("slab", "dom"),
        ),
        out_specs=(P(None, "slab", "dom", None), P(None, "slab", "dom", None)),
        check_vma=False,
    )
```

```python
import functools

import jax
import jax.numpy as jnp
from jax import lax
from jax.experimental import pallas as pl
from jax.experimental.pallas import tpu as pltpu
from jax.sharding import PartitionSpec as P

TILE = 128
ORDER = 4
LANES = 128
SUBLANES = 8

time_step = 0.1
cutoff_sq = 16.0
force_scale = 4.0
length_floor = 0.25


def passed_along(array, axis, by):
    length = lax.axis_size(axis)
    return lax.ppermute(array, axis, [(i, (i + by) % length) for i in range(length)])


def strides_of(domains):
    row_width = max(2, domains // 8)
    return (1, -1, row_width, -row_width)


def round_up(count, step):
    return -(-count // step) * step


class Rows:
    def __init__(self, atoms, bonds, slots):
        self.atom_rows = atoms // LANES
        self.shell_rows = atoms // 2 // LANES
        self.bond_rows = bonds // LANES
        self.slot_rows = slots // LANES
        at = 0
        self.coords = []
        for _ in range(3):
            self.coords.append(at)
            at += self.atom_rows
        self.charge = at
        at += self.atom_rows
        self.mass = at
        at += self.atom_rows
        self.bond_first = at
        at += self.bond_rows
        self.bond_second = at
        at += self.bond_rows
        self.cross_first = at
        at += self.slot_rows
        self.cross_second = at
        at += self.slot_rows
        self.side = at
        at += self.slot_rows
        self.live = at
        at += self.slot_rows
        self.used = at
        self.count = round_up(at, SUBLANES)
        self.shell_terms = (self.bond_rows + 5 * self.slot_rows) * LANES
        self.matrix = self.shell_terms + self.bond_rows * LANES
        self.inner_at = (0, self.shell_terms)
        self.cross_at = self.bond_rows * LANES
        self.disp_used = 3 * self.atom_rows
        self.disp_count = round_up(self.disp_used, SUBLANES)


def take_lanes(table, lanes):
    return jnp.take_along_axis(table, lanes, axis=1, mode="promise_in_bounds")


def pick(tables, index):
    lanes = index & (LANES - 1)
    chunk = index >> 7
    result = take_lanes(tables[0], lanes)
    for k in range(1, len(tables)):
        result = jnp.where(chunk == k, take_lanes(tables[k], lanes), result)
    return result


def fetched(sources, targets, sem_ref):
    copies = [pltpu.make_async_copy(s, t, sem_ref.at[n]) for n, (s, t) in enumerate(zip(sources, targets))]
    for copy in copies:
        copy.start()
    return copies


def pack_kernel(rows, copies, count_ref, *refs):
    sources, (out_ref, rim_ref), targets, sem_ref = refs[:6], refs[6:8], refs[8:14], refs[14]
    for copy in fetched(sources, targets, sem_ref):
        copy.wait()
    coords_ref, charge_ref, mass_ref, bonds_ref, cross_ref, side_ref = targets

    def put(row, value):
        for part in range(value.shape[1] // LANES):
            piece = value[:, part * LANES : (part + 1) * LANES]
            for copy in range(copies):
                out_ref[pl.ds(copy * rows.count + row + part, 1), :] = piece

    shell = rows.shell_rows * LANES
    fields = [coords_ref[c, 0] for c in range(3)] + [charge_ref[0]]
    for c in range(4):
        at = rows.coords[c] if c < 3 else rows.charge
        put(at, fields[c])
        for part in range(rows.shell_rows):
            rim_ref[pl.ds(c * rows.shell_rows + part, 1), :] = fields[c][:, part * LANES : (part + 1) * LANES]
    put(rows.mass, mass_ref[0])
    put(rows.bond_first, bonds_ref[0, 0].astype(jnp.float32))
    put(rows.bond_second, bonds_ref[1, 0].astype(jnp.float32))
    put(rows.cross_first, cross_ref[0, 0].astype(jnp.float32))
    put(rows.cross_second, cross_ref[1, 0].astype(jnp.float32))
    side = side_ref[0]
    put(rows.side, side.astype(jnp.float32))
    slot = lax.broadcasted_iota(jnp.int32, side.shape, 1)
    put(rows.live, jnp.where(slot < count_ref[0, 0], 1.0, 0.0))
    if rows.count > rows.used:
        for copy in range(copies):
            out_ref[pl.ds(copy * rows.count + rows.used, rows.count - rows.used), :] = jnp.zeros(
                (rows.count - rows.used, LANES), jnp.float32
            )


SHRINK = 1.0 / 4.0


TERMS = 32


def narrow(value):
    return value.astype(jnp.bfloat16).astype(jnp.float32)


def split(value):
    high = narrow(value)
    middle = narrow(value - high)
    return high, middle, value - high - middle


def distance_terms(place, offset, own):
    factor = 1.0 if own else -2.0
    terms = []
    for value in place:
        high, middle, low = split(value)
        pick_from = (high, high, middle, middle, high, low) if own else (high, middle, high, middle, low, high)
        terms.extend(factor * part for part in pick_from)
    square = place[0] * place[0] + place[1] * place[1] + place[2] * place[2] + offset
    ones = [jnp.ones_like(square)] * 3
    return terms + (list(split(square)) + ones if own else ones + list(split(square)))


def own_kernel(
    rows,
    coords_hbm,
    charge_hbm,
    velocity_hbm,
    mass_hbm,
    atoms_hbm,
    terms_ref,
    own_ref,
    far_ref,
    index_ref,
    motion_ref,
    coords_ref,
    charge_ref,
    velocity_ref,
    mass_ref,
    sem_ref,
):
    atom_rows = rows.atom_rows
    copies = fetched(
        (coords_hbm, charge_hbm, atoms_hbm.at[0, 0], velocity_hbm, mass_hbm),
        (coords_ref, charge_ref, index_ref, velocity_ref, mass_ref),
        sem_ref,
    )
    down = lax.broadcasted_iota(jnp.int32, (SUBLANES, LANES), 0)
    across = lax.broadcasted_iota(jnp.int32, (SUBLANES, LANES), 1)
    copies[0].wait()
    copies[1].wait()

    def lanes_of(part):
        return slice(part * LANES, (part + 1) * LANES)

    table = []
    for c in range(4):
        field = coords_ref[c, 0] * SHRINK if c < 3 else charge_ref[0]
        table.append(
            [jnp.broadcast_to(field[:, lanes_of(part)], (SUBLANES, LANES)) for part in range(atom_rows)]
        )
    for part in range(atom_rows):
        for pair in range(LANES // SUBLANES // 2):
            halves = []
            for group in (2 * pair, 2 * pair + 1):
                at = part * LANES + group * SUBLANES
                values = [take_lanes(table[c][part], down + group * SUBLANES) for c in range(4)]
                own_ref[pl.ds(at, SUBLANES), :] = values[3] * 8.0
                row = jnp.zeros((SUBLANES, LANES), jnp.float32)
                for lane, term in enumerate(distance_terms(values[:3], 0.0, True)):
                    row = jnp.where(across == lane, term, row)
                halves.append(row)
            at = part * LANES + pair * 2 * SUBLANES
            terms_ref[pl.ds(at, 2 * SUBLANES), :] = jnp.concatenate(halves, axis=0).astype(jnp.bfloat16)
    copies[2].wait()
    for group in range(index_ref.shape[0] // SUBLANES):
        at = pl.ds(group * SUBLANES, SUBLANES)
        index = index_ref[at, :]
        for c in range(4):
            far_ref[c, at, :] = pick(table[c], index)
    copies[3].wait()
    copies[4].wait()
    fields = [velocity_ref[c, 0] for c in range(3)] + [coords_ref[c, 0] * SHRINK for c in range(3)] + [mass_ref[0]]
    for c, field in enumerate(fields):
        for part in range(atom_rows):
            motion_ref[pl.ds(c * atom_rows + part, 1), :] = field[:, lanes_of(part)]


def force_kernel(
    rows,
    copies,
    holders,
    here_ref,
    live_ref,
    block_hbm,
    around_ref,
    below_ref,
    above_ref,
    terms_ref,
    own_ref,
    near_ref,
    index_ref,
    motion_ref,
    out_ref,
    table_ref,
    far_ref,
    far_terms_ref,
    sum_ref,
    block_ref,
    sem_ref,
):
    atom_rows, shell_rows = rows.atom_rows, rows.shell_rows
    tiles = index_ref.shape[0]
    block_copy = pltpu.make_async_copy(block_hbm, block_ref, sem_ref)
    block_copy.start()
    me = here_ref[0]
    starts = [rows.coords[0], rows.coords[1], rows.coords[2], rows.charge]
    entry_rows = 6 * shell_rows
    blocks = around_ref.shape[0] // rows.count

    def broadcast(row):
        return jnp.broadcast_to(row, (SUBLANES, LANES))

    for c in range(4):
        factor = SHRINK if c < 3 else 1.0
        at = 0
        for neighbour in range(4):
            base = lax.rem(me + holders[neighbour], blocks) * rows.count + starts[c]
            for part in range(shell_rows):
                table_ref[c, at] = broadcast(around_ref[pl.ds(base + part, 1), :] * factor)
                at += 1
        for slab_ref in (below_ref, above_ref):
            for part in range(shell_rows):
                table_ref[c, at] = broadcast(slab_ref[pl.ds(c * shell_rows + part, 1), :] * factor)
                at += 1

    for group in range(tiles // SUBLANES):
        at = pl.ds(group * SUBLANES, SUBLANES)
        index = index_ref[at, :]
        lanes = index & (LANES - 1)
        chunk = index >> 7
        values = [near_ref[c, at, :] for c in range(4)]
        for k in range(entry_rows):
            here = chunk == atom_rows + k
            values = [jnp.where(here, take_lanes(table_ref[c, k], lanes), values[c]) for c in range(4)]
        for c in range(4):
            far_ref[c, at, :] = values[c]
        terms = distance_terms(values[:3], 1.0 / cutoff_sq, False)
        terms = terms + [jnp.zeros_like(terms[0])] * (TERMS - len(terms))
        for row, term in enumerate(terms):
            far_terms_ref[pl.ds(group * SUBLANES * TERMS + row, SUBLANES, stride=TERMS), :] = term

    sum_ref[...] = jnp.zeros(sum_ref.shape, jnp.float32)
    block_copy.wait()

    def distances(tile):
        base = pl.multiple_of(block_ref[0, 0, tile] * TILE, TILE)
        far = far_terms_ref[pl.ds(pl.multiple_of(tile * TERMS, TERMS), TERMS), :]
        return jnp.dot(
            terms_ref[pl.ds(base, TILE), :TERMS], far.astype(jnp.bfloat16), preferred_element_type=jnp.float32
        )

    def add_tile(tile, shifted):
        following = distances(jnp.minimum(tile + 1, tiles - 1))
        base = block_ref[0, 0, tile] * TILE
        far = [broadcast(far_ref[c, pl.ds(tile, 1), :]) for c in range(4)]
        for group in range(TILE // SUBLANES):
            at = pl.ds(pl.multiple_of(base + group * SUBLANES, SUBLANES), SUBLANES)
            square = shifted[group * SUBLANES : (group + 1) * SUBLANES, :]
            inverse = pl.reciprocal(square, approx=True)
            switch = jnp.maximum(1.0 + 1.0 / cutoff_sq - square, 0.0)
            weight = inverse * switch
            strength = (inverse - own_ref[at, :] * far[3]) * (weight * weight)
            for c in range(3):
                sum_ref[c, at, :] = sum_ref[c, at, :] + strength * far[c]
            sum_ref[3, at, :] = sum_ref[3, at, :] + strength
        return following

    lax.fori_loop(0, live_ref[0, 0], add_tile, distances(0))

    scale = time_step * time_step * force_scale * 4.0 / 2048.0

    def lane_sums(c, part):
        return jnp.sum(sum_ref[c, pl.ds(part * LANES, LANES), :].T, axis=0, keepdims=True)

    for part in range(atom_rows):
        strength = lane_sums(3, part)
        mass = motion_ref[pl.ds(6 * atom_rows + part, 1), :]
        for c in range(3):
            speed = motion_ref[pl.ds(c * atom_rows + part, 1), :]
            place = motion_ref[pl.ds((3 + c) * atom_rows + part, 1), :]
            moved = time_step * speed + scale * (place * strength - lane_sums(c, part)) * mass
            for copy in range(copies):
                out_ref[pl.ds(copy * rows.disp_count + c * atom_rows + part, 1), :] = moved
    if rows.disp_count > rows.disp_used:
        for copy in range(copies):
            out_ref[pl.ds(copy * rows.disp_count + rows.disp_used, rows.disp_count - rows.disp_used), :] = jnp.zeros(
                (rows.disp_count - rows.disp_used, LANES), jnp.float32
            )


def bond_kernel(rows, domains, strides, around_ref, weight_ref, matrix_ref, key_ref):
    atom_rows, shell_rows = rows.atom_rows, rows.shell_rows

    def load(row):
        return around_ref[pl.ds(row, domains, stride=rows.count), :]

    def index(row):
        return load(row).astype(jnp.int32)

    fields = [[load(at + part) for part in range(atom_rows)] for at in rows.coords + [rows.mass]]

    def weights(first, second, row):
        gap = [first[c] - second[c] for c in range(3)]
        length_sq = gap[0] * gap[0] + gap[1] * gap[1] + gap[2] * gap[2] + length_floor
        scale = lax.rsqrt(length_sq) * lax.rsqrt(first[3] + second[3])
        return [gap[c] * scale for c in range(3)]

    at = 0
    for part in range(rows.bond_rows):
        first = index(rows.bond_first + part)
        second = index(rows.bond_second + part)
        values = weights([pick(f, first) for f in fields], [pick(f, second) for f in fields], at)
        for c in range(3):
            weight_ref[pl.ds((at * 3 + c) * domains, domains), :] = values[c]
        at += 1
    for part in range(rows.slot_rows):
        first = index(rows.cross_first + part)
        second = index(rows.cross_second + part)
        side = load(rows.side + part)
        live = load(rows.live + part)
        other = [jnp.zeros((domains, LANES), jnp.float32) for _ in range(4)]
        for code, stride in enumerate(strides):
            seen = pltpu.roll(second, stride % domains, 0)
            for f in range(4):
                value = pltpu.roll(pick(fields[f][:shell_rows], seen), -stride % domains, 0)
                other[f] = jnp.where(side == code, value, other[f])
            key = jnp.where(side == code, load(rows.cross_second + part), -1.0)
            key_ref[pl.ds((part * 4 + code) * domains, domains), :] = key
        values = weights([pick(f[:shell_rows], first) for f in fields], other, at)
        for c in range(3):
            weight_ref[pl.ds((at * 3 + c) * domains, domains), :] = values[c] * live
        at += 1

    down = lax.broadcasted_iota(jnp.int32, (SUBLANES, LANES), 0)
    group_rows = 4 * SUBLANES

    kind = jnp.bfloat16 if shell_rows * LANES <= 256 else jnp.float32
    across = lax.broadcasted_iota(jnp.int32, (group_rows, LANES), 1).astype(jnp.float32)
    lanes = [(across + float(block * LANES)).astype(kind) for block in range(shell_rows)]

    def column(row, step, half=0):
        row = jnp.broadcast_to(row, (SUBLANES, LANES))
        groups = [take_lanes(row, down + at) for at in range(step * group_rows, (step + 1) * group_rows, SUBLANES)]
        return (jnp.concatenate(groups, axis=0) - float(half * shell_rows * LANES)).astype(kind)

    def put(at, ends, signs):
        for block in range(shell_rows):
            value = jnp.zeros((group_rows, LANES), kind)
            for end, sign in zip(ends, signs):
                value = jnp.where(end == lanes[block], jnp.full((group_rows, LANES), sign, kind), value)
            matrix_ref[pl.ds(at, group_rows), block * LANES : (block + 1) * LANES] = value.astype(matrix_ref.dtype)

    def build(domain, _):
        start = pl.multiple_of(domain * rows.matrix, LANES)
        for part in range(rows.bond_rows):
            first = around_ref[pl.ds(domain * rows.count + rows.bond_first + part, 1), :]
            second = around_ref[pl.ds(domain * rows.count + rows.bond_second + part, 1), :]
            for step in range(LANES // group_rows):
                for half in range(2):
                    ends = (column(first, step, half), column(second, step, half))
                    put(start + rows.inner_at[half] + part * LANES + step * group_rows, ends, (1.0, -1.0))
        for part in range(rows.slot_rows):
            for code in range(5):
                if code == 0:
                    row = around_ref[pl.ds(domain * rows.count + rows.cross_first + part, 1), :]
                else:
                    owner = lax.rem(domain + (-strides[code - 1]) % domains, domains)
                    row = key_ref[pl.ds((part * 4 + code - 1) * domains + owner, 1), :]
                sign = 1.0 if code == 0 else -1.0
                for step in range(LANES // group_rows):
                    at = start + rows.cross_at + (part * 5 + code) * LANES + step * group_rows
                    put(at, (column(row, step),), (sign,))
        return 0

    lax.fori_loop(0, domains, build, 0)


def solve_kernel(
    rows,
    domains,
    strides,
    here_ref,
    around_ref,
    moves_ref,
    weight_ref,
    signs_ref,
    coords_out_ref,
    velocity_out_ref,
    push_ref,
    field_ref,
    matrix_ref,
):
    atom_rows, shell_rows = rows.atom_rows, rows.shell_rows
    bond_rows, slot_rows = rows.bond_rows, rows.slot_rows
    me = here_ref[0]

    def widen(domain, _):
        at = pl.ds(pl.multiple_of(domain * rows.matrix, LANES), rows.matrix)
        matrix_ref[at, :] = signs_ref[at, :].astype(matrix_ref.dtype)
        return 0

    lax.fori_loop(0, domains, widen, 0)

    def load(row):
        return around_ref[pl.ds(row, domains, stride=rows.count), :]

    def index(row):
        return load(row).astype(jnp.int32)

    inner_first = [index(rows.bond_first + p) for p in range(bond_rows)]
    inner_second = [index(rows.bond_second + p) for p in range(bond_rows)]
    cross_first = [index(rows.cross_first + p) for p in range(slot_rows)]
    cross_second = [index(rows.cross_second + p) for p in range(slot_rows)]
    sides = [load(rows.side + p) for p in range(slot_rows)]
    masses = [load(rows.mass + p) for p in range(atom_rows)]

    def weight(at, c):
        return weight_ref[pl.ds((at * 3 + c) * domains, domains), :]

    def project(fields):
        result = []
        for part in range(bond_rows):
            total = 0.0
            for c in range(3):
                ends = pick(fields[c], inner_first[part]) - pick(fields[c], inner_second[part])
                total = total + weight(part, c) * ends
            result.append(total)
        for part in range(slot_rows):
            seen = [pltpu.roll(cross_second[part], stride % domains, 0) for stride in strides]
            total = 0.0
            for c in range(3):
                shell = fields[c][:shell_rows]
                other = 0.0
                for code, stride in enumerate(strides):
                    value = pltpu.roll(pick(shell, seen[code]), -stride % domains, 0)
                    other = jnp.where(sides[part] == code, value, other)
                total = total + weight(bond_rows + part, c) * (pick(shell, cross_first[part]) - other)
            result.append(total)
        return result

    def put_pushes(values):
        for at, value in enumerate(values):
            for c in range(3):
                pushed = weight(at, c) * value
                high = pushed.astype(jnp.bfloat16).astype(jnp.float32)
                push_ref[at, pl.ds(c * domains, domains), :] = high
                push_ref[at, pl.ds((3 + c) * domains, domains), :] = pushed - high

    def pushes_of(at, domain):
        return push_ref[at, pl.ds(domain, SUBLANES, stride=domains), :].astype(jnp.bfloat16)

    def totals(domain, owners):
        inner = [pushes_of(p, domain) for p in range(bond_rows)]
        cross = []
        for part in range(slot_rows):
            cross.extend(pushes_of(bond_rows + part, owner) for owner in [domain] + owners)
        start = domain * rows.matrix
        if not isinstance(start, int):
            start = pl.multiple_of(start, LANES)
        shell_sum = jnp.dot(
            jnp.concatenate(inner + cross, axis=1),
            matrix_ref[pl.ds(start, rows.shell_terms), :],
            preferred_element_type=jnp.float32,
        )
        other_sum = jnp.dot(
            jnp.concatenate(inner, axis=1),
            matrix_ref[pl.ds(start + rows.shell_terms, bond_rows * LANES), :],
            preferred_element_type=jnp.float32,
        )
        return [
            half[:, p * LANES : (p + 1) * LANES] for half in (shell_sum, other_sum) for p in range(shell_rows)
        ]

    def spread(values):
        put_pushes(values)
        for domain in range(domains):
            sums = totals(domain, [(domain - stride) % domains for stride in strides])
            for part in range(atom_rows):
                field_ref[part, pl.ds(domain, SUBLANES, stride=domains), :] = sums[part]
        return [
            [
                masses[part]
                * (
                    field_ref[part, pl.ds(c * domains, domains), :]
                    + field_ref[part, pl.ds((3 + c) * domains, domains), :]
                )
                for part in range(atom_rows)
            ]
            for c in range(3)
        ]

    moves = [
        [moves_ref[pl.ds(c * atom_rows + p, domains, stride=rows.disp_count), :] for p in range(atom_rows)]
        for c in range(3)
    ]
    push_ref[...] = jnp.zeros(push_ref.shape, jnp.float32)
    residue = project(moves)

    def expand(_, carry):
        residue, summed = carry
        change = project(spread(residue))
        residue = [now - step for now, step in zip(residue, change)]
        return residue, [a + b for a, b in zip(summed, residue)]

    residue, summed = lax.fori_loop(0, ORDER, expand, (residue, residue))
    put_pushes(summed)
    sums = totals(me, [lax.rem(me + (-stride) % domains, domains) for stride in strides])
    for part in range(atom_rows):
        lanes = slice(part * LANES, (part + 1) * LANES)
        mass = around_ref[pl.ds(me * rows.count + rows.mass + part, 1), :]
        for c in range(3):
            correction = mass * (sums[part][c : c + 1, :] + sums[part][3 + c : 4 + c, :])
            move = moves_ref[pl.ds(me * rows.disp_count + c * atom_rows + part, 1), :] - correction
            start = around_ref[pl.ds(me * rows.count + rows.coords[c] + part, 1), :]
            coords_out_ref[c, 0, :, lanes] = start + move
            velocity_out_ref[c, 0, :, lanes] = move * (1.0 / time_step)


def vmem(count):
    return [pl.BlockSpec(memory_space=pltpu.VMEM)] * count


def smem(count):
    return [pl.BlockSpec(memory_space=pltpu.SMEM)] * count


def hbm(count):
    return [pl.BlockSpec(memory_space=pltpu.HBM)] * count


def in_hbm(arrays):
    return [pltpu.with_memory_space_constraint(a, pltpu.HBM) for a in arrays]


def params(mebibytes):
    return pltpu.CompilerParams(vmem_limit_bytes=mebibytes * 1024 * 1024)


def cost(flops, moved):
    return pl.CostEstimate(flops=flops, bytes_accessed=moved, transcendentals=0)


def room_for(arrays):
    return [pltpu.VMEM(a.shape, a.dtype) for a in arrays]


def shards(
    coords,
    velocity,
    charge,
    inv_mass,
    tile_block,
    tile_atoms,
    active_tile_count,
    bond_atoms,
    cross_atoms,
    cross_side,
    cross_count,
):
    atoms = coords.shape[-1]
    tiles = tile_atoms.shape[2]
    domains = lax.axis_size("dom")
    strides = strides_of(domains)
    rows = Rows(atoms, bond_atoms.shape[-1], cross_side.shape[-1])
    whole_slab = domains == SUBLANES
    copies = domains if whole_slab else 1
    f32 = jnp.float32

    sent = (coords, charge, inv_mass, bond_atoms, cross_atoms, cross_side)
    packed, rim = pl.pallas_call(
        functools.partial(pack_kernel, rows, copies),
        out_shape=(
            jax.ShapeDtypeStruct((copies * rows.count, LANES), f32),
            jax.ShapeDtypeStruct((4 * rows.shell_rows, LANES), f32),
        ),
        in_specs=smem(1) + hbm(len(sent)),
        out_specs=tuple(vmem(2)),
        scratch_shapes=room_for(sent) + [pltpu.SemaphoreType.DMA((len(sent),))],
        compiler_params=params(4),
        name="pack",
    )(cross_count, *in_hbm(sent))

    alone = (coords, charge, velocity, inv_mass, tile_atoms)
    own = pl.pallas_call(
        functools.partial(own_kernel, rows),
        out_shape=(
            jax.ShapeDtypeStruct((atoms, LANES), jnp.bfloat16),
            jax.ShapeDtypeStruct((atoms, LANES), f32),
            jax.ShapeDtypeStruct((4, tiles, TILE), f32),
            jax.ShapeDtypeStruct((tiles, TILE), jnp.int32),
            jax.ShapeDtypeStruct((7 * rows.atom_rows, LANES), f32),
        ),
        in_specs=hbm(len(alone)),
        out_specs=tuple(vmem(5)),
        scratch_shapes=room_for(alone[:4]) + [pltpu.SemaphoreType.DMA((len(alone),))],
        compiler_params=params(4),
        cost_estimate=cost(64 * atoms * LANES, 16 * atoms * LANES),
        name="own",
    )(*in_hbm(alone))

    below = passed_along(rim, "slab", 1)
    above = passed_along(rim, "slab", -1)
    if whole_slab:
        around = lax.all_to_all(packed, "dom", 0, 0, tiled=True)
        here = lax.axis_index("dom").reshape(1)
        holders = [stride % domains for stride in strides]
    else:
        around = jnp.concatenate([packed] + [passed_along(packed, "dom", -stride) for stride in strides], axis=0)
        here = jnp.zeros(1, jnp.int32)
        holders = [1, 2, 3, 4]

    moves = pl.pallas_call(
        functools.partial(force_kernel, rows, copies, holders),
        out_shape=jax.ShapeDtypeStruct((copies * rows.disp_count, LANES), f32),
        in_specs=smem(2) + hbm(1) + vmem(8),
        out_specs=vmem(1)[0],
        scratch_shapes=[
            pltpu.VMEM((4, 6 * rows.shell_rows, SUBLANES, LANES), f32),
            pltpu.VMEM((4, tiles, LANES), f32),
            pltpu.VMEM((tiles * TERMS, LANES), f32),
            pltpu.VMEM((4, atoms, LANES), f32),
            pltpu.SMEM(tile_block.shape, jnp.int32),
            pltpu.SemaphoreType.DMA(()),
        ],
        compiler_params=params(8),
        cost_estimate=cost(30 * tiles * TILE * TILE, 4 * around.size),
        name="force",
    )(here, active_tile_count, *in_hbm([tile_block]), around, below, above, *own)

    if not whole_slab:
        return by_exchange(rows, strides, around, moves, cross_count)

    constraint_rows = rows.bond_rows + rows.slot_rows
    weight, matrix = pl.pallas_call(
        functools.partial(bond_kernel, rows, domains, strides),
        out_shape=(
            jax.ShapeDtypeStruct((constraint_rows * 3 * domains, LANES), f32),
            jax.ShapeDtypeStruct((domains * rows.matrix, atoms // 2), jnp.float8_e4m3fn),
        ),
        in_specs=vmem(1),
        out_specs=tuple(vmem(2)),
        scratch_shapes=[pltpu.VMEM((rows.slot_rows * 4 * domains, LANES), f32)],
        compiler_params=params(16),
        cost_estimate=cost(8 * domains * rows.matrix * atoms // 2, 4 * around.size),
        name="bonds",
    )(around)

    every_move = lax.all_to_all(moves, "dom", 0, 0, tiled=True)

    return pl.pallas_call(
        functools.partial(solve_kernel, rows, domains, strides),
        out_shape=(
            jax.ShapeDtypeStruct(coords.shape, f32),
            jax.ShapeDtypeStruct(coords.shape, f32),
        ),
        in_specs=smem(1) + vmem(4),
        out_specs=tuple(vmem(2)),
        scratch_shapes=[
            pltpu.VMEM((constraint_rows, SUBLANES * domains, LANES), f32),
            pltpu.VMEM((rows.atom_rows, SUBLANES * domains, LANES), f32),
            pltpu.VMEM(matrix.shape, jnp.bfloat16),
        ],
        compiler_params=params(16),
        name="solve",
    )(here, around, every_move, weight, matrix)


def by_exchange(rows, strides, around, moves, cross_count):
    atom_count = rows.atom_rows * LANES
    shell = rows.shell_rows * LANES
    inside = around.reshape(5, rows.count, LANES)

    def flat(at, count):
        return inside[0, at : at + count].reshape(-1)

    def neighbours(at):
        return inside[1:, at : at + rows.shell_rows].reshape(-1)

    coords = jnp.stack([flat(at, rows.atom_rows) for at in rows.coords])
    inv_mass = flat(rows.mass, rows.atom_rows)
    displace = moves[: rows.disp_used].reshape(3, atom_count)
    left = flat(rows.bond_first, rows.bond_rows).astype(jnp.int32)
    right = flat(rows.bond_second, rows.bond_rows).astype(jnp.int32)
    cross_left = flat(rows.cross_first, rows.slot_rows).astype(jnp.int32)
    cross_right = flat(rows.cross_second, rows.slot_rows).astype(jnp.int32)
    side = flat(rows.side, rows.slot_rows).astype(jnp.int32)
    flag = flat(rows.live, rows.slot_rows)
    cross_index = side * shell + cross_right
    far_coords = jnp.stack([neighbours(at) for at in rows.coords])
    far_mass = neighbours(rows.mass)

    def weights(first, second, mass_first, mass_second):
        gap = first - second
        length = jnp.sqrt(jnp.sum(gap * gap, axis=0) + length_floor)
        return gap / length * lax.rsqrt(mass_first + mass_second)

    inner = weights(coords[:, left], coords[:, right], inv_mass[left], inv_mass[right])
    cross = flag * weights(
        coords[:, cross_left], far_coords[:, cross_index], inv_mass[cross_left], far_mass[cross_index]
    )

    def project(field):
        rim = field[:, :shell]
        far = jnp.concatenate([passed_along(rim, "dom", -stride) for stride in strides], axis=1)
        return (
            jnp.sum(inner * (field[:, left] - field[:, right]), axis=0),
            jnp.sum(cross * (field[:, cross_left] - far[:, cross_index]), axis=0),
        )

    def spread(values):
        pushed = inner * values[0]
        pushed_cross = cross * values[1]
        totals = jnp.zeros((3, atom_count), jnp.float32).at[:, left].add(pushed).at[:, right].add(-pushed)
        totals = totals.at[:, cross_left].add(pushed_cross)
        outward = jnp.zeros((3, 4 * shell), jnp.float32).at[:, cross_index].add(-pushed_cross)
        for code, stride in enumerate(strides):
            totals = totals.at[:, :shell].add(
                passed_along(outward[:, code * shell : (code + 1) * shell], "dom", stride)
            )
        return inv_mass * totals

    residue = project(displace)
    summed = residue
    for _ in range(ORDER):
        change = project(spread(residue))
        residue = tuple(now - step for now, step in zip(residue, change))
        summed = tuple(a + b for a, b in zip(summed, residue))
    move = displace - spread(summed)
    return (
        (coords + move).reshape(3, 1, 1, atom_count),
        (move * (1.0 / time_step)).reshape(3, 1, 1, atom_count),
    )


def solution(mesh):
    return jax.shard_map(
        shards,
        mesh=mesh,
        in_specs=(
            P(None, "slab", "dom", None),
            P(None, "slab", "dom", None),
            P("slab", "dom", None),
            P("slab", "dom", None),
            P("slab", "dom", None),
            P("slab", "dom", None, None),
            P("slab", "dom"),
            P(None, "slab", "dom", None),
            P(None, "slab", "dom", None),
            P("slab", "dom", None),
            P("slab", "dom"),
        ),
        out_specs=(P(None, "slab", "dom", None), P(None, "slab", "dom", None)),
        check_vma=False,
    )
```

```python
import functools

import jax
import jax.numpy as jnp
from jax import lax
from jax.experimental import pallas as pl
from jax.experimental.pallas import tpu as pltpu
from jax.sharding import PartitionSpec as P

TILE = 128
ORDER = 4
LANES = 128
SUBLANES = 8

time_step = 0.1
cutoff_sq = 16.0
force_scale = 4.0
length_floor = 0.25


def passed_along(array, axis, by):
    length = lax.axis_size(axis)
    return lax.ppermute(array, axis, [(i, (i + by) % length) for i in range(length)])


def strides_of(domains):
    row_width = max(2, domains // 8)
    return (1, -1, row_width, -row_width)


def round_up(count, step):
    return -(-count // step) * step


class Rows:
    def __init__(self, atoms, bonds, slots):
        self.atom_rows = atoms // LANES
        self.shell_rows = atoms // 2 // LANES
        self.bond_rows = bonds // LANES
        self.slot_rows = slots // LANES
        at = 0
        self.coords = []
        for _ in range(3):
            self.coords.append(at)
            at += self.atom_rows
        self.charge = at
        at += self.atom_rows
        self.mass = at
        at += self.atom_rows
        self.bond_first = at
        at += self.bond_rows
        self.bond_second = at
        at += self.bond_rows
        self.cross_first = at
        at += self.slot_rows
        self.cross_second = at
        at += self.slot_rows
        self.side = at
        at += self.slot_rows
        self.live = at
        at += self.slot_rows
        self.used = at
        self.count = round_up(at, SUBLANES)
        self.shell_terms = (self.bond_rows + 5 * self.slot_rows) * LANES
        self.matrix = self.shell_terms + self.bond_rows * LANES
        self.inner_at = (0, self.shell_terms)
        self.cross_at = self.bond_rows * LANES
        self.disp_used = 3 * self.atom_rows
        self.disp_count = round_up(self.disp_used, SUBLANES)


def take_lanes(table, lanes):
    return jnp.take_along_axis(table, lanes, axis=1, mode="promise_in_bounds")


def pick(tables, index):
    lanes = index & (LANES - 1)
    chunk = index >> 7
    result = take_lanes(tables[0], lanes)
    for k in range(1, len(tables)):
        result = jnp.where(chunk == k, take_lanes(tables[k], lanes), result)
    return result


def fetched(sources, targets, sem_ref):
    copies = [pltpu.make_async_copy(s, t, sem_ref.at[n]) for n, (s, t) in enumerate(zip(sources, targets))]
    for copy in copies:
        copy.start()
    return copies


def pack_kernel(rows, copies, count_ref, *refs):
    sources, (out_ref, rim_ref), targets, sem_ref = refs[:6], refs[6:8], refs[8:14], refs[14]
    for copy in fetched(sources, targets, sem_ref):
        copy.wait()
    coords_ref, charge_ref, mass_ref, bonds_ref, cross_ref, side_ref = targets

    def put(row, value):
        for part in range(value.shape[1] // LANES):
            piece = value[:, part * LANES : (part + 1) * LANES]
            for copy in range(copies):
                out_ref[pl.ds(copy * rows.count + row + part, 1), :] = piece

    shell = rows.shell_rows * LANES
    fields = [coords_ref[c, 0] for c in range(3)] + [charge_ref[0]]
    for c in range(4):
        at = rows.coords[c] if c < 3 else rows.charge
        put(at, fields[c])
        for part in range(rows.shell_rows):
            rim_ref[pl.ds(c * rows.shell_rows + part, 1), :] = fields[c][:, part * LANES : (part + 1) * LANES]
    put(rows.mass, mass_ref[0])
    put(rows.bond_first, bonds_ref[0, 0].astype(jnp.float32))
    put(rows.bond_second, bonds_ref[1, 0].astype(jnp.float32))
    put(rows.cross_first, cross_ref[0, 0].astype(jnp.float32))
    put(rows.cross_second, cross_ref[1, 0].astype(jnp.float32))
    side = side_ref[0]
    put(rows.side, side.astype(jnp.float32))
    slot = lax.broadcasted_iota(jnp.int32, side.shape, 1)
    put(rows.live, jnp.where(slot < count_ref[0, 0], 1.0, 0.0))
    if rows.count > rows.used:
        for copy in range(copies):
            out_ref[pl.ds(copy * rows.count + rows.used, rows.count - rows.used), :] = jnp.zeros(
                (rows.count - rows.used, LANES), jnp.float32
            )


SHRINK = 1.0 / 4.0
OUT_OF_REACH = 1000.0
TILES_STEP = 2


def own_kernel(
    rows,
    coords_hbm,
    charge_hbm,
    velocity_hbm,
    mass_hbm,
    atoms_hbm,
    own_ref,
    far_ref,
    index_ref,
    motion_ref,
    coords_ref,
    charge_ref,
    velocity_ref,
    mass_ref,
    sem_ref,
):
    atom_rows = rows.atom_rows
    copies = fetched(
        (coords_hbm, charge_hbm, atoms_hbm.at[0, 0], velocity_hbm, mass_hbm),
        (coords_ref, charge_ref, index_ref, velocity_ref, mass_ref),
        sem_ref,
    )
    down = lax.broadcasted_iota(jnp.int32, (SUBLANES, LANES), 0)
    copies[0].wait()
    copies[1].wait()

    def lanes_of(part):
        return slice(part * LANES, (part + 1) * LANES)

    table = []
    for c in range(4):
        field = coords_ref[c, 0] * SHRINK if c < 3 else charge_ref[0]
        table.append(
            [jnp.broadcast_to(field[:, lanes_of(part)], (SUBLANES, LANES)) for part in range(atom_rows)]
        )
    for part in range(atom_rows):
        for group in range(LANES // SUBLANES):
            at = part * LANES + group * SUBLANES
            for c in range(4):
                value = take_lanes(table[c][part], down + group * SUBLANES)
                own_ref[c, pl.ds(at, SUBLANES), :] = value if c < 3 else value * 8.0
    copies[2].wait()
    for group in range(index_ref.shape[0] // SUBLANES):
        at = pl.ds(group * SUBLANES, SUBLANES)
        index = index_ref[at, :]
        for c in range(4):
            far_ref[c, at, :] = pick(table[c], index)
    copies[3].wait()
    copies[4].wait()
    fields = [velocity_ref[c, 0] for c in range(3)] + [mass_ref[0]]
    for c, field in enumerate(fields):
        for part in range(atom_rows):
            motion_ref[pl.ds(c * atom_rows + part, 1), :] = field[:, lanes_of(part)]


def force_kernel(
    rows,
    copies,
    holders,
    here_ref,
    live_ref,
    block_hbm,
    around_ref,
    below_ref,
    above_ref,
    own_ref,
    near_ref,
    index_ref,
    motion_ref,
    out_ref,
    table_ref,
    far_ref,
    sum_ref,
    block_ref,
    sem_ref,
):
    atom_rows, shell_rows = rows.atom_rows, rows.shell_rows
    tiles = index_ref.shape[0]
    block_copy = pltpu.make_async_copy(block_hbm, block_ref, sem_ref)
    block_copy.start()
    me = here_ref[0]
    starts = [rows.coords[0], rows.coords[1], rows.coords[2], rows.charge]
    entry_rows = 6 * shell_rows
    blocks = around_ref.shape[0] // rows.count

    def broadcast(row):
        return jnp.broadcast_to(row, (SUBLANES, LANES))

    for c in range(4):
        factor = SHRINK if c < 3 else 1.0
        at = 0
        for neighbour in range(4):
            base = lax.rem(me + holders[neighbour], blocks) * rows.count + starts[c]
            for part in range(shell_rows):
                table_ref[c, at] = broadcast(around_ref[pl.ds(base + part, 1), :] * factor)
                at += 1
        for slab_ref in (below_ref, above_ref):
            for part in range(shell_rows):
                table_ref[c, at] = broadcast(slab_ref[pl.ds(c * shell_rows + part, 1), :] * factor)
                at += 1

    live = live_ref[0, 0]
    down = lax.broadcasted_iota(jnp.int32, (SUBLANES, LANES), 0)
    for group in range(tiles // SUBLANES):
        at = pl.ds(group * SUBLANES, SUBLANES)
        index = index_ref[at, :]
        lanes = index & (LANES - 1)
        chunk = index >> 7
        values = [near_ref[c, at, :] for c in range(4)]
        for k in range(entry_rows):
            here = chunk == atom_rows + k
            values = [jnp.where(here, take_lanes(table_ref[c, k], lanes), values[c]) for c in range(4)]
        values[0] = jnp.where(down + group * SUBLANES < live, values[0], OUT_OF_REACH)
        for c in range(4):
            far_ref[c, at, :] = values[c]

    sum_ref[...] = jnp.zeros(sum_ref.shape, jnp.float32)
    block_copy.wait()

    def add_tile(tile):
        base = block_ref[0, 0, tile] * TILE
        far = [broadcast(far_ref[c, pl.ds(tile, 1), :]) for c in range(4)]
        for group in range(TILE // SUBLANES):
            at = pl.ds(pl.multiple_of(base + group * SUBLANES, SUBLANES), SUBLANES)
            gap = [own_ref[c, at, :] - far[c] for c in range(3)]
            square = gap[0] * gap[0] + gap[1] * gap[1] + gap[2] * gap[2]
            inverse = pl.reciprocal(square + 1.0 / cutoff_sq, approx=True)
            weight = inverse * jnp.maximum(1.0 - square, 0.0)
            strength = (inverse - own_ref[3, at, :] * far[3]) * (weight * weight)
            for c in range(3):
                sum_ref[c, at, :] = sum_ref[c, at, :] + strength * gap[c]

    def add_tiles(step, _):
        for n in range(TILES_STEP):
            add_tile(step * TILES_STEP + n)
        return 0

    lax.fori_loop(0, lax.div(live + TILES_STEP - 1, TILES_STEP), add_tiles, 0)

    scale = time_step * time_step * force_scale * 4.0 / 2048.0

    def lane_sums(c, part):
        return jnp.sum(sum_ref[c, pl.ds(part * LANES, LANES), :].T, axis=0, keepdims=True)

    for part in range(atom_rows):
        mass = motion_ref[pl.ds(3 * atom_rows + part, 1), :]
        for c in range(3):
            speed = motion_ref[pl.ds(c * atom_rows + part, 1), :]
            moved = time_step * speed + scale * lane_sums(c, part) * mass
            for copy in range(copies):
                out_ref[pl.ds(copy * rows.disp_count + c * atom_rows + part, 1), :] = moved
    if rows.disp_count > rows.disp_used:
        for copy in range(copies):
            out_ref[pl.ds(copy * rows.disp_count + rows.disp_used, rows.disp_count - rows.disp_used), :] = jnp.zeros(
                (rows.disp_count - rows.disp_used, LANES), jnp.float32
            )


def bond_kernel(rows, domains, strides, around_ref, weight_ref, matrix_ref, key_ref):
    atom_rows, shell_rows = rows.atom_rows, rows.shell_rows

    def load(row):
        return around_ref[pl.ds(row, domains, stride=rows.count), :]

    def index(row):
        return load(row).astype(jnp.int32)

    fields = [[load(at + part) for part in range(atom_rows)] for at in rows.coords + [rows.mass]]

    def weights(first, second, row):
        gap = [first[c] - second[c] for c in range(3)]
        length_sq = gap[0] * gap[0] + gap[1] * gap[1] + gap[2] * gap[2] + length_floor
        scale = lax.rsqrt(length_sq) * lax.rsqrt(first[3] + second[3])
        return [gap[c] * scale for c in range(3)]

    at = 0
    for part in range(rows.bond_rows):
        first = index(rows.bond_first + part)
        second = index(rows.bond_second + part)
        values = weights([pick(f, first) for f in fields], [pick(f, second) for f in fields], at)
        for c in range(3):
            weight_ref[pl.ds((at * 3 + c) * domains, domains), :] = values[c]
        at += 1
    for part in range(rows.slot_rows):
        first = index(rows.cross_first + part)
        second = index(rows.cross_second + part)
        side = load(rows.side + part)
        live = load(rows.live + part)
        other = [jnp.zeros((domains, LANES), jnp.float32) for _ in range(4)]
        for code, stride in enumerate(strides):
            seen = pltpu.roll(second, stride % domains, 0)
            for f in range(4):
                value = pltpu.roll(pick(fields[f][:shell_rows], seen), -stride % domains, 0)
                other[f] = jnp.where(side == code, value, other[f])
            key = jnp.where(side == code, load(rows.cross_second + part), -1.0)
            key_ref[pl.ds((part * 4 + code) * domains, domains), :] = key
        values = weights([pick(f[:shell_rows], first) for f in fields], other, at)
        for c in range(3):
            weight_ref[pl.ds((at * 3 + c) * domains, domains), :] = values[c] * live
        at += 1

    down = lax.broadcasted_iota(jnp.int32, (SUBLANES, LANES), 0)
    group_rows = 4 * SUBLANES

    kind = jnp.bfloat16 if shell_rows * LANES <= 256 else jnp.float32
    across = lax.broadcasted_iota(jnp.int32, (group_rows, LANES), 1).astype(jnp.float32)
    lanes = [(across + float(block * LANES)).astype(kind) for block in range(shell_rows)]

    def column(row, step, half=0):
        row = jnp.broadcast_to(row, (SUBLANES, LANES))
        groups = [take_lanes(row, down + at) for at in range(step * group_rows, (step + 1) * group_rows, SUBLANES)]
        return (jnp.concatenate(groups, axis=0) - float(half * shell_rows * LANES)).astype(kind)

    def put(at, ends, signs):
        for block in range(shell_rows):
            value = jnp.zeros((group_rows, LANES), kind)
            for end, sign in zip(ends, signs):
                value = jnp.where(end == lanes[block], jnp.full((group_rows, LANES), sign, kind), value)
            matrix_ref[pl.ds(at, group_rows), block * LANES : (block + 1) * LANES] = value.astype(matrix_ref.dtype)

    def build(domain, _):
        start = pl.multiple_of(domain * rows.matrix, LANES)
        for part in range(rows.bond_rows):
            first = around_ref[pl.ds(domain * rows.count + rows.bond_first + part, 1), :]
            second = around_ref[pl.ds(domain * rows.count + rows.bond_second + part, 1), :]
            for step in range(LANES // group_rows):
                for half in range(2):
                    ends = (column(first, step, half), column(second, step, half))
                    put(start + rows.inner_at[half] + part * LANES + step * group_rows, ends, (1.0, -1.0))
        for part in range(rows.slot_rows):
            for code in range(5):
                if code == 0:
                    row = around_ref[pl.ds(domain * rows.count + rows.cross_first + part, 1), :]
                else:
                    owner = lax.rem(domain + (-strides[code - 1]) % domains, domains)
                    row = key_ref[pl.ds((part * 4 + code - 1) * domains + owner, 1), :]
                sign = 1.0 if code == 0 else -1.0
                for step in range(LANES // group_rows):
                    at = start + rows.cross_at + (part * 5 + code) * LANES + step * group_rows
                    put(at, (column(row, step),), (sign,))
        return 0

    lax.fori_loop(0, domains, build, 0)


def solve_kernel(
    rows,
    domains,
    strides,
    here_ref,
    around_ref,
    moves_ref,
    weight_ref,
    signs_ref,
    coords_out_ref,
    velocity_out_ref,
    push_ref,
    field_ref,
    matrix_ref,
):
    atom_rows, shell_rows = rows.atom_rows, rows.shell_rows
    bond_rows, slot_rows = rows.bond_rows, rows.slot_rows
    me = here_ref[0]

    def widen(domain, _):
        at = pl.ds(pl.multiple_of(domain * rows.matrix, LANES), rows.matrix)
        matrix_ref[at, :] = signs_ref[at, :].astype(matrix_ref.dtype)
        return 0

    lax.fori_loop(0, domains, widen, 0)

    def load(row):
        return around_ref[pl.ds(row, domains, stride=rows.count), :]

    def index(row):
        return load(row).astype(jnp.int32)

    inner_first = [index(rows.bond_first + p) for p in range(bond_rows)]
    inner_second = [index(rows.bond_second + p) for p in range(bond_rows)]
    cross_first = [index(rows.cross_first + p) for p in range(slot_rows)]
    cross_second = [index(rows.cross_second + p) for p in range(slot_rows)]
    sides = [load(rows.side + p) for p in range(slot_rows)]
    masses = [load(rows.mass + p) for p in range(atom_rows)]

    def weight(at, c):
        return weight_ref[pl.ds((at * 3 + c) * domains, domains), :]

    def project(fields):
        result = []
        for part in range(bond_rows):
            total = 0.0
            for c in range(3):
                ends = pick(fields[c], inner_first[part]) - pick(fields[c], inner_second[part])
                total = total + weight(part, c) * ends
            result.append(total)
        for part in range(slot_rows):
            seen = [pltpu.roll(cross_second[part], stride % domains, 0) for stride in strides]
            total = 0.0
            for c in range(3):
                shell = fields[c][:shell_rows]
                other = 0.0
                for code, stride in enumerate(strides):
                    value = pltpu.roll(pick(shell, seen[code]), -stride % domains, 0)
                    other = jnp.where(sides[part] == code, value, other)
                total = total + weight(bond_rows + part, c) * (pick(shell, cross_first[part]) - other)
            result.append(total)
        return result

    def put_pushes(values):
        for at, value in enumerate(values):
            for c in range(3):
                pushed = weight(at, c) * value
                high = pushed.astype(jnp.bfloat16).astype(jnp.float32)
                push_ref[at, pl.ds(c * domains, domains), :] = high
                push_ref[at, pl.ds((3 + c) * domains, domains), :] = pushed - high

    def pushes_of(at, domain):
        return push_ref[at, pl.ds(domain, SUBLANES, stride=domains), :].astype(jnp.bfloat16)

    def totals(domain, owners):
        inner = [pushes_of(p, domain) for p in range(bond_rows)]
        cross = []
        for part in range(slot_rows):
            cross.extend(pushes_of(bond_rows + part, owner) for owner in [domain] + owners)
        start = domain * rows.matrix
        if not isinstance(start, int):
            start = pl.multiple_of(start, LANES)
        shell_sum = jnp.dot(
            jnp.concatenate(inner + cross, axis=1),
            matrix_ref[pl.ds(start, rows.shell_terms), :],
            preferred_element_type=jnp.float32,
        )
        other_sum = jnp.dot(
            jnp.concatenate(inner, axis=1),
            matrix_ref[pl.ds(start + rows.shell_terms, bond_rows * LANES), :],
            preferred_element_type=jnp.float32,
        )
        return [
            half[:, p * LANES : (p + 1) * LANES] for half in (shell_sum, other_sum) for p in range(shell_rows)
        ]

    def spread(values):
        put_pushes(values)
        for domain in range(domains):
            sums = totals(domain, [(domain - stride) % domains for stride in strides])
            for part in range(atom_rows):
                field_ref[part, pl.ds(domain, SUBLANES, stride=domains), :] = sums[part]
        return [
            [
                masses[part]
                * (
                    field_ref[part, pl.ds(c * domains, domains), :]
                    + field_ref[part, pl.ds((3 + c) * domains, domains), :]
                )
                for part in range(atom_rows)
            ]
            for c in range(3)
        ]

    moves = [
        [moves_ref[pl.ds(c * atom_rows + p, domains, stride=rows.disp_count), :] for p in range(atom_rows)]
        for c in range(3)
    ]
    push_ref[...] = jnp.zeros(push_ref.shape, jnp.float32)
    residue = project(moves)

    def expand(_, carry):
        residue, summed = carry
        change = project(spread(residue))
        residue = [now - step for now, step in zip(residue, change)]
        return residue, [a + b for a, b in zip(summed, residue)]

    residue, summed = lax.fori_loop(0, ORDER, expand, (residue, residue))
    put_pushes(summed)
    sums = totals(me, [lax.rem(me + (-stride) % domains, domains) for stride in strides])
    for part in range(atom_rows):
        lanes = slice(part * LANES, (part + 1) * LANES)
        mass = around_ref[pl.ds(me * rows.count + rows.mass + part, 1), :]
        for c in range(3):
            correction = mass * (sums[part][c : c + 1, :] + sums[part][3 + c : 4 + c, :])
            move = moves_ref[pl.ds(me * rows.disp_count + c * atom_rows + part, 1), :] - correction
            start = around_ref[pl.ds(me * rows.count + rows.coords[c] + part, 1), :]
            coords_out_ref[c, 0, :, lanes] = start + move
            velocity_out_ref[c, 0, :, lanes] = move * (1.0 / time_step)


def vmem(count):
    return [pl.BlockSpec(memory_space=pltpu.VMEM)] * count


def smem(count):
    return [pl.BlockSpec(memory_space=pltpu.SMEM)] * count


def hbm(count):
    return [pl.BlockSpec(memory_space=pltpu.HBM)] * count


def in_hbm(arrays):
    return [pltpu.with_memory_space_constraint(a, pltpu.HBM) for a in arrays]


def params(mebibytes):
    return pltpu.CompilerParams(vmem_limit_bytes=mebibytes * 1024 * 1024)


def cost(flops, moved):
    return pl.CostEstimate(flops=flops, bytes_accessed=moved, transcendentals=0)


def room_for(arrays):
    return [pltpu.VMEM(a.shape, a.dtype) for a in arrays]


def shards(
    coords,
    velocity,
    charge,
    inv_mass,
    tile_block,
    tile_atoms,
    active_tile_count,
    bond_atoms,
    cross_atoms,
    cross_side,
    cross_count,
):
    atoms = coords.shape[-1]
    tiles = tile_atoms.shape[2]
    domains = lax.axis_size("dom")
    strides = strides_of(domains)
    rows = Rows(atoms, bond_atoms.shape[-1], cross_side.shape[-1])
    whole_slab = domains == SUBLANES
    copies = domains if whole_slab else 1
    f32 = jnp.float32

    sent = (coords, charge, inv_mass, bond_atoms, cross_atoms, cross_side)
    packed, rim = pl.pallas_call(
        functools.partial(pack_kernel, rows, copies),
        out_shape=(
            jax.ShapeDtypeStruct((copies * rows.count, LANES), f32),
            jax.ShapeDtypeStruct((4 * rows.shell_rows, LANES), f32),
        ),
        in_specs=smem(1) + hbm(len(sent)),
        out_specs=tuple(vmem(2)),
        scratch_shapes=room_for(sent) + [pltpu.SemaphoreType.DMA((len(sent),))],
        compiler_params=params(4),
        name="pack",
    )(cross_count, *in_hbm(sent))

    alone = (coords, charge, velocity, inv_mass, tile_atoms)
    own = pl.pallas_call(
        functools.partial(own_kernel, rows),
        out_shape=(
            jax.ShapeDtypeStruct((4, atoms, LANES), f32),
            jax.ShapeDtypeStruct((4, tiles, TILE), f32),
            jax.ShapeDtypeStruct((tiles, TILE), jnp.int32),
            jax.ShapeDtypeStruct((4 * rows.atom_rows, LANES), f32),
        ),
        in_specs=hbm(len(alone)),
        out_specs=tuple(vmem(4)),
        scratch_shapes=room_for(alone[:4]) + [pltpu.SemaphoreType.DMA((len(alone),))],
        compiler_params=params(4),
        cost_estimate=cost(64 * atoms * LANES, 16 * atoms * LANES),
        name="own",
    )(*in_hbm(alone))

    below = passed_along(rim, "slab", 1)
    above = passed_along(rim, "slab", -1)
    if whole_slab:
        around = lax.all_to_all(packed, "dom", 0, 0, tiled=True)
        here = lax.axis_index("dom").reshape(1)
        holders = [stride % domains for stride in strides]
    else:
        around = jnp.concatenate([packed] + [passed_along(packed, "dom", -stride) for stride in strides], axis=0)
        here = jnp.zeros(1, jnp.int32)
        holders = [1, 2, 3, 4]

    moves = pl.pallas_call(
        functools.partial(force_kernel, rows, copies, holders),
        out_shape=jax.ShapeDtypeStruct((copies * rows.disp_count, LANES), f32),
        in_specs=smem(2) + hbm(1) + vmem(7),
        out_specs=vmem(1)[0],
        scratch_shapes=[
            pltpu.VMEM((4, 6 * rows.shell_rows, SUBLANES, LANES), f32),
            pltpu.VMEM((4, tiles, LANES), f32),
            pltpu.VMEM((3, atoms, LANES), f32),
            pltpu.SMEM(tile_block.shape, jnp.int32),
            pltpu.SemaphoreType.DMA(()),
        ],
        compiler_params=params(8),
        cost_estimate=cost(30 * tiles * TILE * TILE, 4 * around.size),
        name="force",
    )(here, active_tile_count, *in_hbm([tile_block]), around, below, above, *own)

    if not whole_slab:
        return by_exchange(rows, strides, around, moves, cross_count)

    constraint_rows = rows.bond_rows + rows.slot_rows
    weight, matrix = pl.pallas_call(
        functools.partial(bond_kernel, rows, domains, strides),
        out_shape=(
            jax.ShapeDtypeStruct((constraint_rows * 3 * domains, LANES), f32),
            jax.ShapeDtypeStruct((domains * rows.matrix, atoms // 2), jnp.float8_e4m3fn),
        ),
        in_specs=vmem(1),
        out_specs=tuple(vmem(2)),
        scratch_shapes=[pltpu.VMEM((rows.slot_rows * 4 * domains, LANES), f32)],
        compiler_params=params(16),
        cost_estimate=cost(8 * domains * rows.matrix * atoms // 2, 4 * around.size),
        name="bonds",
    )(around)

    every_move = lax.all_to_all(moves, "dom", 0, 0, tiled=True)

    return pl.pallas_call(
        functools.partial(solve_kernel, rows, domains, strides),
        out_shape=(
            jax.ShapeDtypeStruct(coords.shape, f32),
            jax.ShapeDtypeStruct(coords.shape, f32),
        ),
        in_specs=smem(1) + vmem(4),
        out_specs=tuple(vmem(2)),
        scratch_shapes=[
            pltpu.VMEM((constraint_rows, SUBLANES * domains, LANES), f32),
            pltpu.VMEM((rows.atom_rows, SUBLANES * domains, LANES), f32),
            pltpu.VMEM(matrix.shape, jnp.bfloat16),
        ],
        compiler_params=params(16),
        name="solve",
    )(here, around, every_move, weight, matrix)


def by_exchange(rows, strides, around, moves, cross_count):
    atom_count = rows.atom_rows * LANES
    shell = rows.shell_rows * LANES
    inside = around.reshape(5, rows.count, LANES)

    def flat(at, count):
        return inside[0, at : at + count].reshape(-1)

    def neighbours(at):
        return inside[1:, at : at + rows.shell_rows].reshape(-1)

    coords = jnp.stack([flat(at, rows.atom_rows) for at in rows.coords])
    inv_mass = flat(rows.mass, rows.atom_rows)
    displace = moves[: rows.disp_used].reshape(3, atom_count)
    left = flat(rows.bond_first, rows.bond_rows).astype(jnp.int32)
    right = flat(rows.bond_second, rows.bond_rows).astype(jnp.int32)
    cross_left = flat(rows.cross_first, rows.slot_rows).astype(jnp.int32)
    cross_right = flat(rows.cross_second, rows.slot_rows).astype(jnp.int32)
    side = flat(rows.side, rows.slot_rows).astype(jnp.int32)
    flag = flat(rows.live, rows.slot_rows)
    cross_index = side * shell + cross_right
    far_coords = jnp.stack([neighbours(at) for at in rows.coords])
    far_mass = neighbours(rows.mass)

    def weights(first, second, mass_first, mass_second):
        gap = first - second
        length = jnp.sqrt(jnp.sum(gap * gap, axis=0) + length_floor)
        return gap / length * lax.rsqrt(mass_first + mass_second)

    inner = weights(coords[:, left], coords[:, right], inv_mass[left], inv_mass[right])
    cross = flag * weights(
        coords[:, cross_left], far_coords[:, cross_index], inv_mass[cross_left], far_mass[cross_index]
    )

    def project(field):
        rim = field[:, :shell]
        far = jnp.concatenate([passed_along(rim, "dom", -stride) for stride in strides], axis=1)
        return (
            jnp.sum(inner * (field[:, left] - field[:, right]), axis=0),
            jnp.sum(cross * (field[:, cross_left] - far[:, cross_index]), axis=0),
        )

    def spread(values):
        pushed = inner * values[0]
        pushed_cross = cross * values[1]
        totals = jnp.zeros((3, atom_count), jnp.float32).at[:, left].add(pushed).at[:, right].add(-pushed)
        totals = totals.at[:, cross_left].add(pushed_cross)
        outward = jnp.zeros((3, 4 * shell), jnp.float32).at[:, cross_index].add(-pushed_cross)
        for code, stride in enumerate(strides):
            totals = totals.at[:, :shell].add(
                passed_along(outward[:, code * shell : (code + 1) * shell], "dom", stride)
            )
        return inv_mass * totals

    residue = project(displace)
    summed = residue
    for _ in range(ORDER):
        change = project(spread(residue))
        residue = tuple(now - step for now, step in zip(residue, change))
        summed = tuple(a + b for a, b in zip(summed, residue))
    move = displace - spread(summed)
    return (
        (coords + move).reshape(3, 1, 1, atom_count),
        (move * (1.0 / time_step)).reshape(3, 1, 1, atom_count),
    )


def solution(mesh):
    return jax.shard_map(
        shards,
        mesh=mesh,
        in_specs=(
            P(None, "slab", "dom", None),
            P(None, "slab", "dom", None),
            P("slab", "dom", None),
            P("slab", "dom", None),
            P("slab", "dom", None),
            P("slab", "dom", None, None),
            P("slab", "dom"),
            P(None, "slab", "dom", None),
            P(None, "slab", "dom", None),
            P("slab", "dom", None),
            P("slab", "dom"),
        ),
        out_specs=(P(None, "slab", "dom", None), P(None, "slab", "dom", None)),
        check_vma=False,
    )
```

```python
import functools

import jax
import jax.numpy as jnp
from jax import lax
from jax.experimental import pallas as pl
from jax.experimental.pallas import tpu as pltpu
from jax.sharding import PartitionSpec as P

TILE = 128
ORDER = 4
LANES = 128
SUBLANES = 8

time_step = 0.1
cutoff_sq = 16.0
force_scale = 4.0
length_floor = 0.25


def passed_along(array, axis, by):
    length = lax.axis_size(axis)
    return lax.ppermute(array, axis, [(i, (i + by) % length) for i in range(length)])


def strides_of(domains):
    row_width = max(2, domains // 8)
    return (1, -1, row_width, -row_width)


def round_up(count, step):
    return -(-count // step) * step


class Rows:
    def __init__(self, atoms, bonds, slots):
        self.atom_rows = atoms // LANES
        self.shell_rows = atoms // 2 // LANES
        self.bond_rows = bonds // LANES
        self.slot_rows = slots // LANES
        at = 0
        self.coords = []
        for _ in range(3):
            self.coords.append(at)
            at += self.atom_rows
        self.charge = at
        at += self.atom_rows
        self.mass = at
        at += self.atom_rows
        self.bond_first = at
        at += self.bond_rows
        self.bond_second = at
        at += self.bond_rows
        self.cross_first = at
        at += self.slot_rows
        self.cross_second = at
        at += self.slot_rows
        self.side = at
        at += self.slot_rows
        self.live = at
        at += self.slot_rows
        self.used = at
        self.count = round_up(at, SUBLANES)
        self.shell_terms = (self.bond_rows + self.slot_rows) * LANES
        self.inner_at = (0, self.shell_terms)
        self.cross_at = self.bond_rows * LANES
        self.far_at = self.shell_terms + self.bond_rows * LANES
        self.matrix = self.far_at + self.slot_rows * LANES
        self.disp_used = 3 * self.atom_rows
        self.disp_count = round_up(self.disp_used, SUBLANES)


def take_lanes(table, lanes):
    return jnp.take_along_axis(table, lanes, axis=1, mode="promise_in_bounds")


def pick(tables, index):
    lanes = index & (LANES - 1)
    chunk = index >> 7
    result = take_lanes(tables[0], lanes)
    for k in range(1, len(tables)):
        result = jnp.where(chunk == k, take_lanes(tables[k], lanes), result)
    return result


def fetched(sources, targets, sem_ref):
    copies = [pltpu.make_async_copy(s, t, sem_ref.at[n]) for n, (s, t) in enumerate(zip(sources, targets))]
    for copy in copies:
        copy.start()
    return copies


def pack_kernel(rows, copies, count_ref, *refs):
    sources, (out_ref, rim_ref), targets, sem_ref = refs[:6], refs[6:8], refs[8:14], refs[14]
    for copy in fetched(sources, targets, sem_ref):
        copy.wait()
    coords_ref, charge_ref, mass_ref, bonds_ref, cross_ref, side_ref = targets

    def put(row, value):
        for part in range(value.shape[1] // LANES):
            piece = value[:, part * LANES : (part + 1) * LANES]
            for copy in range(copies):
                out_ref[pl.ds(copy * rows.count + row + part, 1), :] = piece

    shell = rows.shell_rows * LANES
    fields = [coords_ref[c, 0] for c in range(3)] + [charge_ref[0]]
    for c in range(4):
        at = rows.coords[c] if c < 3 else rows.charge
        put(at, fields[c])
        for part in range(rows.shell_rows):
            rim_ref[pl.ds(c * rows.shell_rows + part, 1), :] = fields[c][:, part * LANES : (part + 1) * LANES]
    put(rows.mass, mass_ref[0])
    put(rows.bond_first, bonds_ref[0, 0].astype(jnp.float32))
    put(rows.bond_second, bonds_ref[1, 0].astype(jnp.float32))
    put(rows.cross_first, cross_ref[0, 0].astype(jnp.float32))
    put(rows.cross_second, cross_ref[1, 0].astype(jnp.float32))
    side = side_ref[0]
    put(rows.side, side.astype(jnp.float32))
    slot = lax.broadcasted_iota(jnp.int32, side.shape, 1)
    put(rows.live, jnp.where(slot < count_ref[0, 0], 1.0, 0.0))
    if rows.count > rows.used:
        for copy in range(copies):
            out_ref[pl.ds(copy * rows.count + rows.used, rows.count - rows.used), :] = jnp.zeros(
                (rows.count - rows.used, LANES), jnp.float32
            )


SHRINK = 1.0 / 4.0
OUT_OF_REACH = 1000.0
TILES_STEP = 2


def own_kernel(
    rows,
    coords_hbm,
    charge_hbm,
    velocity_hbm,
    mass_hbm,
    atoms_hbm,
    own_ref,
    far_ref,
    index_ref,
    motion_ref,
    coords_ref,
    charge_ref,
    velocity_ref,
    mass_ref,
    sem_ref,
):
    atom_rows = rows.atom_rows
    copies = fetched(
        (coords_hbm, charge_hbm, atoms_hbm.at[0, 0], velocity_hbm, mass_hbm),
        (coords_ref, charge_ref, index_ref, velocity_ref, mass_ref),
        sem_ref,
    )
    down = lax.broadcasted_iota(jnp.int32, (SUBLANES, LANES), 0)
    copies[0].wait()
    copies[1].wait()

    def lanes_of(part):
        return slice(part * LANES, (part + 1) * LANES)

    table = []
    for c in range(4):
        field = coords_ref[c, 0] * SHRINK if c < 3 else charge_ref[0]
        table.append(
            [jnp.broadcast_to(field[:, lanes_of(part)], (SUBLANES, LANES)) for part in range(atom_rows)]
        )
    for part in range(atom_rows):
        for group in range(LANES // SUBLANES):
            at = part * LANES + group * SUBLANES
            for c in range(4):
                value = take_lanes(table[c][part], down + group * SUBLANES)
                own_ref[c, pl.ds(at, SUBLANES), :] = value if c < 3 else value * 8.0
    copies[2].wait()
    for group in range(index_ref.shape[0] // SUBLANES):
        at = pl.ds(group * SUBLANES, SUBLANES)
        index = index_ref[at, :]
        for c in range(4):
            far_ref[c, at, :] = pick(table[c], index)
    copies[3].wait()
    copies[4].wait()
    fields = [velocity_ref[c, 0] for c in range(3)] + [mass_ref[0]]
    for c, field in enumerate(fields):
        for part in range(atom_rows):
            motion_ref[pl.ds(c * atom_rows + part, 1), :] = field[:, lanes_of(part)]


def force_kernel(
    rows,
    copies,
    holders,
    here_ref,
    live_ref,
    block_hbm,
    around_ref,
    below_ref,
    above_ref,
    own_ref,
    near_ref,
    index_ref,
    motion_ref,
    out_ref,
    table_ref,
    far_ref,
    sum_ref,
    block_ref,
    sem_ref,
):
    atom_rows, shell_rows = rows.atom_rows, rows.shell_rows
    tiles = index_ref.shape[0]
    block_copy = pltpu.make_async_copy(block_hbm, block_ref, sem_ref)
    block_copy.start()
    me = here_ref[0]
    starts = [rows.coords[0], rows.coords[1], rows.coords[2], rows.charge]
    entry_rows = 6 * shell_rows
    blocks = around_ref.shape[0] // rows.count

    def broadcast(row):
        return jnp.broadcast_to(row, (SUBLANES, LANES))

    for c in range(4):
        factor = SHRINK if c < 3 else 1.0
        at = 0
        for neighbour in range(4):
            base = lax.rem(me + holders[neighbour], blocks) * rows.count + starts[c]
            for part in range(shell_rows):
                table_ref[c, at] = broadcast(around_ref[pl.ds(base + part, 1), :] * factor)
                at += 1
        for slab_ref in (below_ref, above_ref):
            for part in range(shell_rows):
                table_ref[c, at] = broadcast(slab_ref[pl.ds(c * shell_rows + part, 1), :] * factor)
                at += 1

    live = live_ref[0, 0]
    down = lax.broadcasted_iota(jnp.int32, (SUBLANES, LANES), 0)
    for group in range(tiles // SUBLANES):
        at = pl.ds(group * SUBLANES, SUBLANES)
        index = index_ref[at, :]
        lanes = index & (LANES - 1)
        chunk = index >> 7
        values = [near_ref[c, at, :] for c in range(4)]
        for k in range(entry_rows):
            here = chunk == atom_rows + k
            values = [jnp.where(here, take_lanes(table_ref[c, k], lanes), values[c]) for c in range(4)]
        values[0] = jnp.where(down + group * SUBLANES < live, values[0], OUT_OF_REACH)
        for c in range(4):
            far_ref[c, at, :] = values[c]

    sum_ref[...] = jnp.zeros(sum_ref.shape, jnp.float32)
    block_copy.wait()

    def add_tile(tile):
        base = block_ref[0, 0, tile] * TILE
        far = [broadcast(far_ref[c, pl.ds(tile, 1), :]) for c in range(4)]
        for group in range(TILE // SUBLANES):
            at = pl.ds(pl.multiple_of(base + group * SUBLANES, SUBLANES), SUBLANES)
            gap = [own_ref[c, at, :] - far[c] for c in range(3)]
            square = gap[0] * gap[0] + gap[1] * gap[1] + gap[2] * gap[2]
            inverse = pl.reciprocal(square + 1.0 / cutoff_sq, approx=True)
            weight = inverse * jnp.maximum(1.0 - square, 0.0)
            strength = (inverse - own_ref[3, at, :] * far[3]) * (weight * weight)
            for c in range(3):
                sum_ref[c, at, :] = sum_ref[c, at, :] + strength * gap[c]

    def add_tiles(step, _):
        for n in range(TILES_STEP):
            add_tile(step * TILES_STEP + n)
        return 0

    lax.fori_loop(0, lax.div(live + TILES_STEP - 1, TILES_STEP), add_tiles, 0)

    scale = time_step * time_step * force_scale * 4.0 / 2048.0

    def lane_sums(c, part):
        return jnp.sum(sum_ref[c, pl.ds(part * LANES, LANES), :].T, axis=0, keepdims=True)

    for part in range(atom_rows):
        mass = motion_ref[pl.ds(3 * atom_rows + part, 1), :]
        for c in range(3):
            speed = motion_ref[pl.ds(c * atom_rows + part, 1), :]
            moved = time_step * speed + scale * lane_sums(c, part) * mass
            for copy in range(copies):
                out_ref[pl.ds(copy * rows.disp_count + c * atom_rows + part, 1), :] = moved
    if rows.disp_count > rows.disp_used:
        for copy in range(copies):
            out_ref[pl.ds(copy * rows.disp_count + rows.disp_used, rows.disp_count - rows.disp_used), :] = jnp.zeros(
                (rows.disp_count - rows.disp_used, LANES), jnp.float32
            )


def bond_kernel(rows, domains, strides, around_ref, weight_ref, matrix_ref):
    atom_rows, shell_rows = rows.atom_rows, rows.shell_rows

    def load(row):
        return around_ref[pl.ds(row, domains, stride=rows.count), :]

    def index(row):
        return load(row).astype(jnp.int32)

    fields = [[load(at + part) for part in range(atom_rows)] for at in rows.coords + [rows.mass]]

    def weights(first, second, row):
        gap = [first[c] - second[c] for c in range(3)]
        length_sq = gap[0] * gap[0] + gap[1] * gap[1] + gap[2] * gap[2] + length_floor
        scale = lax.rsqrt(length_sq) * lax.rsqrt(first[3] + second[3])
        return [gap[c] * scale for c in range(3)]

    at = 0
    for part in range(rows.bond_rows):
        first = index(rows.bond_first + part)
        second = index(rows.bond_second + part)
        values = weights([pick(f, first) for f in fields], [pick(f, second) for f in fields], at)
        for c in range(3):
            weight_ref[pl.ds((at * 3 + c) * domains, domains), :] = values[c]
        at += 1
    for part in range(rows.slot_rows):
        first = index(rows.cross_first + part)
        second = index(rows.cross_second + part)
        side = load(rows.side + part)
        live = load(rows.live + part)
        other = [jnp.zeros((domains, LANES), jnp.float32) for _ in range(4)]
        for code, stride in enumerate(strides):
            seen = pltpu.roll(second, stride % domains, 0)
            for f in range(4):
                value = pltpu.roll(pick(fields[f][:shell_rows], seen), -stride % domains, 0)
                other[f] = jnp.where(side == code, value, other[f])
        values = weights([pick(f[:shell_rows], first) for f in fields], other, at)
        for c in range(3):
            weight_ref[pl.ds((at * 3 + c) * domains, domains), :] = values[c] * live
        at += 1

    down = lax.broadcasted_iota(jnp.int32, (SUBLANES, LANES), 0)
    group_rows = 4 * SUBLANES

    kind = jnp.bfloat16 if shell_rows * LANES <= 256 else jnp.float32
    across = lax.broadcasted_iota(jnp.int32, (group_rows, LANES), 1).astype(jnp.float32)
    lanes = [(across + float(block * LANES)).astype(kind) for block in range(shell_rows)]

    def column(row, step, half=0):
        row = jnp.broadcast_to(row, (SUBLANES, LANES))
        groups = [take_lanes(row, down + at) for at in range(step * group_rows, (step + 1) * group_rows, SUBLANES)]
        return (jnp.concatenate(groups, axis=0) - float(half * shell_rows * LANES)).astype(kind)

    def put(at, ends, signs):
        for block in range(shell_rows):
            value = jnp.zeros((group_rows, LANES), kind)
            for end, sign in zip(ends, signs):
                value = jnp.where(end == lanes[block], jnp.full((group_rows, LANES), sign, kind), value)
            matrix_ref[pl.ds(at, group_rows), block * LANES : (block + 1) * LANES] = value.astype(matrix_ref.dtype)

    def build(domain, _):
        start = pl.multiple_of(domain * rows.matrix, LANES)
        for part in range(rows.bond_rows):
            first = around_ref[pl.ds(domain * rows.count + rows.bond_first + part, 1), :]
            second = around_ref[pl.ds(domain * rows.count + rows.bond_second + part, 1), :]
            for step in range(LANES // group_rows):
                for half in range(2):
                    ends = (column(first, step, half), column(second, step, half))
                    put(start + rows.inner_at[half] + part * LANES + step * group_rows, ends, (1.0, -1.0))
        for part in range(rows.slot_rows):
            for row_at, to, sign in (
                (rows.cross_first, rows.cross_at, 1.0),
                (rows.cross_second, rows.far_at, -1.0),
            ):
                row = around_ref[pl.ds(domain * rows.count + row_at + part, 1), :]
                for step in range(LANES // group_rows):
                    put(start + to + part * LANES + step * group_rows, (column(row, step),), (sign,))
        return 0

    lax.fori_loop(0, domains, build, 0)


def solve_kernel(
    rows,
    domains,
    strides,
    here_ref,
    around_ref,
    moves_ref,
    weight_ref,
    matrix_ref,
    coords_out_ref,
    velocity_out_ref,
    push_ref,
    far_push_ref,
    field_ref,
):
    atom_rows, shell_rows = rows.atom_rows, rows.shell_rows
    bond_rows, slot_rows = rows.bond_rows, rows.slot_rows
    me = here_ref[0]

    def load(row):
        return around_ref[pl.ds(row, domains, stride=rows.count), :]

    def index(row):
        return load(row).astype(jnp.int32)

    inner_first = [index(rows.bond_first + p) for p in range(bond_rows)]
    inner_second = [index(rows.bond_second + p) for p in range(bond_rows)]
    cross_first = [index(rows.cross_first + p) for p in range(slot_rows)]
    cross_second = [index(rows.cross_second + p) for p in range(slot_rows)]
    sides = [load(rows.side + p) for p in range(slot_rows)]
    masses = [load(rows.mass + p) for p in range(atom_rows)]

    def weight(at, c):
        return weight_ref[pl.ds((at * 3 + c) * domains, domains), :]

    def project(fields):
        result = []
        for part in range(bond_rows):
            total = 0.0
            for c in range(3):
                ends = pick(fields[c], inner_first[part]) - pick(fields[c], inner_second[part])
                total = total + weight(part, c) * ends
            result.append(total)
        for part in range(slot_rows):
            seen = [pltpu.roll(cross_second[part], stride % domains, 0) for stride in strides]
            total = 0.0
            for c in range(3):
                shell = fields[c][:shell_rows]
                other = 0.0
                for code, stride in enumerate(strides):
                    value = pltpu.roll(pick(shell, seen[code]), -stride % domains, 0)
                    other = jnp.where(sides[part] == code, value, other)
                total = total + weight(bond_rows + part, c) * (pick(shell, cross_first[part]) - other)
            result.append(total)
        return result

    def put_pushes(values):
        for at, value in enumerate(values):
            for c in range(3):
                pushed = weight(at, c) * value
                high = pushed.astype(jnp.bfloat16).astype(jnp.float32)
                for row, part in ((c, high), (3 + c, pushed - high)):
                    push_ref[at, pl.ds(row * domains, domains), :] = part
                    if at >= bond_rows:
                        for code in range(4):
                            far_push_ref[at - bond_rows, pl.ds((code * SUBLANES + row) * domains, domains), :] = (
                                jnp.where(sides[at - bond_rows] == code, part, 0.0)
                            )

    def pushes_of(at, domain):
        return push_ref[at, pl.ds(domain, SUBLANES, stride=domains), :].astype(jnp.bfloat16)

    def product(pushes, domain, at):
        start = domain * rows.matrix + at
        if not isinstance(start, int):
            start = pl.multiple_of(start, LANES)
        pushes = pushes[0] if len(pushes) == 1 else jnp.concatenate(pushes, axis=1)
        result = jnp.dot(
            pushes, matrix_ref[pl.ds(start, pushes.shape[1]), :], preferred_element_type=jnp.float32
        )
        return [result[:, p * LANES : (p + 1) * LANES] for p in range(shell_rows)]

    def inner_totals(domain):
        pushes = [pushes_of(at, domain) for at in range(bond_rows + slot_rows)]
        return product(pushes, domain, 0) + product(pushes[:bond_rows], domain, rows.shell_terms)

    def far_totals(domain, first_row, count):
        pushes = [
            far_push_ref[p, pl.ds(first_row * domains + domain, count, stride=domains), :].astype(jnp.bfloat16)
            for p in range(slot_rows)
        ]
        return product(pushes, domain, rows.far_at)

    def spread(values):
        put_pushes(values)
        for domain in range(domains):
            for part, total in enumerate(inner_totals(domain)):
                field_ref[0, part, pl.ds(domain, SUBLANES, stride=domains), :] = total
            for part, total in enumerate(far_totals(domain, 0, 4 * SUBLANES)):
                for code, stride in enumerate(strides):
                    field_ref[1 + code, part, pl.ds((domain + stride) % domains, SUBLANES, stride=domains), :] = total[
                        code * SUBLANES : (code + 1) * SUBLANES, :
                    ]

        def field(c, part):
            pieces = [
                field_ref[source, part, pl.ds(row * domains, domains), :]
                for source in range(5 if part < shell_rows else 1)
                for row in (c, 3 + c)
            ]
            return masses[part] * functools.reduce(lambda a, b: a + b, pieces)

        return [[field(c, part) for part in range(atom_rows)] for c in range(3)]

    moves = [
        [moves_ref[pl.ds(c * atom_rows + p, domains, stride=rows.disp_count), :] for p in range(atom_rows)]
        for c in range(3)
    ]
    push_ref[...] = jnp.zeros(push_ref.shape, jnp.float32)
    far_push_ref[...] = jnp.zeros(far_push_ref.shape, jnp.float32)
    residue = project(moves)

    def expand(_, carry):
        residue, summed = carry
        change = project(spread(residue))
        residue = [now - step for now, step in zip(residue, change)]
        return residue, [a + b for a, b in zip(summed, residue)]

    residue, summed = lax.fori_loop(0, ORDER, expand, (residue, residue))
    put_pushes(summed)
    sums = inner_totals(me)
    for code, stride in enumerate(strides):
        owner = lax.rem(me + (-stride) % domains, domains)
        for part, total in enumerate(far_totals(owner, code * SUBLANES, SUBLANES)):
            sums[part] = sums[part] + total
    for part in range(atom_rows):
        lanes = slice(part * LANES, (part + 1) * LANES)
        mass = around_ref[pl.ds(me * rows.count + rows.mass + part, 1), :]
        for c in range(3):
            correction = mass * (sums[part][c : c + 1, :] + sums[part][3 + c : 4 + c, :])
            move = moves_ref[pl.ds(me * rows.disp_count + c * atom_rows + part, 1), :] - correction
            start = around_ref[pl.ds(me * rows.count + rows.coords[c] + part, 1), :]
            coords_out_ref[c, 0, :, lanes] = start + move
            velocity_out_ref[c, 0, :, lanes] = move * (1.0 / time_step)


def vmem(count):
    return [pl.BlockSpec(memory_space=pltpu.VMEM)] * count


def smem(count):
    return [pl.BlockSpec(memory_space=pltpu.SMEM)] * count


def hbm(count):
    return [pl.BlockSpec(memory_space=pltpu.HBM)] * count


def in_hbm(arrays):
    return [pltpu.with_memory_space_constraint(a, pltpu.HBM) for a in arrays]


def params(mebibytes):
    return pltpu.CompilerParams(vmem_limit_bytes=mebibytes * 1024 * 1024)


def cost(flops, moved):
    return pl.CostEstimate(flops=flops, bytes_accessed=moved, transcendentals=0)


def room_for(arrays):
    return [pltpu.VMEM(a.shape, a.dtype) for a in arrays]


def shards(
    coords,
    velocity,
    charge,
    inv_mass,
    tile_block,
    tile_atoms,
    active_tile_count,
    bond_atoms,
    cross_atoms,
    cross_side,
    cross_count,
):
    atoms = coords.shape[-1]
    tiles = tile_atoms.shape[2]
    domains = lax.axis_size("dom")
    strides = strides_of(domains)
    rows = Rows(atoms, bond_atoms.shape[-1], cross_side.shape[-1])
    whole_slab = domains == SUBLANES
    copies = domains if whole_slab else 1
    f32 = jnp.float32

    sent = (coords, charge, inv_mass, bond_atoms, cross_atoms, cross_side)
    packed, rim = pl.pallas_call(
        functools.partial(pack_kernel, rows, copies),
        out_shape=(
            jax.ShapeDtypeStruct((copies * rows.count, LANES), f32),
            jax.ShapeDtypeStruct((4 * rows.shell_rows, LANES), f32),
        ),
        in_specs=smem(1) + hbm(len(sent)),
        out_specs=tuple(vmem(2)),
        scratch_shapes=room_for(sent) + [pltpu.SemaphoreType.DMA((len(sent),))],
        compiler_params=params(4),
        name="pack",
    )(cross_count, *in_hbm(sent))

    alone = (coords, charge, velocity, inv_mass, tile_atoms)
    own = pl.pallas_call(
        functools.partial(own_kernel, rows),
        out_shape=(
            jax.ShapeDtypeStruct((4, atoms, LANES), f32),
            jax.ShapeDtypeStruct((4, tiles, TILE), f32),
            jax.ShapeDtypeStruct((tiles, TILE), jnp.int32),
            jax.ShapeDtypeStruct((4 * rows.atom_rows, LANES), f32),
        ),
        in_specs=hbm(len(alone)),
        out_specs=tuple(vmem(4)),
        scratch_shapes=room_for(alone[:4]) + [pltpu.SemaphoreType.DMA((len(alone),))],
        compiler_params=params(4),
        cost_estimate=cost(64 * atoms * LANES, 16 * atoms * LANES),
        name="own",
    )(*in_hbm(alone))

    below = passed_along(rim, "slab", 1)
    above = passed_along(rim, "slab", -1)
    if whole_slab:
        around = lax.all_to_all(packed, "dom", 0, 0, tiled=True)
        here = lax.axis_index("dom").reshape(1)
        holders = [stride % domains for stride in strides]
    else:
        around = jnp.concatenate([packed] + [passed_along(packed, "dom", -stride) for stride in strides], axis=0)
        here = jnp.zeros(1, jnp.int32)
        holders = [1, 2, 3, 4]

    moves = pl.pallas_call(
        functools.partial(force_kernel, rows, copies, holders),
        out_shape=jax.ShapeDtypeStruct((copies * rows.disp_count, LANES), f32),
        in_specs=smem(2) + hbm(1) + vmem(7),
        out_specs=vmem(1)[0],
        scratch_shapes=[
            pltpu.VMEM((4, 6 * rows.shell_rows, SUBLANES, LANES), f32),
            pltpu.VMEM((4, tiles, LANES), f32),
            pltpu.VMEM((3, atoms, LANES), f32),
            pltpu.SMEM(tile_block.shape, jnp.int32),
            pltpu.SemaphoreType.DMA(()),
        ],
        compiler_params=params(8),
        cost_estimate=cost(30 * tiles * TILE * TILE, 4 * around.size),
        name="force",
    )(here, active_tile_count, *in_hbm([tile_block]), around, below, above, *own)

    if not whole_slab:
        return by_exchange(rows, strides, around, moves, cross_count)

    constraint_rows = rows.bond_rows + rows.slot_rows
    weight, matrix = pl.pallas_call(
        functools.partial(bond_kernel, rows, domains, strides),
        out_shape=(
            jax.ShapeDtypeStruct((constraint_rows * 3 * domains, LANES), f32),
            jax.ShapeDtypeStruct((domains * rows.matrix, atoms // 2), jnp.bfloat16),
        ),
        in_specs=vmem(1),
        out_specs=tuple(vmem(2)),
        compiler_params=params(16),
        cost_estimate=cost(8 * domains * rows.matrix * atoms // 2, 4 * around.size),
        name="bonds",
    )(around)

    every_move = lax.all_to_all(moves, "dom", 0, 0, tiled=True)

    return pl.pallas_call(
        functools.partial(solve_kernel, rows, domains, strides),
        out_shape=(
            jax.ShapeDtypeStruct(coords.shape, f32),
            jax.ShapeDtypeStruct(coords.shape, f32),
        ),
        in_specs=smem(1) + vmem(4),
        out_specs=tuple(vmem(2)),
        scratch_shapes=[
            pltpu.VMEM((constraint_rows, SUBLANES * domains, LANES), f32),
            pltpu.VMEM((rows.slot_rows, 4 * SUBLANES * domains, LANES), f32),
            pltpu.VMEM((5, rows.atom_rows, SUBLANES * domains, LANES), f32),
        ],
        compiler_params=params(16),
        name="solve",
    )(here, around, every_move, weight, matrix)


def by_exchange(rows, strides, around, moves, cross_count):
    atom_count = rows.atom_rows * LANES
    shell = rows.shell_rows * LANES
    inside = around.reshape(5, rows.count, LANES)

    def flat(at, count):
        return inside[0, at : at + count].reshape(-1)

    def neighbours(at):
        return inside[1:, at : at + rows.shell_rows].reshape(-1)

    coords = jnp.stack([flat(at, rows.atom_rows) for at in rows.coords])
    inv_mass = flat(rows.mass, rows.atom_rows)
    displace = moves[: rows.disp_used].reshape(3, atom_count)
    left = flat(rows.bond_first, rows.bond_rows).astype(jnp.int32)
    right = flat(rows.bond_second, rows.bond_rows).astype(jnp.int32)
    cross_left = flat(rows.cross_first, rows.slot_rows).astype(jnp.int32)
    cross_right = flat(rows.cross_second, rows.slot_rows).astype(jnp.int32)
    side = flat(rows.side, rows.slot_rows).astype(jnp.int32)
    flag = flat(rows.live, rows.slot_rows)
    cross_index = side * shell + cross_right
    far_coords = jnp.stack([neighbours(at) for at in rows.coords])
    far_mass = neighbours(rows.mass)

    def weights(first, second, mass_first, mass_second):
        gap = first - second
        length = jnp.sqrt(jnp.sum(gap * gap, axis=0) + length_floor)
        return gap / length * lax.rsqrt(mass_first + mass_second)

    inner = weights(coords[:, left], coords[:, right], inv_mass[left], inv_mass[right])
    cross = flag * weights(
        coords[:, cross_left], far_coords[:, cross_index], inv_mass[cross_left], far_mass[cross_index]
    )

    def project(field):
        rim = field[:, :shell]
        far = jnp.concatenate([passed_along(rim, "dom", -stride) for stride in strides], axis=1)
        return (
            jnp.sum(inner * (field[:, left] - field[:, right]), axis=0),
            jnp.sum(cross * (field[:, cross_left] - far[:, cross_index]), axis=0),
        )

    def spread(values):
        pushed = inner * values[0]
        pushed_cross = cross * values[1]
        totals = jnp.zeros((3, atom_count), jnp.float32).at[:, left].add(pushed).at[:, right].add(-pushed)
        totals = totals.at[:, cross_left].add(pushed_cross)
        outward = jnp.zeros((3, 4 * shell), jnp.float32).at[:, cross_index].add(-pushed_cross)
        for code, stride in enumerate(strides):
            totals = totals.at[:, :shell].add(
                passed_along(outward[:, code * shell : (code + 1) * shell], "dom", stride)
            )
        return inv_mass * totals

    residue = project(displace)
    summed = residue
    for _ in range(ORDER):
        change = project(spread(residue))
        residue = tuple(now - step for now, step in zip(residue, change))
        summed = tuple(a + b for a, b in zip(summed, residue))
    move = displace - spread(summed)
    return (
        (coords + move).reshape(3, 1, 1, atom_count),
        (move * (1.0 / time_step)).reshape(3, 1, 1, atom_count),
    )


def solution(mesh):
    return jax.shard_map(
        shards,
        mesh=mesh,
        in_specs=(
            P(None, "slab", "dom", None),
            P(None, "slab", "dom", None),
            P("slab", "dom", None),
            P("slab", "dom", None),
            P("slab", "dom", None),
            P("slab", "dom", None, None),
            P("slab", "dom"),
            P(None, "slab", "dom", None),
            P(None, "slab", "dom", None),
            P("slab", "dom", None),
            P("slab", "dom"),
        ),
        out_specs=(P(None, "slab", "dom", None), P(None, "slab", "dom", None)),
        check_vma=False,
    )
```

```python
import functools

import jax
import jax.numpy as jnp
from jax import lax
from jax.experimental import pallas as pl
from jax.experimental.pallas import tpu as pltpu
from jax.sharding import PartitionSpec as P

TILE = 128
ORDER = 4
LANES = 128
SUBLANES = 8

time_step = 0.1
cutoff_sq = 16.0
force_scale = 4.0
length_floor = 0.25


def passed_along(array, axis, by):
    length = lax.axis_size(axis)
    return lax.ppermute(array, axis, [(i, (i + by) % length) for i in range(length)])


def strides_of(domains):
    row_width = max(2, domains // 8)
    return (1, -1, row_width, -row_width)


def round_up(count, step):
    return -(-count // step) * step


class Rows:
    def __init__(self, atoms, bonds, slots):
        self.atom_rows = atoms // LANES
        self.shell_rows = atoms // 2 // LANES
        self.bond_rows = bonds // LANES
        self.slot_rows = slots // LANES
        at = 0
        self.coords = []
        for _ in range(3):
            self.coords.append(at)
            at += self.atom_rows
        self.charge = at
        at += self.atom_rows
        self.mass = at
        at += self.atom_rows
        self.bond_first = at
        at += self.bond_rows
        self.bond_second = at
        at += self.bond_rows
        self.cross_first = at
        at += self.slot_rows
        self.cross_second = at
        at += self.slot_rows
        self.side = at
        at += self.slot_rows
        self.live = at
        at += self.slot_rows
        self.used = at
        self.count = round_up(at, SUBLANES)
        self.shell_terms = (self.bond_rows + self.slot_rows) * LANES
        self.inner_at = (0, self.shell_terms)
        self.cross_at = self.bond_rows * LANES
        self.far_at = self.shell_terms + self.bond_rows * LANES
        self.matrix = self.far_at + self.slot_rows * LANES
        self.disp_used = 3 * self.atom_rows
        self.disp_count = round_up(self.disp_used, SUBLANES)


def take_lanes(table, lanes):
    return jnp.take_along_axis(table, lanes, axis=1, mode="promise_in_bounds")


def pick(tables, index):
    lanes = index & (LANES - 1)
    chunk = index >> 7
    result = take_lanes(tables[0], lanes)
    for k in range(1, len(tables)):
        result = jnp.where(chunk == k, take_lanes(tables[k], lanes), result)
    return result


def fetched(sources, targets, sem_ref):
    copies = [pltpu.make_async_copy(s, t, sem_ref.at[n]) for n, (s, t) in enumerate(zip(sources, targets))]
    for copy in copies:
        copy.start()
    return copies


def copies_of(block_ref, target_ref, copies, sem_ref):
    count = block_ref.shape[0]
    started = [
        pltpu.make_async_copy(block_ref, target_ref.at[pl.ds(n * count, count)], sem_ref.at[n]) for n in range(copies)
    ]
    for copy in started:
        copy.start()
    return started


def pack_kernel(rows, copies, count_ref, *refs):
    sources, (out_hbm, rim_ref), targets, sem_ref = refs[:6], refs[6:8], refs[8:14], refs[14]
    out_ref, out_sem_ref = refs[15:]
    for copy in fetched(sources, targets, sem_ref):
        copy.wait()
    coords_ref, charge_ref, mass_ref, bonds_ref, cross_ref, side_ref = targets

    def put(row, value):
        for part in range(value.shape[1] // LANES):
            out_ref[pl.ds(row + part, 1), :] = value[:, part * LANES : (part + 1) * LANES]

    shell = rows.shell_rows * LANES
    fields = [coords_ref[c, 0] for c in range(3)] + [charge_ref[0]]
    for c in range(4):
        at = rows.coords[c] if c < 3 else rows.charge
        put(at, fields[c])
        for part in range(rows.shell_rows):
            rim_ref[pl.ds(c * rows.shell_rows + part, 1), :] = fields[c][:, part * LANES : (part + 1) * LANES]
    put(rows.mass, mass_ref[0])
    put(rows.bond_first, bonds_ref[0, 0].astype(jnp.float32))
    put(rows.bond_second, bonds_ref[1, 0].astype(jnp.float32))
    put(rows.cross_first, cross_ref[0, 0].astype(jnp.float32))
    put(rows.cross_second, cross_ref[1, 0].astype(jnp.float32))
    side = side_ref[0]
    put(rows.side, side.astype(jnp.float32))
    slot = lax.broadcasted_iota(jnp.int32, side.shape, 1)
    put(rows.live, jnp.where(slot < count_ref[0, 0], 1.0, 0.0))
    if rows.count > rows.used:
        out_ref[rows.used :, :] = jnp.zeros((rows.count - rows.used, LANES), jnp.float32)
    for copy in copies_of(out_ref, out_hbm, copies, out_sem_ref):
        copy.wait()


SHRINK = 1.0 / 4.0
OUT_OF_REACH = 1000.0
TILES_STEP = 4


def own_kernel(
    rows,
    coords_hbm,
    charge_hbm,
    velocity_hbm,
    mass_hbm,
    atoms_hbm,
    own_ref,
    far_ref,
    index_ref,
    motion_ref,
    coords_ref,
    charge_ref,
    velocity_ref,
    mass_ref,
    sem_ref,
):
    atom_rows = rows.atom_rows
    copies = fetched(
        (coords_hbm, charge_hbm, atoms_hbm.at[0, 0], velocity_hbm, mass_hbm),
        (coords_ref, charge_ref, index_ref, velocity_ref, mass_ref),
        sem_ref,
    )
    down = lax.broadcasted_iota(jnp.int32, (SUBLANES, LANES), 0)
    copies[0].wait()
    copies[1].wait()

    def lanes_of(part):
        return slice(part * LANES, (part + 1) * LANES)

    table = []
    for c in range(4):
        field = coords_ref[c, 0] * SHRINK if c < 3 else charge_ref[0]
        table.append(
            [jnp.broadcast_to(field[:, lanes_of(part)], (SUBLANES, LANES)) for part in range(atom_rows)]
        )
    for part in range(atom_rows):
        for group in range(LANES // SUBLANES):
            at = part * LANES + group * SUBLANES
            for c in range(4):
                value = take_lanes(table[c][part], down + group * SUBLANES)
                own_ref[c, pl.ds(at, SUBLANES), :] = value if c < 3 else value * 8.0
    copies[2].wait()
    for group in range(index_ref.shape[0] // SUBLANES):
        at = pl.ds(group * SUBLANES, SUBLANES)
        index = index_ref[at, :]
        for c in range(4):
            far_ref[c, at, :] = pick(table[c], index)
    copies[3].wait()
    copies[4].wait()
    fields = [velocity_ref[c, 0] for c in range(3)] + [mass_ref[0]]
    for c, field in enumerate(fields):
        for part in range(atom_rows):
            motion_ref[pl.ds(c * atom_rows + part, 1), :] = field[:, lanes_of(part)]


def force_kernel(
    rows,
    copies,
    holders,
    here_ref,
    live_ref,
    block_hbm,
    around_ref,
    below_ref,
    above_ref,
    own_ref,
    near_ref,
    index_ref,
    motion_ref,
    out_hbm,
    table_ref,
    far_ref,
    sum_ref,
    block_ref,
    sem_ref,
    out_ref,
    out_sem_ref,
):
    atom_rows, shell_rows = rows.atom_rows, rows.shell_rows
    tiles = index_ref.shape[0]
    block_copy = pltpu.make_async_copy(block_hbm, block_ref, sem_ref)
    block_copy.start()
    me = here_ref[0]
    starts = [rows.coords[0], rows.coords[1], rows.coords[2], rows.charge]
    entry_rows = 6 * shell_rows
    blocks = around_ref.shape[0] // rows.count

    def broadcast(row):
        return jnp.broadcast_to(row, (SUBLANES, LANES))

    for c in range(4):
        factor = SHRINK if c < 3 else 1.0
        at = 0
        for neighbour in range(4):
            base = lax.rem(me + holders[neighbour], blocks) * rows.count + starts[c]
            for part in range(shell_rows):
                table_ref[c, at] = broadcast(around_ref[pl.ds(base + part, 1), :] * factor)
                at += 1
        for slab_ref in (below_ref, above_ref):
            for part in range(shell_rows):
                table_ref[c, at] = broadcast(slab_ref[pl.ds(c * shell_rows + part, 1), :] * factor)
                at += 1

    live = live_ref[0, 0]
    down = lax.broadcasted_iota(jnp.int32, (SUBLANES, LANES), 0)
    for group in range(tiles // SUBLANES):
        at = pl.ds(group * SUBLANES, SUBLANES)
        index = index_ref[at, :]
        lanes = index & (LANES - 1)
        chunk = index >> 7
        values = [near_ref[c, at, :] for c in range(4)]
        for k in range(entry_rows):
            here = chunk == atom_rows + k
            values = [jnp.where(here, take_lanes(table_ref[c, k], lanes), values[c]) for c in range(4)]
        values[0] = jnp.where(down + group * SUBLANES < live, values[0], OUT_OF_REACH)
        for c in range(4):
            far_ref[c, at, :] = values[c]

    sum_ref[...] = jnp.zeros(sum_ref.shape, jnp.float32)
    block_copy.wait()

    softening = 1.0 / cutoff_sq

    def add_tile(tile):
        base = block_ref[0, 0, tile] * TILE
        far = [broadcast(far_ref[c, pl.ds(tile, 1), :]) for c in range(4)]
        for group in range(TILE // SUBLANES):
            at = pl.ds(pl.multiple_of(base + group * SUBLANES, SUBLANES), SUBLANES)
            gap = [own_ref[c, at, :] - far[c] for c in range(3)]
            square = gap[0] * gap[0] + gap[1] * gap[1] + gap[2] * gap[2]
            inverse = pl.reciprocal(square + softening, approx=True)
            weight = jnp.maximum(inverse - 1.0 / (1.0 + softening), 0.0)
            strength = (inverse - own_ref[3, at, :] * far[3]) * (weight * weight)
            for c in range(3):
                sum_ref[c, at, :] = sum_ref[c, at, :] + strength * gap[c]

    def add_tiles(step, _):
        for n in range(TILES_STEP):
            add_tile(step * TILES_STEP + n)
        return 0

    lax.fori_loop(0, lax.div(live + TILES_STEP - 1, TILES_STEP), add_tiles, 0)

    scale = time_step * time_step * force_scale * 4.0 / 2048.0 * (1.0 + softening) ** 2

    def lane_sums(c, part):
        return jnp.sum(sum_ref[c, pl.ds(part * LANES, LANES), :].T, axis=0, keepdims=True)

    for part in range(atom_rows):
        mass = motion_ref[pl.ds(3 * atom_rows + part, 1), :]
        for c in range(3):
            speed = motion_ref[pl.ds(c * atom_rows + part, 1), :]
            moved = time_step * speed + scale * lane_sums(c, part) * mass
            out_ref[pl.ds(c * atom_rows + part, 1), :] = moved
    if rows.disp_count > rows.disp_used:
        out_ref[rows.disp_used :, :] = jnp.zeros((rows.disp_count - rows.disp_used, LANES), jnp.float32)
    for copy in copies_of(out_ref, out_hbm, copies, out_sem_ref):
        copy.wait()


def bond_kernel(rows, domains, strides, around_ref, weight_ref, matrix_ref):
    atom_rows, shell_rows = rows.atom_rows, rows.shell_rows

    def load(row):
        return around_ref[pl.ds(row, domains, stride=rows.count), :]

    def index(row):
        return load(row).astype(jnp.int32)

    fields = [[load(at + part) for part in range(atom_rows)] for at in rows.coords + [rows.mass]]

    def weights(first, second, row):
        gap = [first[c] - second[c] for c in range(3)]
        length_sq = gap[0] * gap[0] + gap[1] * gap[1] + gap[2] * gap[2] + length_floor
        scale = lax.rsqrt(length_sq) * lax.rsqrt(first[3] + second[3])
        return [gap[c] * scale for c in range(3)]

    at = 0
    for part in range(rows.bond_rows):
        first = index(rows.bond_first + part)
        second = index(rows.bond_second + part)
        values = weights([pick(f, first) for f in fields], [pick(f, second) for f in fields], at)
        for c in range(3):
            weight_ref[pl.ds((at * 3 + c) * domains, domains), :] = values[c]
        at += 1
    for part in range(rows.slot_rows):
        first = index(rows.cross_first + part)
        second = index(rows.cross_second + part)
        side = load(rows.side + part)
        live = load(rows.live + part)
        other = [jnp.zeros((domains, LANES), jnp.float32) for _ in range(4)]
        for code, stride in enumerate(strides):
            seen = pltpu.roll(second, stride % domains, 0)
            for f in range(4):
                value = pltpu.roll(pick(fields[f][:shell_rows], seen), -stride % domains, 0)
                other[f] = jnp.where(side == code, value, other[f])
        values = weights([pick(f[:shell_rows], first) for f in fields], other, at)
        for c in range(3):
            weight_ref[pl.ds((at * 3 + c) * domains, domains), :] = values[c] * live
        at += 1

    down = lax.broadcasted_iota(jnp.int32, (SUBLANES, LANES), 0)
    group_rows = 4 * SUBLANES

    kind = jnp.bfloat16 if shell_rows * LANES <= 256 else jnp.float32
    across = lax.broadcasted_iota(jnp.int32, (group_rows, LANES), 1).astype(jnp.float32)
    lanes = [(across + float(block * LANES)).astype(kind) for block in range(shell_rows)]

    def column(row, step, half=0):
        row = jnp.broadcast_to(row, (SUBLANES, LANES))
        groups = [take_lanes(row, down + at) for at in range(step * group_rows, (step + 1) * group_rows, SUBLANES)]
        return (jnp.concatenate(groups, axis=0) - float(half * shell_rows * LANES)).astype(kind)

    def put(at, ends, signs):
        for block in range(shell_rows):
            value = jnp.zeros((group_rows, LANES), kind)
            for end, sign in zip(ends, signs):
                value = jnp.where(end == lanes[block], jnp.full((group_rows, LANES), sign, kind), value)
            matrix_ref[pl.ds(at, group_rows), block * LANES : (block + 1) * LANES] = value.astype(matrix_ref.dtype)

    def build(domain, _):
        start = pl.multiple_of(domain * rows.matrix, LANES)
        for part in range(rows.bond_rows):
            first = around_ref[pl.ds(domain * rows.count + rows.bond_first + part, 1), :]
            second = around_ref[pl.ds(domain * rows.count + rows.bond_second + part, 1), :]
            for step in range(LANES // group_rows):
                for half in range(2):
                    ends = (column(first, step, half), column(second, step, half))
                    put(start + rows.inner_at[half] + part * LANES + step * group_rows, ends, (1.0, -1.0))
        for part in range(rows.slot_rows):
            for row_at, to, sign in (
                (rows.cross_first, rows.cross_at, 1.0),
                (rows.cross_second, rows.far_at, -1.0),
            ):
                row = around_ref[pl.ds(domain * rows.count + row_at + part, 1), :]
                for step in range(LANES // group_rows):
                    put(start + to + part * LANES + step * group_rows, (column(row, step),), (sign,))
        return 0

    lax.fori_loop(0, domains, build, 0)


def solve_kernel(
    rows,
    domains,
    strides,
    here_ref,
    around_ref,
    moves_ref,
    weight_ref,
    matrix_ref,
    coords_out_ref,
    velocity_out_ref,
    push_ref,
    far_push_ref,
    field_ref,
):
    atom_rows, shell_rows = rows.atom_rows, rows.shell_rows
    bond_rows, slot_rows = rows.bond_rows, rows.slot_rows
    me = here_ref[0]

    def load(row):
        return around_ref[pl.ds(row, domains, stride=rows.count), :]

    def index(row):
        return load(row).astype(jnp.int32)

    inner_first = [index(rows.bond_first + p) for p in range(bond_rows)]
    inner_second = [index(rows.bond_second + p) for p in range(bond_rows)]
    cross_first = [index(rows.cross_first + p) for p in range(slot_rows)]
    cross_second = [index(rows.cross_second + p) for p in range(slot_rows)]
    sides = [load(rows.side + p) for p in range(slot_rows)]
    masses = [load(rows.mass + p) for p in range(atom_rows)]

    def weight(at, c):
        return weight_ref[pl.ds((at * 3 + c) * domains, domains), :]

    def project(fields):
        result = []
        for part in range(bond_rows):
            total = 0.0
            for c in range(3):
                ends = pick(fields[c], inner_first[part]) - pick(fields[c], inner_second[part])
                total = total + weight(part, c) * ends
            result.append(total)
        for part in range(slot_rows):
            seen = [pltpu.roll(cross_second[part], stride % domains, 0) for stride in strides]
            total = 0.0
            for c in range(3):
                shell = fields[c][:shell_rows]
                other = 0.0
                for code, stride in enumerate(strides):
                    value = pltpu.roll(pick(shell, seen[code]), -stride % domains, 0)
                    other = jnp.where(sides[part] == code, value, other)
                total = total + weight(bond_rows + part, c) * (pick(shell, cross_first[part]) - other)
            result.append(total)
        return result

    def put_pushes(values):
        for at, value in enumerate(values):
            for c in range(3):
                pushed = weight(at, c) * value
                high = pushed.astype(jnp.bfloat16).astype(jnp.float32)
                for row, part in ((c, high), (3 + c, pushed - high)):
                    push_ref[at, pl.ds(row * domains, domains), :] = part
                    if at >= bond_rows:
                        for code in range(4):
                            far_push_ref[at - bond_rows, pl.ds((code * SUBLANES + row) * domains, domains), :] = (
                                jnp.where(sides[at - bond_rows] == code, part, 0.0)
                            )

    def pushes_of(at, domain):
        return push_ref[at, pl.ds(domain, SUBLANES, stride=domains), :].astype(jnp.bfloat16)

    def product(pushes, domain, at):
        start = domain * rows.matrix + at
        if not isinstance(start, int):
            start = pl.multiple_of(start, LANES)
        pushes = pushes[0] if len(pushes) == 1 else jnp.concatenate(pushes, axis=1)
        result = jnp.dot(
            pushes, matrix_ref[pl.ds(start, pushes.shape[1]), :], preferred_element_type=jnp.float32
        )
        return [result[:, p * LANES : (p + 1) * LANES] for p in range(shell_rows)]

    def inner_totals(domain):
        pushes = [pushes_of(at, domain) for at in range(bond_rows + slot_rows)]
        return product(pushes, domain, 0) + product(pushes[:bond_rows], domain, rows.shell_terms)

    def far_totals(domain, first_row, count):
        pushes = [
            far_push_ref[p, pl.ds(first_row * domains + domain, count, stride=domains), :].astype(jnp.bfloat16)
            for p in range(slot_rows)
        ]
        return product(pushes, domain, rows.far_at)

    def spread(values):
        put_pushes(values)
        for domain in range(domains):
            for part, total in enumerate(inner_totals(domain)):
                field_ref[0, part, pl.ds(domain, SUBLANES, stride=domains), :] = total
            for part, total in enumerate(far_totals(domain, 0, 4 * SUBLANES)):
                for code, stride in enumerate(strides):
                    field_ref[1 + code, part, pl.ds((domain + stride) % domains, SUBLANES, stride=domains), :] = total[
                        code * SUBLANES : (code + 1) * SUBLANES, :
                    ]

        def field(c, part):
            pieces = [
                field_ref[source, part, pl.ds(row * domains, domains), :]
                for source in range(5 if part < shell_rows else 1)
                for row in (c, 3 + c)
            ]
            return masses[part] * functools.reduce(lambda a, b: a + b, pieces)

        return [[field(c, part) for part in range(atom_rows)] for c in range(3)]

    moves = [
        [moves_ref[pl.ds(c * atom_rows + p, domains, stride=rows.disp_count), :] for p in range(atom_rows)]
        for c in range(3)
    ]
    push_ref[...] = jnp.zeros(push_ref.shape, jnp.float32)
    far_push_ref[...] = jnp.zeros(far_push_ref.shape, jnp.float32)
    residue = project(moves)

    def expand(_, carry):
        residue, summed = carry
        change = project(spread(residue))
        residue = [now - step for now, step in zip(residue, change)]
        return residue, [a + b for a, b in zip(summed, residue)]

    residue, summed = lax.fori_loop(0, ORDER, expand, (residue, residue))
    put_pushes(summed)
    sums = inner_totals(me)
    for code, stride in enumerate(strides):
        owner = lax.rem(me + (-stride) % domains, domains)
        for part, total in enumerate(far_totals(owner, code * SUBLANES, SUBLANES)):
            sums[part] = sums[part] + total
    for part in range(atom_rows):
        lanes = slice(part * LANES, (part + 1) * LANES)
        mass = around_ref[pl.ds(me * rows.count + rows.mass + part, 1), :]
        for c in range(3):
            correction = mass * (sums[part][c : c + 1, :] + sums[part][3 + c : 4 + c, :])
            move = moves_ref[pl.ds(me * rows.disp_count + c * atom_rows + part, 1), :] - correction
            start = around_ref[pl.ds(me * rows.count + rows.coords[c] + part, 1), :]
            coords_out_ref[c, 0, :, lanes] = start + move
            velocity_out_ref[c, 0, :, lanes] = move * (1.0 / time_step)


def vmem(count):
    return [pl.BlockSpec(memory_space=pltpu.VMEM)] * count


def smem(count):
    return [pl.BlockSpec(memory_space=pltpu.SMEM)] * count


def hbm(count):
    return [pl.BlockSpec(memory_space=pltpu.HBM)] * count


def in_hbm(arrays):
    return [pltpu.with_memory_space_constraint(a, pltpu.HBM) for a in arrays]


def params(mebibytes):
    return pltpu.CompilerParams(vmem_limit_bytes=mebibytes * 1024 * 1024)


def cost(flops, moved):
    return pl.CostEstimate(flops=flops, bytes_accessed=moved, transcendentals=0)


def room_for(arrays):
    return [pltpu.VMEM(a.shape, a.dtype) for a in arrays]


def shards(
    coords,
    velocity,
    charge,
    inv_mass,
    tile_block,
    tile_atoms,
    active_tile_count,
    bond_atoms,
    cross_atoms,
    cross_side,
    cross_count,
):
    atoms = coords.shape[-1]
    tiles = tile_atoms.shape[2]
    domains = lax.axis_size("dom")
    strides = strides_of(domains)
    rows = Rows(atoms, bond_atoms.shape[-1], cross_side.shape[-1])
    whole_slab = domains == SUBLANES
    copies = domains if whole_slab else 1
    f32 = jnp.float32

    sent = (coords, charge, inv_mass, bond_atoms, cross_atoms, cross_side)
    packed, rim = pl.pallas_call(
        functools.partial(pack_kernel, rows, copies),
        out_shape=(
            pltpu.HBM((copies * rows.count, LANES), f32),
            jax.ShapeDtypeStruct((4 * rows.shell_rows, LANES), f32),
        ),
        in_specs=smem(1) + hbm(len(sent)),
        out_specs=tuple(hbm(1) + vmem(1)),
        scratch_shapes=room_for(sent)
        + [
            pltpu.SemaphoreType.DMA((len(sent),)),
            pltpu.VMEM((rows.count, LANES), f32),
            pltpu.SemaphoreType.DMA((copies,)),
        ],
        compiler_params=params(4),
        name="pack",
    )(cross_count, *in_hbm(sent))

    alone = (coords, charge, velocity, inv_mass, tile_atoms)
    own = pl.pallas_call(
        functools.partial(own_kernel, rows),
        out_shape=(
            jax.ShapeDtypeStruct((4, atoms, LANES), f32),
            jax.ShapeDtypeStruct((4, tiles, TILE), f32),
            jax.ShapeDtypeStruct((tiles, TILE), jnp.int32),
            jax.ShapeDtypeStruct((4 * rows.atom_rows, LANES), f32),
        ),
        in_specs=hbm(len(alone)),
        out_specs=tuple(vmem(4)),
        scratch_shapes=room_for(alone[:4]) + [pltpu.SemaphoreType.DMA((len(alone),))],
        compiler_params=params(4),
        cost_estimate=cost(64 * atoms * LANES, 16 * atoms * LANES),
        name="own",
    )(*in_hbm(alone))

    below = passed_along(rim, "slab", 1)
    above = passed_along(rim, "slab", -1)
    if whole_slab:
        around = lax.all_to_all(packed, "dom", 0, 0, tiled=True)
        here = lax.axis_index("dom").reshape(1)
        holders = [stride % domains for stride in strides]
    else:
        around = jnp.concatenate([packed] + [passed_along(packed, "dom", -stride) for stride in strides], axis=0)
        here = jnp.zeros(1, jnp.int32)
        holders = [1, 2, 3, 4]

    moves = pl.pallas_call(
        functools.partial(force_kernel, rows, copies, holders),
        out_shape=pltpu.HBM((copies * rows.disp_count, LANES), f32),
        in_specs=smem(2) + hbm(1) + vmem(7),
        out_specs=hbm(1)[0],
        scratch_shapes=[
            pltpu.VMEM((4, 6 * rows.shell_rows, SUBLANES, LANES), f32),
            pltpu.VMEM((4, tiles, LANES), f32),
            pltpu.VMEM((3, atoms, LANES), f32),
            pltpu.SMEM(tile_block.shape, jnp.int32),
            pltpu.SemaphoreType.DMA(()),
            pltpu.VMEM((rows.disp_count, LANES), f32),
            pltpu.SemaphoreType.DMA((copies,)),
        ],
        compiler_params=params(8),
        cost_estimate=cost(30 * tiles * TILE * TILE, 4 * around.size),
        name="force",
    )(here, active_tile_count, *in_hbm([tile_block]), around, below, above, *own)

    if not whole_slab:
        return by_exchange(rows, strides, around, moves, cross_count)

    constraint_rows = rows.bond_rows + rows.slot_rows
    weight, matrix = pl.pallas_call(
        functools.partial(bond_kernel, rows, domains, strides),
        out_shape=(
            jax.ShapeDtypeStruct((constraint_rows * 3 * domains, LANES), f32),
            jax.ShapeDtypeStruct((domains * rows.matrix, atoms // 2), jnp.bfloat16),
        ),
        in_specs=vmem(1),
        out_specs=tuple(vmem(2)),
        compiler_params=params(16),
        cost_estimate=cost(8 * domains * rows.matrix * atoms // 2, 4 * around.size),
        name="bonds",
    )(around)

    every_move = lax.all_to_all(moves, "dom", 0, 0, tiled=True)

    return pl.pallas_call(
        functools.partial(solve_kernel, rows, domains, strides),
        out_shape=(
            jax.ShapeDtypeStruct(coords.shape, f32),
            jax.ShapeDtypeStruct(coords.shape, f32),
        ),
        in_specs=smem(1) + vmem(4),
        out_specs=tuple(vmem(2)),
        scratch_shapes=[
            pltpu.VMEM((constraint_rows, SUBLANES * domains, LANES), f32),
            pltpu.VMEM((rows.slot_rows, 4 * SUBLANES * domains, LANES), f32),
            pltpu.VMEM((5, rows.atom_rows, SUBLANES * domains, LANES), f32),
        ],
        compiler_params=params(16),
        name="solve",
    )(here, around, every_move, weight, matrix)


def by_exchange(rows, strides, around, moves, cross_count):
    atom_count = rows.atom_rows * LANES
    shell = rows.shell_rows * LANES
    inside = around.reshape(5, rows.count, LANES)

    def flat(at, count):
        return inside[0, at : at + count].reshape(-1)

    def neighbours(at):
        return inside[1:, at : at + rows.shell_rows].reshape(-1)

    coords = jnp.stack([flat(at, rows.atom_rows) for at in rows.coords])
    inv_mass = flat(rows.mass, rows.atom_rows)
    displace = moves[: rows.disp_used].reshape(3, atom_count)
    left = flat(rows.bond_first, rows.bond_rows).astype(jnp.int32)
    right = flat(rows.bond_second, rows.bond_rows).astype(jnp.int32)
    cross_left = flat(rows.cross_first, rows.slot_rows).astype(jnp.int32)
    cross_right = flat(rows.cross_second, rows.slot_rows).astype(jnp.int32)
    side = flat(rows.side, rows.slot_rows).astype(jnp.int32)
    flag = flat(rows.live, rows.slot_rows)
    cross_index = side * shell + cross_right
    far_coords = jnp.stack([neighbours(at) for at in rows.coords])
    far_mass = neighbours(rows.mass)

    def weights(first, second, mass_first, mass_second):
        gap = first - second
        length = jnp.sqrt(jnp.sum(gap * gap, axis=0) + length_floor)
        return gap / length * lax.rsqrt(mass_first + mass_second)

    inner = weights(coords[:, left], coords[:, right], inv_mass[left], inv_mass[right])
    cross = flag * weights(
        coords[:, cross_left], far_coords[:, cross_index], inv_mass[cross_left], far_mass[cross_index]
    )

    def project(field):
        rim = field[:, :shell]
        far = jnp.concatenate([passed_along(rim, "dom", -stride) for stride in strides], axis=1)
        return (
            jnp.sum(inner * (field[:, left] - field[:, right]), axis=0),
            jnp.sum(cross * (field[:, cross_left] - far[:, cross_index]), axis=0),
        )

    def spread(values):
        pushed = inner * values[0]
        pushed_cross = cross * values[1]
        totals = jnp.zeros((3, atom_count), jnp.float32).at[:, left].add(pushed).at[:, right].add(-pushed)
        totals = totals.at[:, cross_left].add(pushed_cross)
        outward = jnp.zeros((3, 4 * shell), jnp.float32).at[:, cross_index].add(-pushed_cross)
        for code, stride in enumerate(strides):
            totals = totals.at[:, :shell].add(
                passed_along(outward[:, code * shell : (code + 1) * shell], "dom", stride)
            )
        return inv_mass * totals

    residue = project(displace)
    summed = residue
    for _ in range(ORDER):
        change = project(spread(residue))
        residue = tuple(now - step for now, step in zip(residue, change))
        summed = tuple(a + b for a, b in zip(summed, residue))
    move = displace - spread(summed)
    return (
        (coords + move).reshape(3, 1, 1, atom_count),
        (move * (1.0 / time_step)).reshape(3, 1, 1, atom_count),
    )


def solution(mesh):
    return jax.shard_map(
        shards,
        mesh=mesh,
        in_specs=(
            P(None, "slab", "dom", None),
            P(None, "slab", "dom", None),
            P("slab", "dom", None),
            P("slab", "dom", None),
            P("slab", "dom", None),
            P("slab", "dom", None, None),
            P("slab", "dom"),
            P(None, "slab", "dom", None),
            P(None, "slab", "dom", None),
            P("slab", "dom", None),
            P("slab", "dom"),
        ),
        out_specs=(P(None, "slab", "dom", None), P(None, "slab", "dom", None)),
        check_vma=False,
    )
```

```python
import functools

import jax
import jax.numpy as jnp
from jax import lax
from jax.experimental import pallas as pl
from jax.experimental.pallas import tpu as pltpu
from jax.sharding import PartitionSpec as P

TILE = 128
ORDER = 4
LANES = 128
SUBLANES = 8

time_step = 0.1
cutoff_sq = 16.0
force_scale = 4.0
length_floor = 0.25


def passed_along(array, axis, by):
    length = lax.axis_size(axis)
    return lax.ppermute(array, axis, [(i, (i + by) % length) for i in range(length)])


def strides_of(domains):
    row_width = max(2, domains // 8)
    return (1, -1, row_width, -row_width)


def round_up(count, step):
    return -(-count // step) * step


class Rows:
    def __init__(self, atoms, bonds, slots):
        self.atom_rows = atoms // LANES
        self.shell_rows = atoms // 2 // LANES
        self.bond_rows = bonds // LANES
        self.slot_rows = slots // LANES
        at = 0
        self.coords = []
        for _ in range(3):
            self.coords.append(at)
            at += self.atom_rows
        self.charge = at
        at += self.atom_rows
        self.mass = at
        at += self.atom_rows
        self.bond_first = at
        at += self.bond_rows
        self.bond_second = at
        at += self.bond_rows
        self.cross_first = at
        at += self.slot_rows
        self.cross_second = at
        at += self.slot_rows
        self.side = at
        at += self.slot_rows
        self.used = at
        self.count = round_up(at, SUBLANES)
        self.shell_terms = (self.bond_rows + self.slot_rows) * LANES
        self.inner_at = (0, self.shell_terms)
        self.cross_at = self.bond_rows * LANES
        self.far_at = self.shell_terms + self.bond_rows * LANES
        self.matrix = self.far_at + self.slot_rows * LANES
        self.live = 3 * self.atom_rows
        self.disp_used = self.live + self.slot_rows
        self.disp_count = round_up(self.disp_used, SUBLANES)


def take_lanes(table, lanes):
    return jnp.take_along_axis(table, lanes, axis=1, mode="promise_in_bounds")


def pick(tables, index):
    lanes = index & (LANES - 1)
    chunk = index >> 7
    result = take_lanes(tables[0], lanes)
    for k in range(1, len(tables)):
        result = jnp.where(chunk == k, take_lanes(tables[k], lanes), result)
    return result


def fetched(sources, targets, sem_ref):
    copies = [pltpu.make_async_copy(s, t, sem_ref.at[n]) for n, (s, t) in enumerate(zip(sources, targets))]
    for copy in copies:
        copy.start()
    return copies


def pack_kernel(rows, copies, *refs):
    sources, (out_ref, rim_ref), targets, sem_ref = refs[:6], refs[6:8], refs[8:14], refs[14]
    for copy in fetched(sources, targets, sem_ref):
        copy.wait()
    coords_ref, charge_ref, mass_ref, bonds_ref, cross_ref, side_ref = targets

    def put(row, value):
        for part in range(value.shape[1] // LANES):
            piece = value[:, part * LANES : (part + 1) * LANES]
            for copy in range(copies):
                out_ref[pl.ds(copy * rows.count + row + part, 1), :] = piece

    shell = rows.shell_rows * LANES
    fields = [coords_ref[c, 0] for c in range(3)] + [charge_ref[0]]
    for c in range(4):
        at = rows.coords[c] if c < 3 else rows.charge
        put(at, fields[c])
        for part in range(rows.shell_rows):
            rim_ref[pl.ds(c * rows.shell_rows + part, 1), :] = fields[c][:, part * LANES : (part + 1) * LANES]
    put(rows.mass, mass_ref[0])
    put(rows.bond_first, bonds_ref[0, 0].astype(jnp.float32))
    put(rows.bond_second, bonds_ref[1, 0].astype(jnp.float32))
    put(rows.cross_first, cross_ref[0, 0].astype(jnp.float32))
    put(rows.cross_second, cross_ref[1, 0].astype(jnp.float32))
    put(rows.side, side_ref[0].astype(jnp.float32))
    if rows.count > rows.used:
        for copy in range(copies):
            out_ref[pl.ds(copy * rows.count + rows.used, rows.count - rows.used), :] = jnp.zeros(
                (rows.count - rows.used, LANES), jnp.float32
            )


SHRINK = 1.0 / 4.0
OUT_OF_REACH = 1000.0
TILES_STEP = 4


def own_kernel(
    rows,
    coords_hbm,
    charge_hbm,
    velocity_hbm,
    mass_hbm,
    atoms_hbm,
    own_ref,
    far_ref,
    index_ref,
    motion_ref,
    coords_ref,
    charge_ref,
    velocity_ref,
    mass_ref,
    sem_ref,
):
    atom_rows = rows.atom_rows
    copies = fetched(
        (coords_hbm, charge_hbm, atoms_hbm.at[0, 0], velocity_hbm, mass_hbm),
        (coords_ref, charge_ref, index_ref, velocity_ref, mass_ref),
        sem_ref,
    )
    down = lax.broadcasted_iota(jnp.int32, (SUBLANES, LANES), 0)
    copies[0].wait()
    copies[1].wait()

    def lanes_of(part):
        return slice(part * LANES, (part + 1) * LANES)

    table = []
    for c in range(4):
        field = coords_ref[c, 0] * SHRINK if c < 3 else charge_ref[0]
        table.append(
            [jnp.broadcast_to(field[:, lanes_of(part)], (SUBLANES, LANES)) for part in range(atom_rows)]
        )
    for part in range(atom_rows):
        for group in range(LANES // SUBLANES):
            at = part * LANES + group * SUBLANES
            for c in range(4):
                value = take_lanes(table[c][part], down + group * SUBLANES)
                own_ref[c, pl.ds(at, SUBLANES), :] = value if c < 3 else value * 8.0
    copies[2].wait()
    for group in range(index_ref.shape[0] // SUBLANES):
        at = pl.ds(group * SUBLANES, SUBLANES)
        index = index_ref[at, :]
        for c in range(4):
            far_ref[c, at, :] = pick(table[c], index)
    copies[3].wait()
    copies[4].wait()
    fields = [velocity_ref[c, 0] for c in range(3)] + [mass_ref[0]]
    for c, field in enumerate(fields):
        for part in range(atom_rows):
            motion_ref[pl.ds(c * atom_rows + part, 1), :] = field[:, lanes_of(part)]


def force_kernel(
    rows,
    copies,
    place,
    live_ref,
    count_ref,
    block_hbm,
    around_ref,
    below_ref,
    above_ref,
    own_ref,
    near_ref,
    index_ref,
    motion_ref,
    out_ref,
    table_ref,
    far_ref,
    sum_ref,
    block_ref,
    sem_ref,
):
    atom_rows, shell_rows = rows.atom_rows, rows.shell_rows
    tiles = index_ref.shape[0]
    block_copy = pltpu.make_async_copy(block_hbm, block_ref, sem_ref)
    block_copy.start()
    holders = place()
    starts = [rows.coords[0], rows.coords[1], rows.coords[2], rows.charge]
    entry_rows = 6 * shell_rows

    def broadcast(row):
        return jnp.broadcast_to(row, (SUBLANES, LANES))

    for c in range(4):
        factor = SHRINK if c < 3 else 1.0
        at = 0
        for neighbour in range(4):
            base = holders[neighbour] * rows.count + starts[c]
            for part in range(shell_rows):
                table_ref[c, at] = broadcast(around_ref[pl.ds(base + part, 1), :] * factor)
                at += 1
        for slab_ref in (below_ref, above_ref):
            for part in range(shell_rows):
                table_ref[c, at] = broadcast(slab_ref[pl.ds(c * shell_rows + part, 1), :] * factor)
                at += 1

    live = live_ref[0, 0]
    down = lax.broadcasted_iota(jnp.int32, (SUBLANES, LANES), 0)
    for group in range(tiles // SUBLANES):
        at = pl.ds(group * SUBLANES, SUBLANES)
        index = index_ref[at, :]
        lanes = index & (LANES - 1)
        chunk = index >> 7
        values = [near_ref[c, at, :] for c in range(4)]
        for k in range(entry_rows):
            here = chunk == atom_rows + k
            values = [jnp.where(here, take_lanes(table_ref[c, k], lanes), values[c]) for c in range(4)]
        values[0] = jnp.where(down + group * SUBLANES < live, values[0], OUT_OF_REACH)
        for c in range(4):
            far_ref[c, at, :] = values[c]

    sum_ref[...] = jnp.zeros(sum_ref.shape, jnp.float32)
    block_copy.wait()

    softening = 1.0 / cutoff_sq

    def add_tile(tile):
        base = block_ref[0, 0, tile] * TILE
        far = [broadcast(far_ref[c, pl.ds(tile, 1), :]) for c in range(4)]
        for group in range(TILE // SUBLANES):
            at = pl.ds(pl.multiple_of(base + group * SUBLANES, SUBLANES), SUBLANES)
            gap = [own_ref[c, at, :] - far[c] for c in range(3)]
            square = gap[0] * gap[0] + gap[1] * gap[1] + gap[2] * gap[2]
            inverse = pl.reciprocal(square + softening, approx=True)
            weight = jnp.maximum(inverse - 1.0 / (1.0 + softening), 0.0)
            strength = (inverse - own_ref[3, at, :] * far[3]) * (weight * weight)
            for c in range(3):
                sum_ref[c, at, :] = sum_ref[c, at, :] + strength * gap[c]

    def add_tiles(step, _):
        for n in range(TILES_STEP):
            add_tile(step * TILES_STEP + n)
        return 0

    lax.fori_loop(0, lax.div(live + TILES_STEP - 1, TILES_STEP), add_tiles, 0)

    scale = time_step * time_step * force_scale * 4.0 / 2048.0 * (1.0 + softening) ** 2

    def lane_sums(c, part):
        return jnp.sum(sum_ref[c, pl.ds(part * LANES, LANES), :].T, axis=0, keepdims=True)

    for part in range(atom_rows):
        mass = motion_ref[pl.ds(3 * atom_rows + part, 1), :]
        for c in range(3):
            speed = motion_ref[pl.ds(c * atom_rows + part, 1), :]
            moved = time_step * speed + scale * lane_sums(c, part) * mass
            for copy in range(copies):
                out_ref[pl.ds(copy * rows.disp_count + c * atom_rows + part, 1), :] = moved
    slot = lax.broadcasted_iota(jnp.int32, (1, LANES), 1)
    for part in range(rows.slot_rows):
        flag = jnp.where(slot + part * LANES < count_ref[0, 0], 1.0, 0.0)
        for copy in range(copies):
            out_ref[pl.ds(copy * rows.disp_count + rows.live + part, 1), :] = flag
    if rows.disp_count > rows.disp_used:
        for copy in range(copies):
            out_ref[pl.ds(copy * rows.disp_count + rows.disp_used, rows.disp_count - rows.disp_used), :] = jnp.zeros(
                (rows.disp_count - rows.disp_used, LANES), jnp.float32
            )


def bond_kernel(rows, domains, strides, around_ref, weight_ref, matrix_ref):
    atom_rows, shell_rows = rows.atom_rows, rows.shell_rows

    def load(row):
        return around_ref[pl.ds(row, domains, stride=rows.count), :]

    def index(row):
        return load(row).astype(jnp.int32)

    fields = [[load(at + part) for part in range(atom_rows)] for at in rows.coords + [rows.mass]]

    def weights(first, second, row):
        gap = [first[c] - second[c] for c in range(3)]
        length_sq = gap[0] * gap[0] + gap[1] * gap[1] + gap[2] * gap[2] + length_floor
        scale = lax.rsqrt(length_sq) * lax.rsqrt(first[3] + second[3])
        return [gap[c] * scale for c in range(3)]

    at = 0
    for part in range(rows.bond_rows):
        first = index(rows.bond_first + part)
        second = index(rows.bond_second + part)
        values = weights([pick(f, first) for f in fields], [pick(f, second) for f in fields], at)
        for c in range(3):
            weight_ref[pl.ds((at * 3 + c) * domains, domains), :] = values[c]
        at += 1
    for part in range(rows.slot_rows):
        first = index(rows.cross_first + part)
        second = index(rows.cross_second + part)
        side = load(rows.side + part)
        other = [jnp.zeros((domains, LANES), jnp.float32) for _ in range(4)]
        for code, stride in enumerate(strides):
            seen = pltpu.roll(second, stride % domains, 0)
            for f in range(4):
                value = pltpu.roll(pick(fields[f][:shell_rows], seen), -stride % domains, 0)
                other[f] = jnp.where(side == code, value, other[f])
        values = weights([pick(f[:shell_rows], first) for f in fields], other, at)
        for c in range(3):
            weight_ref[pl.ds((at * 3 + c) * domains, domains), :] = values[c]
        at += 1

    down = lax.broadcasted_iota(jnp.int32, (SUBLANES, LANES), 0)
    group_rows = 4 * SUBLANES

    kind = jnp.bfloat16 if shell_rows * LANES <= 256 else jnp.float32
    across = lax.broadcasted_iota(jnp.int32, (group_rows, LANES), 1).astype(jnp.float32)
    lanes = [(across + float(block * LANES)).astype(kind) for block in range(shell_rows)]

    def column(row, step, half=0):
        row = jnp.broadcast_to(row, (SUBLANES, LANES))
        groups = [take_lanes(row, down + at) for at in range(step * group_rows, (step + 1) * group_rows, SUBLANES)]
        return (jnp.concatenate(groups, axis=0) - float(half * shell_rows * LANES)).astype(kind)

    def put(at, ends, signs):
        for block in range(shell_rows):
            value = jnp.zeros((group_rows, LANES), kind)
            for end, sign in zip(ends, signs):
                value = jnp.where(end == lanes[block], jnp.full((group_rows, LANES), sign, kind), value)
            matrix_ref[pl.ds(at, group_rows), block * LANES : (block + 1) * LANES] = value.astype(matrix_ref.dtype)

    def build(domain, _):
        start = pl.multiple_of(domain * rows.matrix, LANES)
        for part in range(rows.bond_rows):
            first = around_ref[pl.ds(domain * rows.count + rows.bond_first + part, 1), :]
            second = around_ref[pl.ds(domain * rows.count + rows.bond_second + part, 1), :]
            for step in range(LANES // group_rows):
                for half in range(2):
                    ends = (column(first, step, half), column(second, step, half))
                    put(start + rows.inner_at[half] + part * LANES + step * group_rows, ends, (1.0, -1.0))
        for part in range(rows.slot_rows):
            for row_at, to, sign in (
                (rows.cross_first, rows.cross_at, 1.0),
                (rows.cross_second, rows.far_at, -1.0),
            ):
                row = around_ref[pl.ds(domain * rows.count + row_at + part, 1), :]
                for step in range(LANES // group_rows):
                    put(start + to + part * LANES + step * group_rows, (column(row, step),), (sign,))
        return 0

    lax.fori_loop(0, domains, build, 0)


def solve_kernel(
    rows,
    domains,
    strides,
    around_ref,
    moves_ref,
    weight_ref,
    matrix_ref,
    coords_out_ref,
    velocity_out_ref,
    push_ref,
    far_push_ref,
    field_ref,
):
    atom_rows, shell_rows = rows.atom_rows, rows.shell_rows
    bond_rows, slot_rows = rows.bond_rows, rows.slot_rows
    me = lax.axis_index("dom")

    def load(row):
        return around_ref[pl.ds(row, domains, stride=rows.count), :]

    def index(row):
        return load(row).astype(jnp.int32)

    inner_first = [index(rows.bond_first + p) for p in range(bond_rows)]
    inner_second = [index(rows.bond_second + p) for p in range(bond_rows)]
    cross_first = [index(rows.cross_first + p) for p in range(slot_rows)]
    cross_second = [index(rows.cross_second + p) for p in range(slot_rows)]
    sides = [load(rows.side + p) for p in range(slot_rows)]
    masses = [load(rows.mass + p) for p in range(atom_rows)]

    def move_rows(row):
        return moves_ref[pl.ds(row, domains, stride=rows.disp_count), :]

    def weight(at, c):
        value = weight_ref[pl.ds((at * 3 + c) * domains, domains), :]
        return value if at < bond_rows else value * live[at - bond_rows]

    live = [move_rows(rows.live + p) for p in range(slot_rows)]

    def project(fields):
        result = []
        for part in range(bond_rows):
            total = 0.0
            for c in range(3):
                ends = pick(fields[c], inner_first[part]) - pick(fields[c], inner_second[part])
                total = total + weight(part, c) * ends
            result.append(total)
        for part in range(slot_rows):
            seen = [pltpu.roll(cross_second[part], stride % domains, 0) for stride in strides]
            total = 0.0
            for c in range(3):
                shell = fields[c][:shell_rows]
                other = 0.0
                for code, stride in enumerate(strides):
                    value = pltpu.roll(pick(shell, seen[code]), -stride % domains, 0)
                    other = jnp.where(sides[part] == code, value, other)
                total = total + weight(bond_rows + part, c) * (pick(shell, cross_first[part]) - other)
            result.append(total)
        return result

    def put_pushes(values):
        for at, value in enumerate(values):
            for c in range(3):
                pushed = weight(at, c) * value
                high = pushed.astype(jnp.bfloat16).astype(jnp.float32)
                for row, part in ((c, high), (3 + c, pushed - high)):
                    push_ref[at, pl.ds(row * domains, domains), :] = part
                    if at >= bond_rows:
                        for code in range(4):
                            far_push_ref[at - bond_rows, pl.ds((code * SUBLANES + row) * domains, domains), :] = (
                                jnp.where(sides[at - bond_rows] == code, part, 0.0)
                            )

    def pushes_of(at, domain):
        return push_ref[at, pl.ds(domain, SUBLANES, stride=domains), :].astype(jnp.bfloat16)

    def product(pushes, domain, at):
        start = domain * rows.matrix + at
        if not isinstance(start, int):
            start = pl.multiple_of(start, LANES)
        pushes = pushes[0] if len(pushes) == 1 else jnp.concatenate(pushes, axis=1)
        result = jnp.dot(
            pushes, matrix_ref[pl.ds(start, pushes.shape[1]), :], preferred_element_type=jnp.float32
        )
        return [result[:, p * LANES : (p + 1) * LANES] for p in range(shell_rows)]

    def inner_totals(domain):
        pushes = [pushes_of(at, domain) for at in range(bond_rows + slot_rows)]
        return product(pushes, domain, 0) + product(pushes[:bond_rows], domain, rows.shell_terms)

    def far_totals(domain, first_row, count):
        pushes = [
            far_push_ref[p, pl.ds(first_row * domains + domain, count, stride=domains), :].astype(jnp.bfloat16)
            for p in range(slot_rows)
        ]
        return product(pushes, domain, rows.far_at)

    def spread(values):
        put_pushes(values)
        for domain in range(domains):
            for part, total in enumerate(inner_totals(domain)):
                field_ref[0, part, pl.ds(domain, SUBLANES, stride=domains), :] = total
            for part, total in enumerate(far_totals(domain, 0, 4 * SUBLANES)):
                for code, stride in enumerate(strides):
                    field_ref[1 + code, part, pl.ds((domain + stride) % domains, SUBLANES, stride=domains), :] = total[
                        code * SUBLANES : (code + 1) * SUBLANES, :
                    ]

        def field(c, part):
            pieces = [
                field_ref[source, part, pl.ds(row * domains, domains), :]
                for source in range(5 if part < shell_rows else 1)
                for row in (c, 3 + c)
            ]
            return masses[part] * functools.reduce(lambda a, b: a + b, pieces)

        return [[field(c, part) for part in range(atom_rows)] for c in range(3)]

    moves = [
        [move_rows(c * atom_rows + p) for p in range(atom_rows)]
        for c in range(3)
    ]
    push_ref[...] = jnp.zeros(push_ref.shape, jnp.float32)
    far_push_ref[...] = jnp.zeros(far_push_ref.shape, jnp.float32)
    residue = project(moves)

    def expand(_, carry):
        residue, summed = carry
        change = project(spread(residue))
        residue = [now - step for now, step in zip(residue, change)]
        return residue, [a + b for a, b in zip(summed, residue)]

    residue, summed = lax.fori_loop(0, ORDER, expand, (residue, residue))
    put_pushes(summed)
    sums = inner_totals(me)
    for code, stride in enumerate(strides):
        owner = lax.rem(me + (-stride) % domains, domains)
        for part, total in enumerate(far_totals(owner, code * SUBLANES, SUBLANES)):
            sums[part] = sums[part] + total
    for part in range(atom_rows):
        lanes = slice(part * LANES, (part + 1) * LANES)
        mass = around_ref[pl.ds(me * rows.count + rows.mass + part, 1), :]
        for c in range(3):
            correction = mass * (sums[part][c : c + 1, :] + sums[part][3 + c : 4 + c, :])
            move = moves_ref[pl.ds(me * rows.disp_count + c * atom_rows + part, 1), :] - correction
            start = around_ref[pl.ds(me * rows.count + rows.coords[c] + part, 1), :]
            coords_out_ref[c, 0, :, lanes] = start + move
            velocity_out_ref[c, 0, :, lanes] = move * (1.0 / time_step)


def vmem(count):
    return [pl.BlockSpec(memory_space=pltpu.VMEM)] * count


def smem(count):
    return [pl.BlockSpec(memory_space=pltpu.SMEM)] * count


def hbm(count):
    return [pl.BlockSpec(memory_space=pltpu.HBM)] * count


def in_hbm(arrays):
    return [pltpu.with_memory_space_constraint(a, pltpu.HBM) for a in arrays]


def params(mebibytes):
    return pltpu.CompilerParams(vmem_limit_bytes=mebibytes * 1024 * 1024)


def cost(flops, moved):
    return pl.CostEstimate(flops=flops, bytes_accessed=moved, transcendentals=0)


def room_for(arrays):
    return [pltpu.VMEM(a.shape, a.dtype) for a in arrays]


def shards(
    coords,
    velocity,
    charge,
    inv_mass,
    tile_block,
    tile_atoms,
    active_tile_count,
    bond_atoms,
    cross_atoms,
    cross_side,
    cross_count,
):
    atoms = coords.shape[-1]
    tiles = tile_atoms.shape[2]
    domains = lax.axis_size("dom")
    strides = strides_of(domains)
    rows = Rows(atoms, bond_atoms.shape[-1], cross_side.shape[-1])
    whole_slab = domains == SUBLANES
    copies = domains if whole_slab else 1
    f32 = jnp.float32

    sent = (coords, charge, inv_mass, bond_atoms, cross_atoms, cross_side)
    packed, rim = pl.pallas_call(
        functools.partial(pack_kernel, rows, copies),
        out_shape=(
            jax.ShapeDtypeStruct((copies * rows.count, LANES), f32),
            jax.ShapeDtypeStruct((4 * rows.shell_rows, LANES), f32),
        ),
        in_specs=hbm(len(sent)),
        out_specs=tuple(vmem(2)),
        scratch_shapes=room_for(sent) + [pltpu.SemaphoreType.DMA((len(sent),))],
        compiler_params=params(4),
        name="pack",
    )(*in_hbm(sent))

    alone = (coords, charge, velocity, inv_mass, tile_atoms)
    own = pl.pallas_call(
        functools.partial(own_kernel, rows),
        out_shape=(
            jax.ShapeDtypeStruct((4, atoms, LANES), f32),
            jax.ShapeDtypeStruct((4, tiles, TILE), f32),
            jax.ShapeDtypeStruct((tiles, TILE), jnp.int32),
            jax.ShapeDtypeStruct((4 * rows.atom_rows, LANES), f32),
        ),
        in_specs=hbm(len(alone)),
        out_specs=tuple(vmem(4)),
        scratch_shapes=room_for(alone[:4]) + [pltpu.SemaphoreType.DMA((len(alone),))],
        compiler_params=params(4),
        cost_estimate=cost(64 * atoms * LANES, 16 * atoms * LANES),
        name="own",
    )(*in_hbm(alone))

    below = passed_along(rim, "slab", 1)
    above = passed_along(rim, "slab", -1)
    if whole_slab:
        around = lax.all_to_all(packed, "dom", 0, 0, tiled=True)

        def place():
            me = lax.axis_index("dom")
            return [lax.rem(me + stride % domains, domains) for stride in strides]

    else:
        around = jnp.concatenate([packed] + [passed_along(packed, "dom", -stride) for stride in strides], axis=0)

        def place():
            return [1, 2, 3, 4]


    moves = pl.pallas_call(
        functools.partial(force_kernel, rows, copies, place),
        out_shape=jax.ShapeDtypeStruct((copies * rows.disp_count, LANES), f32),
        in_specs=smem(2) + hbm(1) + vmem(7),
        out_specs=vmem(1)[0],
        scratch_shapes=[
            pltpu.VMEM((4, 6 * rows.shell_rows, SUBLANES, LANES), f32),
            pltpu.VMEM((4, tiles, LANES), f32),
            pltpu.VMEM((3, atoms, LANES), f32),
            pltpu.SMEM(tile_block.shape, jnp.int32),
            pltpu.SemaphoreType.DMA(()),
        ],
        compiler_params=params(8),
        cost_estimate=cost(30 * tiles * TILE * TILE, 4 * around.size),
        name="force",
    )(active_tile_count, cross_count, *in_hbm([tile_block]), around, below, above, *own)

    if not whole_slab:
        return by_exchange(rows, strides, around, moves, cross_count)

    constraint_rows = rows.bond_rows + rows.slot_rows
    weight, matrix = pl.pallas_call(
        functools.partial(bond_kernel, rows, domains, strides),
        out_shape=(
            jax.ShapeDtypeStruct((constraint_rows * 3 * domains, LANES), f32),
            jax.ShapeDtypeStruct((domains * rows.matrix, atoms // 2), jnp.bfloat16),
        ),
        in_specs=vmem(1),
        out_specs=tuple(vmem(2)),
        compiler_params=params(16),
        cost_estimate=cost(8 * domains * rows.matrix * atoms // 2, 4 * around.size),
        name="bonds",
    )(around)

    every_move = lax.all_to_all(moves, "dom", 0, 0, tiled=True)

    return pl.pallas_call(
        functools.partial(solve_kernel, rows, domains, strides),
        out_shape=(
            jax.ShapeDtypeStruct(coords.shape, f32),
            jax.ShapeDtypeStruct(coords.shape, f32),
        ),
        in_specs=vmem(4),
        out_specs=tuple(vmem(2)),
        scratch_shapes=[
            pltpu.VMEM((constraint_rows, SUBLANES * domains, LANES), f32),
            pltpu.VMEM((rows.slot_rows, 4 * SUBLANES * domains, LANES), f32),
            pltpu.VMEM((5, rows.atom_rows, SUBLANES * domains, LANES), f32),
        ],
        compiler_params=params(16),
        name="solve",
    )(around, every_move, weight, matrix)


def by_exchange(rows, strides, around, moves, cross_count):
    atom_count = rows.atom_rows * LANES
    shell = rows.shell_rows * LANES
    inside = around.reshape(5, rows.count, LANES)

    def flat(at, count):
        return inside[0, at : at + count].reshape(-1)

    def neighbours(at):
        return inside[1:, at : at + rows.shell_rows].reshape(-1)

    coords = jnp.stack([flat(at, rows.atom_rows) for at in rows.coords])
    inv_mass = flat(rows.mass, rows.atom_rows)
    displace = moves[: rows.live].reshape(3, atom_count)
    left = flat(rows.bond_first, rows.bond_rows).astype(jnp.int32)
    right = flat(rows.bond_second, rows.bond_rows).astype(jnp.int32)
    cross_left = flat(rows.cross_first, rows.slot_rows).astype(jnp.int32)
    cross_right = flat(rows.cross_second, rows.slot_rows).astype(jnp.int32)
    side = flat(rows.side, rows.slot_rows).astype(jnp.int32)
    flag = moves[rows.live : rows.disp_used].reshape(-1)
    cross_index = side * shell + cross_right
    far_coords = jnp.stack([neighbours(at) for at in rows.coords])
    far_mass = neighbours(rows.mass)

    def weights(first, second, mass_first, mass_second):
        gap = first - second
        length = jnp.sqrt(jnp.sum(gap * gap, axis=0) + length_floor)
        return gap / length * lax.rsqrt(mass_first + mass_second)

    inner = weights(coords[:, left], coords[:, right], inv_mass[left], inv_mass[right])
    cross = flag * weights(
        coords[:, cross_left], far_coords[:, cross_index], inv_mass[cross_left], far_mass[cross_index]
    )

    def project(field):
        rim = field[:, :shell]
        far = jnp.concatenate([passed_along(rim, "dom", -stride) for stride in strides], axis=1)
        return (
            jnp.sum(inner * (field[:, left] - field[:, right]), axis=0),
            jnp.sum(cross * (field[:, cross_left] - far[:, cross_index]), axis=0),
        )

    def spread(values):
        pushed = inner * values[0]
        pushed_cross = cross * values[1]
        totals = jnp.zeros((3, atom_count), jnp.float32).at[:, left].add(pushed).at[:, right].add(-pushed)
        totals = totals.at[:, cross_left].add(pushed_cross)
        outward = jnp.zeros((3, 4 * shell), jnp.float32).at[:, cross_index].add(-pushed_cross)
        for code, stride in enumerate(strides):
            totals = totals.at[:, :shell].add(
                passed_along(outward[:, code * shell : (code + 1) * shell], "dom", stride)
            )
        return inv_mass * totals

    residue = project(displace)
    summed = residue
    for _ in range(ORDER):
        change = project(spread(residue))
        residue = tuple(now - step for now, step in zip(residue, change))
        summed = tuple(a + b for a, b in zip(summed, residue))
    move = displace - spread(summed)
    return (
        (coords + move).reshape(3, 1, 1, atom_count),
        (move * (1.0 / time_step)).reshape(3, 1, 1, atom_count),
    )


def solution(mesh):
    return jax.shard_map(
        shards,
        mesh=mesh,
        in_specs=(
            P(None, "slab", "dom", None),
            P(None, "slab", "dom", None),
            P("slab", "dom", None),
            P("slab", "dom", None),
            P("slab", "dom", None),
            P("slab", "dom", None, None),
            P("slab", "dom"),
            P(None, "slab", "dom", None),
            P(None, "slab", "dom", None),
            P("slab", "dom", None),
            P("slab", "dom"),
        ),
        out_specs=(P(None, "slab", "dom", None), P(None, "slab", "dom", None)),
        check_vma=False,
    )
```

```python
import functools

import jax
import jax.numpy as jnp
from jax import lax
from jax.experimental import pallas as pl
from jax.experimental.pallas import tpu as pltpu
from jax.sharding import PartitionSpec as P

TILE = 128
ORDER = 4
LANES = 128
SUBLANES = 8

time_step = 0.1
cutoff_sq = 16.0
force_scale = 4.0
length_floor = 0.25


def passed_along(array, axis, by):
    length = lax.axis_size(axis)
    return lax.ppermute(array, axis, [(i, (i + by) % length) for i in range(length)])


def first_of(domains):
    return domains // 4


def from_slab(blocks):
    length = lax.axis_size("dom")
    order = [(first_of(length) + i) % length for i in range(length)]
    return lax.all_to_all(blocks, "dom", 0, 0, axis_index_groups=[order], tiled=True)


def place_of(stride=0):
    length = lax.axis_size("dom")
    return lax.rem(lax.axis_index("dom") + (stride - first_of(length)) % length, length)


def strides_of(domains):
    row_width = max(2, domains // 8)
    return (1, -1, row_width, -row_width)


def round_up(count, step):
    return -(-count // step) * step


class Rows:
    def __init__(self, atoms, bonds, slots):
        self.atom_rows = atoms // LANES
        self.shell_rows = atoms // 2 // LANES
        self.bond_rows = bonds // LANES
        self.slot_rows = slots // LANES
        at = 0
        self.coords = []
        for _ in range(3):
            self.coords.append(at)
            at += self.atom_rows
        self.charge = at
        at += self.atom_rows
        self.mass = at
        at += self.atom_rows
        self.bond_first = at
        at += self.bond_rows
        self.bond_second = at
        at += self.bond_rows
        self.cross_first = at
        at += self.slot_rows
        self.cross_second = at
        at += self.slot_rows
        self.side = at
        at += self.slot_rows
        self.used = at
        self.count = round_up(at, SUBLANES)
        self.shell_terms = (self.bond_rows + self.slot_rows) * LANES
        self.inner_at = (0, self.shell_terms)
        self.cross_at = self.bond_rows * LANES
        self.far_at = self.shell_terms + self.bond_rows * LANES
        self.matrix = self.far_at + self.slot_rows * LANES
        self.live = 3 * self.atom_rows
        self.disp_used = self.live + self.slot_rows
        self.disp_count = round_up(self.disp_used, SUBLANES)


def take_lanes(table, lanes):
    return jnp.take_along_axis(table, lanes, axis=1, mode="promise_in_bounds")


def pick(tables, index):
    lanes = index & (LANES - 1)
    chunk = index >> 7
    result = take_lanes(tables[0], lanes)
    for k in range(1, len(tables)):
        result = jnp.where(chunk == k, take_lanes(tables[k], lanes), result)
    return result


def fetched(sources, targets, sem_ref):
    copies = [pltpu.make_async_copy(s, t, sem_ref.at[n]) for n, (s, t) in enumerate(zip(sources, targets))]
    for copy in copies:
        copy.start()
    return copies


def pack_kernel(rows, copies, *refs):
    sources, (out_ref, rim_ref), targets, sem_ref = refs[:6], refs[6:8], refs[8:14], refs[14]
    for copy in fetched(sources, targets, sem_ref):
        copy.wait()
    coords_ref, charge_ref, mass_ref, bonds_ref, cross_ref, side_ref = targets

    def put(row, value):
        for part in range(value.shape[1] // LANES):
            piece = value[:, part * LANES : (part + 1) * LANES]
            for copy in range(copies):
                out_ref[pl.ds(copy * rows.count + row + part, 1), :] = piece

    shell = rows.shell_rows * LANES
    fields = [coords_ref[c, 0] for c in range(3)] + [charge_ref[0]]
    for c in range(4):
        at = rows.coords[c] if c < 3 else rows.charge
        put(at, fields[c])
        for part in range(rows.shell_rows):
            rim_ref[pl.ds(c * rows.shell_rows + part, 1), :] = fields[c][:, part * LANES : (part + 1) * LANES]
    put(rows.mass, mass_ref[0])
    put(rows.bond_first, bonds_ref[0, 0].astype(jnp.float32))
    put(rows.bond_second, bonds_ref[1, 0].astype(jnp.float32))
    put(rows.cross_first, cross_ref[0, 0].astype(jnp.float32))
    put(rows.cross_second, cross_ref[1, 0].astype(jnp.float32))
    put(rows.side, side_ref[0].astype(jnp.float32))
    if rows.count > rows.used:
        for copy in range(copies):
            out_ref[pl.ds(copy * rows.count + rows.used, rows.count - rows.used), :] = jnp.zeros(
                (rows.count - rows.used, LANES), jnp.float32
            )


SHRINK = 1.0 / 4.0
OUT_OF_REACH = 1000.0
TILES_STEP = 4


def own_kernel(
    rows,
    coords_hbm,
    charge_hbm,
    velocity_hbm,
    mass_hbm,
    atoms_hbm,
    own_ref,
    far_ref,
    index_ref,
    motion_ref,
    coords_ref,
    charge_ref,
    velocity_ref,
    mass_ref,
    sem_ref,
):
    atom_rows = rows.atom_rows
    copies = fetched(
        (coords_hbm, charge_hbm, atoms_hbm.at[0, 0], velocity_hbm, mass_hbm),
        (coords_ref, charge_ref, index_ref, velocity_ref, mass_ref),
        sem_ref,
    )
    down = lax.broadcasted_iota(jnp.int32, (SUBLANES, LANES), 0)
    copies[0].wait()
    copies[1].wait()

    def lanes_of(part):
        return slice(part * LANES, (part + 1) * LANES)

    table = []
    for c in range(4):
        field = coords_ref[c, 0] * SHRINK if c < 3 else charge_ref[0]
        table.append(
            [jnp.broadcast_to(field[:, lanes_of(part)], (SUBLANES, LANES)) for part in range(atom_rows)]
        )
    for part in range(atom_rows):
        for group in range(LANES // SUBLANES):
            at = part * LANES + group * SUBLANES
            for c in range(4):
                value = take_lanes(table[c][part], down + group * SUBLANES)
                own_ref[c, pl.ds(at, SUBLANES), :] = value if c < 3 else value * 8.0
    copies[2].wait()
    for group in range(index_ref.shape[0] // SUBLANES):
        at = pl.ds(group * SUBLANES, SUBLANES)
        index = index_ref[at, :]
        for c in range(4):
            far_ref[c, at, :] = pick(table[c], index)
    copies[3].wait()
    copies[4].wait()
    fields = [velocity_ref[c, 0] for c in range(3)] + [mass_ref[0]]
    for c, field in enumerate(fields):
        for part in range(atom_rows):
            motion_ref[pl.ds(c * atom_rows + part, 1), :] = field[:, lanes_of(part)]


def force_kernel(
    rows,
    copies,
    place,
    live_ref,
    count_ref,
    block_hbm,
    around_ref,
    below_ref,
    above_ref,
    own_ref,
    near_ref,
    index_ref,
    motion_ref,
    out_ref,
    table_ref,
    far_ref,
    sum_ref,
    block_ref,
    sem_ref,
):
    atom_rows, shell_rows = rows.atom_rows, rows.shell_rows
    tiles = index_ref.shape[0]
    block_copy = pltpu.make_async_copy(block_hbm, block_ref, sem_ref)
    block_copy.start()
    holders = place()
    starts = [rows.coords[0], rows.coords[1], rows.coords[2], rows.charge]
    entry_rows = 6 * shell_rows

    def broadcast(row):
        return jnp.broadcast_to(row, (SUBLANES, LANES))

    for c in range(4):
        factor = SHRINK if c < 3 else 1.0
        at = 0
        for neighbour in range(4):
            base = holders[neighbour] * rows.count + starts[c]
            for part in range(shell_rows):
                table_ref[c, at] = broadcast(around_ref[pl.ds(base + part, 1), :] * factor)
                at += 1
        for slab_ref in (below_ref, above_ref):
            for part in range(shell_rows):
                table_ref[c, at] = broadcast(slab_ref[pl.ds(c * shell_rows + part, 1), :] * factor)
                at += 1

    live = live_ref[0, 0]
    down = lax.broadcasted_iota(jnp.int32, (SUBLANES, LANES), 0)
    for group in range(tiles // SUBLANES):
        at = pl.ds(group * SUBLANES, SUBLANES)
        index = index_ref[at, :]
        lanes = index & (LANES - 1)
        chunk = index >> 7
        values = [near_ref[c, at, :] for c in range(4)]
        for k in range(entry_rows):
            here = chunk == atom_rows + k
            values = [jnp.where(here, take_lanes(table_ref[c, k], lanes), values[c]) for c in range(4)]
        values[0] = jnp.where(down + group * SUBLANES < live, values[0], OUT_OF_REACH)
        for c in range(4):
            far_ref[c, at, :] = values[c]

    sum_ref[...] = jnp.zeros(sum_ref.shape, jnp.float32)
    block_copy.wait()

    softening = 1.0 / cutoff_sq

    def add_tile(tile):
        base = block_ref[0, 0, tile] * TILE
        far = [broadcast(far_ref[c, pl.ds(tile, 1), :]) for c in range(4)]
        for group in range(TILE // SUBLANES):
            at = pl.ds(pl.multiple_of(base + group * SUBLANES, SUBLANES), SUBLANES)
            gap = [own_ref[c, at, :] - far[c] for c in range(3)]
            square = gap[0] * gap[0] + gap[1] * gap[1] + gap[2] * gap[2]
            inverse = pl.reciprocal(square + softening, approx=True)
            weight = jnp.maximum(inverse - 1.0 / (1.0 + softening), 0.0)
            strength = (inverse - own_ref[3, at, :] * far[3]) * (weight * weight)
            for c in range(3):
                sum_ref[c, at, :] = sum_ref[c, at, :] + strength * gap[c]

    def add_tiles(step, _):
        for n in range(TILES_STEP):
            add_tile(step * TILES_STEP + n)
        return 0

    lax.fori_loop(0, lax.div(live + TILES_STEP - 1, TILES_STEP), add_tiles, 0)

    scale = time_step * time_step * force_scale * 4.0 / 2048.0 * (1.0 + softening) ** 2

    def lane_sums(c, part):
        return jnp.sum(sum_ref[c, pl.ds(part * LANES, LANES), :].T, axis=0, keepdims=True)

    for part in range(atom_rows):
        mass = motion_ref[pl.ds(3 * atom_rows + part, 1), :]
        for c in range(3):
            speed = motion_ref[pl.ds(c * atom_rows + part, 1), :]
            moved = time_step * speed + scale * lane_sums(c, part) * mass
            for copy in range(copies):
                out_ref[pl.ds(copy * rows.disp_count + c * atom_rows + part, 1), :] = moved
    slot = lax.broadcasted_iota(jnp.int32, (1, LANES), 1)
    for part in range(rows.slot_rows):
        flag = jnp.where(slot + part * LANES < count_ref[0, 0], 1.0, 0.0)
        for copy in range(copies):
            out_ref[pl.ds(copy * rows.disp_count + rows.live + part, 1), :] = flag
    if rows.disp_count > rows.disp_used:
        for copy in range(copies):
            out_ref[pl.ds(copy * rows.disp_count + rows.disp_used, rows.disp_count - rows.disp_used), :] = jnp.zeros(
                (rows.disp_count - rows.disp_used, LANES), jnp.float32
            )


def bond_kernel(rows, domains, strides, around_ref, weight_ref, matrix_ref):
    atom_rows, shell_rows = rows.atom_rows, rows.shell_rows

    def load(row):
        return around_ref[pl.ds(row, domains, stride=rows.count), :]

    def index(row):
        return load(row).astype(jnp.int32)

    fields = [[load(at + part) for part in range(atom_rows)] for at in rows.coords + [rows.mass]]

    def weights(first, second, row):
        gap = [first[c] - second[c] for c in range(3)]
        length_sq = gap[0] * gap[0] + gap[1] * gap[1] + gap[2] * gap[2] + length_floor
        scale = lax.rsqrt(length_sq) * lax.rsqrt(first[3] + second[3])
        return [gap[c] * scale for c in range(3)]

    at = 0
    for part in range(rows.bond_rows):
        first = index(rows.bond_first + part)
        second = index(rows.bond_second + part)
        values = weights([pick(f, first) for f in fields], [pick(f, second) for f in fields], at)
        for c in range(3):
            weight_ref[pl.ds((at * 3 + c) * domains, domains), :] = values[c]
        at += 1
    for part in range(rows.slot_rows):
        first = index(rows.cross_first + part)
        second = index(rows.cross_second + part)
        side = load(rows.side + part)
        other = [jnp.zeros((domains, LANES), jnp.float32) for _ in range(4)]
        for code, stride in enumerate(strides):
            seen = pltpu.roll(second, stride % domains, 0)
            for f in range(4):
                value = pltpu.roll(pick(fields[f][:shell_rows], seen), -stride % domains, 0)
                other[f] = jnp.where(side == code, value, other[f])
        values = weights([pick(f[:shell_rows], first) for f in fields], other, at)
        for c in range(3):
            weight_ref[pl.ds((at * 3 + c) * domains, domains), :] = values[c]
        at += 1

    down = lax.broadcasted_iota(jnp.int32, (SUBLANES, LANES), 0)
    group_rows = 4 * SUBLANES

    kind = jnp.bfloat16 if shell_rows * LANES <= 256 else jnp.float32
    across = lax.broadcasted_iota(jnp.int32, (group_rows, LANES), 1).astype(jnp.float32)
    lanes = [(across + float(block * LANES)).astype(kind) for block in range(shell_rows)]

    def column(row, step, half=0):
        row = jnp.broadcast_to(row, (SUBLANES, LANES))
        groups = [take_lanes(row, down + at) for at in range(step * group_rows, (step + 1) * group_rows, SUBLANES)]
        return (jnp.concatenate(groups, axis=0) - float(half * shell_rows * LANES)).astype(kind)

    def put(at, ends, signs):
        for block in range(shell_rows):
            value = jnp.zeros((group_rows, LANES), kind)
            for end, sign in zip(ends, signs):
                value = jnp.where(end == lanes[block], jnp.full((group_rows, LANES), sign, kind), value)
            matrix_ref[pl.ds(at, group_rows), block * LANES : (block + 1) * LANES] = value.astype(matrix_ref.dtype)

    def build(domain, _):
        start = pl.multiple_of(domain * rows.matrix, LANES)
        for part in range(rows.bond_rows):
            first = around_ref[pl.ds(domain * rows.count + rows.bond_first + part, 1), :]
            second = around_ref[pl.ds(domain * rows.count + rows.bond_second + part, 1), :]
            for step in range(LANES // group_rows):
                for half in range(2):
                    ends = (column(first, step, half), column(second, step, half))
                    put(start + rows.inner_at[half] + part * LANES + step * group_rows, ends, (1.0, -1.0))
        for part in range(rows.slot_rows):
            for row_at, to, sign in (
                (rows.cross_first, rows.cross_at, 1.0),
                (rows.cross_second, rows.far_at, -1.0),
            ):
                row = around_ref[pl.ds(domain * rows.count + row_at + part, 1), :]
                for step in range(LANES // group_rows):
                    put(start + to + part * LANES + step * group_rows, (column(row, step),), (sign,))
        return 0

    lax.fori_loop(0, domains, build, 0)


def solve_kernel(
    rows,
    domains,
    strides,
    around_ref,
    moves_ref,
    weight_ref,
    matrix_ref,
    coords_out_ref,
    velocity_out_ref,
    push_ref,
    far_push_ref,
    field_ref,
):
    atom_rows, shell_rows = rows.atom_rows, rows.shell_rows
    bond_rows, slot_rows = rows.bond_rows, rows.slot_rows
    me = place_of()

    def load(row):
        return around_ref[pl.ds(row, domains, stride=rows.count), :]

    def index(row):
        return load(row).astype(jnp.int32)

    inner_first = [index(rows.bond_first + p) for p in range(bond_rows)]
    inner_second = [index(rows.bond_second + p) for p in range(bond_rows)]
    cross_first = [index(rows.cross_first + p) for p in range(slot_rows)]
    cross_second = [index(rows.cross_second + p) for p in range(slot_rows)]
    sides = [load(rows.side + p) for p in range(slot_rows)]
    masses = [load(rows.mass + p) for p in range(atom_rows)]

    def move_rows(row):
        return moves_ref[pl.ds(row, domains, stride=rows.disp_count), :]

    def weight(at, c):
        value = weight_ref[pl.ds((at * 3 + c) * domains, domains), :]
        return value if at < bond_rows else value * live[at - bond_rows]

    live = [move_rows(rows.live + p) for p in range(slot_rows)]

    def project(fields):
        result = []
        for part in range(bond_rows):
            total = 0.0
            for c in range(3):
                ends = pick(fields[c], inner_first[part]) - pick(fields[c], inner_second[part])
                total = total + weight(part, c) * ends
            result.append(total)
        for part in range(slot_rows):
            seen = [pltpu.roll(cross_second[part], stride % domains, 0) for stride in strides]
            total = 0.0
            for c in range(3):
                shell = fields[c][:shell_rows]
                other = 0.0
                for code, stride in enumerate(strides):
                    value = pltpu.roll(pick(shell, seen[code]), -stride % domains, 0)
                    other = jnp.where(sides[part] == code, value, other)
                total = total + weight(bond_rows + part, c) * (pick(shell, cross_first[part]) - other)
            result.append(total)
        return result

    def put_pushes(values):
        for at, value in enumerate(values):
            for c in range(3):
                pushed = weight(at, c) * value
                high = pushed.astype(jnp.bfloat16).astype(jnp.float32)
                for row, part in ((c, high), (3 + c, pushed - high)):
                    push_ref[at, pl.ds(row * domains, domains), :] = part
                    if at >= bond_rows:
                        for code in range(4):
                            far_push_ref[at - bond_rows, pl.ds((code * SUBLANES + row) * domains, domains), :] = (
                                jnp.where(sides[at - bond_rows] == code, part, 0.0)
                            )

    def pushes_of(at, domain):
        return push_ref[at, pl.ds(domain, SUBLANES, stride=domains), :].astype(jnp.bfloat16)

    def product(pushes, domain, at):
        start = domain * rows.matrix + at
        if not isinstance(start, int):
            start = pl.multiple_of(start, LANES)
        pushes = pushes[0] if len(pushes) == 1 else jnp.concatenate(pushes, axis=1)
        result = jnp.dot(
            pushes, matrix_ref[pl.ds(start, pushes.shape[1]), :], preferred_element_type=jnp.float32
        )
        return [result[:, p * LANES : (p + 1) * LANES] for p in range(shell_rows)]

    def inner_totals(domain):
        pushes = [pushes_of(at, domain) for at in range(bond_rows + slot_rows)]
        return product(pushes, domain, 0) + product(pushes[:bond_rows], domain, rows.shell_terms)

    def far_totals(domain, first_row, count):
        pushes = [
            far_push_ref[p, pl.ds(first_row * domains + domain, count, stride=domains), :].astype(jnp.bfloat16)
            for p in range(slot_rows)
        ]
        return product(pushes, domain, rows.far_at)

    def spread(values):
        put_pushes(values)
        for domain in range(domains):
            for part, total in enumerate(inner_totals(domain)):
                field_ref[0, part, pl.ds(domain, SUBLANES, stride=domains), :] = total
            for part, total in enumerate(far_totals(domain, 0, 4 * SUBLANES)):
                for code, stride in enumerate(strides):
                    field_ref[1 + code, part, pl.ds((domain + stride) % domains, SUBLANES, stride=domains), :] = total[
                        code * SUBLANES : (code + 1) * SUBLANES, :
                    ]

        def field(c, part):
            pieces = [
                field_ref[source, part, pl.ds(row * domains, domains), :]
                for source in range(5 if part < shell_rows else 1)
                for row in (c, 3 + c)
            ]
            return masses[part] * functools.reduce(lambda a, b: a + b, pieces)

        return [[field(c, part) for part in range(atom_rows)] for c in range(3)]

    moves = [
        [move_rows(c * atom_rows + p) for p in range(atom_rows)]
        for c in range(3)
    ]
    push_ref[...] = jnp.zeros(push_ref.shape, jnp.float32)
    far_push_ref[...] = jnp.zeros(far_push_ref.shape, jnp.float32)
    residue = project(moves)

    def expand(_, carry):
        residue, summed = carry
        change = project(spread(residue))
        residue = [now - step for now, step in zip(residue, change)]
        return residue, [a + b for a, b in zip(summed, residue)]

    residue, summed = lax.fori_loop(0, ORDER, expand, (residue, residue))
    put_pushes(summed)
    sums = inner_totals(me)
    for code, stride in enumerate(strides):
        owner = lax.rem(me + (-stride) % domains, domains)
        for part, total in enumerate(far_totals(owner, code * SUBLANES, SUBLANES)):
            sums[part] = sums[part] + total
    for part in range(atom_rows):
        lanes = slice(part * LANES, (part + 1) * LANES)
        mass = around_ref[pl.ds(me * rows.count + rows.mass + part, 1), :]
        for c in range(3):
            correction = mass * (sums[part][c : c + 1, :] + sums[part][3 + c : 4 + c, :])
            move = moves_ref[pl.ds(me * rows.disp_count + c * atom_rows + part, 1), :] - correction
            start = around_ref[pl.ds(me * rows.count + rows.coords[c] + part, 1), :]
            coords_out_ref[c, 0, :, lanes] = start + move
            velocity_out_ref[c, 0, :, lanes] = move * (1.0 / time_step)


def vmem(count):
    return [pl.BlockSpec(memory_space=pltpu.VMEM)] * count


def smem(count):
    return [pl.BlockSpec(memory_space=pltpu.SMEM)] * count


def hbm(count):
    return [pl.BlockSpec(memory_space=pltpu.HBM)] * count


def in_hbm(arrays):
    return [pltpu.with_memory_space_constraint(a, pltpu.HBM) for a in arrays]


def params(mebibytes):
    return pltpu.CompilerParams(vmem_limit_bytes=mebibytes * 1024 * 1024)


def cost(flops, moved):
    return pl.CostEstimate(flops=flops, bytes_accessed=moved, transcendentals=0)


def room_for(arrays):
    return [pltpu.VMEM(a.shape, a.dtype) for a in arrays]


def shards(
    coords,
    velocity,
    charge,
    inv_mass,
    tile_block,
    tile_atoms,
    active_tile_count,
    bond_atoms,
    cross_atoms,
    cross_side,
    cross_count,
):
    atoms = coords.shape[-1]
    tiles = tile_atoms.shape[2]
    domains = lax.axis_size("dom")
    strides = strides_of(domains)
    rows = Rows(atoms, bond_atoms.shape[-1], cross_side.shape[-1])
    whole_slab = domains == SUBLANES
    copies = domains if whole_slab else 1
    f32 = jnp.float32

    sent = (coords, charge, inv_mass, bond_atoms, cross_atoms, cross_side)
    packed, rim = pl.pallas_call(
        functools.partial(pack_kernel, rows, copies),
        out_shape=(
            jax.ShapeDtypeStruct((copies * rows.count, LANES), f32),
            jax.ShapeDtypeStruct((4 * rows.shell_rows, LANES), f32),
        ),
        in_specs=hbm(len(sent)),
        out_specs=tuple(vmem(2)),
        scratch_shapes=room_for(sent) + [pltpu.SemaphoreType.DMA((len(sent),))],
        compiler_params=params(4),
        name="pack",
    )(*in_hbm(sent))

    alone = (coords, charge, velocity, inv_mass, tile_atoms)
    own = pl.pallas_call(
        functools.partial(own_kernel, rows),
        out_shape=(
            jax.ShapeDtypeStruct((4, atoms, LANES), f32),
            jax.ShapeDtypeStruct((4, tiles, TILE), f32),
            jax.ShapeDtypeStruct((tiles, TILE), jnp.int32),
            jax.ShapeDtypeStruct((4 * rows.atom_rows, LANES), f32),
        ),
        in_specs=hbm(len(alone)),
        out_specs=tuple(vmem(4)),
        scratch_shapes=room_for(alone[:4]) + [pltpu.SemaphoreType.DMA((len(alone),))],
        compiler_params=params(4),
        cost_estimate=cost(64 * atoms * LANES, 16 * atoms * LANES),
        name="own",
    )(*in_hbm(alone))

    below = passed_along(rim, "slab", 1)
    above = passed_along(rim, "slab", -1)
    if whole_slab:
        around = from_slab(packed)

        def place():
            return [place_of(stride) for stride in strides]

    else:
        around = jnp.concatenate([packed] + [passed_along(packed, "dom", -stride) for stride in strides], axis=0)

        def place():
            return [1, 2, 3, 4]


    moves = pl.pallas_call(
        functools.partial(force_kernel, rows, copies, place),
        out_shape=jax.ShapeDtypeStruct((copies * rows.disp_count, LANES), f32),
        in_specs=smem(2) + hbm(1) + vmem(7),
        out_specs=vmem(1)[0],
        scratch_shapes=[
            pltpu.VMEM((4, 6 * rows.shell_rows, SUBLANES, LANES), f32),
            pltpu.VMEM((4, tiles, LANES), f32),
            pltpu.VMEM((3, atoms, LANES), f32),
            pltpu.SMEM(tile_block.shape, jnp.int32),
            pltpu.SemaphoreType.DMA(()),
        ],
        compiler_params=params(8),
        cost_estimate=cost(30 * tiles * TILE * TILE, 4 * around.size),
        name="force",
    )(active_tile_count, cross_count, *in_hbm([tile_block]), around, below, above, *own)

    if not whole_slab:
        return by_exchange(rows, strides, around, moves, cross_count)

    constraint_rows = rows.bond_rows + rows.slot_rows
    weight, matrix = pl.pallas_call(
        functools.partial(bond_kernel, rows, domains, strides),
        out_shape=(
            jax.ShapeDtypeStruct((constraint_rows * 3 * domains, LANES), f32),
            jax.ShapeDtypeStruct((domains * rows.matrix, atoms // 2), jnp.bfloat16),
        ),
        in_specs=vmem(1),
        out_specs=tuple(vmem(2)),
        compiler_params=params(16),
        cost_estimate=cost(8 * domains * rows.matrix * atoms // 2, 4 * around.size),
        name="bonds",
    )(around)

    every_move = from_slab(moves)

    return pl.pallas_call(
        functools.partial(solve_kernel, rows, domains, strides),
        out_shape=(
            jax.ShapeDtypeStruct(coords.shape, f32),
            jax.ShapeDtypeStruct(coords.shape, f32),
        ),
        in_specs=vmem(4),
        out_specs=tuple(vmem(2)),
        scratch_shapes=[
            pltpu.VMEM((constraint_rows, SUBLANES * domains, LANES), f32),
            pltpu.VMEM((rows.slot_rows, 4 * SUBLANES * domains, LANES), f32),
            pltpu.VMEM((5, rows.atom_rows, SUBLANES * domains, LANES), f32),
        ],
        compiler_params=params(16),
        name="solve",
    )(around, every_move, weight, matrix)


def by_exchange(rows, strides, around, moves, cross_count):
    atom_count = rows.atom_rows * LANES
    shell = rows.shell_rows * LANES
    inside = around.reshape(5, rows.count, LANES)

    def flat(at, count):
        return inside[0, at : at + count].reshape(-1)

    def neighbours(at):
        return inside[1:, at : at + rows.shell_rows].reshape(-1)

    coords = jnp.stack([flat(at, rows.atom_rows) for at in rows.coords])
    inv_mass = flat(rows.mass, rows.atom_rows)
    displace = moves[: rows.live].reshape(3, atom_count)
    left = flat(rows.bond_first, rows.bond_rows).astype(jnp.int32)
    right = flat(rows.bond_second, rows.bond_rows).astype(jnp.int32)
    cross_left = flat(rows.cross_first, rows.slot_rows).astype(jnp.int32)
    cross_right = flat(rows.cross_second, rows.slot_rows).astype(jnp.int32)
    side = flat(rows.side, rows.slot_rows).astype(jnp.int32)
    flag = moves[rows.live : rows.disp_used].reshape(-1)
    cross_index = side * shell + cross_right
    far_coords = jnp.stack([neighbours(at) for at in rows.coords])
    far_mass = neighbours(rows.mass)

    def weights(first, second, mass_first, mass_second):
        gap = first - second
        length = jnp.sqrt(jnp.sum(gap * gap, axis=0) + length_floor)
        return gap / length * lax.rsqrt(mass_first + mass_second)

    inner = weights(coords[:, left], coords[:, right], inv_mass[left], inv_mass[right])
    cross = flag * weights(
        coords[:, cross_left], far_coords[:, cross_index], inv_mass[cross_left], far_mass[cross_index]
    )

    def project(field):
        rim = field[:, :shell]
        far = jnp.concatenate([passed_along(rim, "dom", -stride) for stride in strides], axis=1)
        return (
            jnp.sum(inner * (field[:, left] - field[:, right]), axis=0),
            jnp.sum(cross * (field[:, cross_left] - far[:, cross_index]), axis=0),
        )

    def spread(values):
        pushed = inner * values[0]
        pushed_cross = cross * values[1]
        totals = jnp.zeros((3, atom_count), jnp.float32).at[:, left].add(pushed).at[:, right].add(-pushed)
        totals = totals.at[:, cross_left].add(pushed_cross)
        outward = jnp.zeros((3, 4 * shell), jnp.float32).at[:, cross_index].add(-pushed_cross)
        for code, stride in enumerate(strides):
            totals = totals.at[:, :shell].add(
                passed_along(outward[:, code * shell : (code + 1) * shell], "dom", stride)
            )
        return inv_mass * totals

    residue = project(displace)
    summed = residue
    for _ in range(ORDER):
        change = project(spread(residue))
        residue = tuple(now - step for now, step in zip(residue, change))
        summed = tuple(a + b for a, b in zip(summed, residue))
    move = displace - spread(summed)
    return (
        (coords + move).reshape(3, 1, 1, atom_count),
        (move * (1.0 / time_step)).reshape(3, 1, 1, atom_count),
    )


def solution(mesh):
    return jax.shard_map(
        shards,
        mesh=mesh,
        in_specs=(
            P(None, "slab", "dom", None),
            P(None, "slab", "dom", None),
            P("slab", "dom", None),
            P("slab", "dom", None),
            P("slab", "dom", None),
            P("slab", "dom", None, None),
            P("slab", "dom"),
            P(None, "slab", "dom", None),
            P(None, "slab", "dom", None),
            P("slab", "dom", None),
            P("slab", "dom"),
        ),
        out_specs=(P(None, "slab", "dom", None), P(None, "slab", "dom", None)),
        check_vma=False,
    )
```

```python
import functools

import jax
import jax.numpy as jnp
from jax import lax
from jax.experimental import pallas as pl
from jax.experimental.pallas import tpu as pltpu
from jax.sharding import PartitionSpec as P

TILE = 128
ORDER = 4
LANES = 128
SUBLANES = 8

time_step = 0.1
cutoff_sq = 16.0
force_scale = 4.0
length_floor = 0.25


def passed_along(array, axis, by):
    length = lax.axis_size(axis)
    return lax.ppermute(array, axis, [(i, (i + by) % length) for i in range(length)])


def first_of(domains):
    return domains - 1


def from_slab(blocks):
    length = lax.axis_size("dom")
    order = [(first_of(length) + i) % length for i in range(length)]
    return lax.all_to_all(blocks, "dom", 0, 0, axis_index_groups=[order], tiled=True)


def place_of(stride=0):
    length = lax.axis_size("dom")
    return lax.rem(lax.axis_index("dom") + (stride - first_of(length)) % length, length)


def strides_of(domains):
    row_width = max(2, domains // 8)
    return (1, -1, row_width, -row_width)


def round_up(count, step):
    return -(-count // step) * step


class Rows:
    def __init__(self, atoms, bonds, slots):
        self.atom_rows = atoms // LANES
        self.shell_rows = atoms // 2 // LANES
        self.bond_rows = bonds // LANES
        self.slot_rows = slots // LANES
        at = 0
        self.coords = []
        for _ in range(3):
            self.coords.append(at)
            at += self.atom_rows
        self.charge = at
        at += self.atom_rows
        self.mass = at
        at += self.atom_rows
        self.bond_first = at
        at += self.bond_rows
        self.bond_second = at
        at += self.bond_rows
        self.cross_first = at
        at += self.slot_rows
        self.cross_second = at
        at += self.slot_rows
        self.side = at
        at += self.slot_rows
        self.used = at
        self.count = round_up(at, SUBLANES)
        self.shell_terms = (self.bond_rows + self.slot_rows) * LANES
        self.inner_at = (0, self.shell_terms)
        self.cross_at = self.bond_rows * LANES
        self.far_at = self.shell_terms + self.bond_rows * LANES
        self.matrix = self.far_at + self.slot_rows * LANES
        self.live = 3 * self.atom_rows
        self.disp_used = self.live + self.slot_rows
        self.disp_count = round_up(self.disp_used, SUBLANES)


def take_lanes(table, lanes):
    return jnp.take_along_axis(table, lanes, axis=1, mode="promise_in_bounds")


def pick(tables, index):
    lanes = index & (LANES - 1)
    chunk = index >> 7
    result = take_lanes(tables[0], lanes)
    for k in range(1, len(tables)):
        result = jnp.where(chunk == k, take_lanes(tables[k], lanes), result)
    return result


def fetched(sources, targets, sem_ref):
    copies = [pltpu.make_async_copy(s, t, sem_ref.at[n]) for n, (s, t) in enumerate(zip(sources, targets))]
    for copy in copies:
        copy.start()
    return copies


def pack_kernel(rows, copies, *refs):
    sources, (out_ref, rim_ref), targets, sem_ref = refs[:6], refs[6:8], refs[8:14], refs[14]
    for copy in fetched(sources, targets, sem_ref):
        copy.wait()
    coords_ref, charge_ref, mass_ref, bonds_ref, cross_ref, side_ref = targets

    def put(row, value):
        for part in range(value.shape[1] // LANES):
            piece = value[:, part * LANES : (part + 1) * LANES]
            for copy in range(copies):
                out_ref[pl.ds(copy * rows.count + row + part, 1), :] = piece

    shell = rows.shell_rows * LANES
    fields = [coords_ref[c, 0] for c in range(3)] + [charge_ref[0]]
    for c in range(4):
        at = rows.coords[c] if c < 3 else rows.charge
        put(at, fields[c])
        for part in range(rows.shell_rows):
            rim_ref[pl.ds(c * rows.shell_rows + part, 1), :] = fields[c][:, part * LANES : (part + 1) * LANES]
    put(rows.mass, mass_ref[0])
    put(rows.bond_first, bonds_ref[0, 0].astype(jnp.float32))
    put(rows.bond_second, bonds_ref[1, 0].astype(jnp.float32))
    put(rows.cross_first, cross_ref[0, 0].astype(jnp.float32))
    put(rows.cross_second, cross_ref[1, 0].astype(jnp.float32))
    put(rows.side, side_ref[0].astype(jnp.float32))
    if rows.count > rows.used:
        for copy in range(copies):
            out_ref[pl.ds(copy * rows.count + rows.used, rows.count - rows.used), :] = jnp.zeros(
                (rows.count - rows.used, LANES), jnp.float32
            )


SHRINK = 1.0 / 4.0
OUT_OF_REACH = 1000.0
TILES_STEP = 4


def own_kernel(
    rows,
    coords_hbm,
    charge_hbm,
    velocity_hbm,
    mass_hbm,
    atoms_hbm,
    own_ref,
    far_ref,
    index_ref,
    motion_ref,
    coords_ref,
    charge_ref,
    velocity_ref,
    mass_ref,
    sem_ref,
):
    atom_rows = rows.atom_rows
    copies = fetched(
        (coords_hbm, charge_hbm, atoms_hbm.at[0, 0], velocity_hbm, mass_hbm),
        (coords_ref, charge_ref, index_ref, velocity_ref, mass_ref),
        sem_ref,
    )
    down = lax.broadcasted_iota(jnp.int32, (SUBLANES, LANES), 0)
    copies[0].wait()
    copies[1].wait()

    def lanes_of(part):
        return slice(part * LANES, (part + 1) * LANES)

    table = []
    for c in range(4):
        field = coords_ref[c, 0] * SHRINK if c < 3 else charge_ref[0]
        table.append(
            [jnp.broadcast_to(field[:, lanes_of(part)], (SUBLANES, LANES)) for part in range(atom_rows)]
        )
    for part in range(atom_rows):
        for group in range(LANES // SUBLANES):
            at = part * LANES + group * SUBLANES
            for c in range(4):
                value = take_lanes(table[c][part], down + group * SUBLANES)
                own_ref[c, pl.ds(at, SUBLANES), :] = value if c < 3 else value * 8.0
    copies[2].wait()
    for group in range(index_ref.shape[0] // SUBLANES):
        at = pl.ds(group * SUBLANES, SUBLANES)
        index = index_ref[at, :]
        for c in range(4):
            far_ref[c, at, :] = pick(table[c], index)
    copies[3].wait()
    copies[4].wait()
    fields = [velocity_ref[c, 0] for c in range(3)] + [mass_ref[0]]
    for c, field in enumerate(fields):
        for part in range(atom_rows):
            motion_ref[pl.ds(c * atom_rows + part, 1), :] = field[:, lanes_of(part)]


def force_kernel(
    rows,
    copies,
    place,
    live_ref,
    count_ref,
    block_hbm,
    around_ref,
    below_ref,
    above_ref,
    own_ref,
    near_ref,
    index_ref,
    motion_ref,
    out_ref,
    table_ref,
    far_ref,
    sum_ref,
    block_ref,
    sem_ref,
):
    atom_rows, shell_rows = rows.atom_rows, rows.shell_rows
    tiles = index_ref.shape[0]
    block_copy = pltpu.make_async_copy(block_hbm, block_ref, sem_ref)
    block_copy.start()
    holders = place()
    starts = [rows.coords[0], rows.coords[1], rows.coords[2], rows.charge]
    entry_rows = 6 * shell_rows

    def broadcast(row):
        return jnp.broadcast_to(row, (SUBLANES, LANES))

    for c in range(4):
        factor = SHRINK if c < 3 else 1.0
        at = 0
        for neighbour in range(4):
            base = holders[neighbour] * rows.count + starts[c]
            for part in range(shell_rows):
                table_ref[c, at] = broadcast(around_ref[pl.ds(base + part, 1), :] * factor)
                at += 1
        for slab_ref in (below_ref, above_ref):
            for part in range(shell_rows):
                table_ref[c, at] = broadcast(slab_ref[pl.ds(c * shell_rows + part, 1), :] * factor)
                at += 1

    live = live_ref[0, 0]
    down = lax.broadcasted_iota(jnp.int32, (SUBLANES, LANES), 0)
    for group in range(tiles // SUBLANES):
        at = pl.ds(group * SUBLANES, SUBLANES)
        index = index_ref[at, :]
        lanes = index & (LANES - 1)
        chunk = index >> 7
        values = [near_ref[c, at, :] for c in range(4)]
        for k in range(entry_rows):
            here = chunk == atom_rows + k
            values = [jnp.where(here, take_lanes(table_ref[c, k], lanes), values[c]) for c in range(4)]
        values[0] = jnp.where(down + group * SUBLANES < live, values[0], OUT_OF_REACH)
        for c in range(4):
            far_ref[c, at, :] = values[c]

    sum_ref[...] = jnp.zeros(sum_ref.shape, jnp.float32)
    block_copy.wait()

    softening = 1.0 / cutoff_sq

    def add_tile(tile):
        base = block_ref[0, 0, tile] * TILE
        far = [broadcast(far_ref[c, pl.ds(tile, 1), :]) for c in range(4)]
        for group in range(TILE // SUBLANES):
            at = pl.ds(pl.multiple_of(base + group * SUBLANES, SUBLANES), SUBLANES)
            gap = [own_ref[c, at, :] - far[c] for c in range(3)]
            square = gap[0] * gap[0] + gap[1] * gap[1] + gap[2] * gap[2]
            inverse = pl.reciprocal(square + softening, approx=True)
            weight = jnp.maximum(inverse - 1.0 / (1.0 + softening), 0.0)
            strength = (inverse - own_ref[3, at, :] * far[3]) * (weight * weight)
            for c in range(3):
                sum_ref[c, at, :] = sum_ref[c, at, :] + strength * gap[c]

    def add_tiles(step, _):
        for n in range(TILES_STEP):
            add_tile(step * TILES_STEP + n)
        return 0

    lax.fori_loop(0, lax.div(live + TILES_STEP - 1, TILES_STEP), add_tiles, 0)

    scale = time_step * time_step * force_scale * 4.0 / 2048.0 * (1.0 + softening) ** 2

    def lane_sums(c, part):
        return jnp.sum(sum_ref[c, pl.ds(part * LANES, LANES), :].T, axis=0, keepdims=True)

    for part in range(atom_rows):
        mass = motion_ref[pl.ds(3 * atom_rows + part, 1), :]
        for c in range(3):
            speed = motion_ref[pl.ds(c * atom_rows + part, 1), :]
            moved = time_step * speed + scale * lane_sums(c, part) * mass
            for copy in range(copies):
                out_ref[pl.ds(copy * rows.disp_count + c * atom_rows + part, 1), :] = moved
    slot = lax.broadcasted_iota(jnp.int32, (1, LANES), 1)
    for part in range(rows.slot_rows):
        flag = jnp.where(slot + part * LANES < count_ref[0, 0], 1.0, 0.0)
        for copy in range(copies):
            out_ref[pl.ds(copy * rows.disp_count + rows.live + part, 1), :] = flag
    if rows.disp_count > rows.disp_used:
        for copy in range(copies):
            out_ref[pl.ds(copy * rows.disp_count + rows.disp_used, rows.disp_count - rows.disp_used), :] = jnp.zeros(
                (rows.disp_count - rows.disp_used, LANES), jnp.float32
            )


def bond_kernel(rows, domains, strides, around_ref, weight_ref, matrix_ref):
    atom_rows, shell_rows = rows.atom_rows, rows.shell_rows

    def load(row):
        return around_ref[pl.ds(row, domains, stride=rows.count), :]

    def index(row):
        return load(row).astype(jnp.int32)

    fields = [[load(at + part) for part in range(atom_rows)] for at in rows.coords + [rows.mass]]

    def weights(first, second, row):
        gap = [first[c] - second[c] for c in range(3)]
        length_sq = gap[0] * gap[0] + gap[1] * gap[1] + gap[2] * gap[2] + length_floor
        scale = lax.rsqrt(length_sq) * lax.rsqrt(first[3] + second[3])
        return [gap[c] * scale for c in range(3)]

    at = 0
    for part in range(rows.bond_rows):
        first = index(rows.bond_first + part)
        second = index(rows.bond_second + part)
        values = weights([pick(f, first) for f in fields], [pick(f, second) for f in fields], at)
        for c in range(3):
            weight_ref[pl.ds((at * 3 + c) * domains, domains), :] = values[c]
        at += 1
    for part in range(rows.slot_rows):
        first = index(rows.cross_first + part)
        second = index(rows.cross_second + part)
        side = load(rows.side + part)
        other = [jnp.zeros((domains, LANES), jnp.float32) for _ in range(4)]
        for code, stride in enumerate(strides):
            seen = pltpu.roll(second, stride % domains, 0)
            for f in range(4):
                value = pltpu.roll(pick(fields[f][:shell_rows], seen), -stride % domains, 0)
                other[f] = jnp.where(side == code, value, other[f])
        values = weights([pick(f[:shell_rows], first) for f in fields], other, at)
        for c in range(3):
            weight_ref[pl.ds((at * 3 + c) * domains, domains), :] = values[c]
        at += 1

    down = lax.broadcasted_iota(jnp.int32, (SUBLANES, LANES), 0)
    group_rows = 4 * SUBLANES

    kind = jnp.bfloat16 if shell_rows * LANES <= 256 else jnp.float32
    across = lax.broadcasted_iota(jnp.int32, (group_rows, LANES), 1).astype(jnp.float32)
    lanes = [(across + float(block * LANES)).astype(kind) for block in range(shell_rows)]

    def column(row, step, half=0):
        row = jnp.broadcast_to(row, (SUBLANES, LANES))
        groups = [take_lanes(row, down + at) for at in range(step * group_rows, (step + 1) * group_rows, SUBLANES)]
        return (jnp.concatenate(groups, axis=0) - float(half * shell_rows * LANES)).astype(kind)

    def put(at, ends, signs):
        for block in range(shell_rows):
            value = jnp.zeros((group_rows, LANES), kind)
            for end, sign in zip(ends, signs):
                value = jnp.where(end == lanes[block], jnp.full((group_rows, LANES), sign, kind), value)
            matrix_ref[pl.ds(at, group_rows), block * LANES : (block + 1) * LANES] = value.astype(matrix_ref.dtype)

    def build(domain, _):
        start = pl.multiple_of(domain * rows.matrix, LANES)
        for part in range(rows.bond_rows):
            first = around_ref[pl.ds(domain * rows.count + rows.bond_first + part, 1), :]
            second = around_ref[pl.ds(domain * rows.count + rows.bond_second + part, 1), :]
            for step in range(LANES // group_rows):
                for half in range(2):
                    ends = (column(first, step, half), column(second, step, half))
                    put(start + rows.inner_at[half] + part * LANES + step * group_rows, ends, (1.0, -1.0))
        for part in range(rows.slot_rows):
            for row_at, to, sign in (
                (rows.cross_first, rows.cross_at, 1.0),
                (rows.cross_second, rows.far_at, -1.0),
            ):
                row = around_ref[pl.ds(domain * rows.count + row_at + part, 1), :]
                for step in range(LANES // group_rows):
                    put(start + to + part * LANES + step * group_rows, (column(row, step),), (sign,))
        return 0

    lax.fori_loop(0, domains, build, 0)


def solve_kernel(
    rows,
    domains,
    strides,
    around_ref,
    moves_ref,
    weight_ref,
    matrix_ref,
    coords_out_ref,
    velocity_out_ref,
    push_ref,
    far_push_ref,
    field_ref,
):
    atom_rows, shell_rows = rows.atom_rows, rows.shell_rows
    bond_rows, slot_rows = rows.bond_rows, rows.slot_rows
    me = place_of()

    def load(row):
        return around_ref[pl.ds(row, domains, stride=rows.count), :]

    def index(row):
        return load(row).astype(jnp.int32)

    inner_first = [index(rows.bond_first + p) for p in range(bond_rows)]
    inner_second = [index(rows.bond_second + p) for p in range(bond_rows)]
    cross_first = [index(rows.cross_first + p) for p in range(slot_rows)]
    cross_second = [index(rows.cross_second + p) for p in range(slot_rows)]
    sides = [load(rows.side + p) for p in range(slot_rows)]
    masses = [load(rows.mass + p) for p in range(atom_rows)]

    def move_rows(row):
        return moves_ref[pl.ds(row, domains, stride=rows.disp_count), :]

    def weight(at, c):
        value = weight_ref[pl.ds((at * 3 + c) * domains, domains), :]
        return value if at < bond_rows else value * live[at - bond_rows]

    live = [move_rows(rows.live + p) for p in range(slot_rows)]

    def project(fields):
        result = []
        for part in range(bond_rows):
            total = 0.0
            for c in range(3):
                ends = pick(fields[c], inner_first[part]) - pick(fields[c], inner_second[part])
                total = total + weight(part, c) * ends
            result.append(total)
        for part in range(slot_rows):
            seen = [pltpu.roll(cross_second[part], stride % domains, 0) for stride in strides]
            total = 0.0
            for c in range(3):
                shell = fields[c][:shell_rows]
                other = 0.0
                for code, stride in enumerate(strides):
                    value = pltpu.roll(pick(shell, seen[code]), -stride % domains, 0)
                    other = jnp.where(sides[part] == code, value, other)
                total = total + weight(bond_rows + part, c) * (pick(shell, cross_first[part]) - other)
            result.append(total)
        return result

    def put_pushes(values):
        for at, value in enumerate(values):
            for c in range(3):
                pushed = weight(at, c) * value
                high = pushed.astype(jnp.bfloat16).astype(jnp.float32)
                for row, part in ((c, high), (3 + c, pushed - high)):
                    push_ref[at, pl.ds(row * domains, domains), :] = part
                    if at >= bond_rows:
                        for code in range(4):
                            far_push_ref[at - bond_rows, pl.ds((code * SUBLANES + row) * domains, domains), :] = (
                                jnp.where(sides[at - bond_rows] == code, part, 0.0)
                            )

    def pushes_of(at, domain):
        return push_ref[at, pl.ds(domain, SUBLANES, stride=domains), :].astype(jnp.bfloat16)

    def product(pushes, domain, at):
        start = domain * rows.matrix + at
        if not isinstance(start, int):
            start = pl.multiple_of(start, LANES)
        pushes = pushes[0] if len(pushes) == 1 else jnp.concatenate(pushes, axis=1)
        result = jnp.dot(
            pushes, matrix_ref[pl.ds(start, pushes.shape[1]), :], preferred_element_type=jnp.float32
        )
        return [result[:, p * LANES : (p + 1) * LANES] for p in range(shell_rows)]

    def inner_totals(domain):
        pushes = [pushes_of(at, domain) for at in range(bond_rows + slot_rows)]
        return product(pushes, domain, 0) + product(pushes[:bond_rows], domain, rows.shell_terms)

    def far_totals(domain, first_row, count):
        pushes = [
            far_push_ref[p, pl.ds(first_row * domains + domain, count, stride=domains), :].astype(jnp.bfloat16)
            for p in range(slot_rows)
        ]
        return product(pushes, domain, rows.far_at)

    def spread(values):
        put_pushes(values)
        for domain in range(domains):
            for part, total in enumerate(inner_totals(domain)):
                field_ref[0, part, pl.ds(domain, SUBLANES, stride=domains), :] = total
            for part, total in enumerate(far_totals(domain, 0, 4 * SUBLANES)):
                for code, stride in enumerate(strides):
                    field_ref[1 + code, part, pl.ds((domain + stride) % domains, SUBLANES, stride=domains), :] = total[
                        code * SUBLANES : (code + 1) * SUBLANES, :
                    ]

        def field(c, part):
            pieces = [
                field_ref[source, part, pl.ds(row * domains, domains), :]
                for source in range(5 if part < shell_rows else 1)
                for row in (c, 3 + c)
            ]
            return masses[part] * functools.reduce(lambda a, b: a + b, pieces)

        return [[field(c, part) for part in range(atom_rows)] for c in range(3)]

    moves = [
        [move_rows(c * atom_rows + p) for p in range(atom_rows)]
        for c in range(3)
    ]
    push_ref[...] = jnp.zeros(push_ref.shape, jnp.float32)
    far_push_ref[...] = jnp.zeros(far_push_ref.shape, jnp.float32)
    residue = project(moves)

    def expand(_, carry):
        residue, summed = carry
        change = project(spread(residue))
        residue = [now - step for now, step in zip(residue, change)]
        return residue, [a + b for a, b in zip(summed, residue)]

    residue, summed = lax.fori_loop(0, ORDER, expand, (residue, residue))
    put_pushes(summed)
    sums = inner_totals(me)
    for code, stride in enumerate(strides):
        owner = lax.rem(me + (-stride) % domains, domains)
        for part, total in enumerate(far_totals(owner, code * SUBLANES, SUBLANES)):
            sums[part] = sums[part] + total
    for part in range(atom_rows):
        lanes = slice(part * LANES, (part + 1) * LANES)
        mass = around_ref[pl.ds(me * rows.count + rows.mass + part, 1), :]
        for c in range(3):
            correction = mass * (sums[part][c : c + 1, :] + sums[part][3 + c : 4 + c, :])
            move = moves_ref[pl.ds(me * rows.disp_count + c * atom_rows + part, 1), :] - correction
            start = around_ref[pl.ds(me * rows.count + rows.coords[c] + part, 1), :]
            coords_out_ref[c, 0, :, lanes] = start + move
            velocity_out_ref[c, 0, :, lanes] = move * (1.0 / time_step)


def vmem(count):
    return [pl.BlockSpec(memory_space=pltpu.VMEM)] * count


def smem(count):
    return [pl.BlockSpec(memory_space=pltpu.SMEM)] * count


def hbm(count):
    return [pl.BlockSpec(memory_space=pltpu.HBM)] * count


def in_hbm(arrays):
    return [pltpu.with_memory_space_constraint(a, pltpu.HBM) for a in arrays]


def params(mebibytes):
    return pltpu.CompilerParams(vmem_limit_bytes=mebibytes * 1024 * 1024)


def cost(flops, moved):
    return pl.CostEstimate(flops=flops, bytes_accessed=moved, transcendentals=0)


def room_for(arrays):
    return [pltpu.VMEM(a.shape, a.dtype) for a in arrays]


def shards(
    coords,
    velocity,
    charge,
    inv_mass,
    tile_block,
    tile_atoms,
    active_tile_count,
    bond_atoms,
    cross_atoms,
    cross_side,
    cross_count,
):
    atoms = coords.shape[-1]
    tiles = tile_atoms.shape[2]
    domains = lax.axis_size("dom")
    strides = strides_of(domains)
    rows = Rows(atoms, bond_atoms.shape[-1], cross_side.shape[-1])
    whole_slab = domains == SUBLANES
    copies = domains if whole_slab else 1
    f32 = jnp.float32

    sent = (coords, charge, inv_mass, bond_atoms, cross_atoms, cross_side)
    packed, rim = pl.pallas_call(
        functools.partial(pack_kernel, rows, copies),
        out_shape=(
            jax.ShapeDtypeStruct((copies * rows.count, LANES), f32),
            jax.ShapeDtypeStruct((4 * rows.shell_rows, LANES), f32),
        ),
        in_specs=hbm(len(sent)),
        out_specs=tuple(vmem(2)),
        scratch_shapes=room_for(sent) + [pltpu.SemaphoreType.DMA((len(sent),))],
        compiler_params=params(4),
        name="pack",
    )(*in_hbm(sent))

    alone = (coords, charge, velocity, inv_mass, tile_atoms)
    own = pl.pallas_call(
        functools.partial(own_kernel, rows),
        out_shape=(
            jax.ShapeDtypeStruct((4, atoms, LANES), f32),
            jax.ShapeDtypeStruct((4, tiles, TILE), f32),
            jax.ShapeDtypeStruct((tiles, TILE), jnp.int32),
            jax.ShapeDtypeStruct((4 * rows.atom_rows, LANES), f32),
        ),
        in_specs=hbm(len(alone)),
        out_specs=tuple(vmem(4)),
        scratch_shapes=room_for(alone[:4]) + [pltpu.SemaphoreType.DMA((len(alone),))],
        compiler_params=params(4),
        cost_estimate=cost(64 * atoms * LANES, 16 * atoms * LANES),
        name="own",
    )(*in_hbm(alone))

    below = passed_along(rim, "slab", 1)
    above = passed_along(rim, "slab", -1)
    if whole_slab:
        around = from_slab(packed)

        def place():
            return [place_of(stride) for stride in strides]

    else:
        around = jnp.concatenate([packed] + [passed_along(packed, "dom", -stride) for stride in strides], axis=0)

        def place():
            return [1, 2, 3, 4]


    moves = pl.pallas_call(
        functools.partial(force_kernel, rows, copies, place),
        out_shape=jax.ShapeDtypeStruct((copies * rows.disp_count, LANES), f32),
        in_specs=smem(2) + hbm(1) + vmem(7),
        out_specs=vmem(1)[0],
        scratch_shapes=[
            pltpu.VMEM((4, 6 * rows.shell_rows, SUBLANES, LANES), f32),
            pltpu.VMEM((4, tiles, LANES), f32),
            pltpu.VMEM((3, atoms, LANES), f32),
            pltpu.SMEM(tile_block.shape, jnp.int32),
            pltpu.SemaphoreType.DMA(()),
        ],
        compiler_params=params(8),
        cost_estimate=cost(30 * tiles * TILE * TILE, 4 * around.size),
        name="force",
    )(active_tile_count, cross_count, *in_hbm([tile_block]), around, below, above, *own)

    if not whole_slab:
        return by_exchange(rows, strides, around, moves, cross_count)

    constraint_rows = rows.bond_rows + rows.slot_rows
    weight, matrix = pl.pallas_call(
        functools.partial(bond_kernel, rows, domains, strides),
        out_shape=(
            jax.ShapeDtypeStruct((constraint_rows * 3 * domains, LANES), f32),
            jax.ShapeDtypeStruct((domains * rows.matrix, atoms // 2), jnp.bfloat16),
        ),
        in_specs=vmem(1),
        out_specs=tuple(vmem(2)),
        compiler_params=params(16),
        cost_estimate=cost(8 * domains * rows.matrix * atoms // 2, 4 * around.size),
        name="bonds",
    )(around)

    every_move = from_slab(moves)

    return pl.pallas_call(
        functools.partial(solve_kernel, rows, domains, strides),
        out_shape=(
            jax.ShapeDtypeStruct(coords.shape, f32),
            jax.ShapeDtypeStruct(coords.shape, f32),
        ),
        in_specs=vmem(4),
        out_specs=tuple(vmem(2)),
        scratch_shapes=[
            pltpu.VMEM((constraint_rows, SUBLANES * domains, LANES), f32),
            pltpu.VMEM((rows.slot_rows, 4 * SUBLANES * domains, LANES), f32),
            pltpu.VMEM((5, rows.atom_rows, SUBLANES * domains, LANES), f32),
        ],
        compiler_params=params(16),
        name="solve",
    )(around, every_move, weight, matrix)


def by_exchange(rows, strides, around, moves, cross_count):
    atom_count = rows.atom_rows * LANES
    shell = rows.shell_rows * LANES
    inside = around.reshape(5, rows.count, LANES)

    def flat(at, count):
        return inside[0, at : at + count].reshape(-1)

    def neighbours(at):
        return inside[1:, at : at + rows.shell_rows].reshape(-1)

    coords = jnp.stack([flat(at, rows.atom_rows) for at in rows.coords])
    inv_mass = flat(rows.mass, rows.atom_rows)
    displace = moves[: rows.live].reshape(3, atom_count)
    left = flat(rows.bond_first, rows.bond_rows).astype(jnp.int32)
    right = flat(rows.bond_second, rows.bond_rows).astype(jnp.int32)
    cross_left = flat(rows.cross_first, rows.slot_rows).astype(jnp.int32)
    cross_right = flat(rows.cross_second, rows.slot_rows).astype(jnp.int32)
    side = flat(rows.side, rows.slot_rows).astype(jnp.int32)
    flag = moves[rows.live : rows.disp_used].reshape(-1)
    cross_index = side * shell + cross_right
    far_coords = jnp.stack([neighbours(at) for at in rows.coords])
    far_mass = neighbours(rows.mass)

    def weights(first, second, mass_first, mass_second):
        gap = first - second
        length = jnp.sqrt(jnp.sum(gap * gap, axis=0) + length_floor)
        return gap / length * lax.rsqrt(mass_first + mass_second)

    inner = weights(coords[:, left], coords[:, right], inv_mass[left], inv_mass[right])
    cross = flag * weights(
        coords[:, cross_left], far_coords[:, cross_index], inv_mass[cross_left], far_mass[cross_index]
    )

    def project(field):
        rim = field[:, :shell]
        far = jnp.concatenate([passed_along(rim, "dom", -stride) for stride in strides], axis=1)
        return (
            jnp.sum(inner * (field[:, left] - field[:, right]), axis=0),
            jnp.sum(cross * (field[:, cross_left] - far[:, cross_index]), axis=0),
        )

    def spread(values):
        pushed = inner * values[0]
        pushed_cross = cross * values[1]
        totals = jnp.zeros((3, atom_count), jnp.float32).at[:, left].add(pushed).at[:, right].add(-pushed)
        totals = totals.at[:, cross_left].add(pushed_cross)
        outward = jnp.zeros((3, 4 * shell), jnp.float32).at[:, cross_index].add(-pushed_cross)
        for code, stride in enumerate(strides):
            totals = totals.at[:, :shell].add(
                passed_along(outward[:, code * shell : (code + 1) * shell], "dom", stride)
            )
        return inv_mass * totals

    residue = project(displace)
    summed = residue
    for _ in range(ORDER):
        change = project(spread(residue))
        residue = tuple(now - step for now, step in zip(residue, change))
        summed = tuple(a + b for a, b in zip(summed, residue))
    move = displace - spread(summed)
    return (
        (coords + move).reshape(3, 1, 1, atom_count),
        (move * (1.0 / time_step)).reshape(3, 1, 1, atom_count),
    )


def solution(mesh):
    return jax.shard_map(
        shards,
        mesh=mesh,
        in_specs=(
            P(None, "slab", "dom", None),
            P(None, "slab", "dom", None),
            P("slab", "dom", None),
            P("slab", "dom", None),
            P("slab", "dom", None),
            P("slab", "dom", None, None),
            P("slab", "dom"),
            P(None, "slab", "dom", None),
            P(None, "slab", "dom", None),
            P("slab", "dom", None),
            P("slab", "dom"),
        ),
        out_specs=(P(None, "slab", "dom", None), P(None, "slab", "dom", None)),
        check_vma=False,
    )
```

```python
import functools

import jax
import jax.numpy as jnp
from jax import lax
from jax.experimental import pallas as pl
from jax.experimental.pallas import tpu as pltpu
from jax.sharding import PartitionSpec as P

TILE = 128
ORDER = 4
LANES = 128
SUBLANES = 8

time_step = 0.1
cutoff_sq = 16.0
force_scale = 4.0
length_floor = 0.25


def passed_along(array, axis, by):
    length = lax.axis_size(axis)
    return lax.ppermute(array, axis, [(i, (i + by) % length) for i in range(length)])


def first_of(domains):
    return domains - 1


def from_slab(blocks):
    length = lax.axis_size("dom")
    order = [(first_of(length) + i) % length for i in range(length)]
    return lax.all_to_all(blocks, "dom", 0, 0, axis_index_groups=[order], tiled=True)


def place_of(stride=0):
    length = lax.axis_size("dom")
    return lax.rem(lax.axis_index("dom") + (stride - first_of(length)) % length, length)


def strides_of(domains):
    row_width = max(2, domains // 8)
    return (1, -1, row_width, -row_width)


def round_up(count, step):
    return -(-count // step) * step


class Rows:
    def __init__(self, atoms, bonds, slots):
        self.atom_rows = atoms // LANES
        self.shell_rows = atoms // 2 // LANES
        self.bond_rows = bonds // LANES
        self.slot_rows = slots // LANES
        at = 0
        self.coords = []
        for _ in range(3):
            self.coords.append(at)
            at += self.atom_rows
        self.charge = at
        at += self.atom_rows
        self.mass = at
        at += self.atom_rows
        self.bond_first = at
        at += self.bond_rows
        self.bond_second = at
        at += self.bond_rows
        self.cross_first = at
        at += self.slot_rows
        self.cross_second = at
        at += self.slot_rows
        self.side = at
        at += self.slot_rows
        self.used = at
        self.count = round_up(at, SUBLANES)
        self.inner_at = (0, self.bond_rows * LANES)
        self.cross_at = 2 * self.bond_rows * LANES
        self.far_at = self.cross_at + self.slot_rows * LANES
        self.matrix = self.far_at + self.slot_rows * LANES
        self.live = 3 * self.atom_rows
        self.disp_used = self.live + self.slot_rows
        self.disp_count = round_up(self.disp_used, SUBLANES)


def take_lanes(table, lanes):
    return jnp.take_along_axis(table, lanes, axis=1, mode="promise_in_bounds")


def pick(tables, index):
    lanes = index & (LANES - 1)
    chunk = index >> 7
    result = take_lanes(tables[0], lanes)
    for k in range(1, len(tables)):
        result = jnp.where(chunk == k, take_lanes(tables[k], lanes), result)
    return result


def fetched(sources, targets, sem_ref):
    copies = [pltpu.make_async_copy(s, t, sem_ref.at[n]) for n, (s, t) in enumerate(zip(sources, targets))]
    for copy in copies:
        copy.start()
    return copies


def pack_kernel(rows, copies, *refs):
    sources, (out_ref, rim_ref), targets, sem_ref = refs[:6], refs[6:8], refs[8:14], refs[14]
    for copy in fetched(sources, targets, sem_ref):
        copy.wait()
    coords_ref, charge_ref, mass_ref, bonds_ref, cross_ref, side_ref = targets

    def put(row, value):
        for part in range(value.shape[1] // LANES):
            piece = value[:, part * LANES : (part + 1) * LANES]
            for copy in range(copies):
                out_ref[pl.ds(copy * rows.count + row + part, 1), :] = piece

    shell = rows.shell_rows * LANES
    fields = [coords_ref[c, 0] for c in range(3)] + [charge_ref[0]]
    for c in range(4):
        at = rows.coords[c] if c < 3 else rows.charge
        put(at, fields[c])
        for part in range(rows.shell_rows):
            rim_ref[pl.ds(c * rows.shell_rows + part, 1), :] = fields[c][:, part * LANES : (part + 1) * LANES]
    put(rows.mass, mass_ref[0])
    put(rows.bond_first, bonds_ref[0, 0].astype(jnp.float32))
    put(rows.bond_second, bonds_ref[1, 0].astype(jnp.float32))
    put(rows.cross_first, cross_ref[0, 0].astype(jnp.float32))
    put(rows.cross_second, cross_ref[1, 0].astype(jnp.float32))
    put(rows.side, side_ref[0].astype(jnp.float32))
    if rows.count > rows.used:
        for copy in range(copies):
            out_ref[pl.ds(copy * rows.count + rows.used, rows.count - rows.used), :] = jnp.zeros(
                (rows.count - rows.used, LANES), jnp.float32
            )


SHRINK = 1.0 / 4.0
OUT_OF_REACH = 1000.0
TILES_STEP = 4


def own_kernel(
    rows,
    coords_hbm,
    charge_hbm,
    velocity_hbm,
    mass_hbm,
    atoms_hbm,
    own_ref,
    far_ref,
    index_ref,
    motion_ref,
    coords_ref,
    charge_ref,
    velocity_ref,
    mass_ref,
    sem_ref,
):
    atom_rows = rows.atom_rows
    copies = fetched(
        (coords_hbm, charge_hbm, atoms_hbm.at[0, 0], velocity_hbm, mass_hbm),
        (coords_ref, charge_ref, index_ref, velocity_ref, mass_ref),
        sem_ref,
    )
    down = lax.broadcasted_iota(jnp.int32, (SUBLANES, LANES), 0)
    copies[0].wait()
    copies[1].wait()

    def lanes_of(part):
        return slice(part * LANES, (part + 1) * LANES)

    table = []
    for c in range(4):
        field = coords_ref[c, 0] * SHRINK if c < 3 else charge_ref[0]
        table.append(
            [jnp.broadcast_to(field[:, lanes_of(part)], (SUBLANES, LANES)) for part in range(atom_rows)]
        )
    for part in range(atom_rows):
        for group in range(LANES // SUBLANES):
            at = part * LANES + group * SUBLANES
            for c in range(4):
                value = take_lanes(table[c][part], down + group * SUBLANES)
                own_ref[c, pl.ds(at, SUBLANES), :] = value if c < 3 else value * 8.0
    copies[2].wait()
    for group in range(index_ref.shape[0] // SUBLANES):
        at = pl.ds(group * SUBLANES, SUBLANES)
        index = index_ref[at, :]
        for c in range(4):
            far_ref[c, at, :] = pick(table[c], index)
    copies[3].wait()
    copies[4].wait()
    fields = [velocity_ref[c, 0] for c in range(3)] + [mass_ref[0]]
    for c, field in enumerate(fields):
        for part in range(atom_rows):
            motion_ref[pl.ds(c * atom_rows + part, 1), :] = field[:, lanes_of(part)]


def force_kernel(
    rows,
    copies,
    place,
    live_ref,
    count_ref,
    block_hbm,
    around_ref,
    below_ref,
    above_ref,
    own_ref,
    near_ref,
    index_ref,
    motion_ref,
    out_ref,
    table_ref,
    far_ref,
    sum_ref,
    block_ref,
    sem_ref,
):
    atom_rows, shell_rows = rows.atom_rows, rows.shell_rows
    tiles = index_ref.shape[0]
    block_copy = pltpu.make_async_copy(block_hbm, block_ref, sem_ref)
    block_copy.start()
    holders = place()
    starts = [rows.coords[0], rows.coords[1], rows.coords[2], rows.charge]
    entry_rows = 6 * shell_rows

    def broadcast(row):
        return jnp.broadcast_to(row, (SUBLANES, LANES))

    for c in range(4):
        factor = SHRINK if c < 3 else 1.0
        at = 0
        for neighbour in range(4):
            base = holders[neighbour] * rows.count + starts[c]
            for part in range(shell_rows):
                table_ref[c, at] = broadcast(around_ref[pl.ds(base + part, 1), :] * factor)
                at += 1
        for slab_ref in (below_ref, above_ref):
            for part in range(shell_rows):
                table_ref[c, at] = broadcast(slab_ref[pl.ds(c * shell_rows + part, 1), :] * factor)
                at += 1

    live = live_ref[0, 0]
    down = lax.broadcasted_iota(jnp.int32, (SUBLANES, LANES), 0)
    for group in range(tiles // SUBLANES):
        at = pl.ds(group * SUBLANES, SUBLANES)
        index = index_ref[at, :]
        lanes = index & (LANES - 1)
        chunk = index >> 7
        values = [near_ref[c, at, :] for c in range(4)]
        for k in range(entry_rows):
            here = chunk == atom_rows + k
            values = [jnp.where(here, take_lanes(table_ref[c, k], lanes), values[c]) for c in range(4)]
        values[0] = jnp.where(down + group * SUBLANES < live, values[0], OUT_OF_REACH)
        for c in range(4):
            far_ref[c, at, :] = values[c]

    sum_ref[...] = jnp.zeros(sum_ref.shape, jnp.float32)
    block_copy.wait()

    softening = 1.0 / cutoff_sq

    def add_tile(tile):
        base = block_ref[0, 0, tile] * TILE
        far = [broadcast(far_ref[c, pl.ds(tile, 1), :]) for c in range(4)]
        for group in range(TILE // SUBLANES):
            at = pl.ds(pl.multiple_of(base + group * SUBLANES, SUBLANES), SUBLANES)
            gap = [own_ref[c, at, :] - far[c] for c in range(3)]
            square = gap[0] * gap[0] + gap[1] * gap[1] + gap[2] * gap[2]
            inverse = pl.reciprocal(square + softening, approx=True)
            weight = jnp.maximum(inverse - 1.0 / (1.0 + softening), 0.0)
            strength = (inverse - own_ref[3, at, :] * far[3]) * (weight * weight)
            for c in range(3):
                sum_ref[c, at, :] = sum_ref[c, at, :] + strength * gap[c]

    def add_tiles(step, _):
        for n in range(TILES_STEP):
            add_tile(step * TILES_STEP + n)
        return 0

    lax.fori_loop(0, lax.div(live + TILES_STEP - 1, TILES_STEP), add_tiles, 0)

    scale = time_step * time_step * force_scale * 4.0 / 2048.0 * (1.0 + softening) ** 2

    def lane_sums(c, part):
        return jnp.sum(sum_ref[c, pl.ds(part * LANES, LANES), :].T, axis=0, keepdims=True)

    for part in range(atom_rows):
        mass = motion_ref[pl.ds(3 * atom_rows + part, 1), :]
        for c in range(3):
            speed = motion_ref[pl.ds(c * atom_rows + part, 1), :]
            moved = time_step * speed + scale * lane_sums(c, part) * mass
            for copy in range(copies):
                out_ref[pl.ds(copy * rows.disp_count + c * atom_rows + part, 1), :] = moved
    slot = lax.broadcasted_iota(jnp.int32, (1, LANES), 1)
    for part in range(rows.slot_rows):
        flag = jnp.where(slot + part * LANES < count_ref[0, 0], 1.0, 0.0)
        for copy in range(copies):
            out_ref[pl.ds(copy * rows.disp_count + rows.live + part, 1), :] = flag
    if rows.disp_count > rows.disp_used:
        for copy in range(copies):
            out_ref[pl.ds(copy * rows.disp_count + rows.disp_used, rows.disp_count - rows.disp_used), :] = jnp.zeros(
                (rows.disp_count - rows.disp_used, LANES), jnp.float32
            )


def bond_kernel(rows, domains, strides, around_ref, weight_ref, matrix_ref):
    atom_rows, shell_rows = rows.atom_rows, rows.shell_rows

    def load(row):
        return around_ref[pl.ds(row, domains, stride=rows.count), :]

    def index(row):
        return load(row).astype(jnp.int32)

    fields = [[load(at + part) for part in range(atom_rows)] for at in rows.coords + [rows.mass]]

    def weights(first, second, row):
        gap = [first[c] - second[c] for c in range(3)]
        length_sq = gap[0] * gap[0] + gap[1] * gap[1] + gap[2] * gap[2] + length_floor
        scale = lax.rsqrt(length_sq) * lax.rsqrt(first[3] + second[3])
        return [gap[c] * scale for c in range(3)]

    at = 0
    for part in range(rows.bond_rows):
        first = index(rows.bond_first + part)
        second = index(rows.bond_second + part)
        values = weights([pick(f, first) for f in fields], [pick(f, second) for f in fields], at)
        for c in range(3):
            weight_ref[pl.ds((at * 3 + c) * domains, domains), :] = values[c]
        at += 1
    for part in range(rows.slot_rows):
        first = index(rows.cross_first + part)
        second = index(rows.cross_second + part)
        side = load(rows.side + part)
        other = [jnp.zeros((domains, LANES), jnp.float32) for _ in range(4)]
        for code, stride in enumerate(strides):
            seen = pltpu.roll(second, stride % domains, 0)
            for f in range(4):
                value = pltpu.roll(pick(fields[f][:shell_rows], seen), -stride % domains, 0)
                other[f] = jnp.where(side == code, value, other[f])
        values = weights([pick(f[:shell_rows], first) for f in fields], other, at)
        for c in range(3):
            weight_ref[pl.ds((at * 3 + c) * domains, domains), :] = values[c]
        at += 1

    down = lax.broadcasted_iota(jnp.int32, (SUBLANES, LANES), 0)
    group_rows = 4 * SUBLANES

    kind = jnp.bfloat16 if shell_rows * LANES <= 256 else jnp.float32
    across = lax.broadcasted_iota(jnp.int32, (group_rows, LANES), 1).astype(jnp.float32)
    lanes = [(across + float(block * LANES)).astype(kind) for block in range(shell_rows)]

    def column(row, step, half=0):
        row = jnp.broadcast_to(row, (SUBLANES, LANES))
        groups = [take_lanes(row, down + at) for at in range(step * group_rows, (step + 1) * group_rows, SUBLANES)]
        return (jnp.concatenate(groups, axis=0) - float(half * shell_rows * LANES)).astype(kind)

    def put(at, ends, signs):
        for block in range(shell_rows):
            value = jnp.zeros((group_rows, LANES), kind)
            for end, sign in zip(ends, signs):
                value = jnp.where(end == lanes[block], jnp.full((group_rows, LANES), sign, kind), value)
            matrix_ref[pl.ds(at, group_rows), block * LANES : (block + 1) * LANES] = value.astype(matrix_ref.dtype)

    def build(domain, _):
        start = pl.multiple_of(domain * rows.matrix, LANES)
        for part in range(rows.bond_rows):
            first = around_ref[pl.ds(domain * rows.count + rows.bond_first + part, 1), :]
            second = around_ref[pl.ds(domain * rows.count + rows.bond_second + part, 1), :]
            for step in range(LANES // group_rows):
                for half in range(2):
                    ends = (column(first, step, half), column(second, step, half))
                    put(start + rows.inner_at[half] + part * LANES + step * group_rows, ends, (1.0, -1.0))
        for part in range(rows.slot_rows):
            for row_at, to, sign in (
                (rows.cross_first, rows.cross_at, 1.0),
                (rows.cross_second, rows.far_at, -1.0),
            ):
                row = around_ref[pl.ds(domain * rows.count + row_at + part, 1), :]
                for step in range(LANES // group_rows):
                    put(start + to + part * LANES + step * group_rows, (column(row, step),), (sign,))
        return 0

    lax.fori_loop(0, domains, build, 0)


def solve_kernel(
    rows,
    domains,
    strides,
    around_ref,
    moves_ref,
    weight_ref,
    matrix_ref,
    coords_out_ref,
    velocity_out_ref,
    push_ref,
    far_push_ref,
    field_ref,
):
    atom_rows, shell_rows = rows.atom_rows, rows.shell_rows
    bond_rows, slot_rows = rows.bond_rows, rows.slot_rows
    me = place_of()

    def load(row):
        return around_ref[pl.ds(row, domains, stride=rows.count), :]

    def index(row):
        return load(row).astype(jnp.int32)

    inner_first = [index(rows.bond_first + p) for p in range(bond_rows)]
    inner_second = [index(rows.bond_second + p) for p in range(bond_rows)]
    cross_first = [index(rows.cross_first + p) for p in range(slot_rows)]
    cross_second = [index(rows.cross_second + p) for p in range(slot_rows)]
    sides = [load(rows.side + p) for p in range(slot_rows)]
    masses = [load(rows.mass + p) for p in range(atom_rows)]

    def move_rows(row):
        return moves_ref[pl.ds(row, domains, stride=rows.disp_count), :]

    def weight(at, c):
        value = weight_ref[pl.ds((at * 3 + c) * domains, domains), :]
        return value if at < bond_rows else value * live[at - bond_rows]

    live = [move_rows(rows.live + p) for p in range(slot_rows)]

    def project(fields):
        result = []
        for part in range(bond_rows):
            total = 0.0
            for c in range(3):
                ends = pick(fields[c], inner_first[part]) - pick(fields[c], inner_second[part])
                total = total + weight(part, c) * ends
            result.append(total)
        for part in range(slot_rows):
            seen = [pltpu.roll(cross_second[part], stride % domains, 0) for stride in strides]
            total = 0.0
            for c in range(3):
                shell = fields[c][:shell_rows]
                other = 0.0
                for code, stride in enumerate(strides):
                    value = pltpu.roll(pick(shell, seen[code]), -stride % domains, 0)
                    other = jnp.where(sides[part] == code, value, other)
                total = total + weight(bond_rows + part, c) * (pick(shell, cross_first[part]) - other)
            result.append(total)
        return result

    def put_pushes(values):
        for at, value in enumerate(values):
            for c in range(3):
                pushed = weight(at, c) * value
                high = pushed.astype(jnp.bfloat16).astype(jnp.float32)
                for row, part in ((c, high), (3 + c, pushed - high)):
                    push_ref[at, pl.ds(row * domains, domains), :] = part
                    if at >= bond_rows:
                        for code in range(4):
                            far_push_ref[at - bond_rows, pl.ds((code * SUBLANES + row) * domains, domains), :] = (
                                jnp.where(sides[at - bond_rows] == code, part, 0.0)
                            )

    def rows_of(ref, at, domain, first=0, count=SUBLANES):
        return ref[at, pl.ds(first * domains + domain, count, stride=domains), :]

    def side_by_side(pieces):
        return pieces[0] if len(pieces) == 1 else jnp.concatenate(pieces, axis=1)

    def product(pushes, domain, at):
        start = domain * rows.matrix + at
        if not isinstance(start, int):
            start = pl.multiple_of(start, LANES)
        result = jnp.dot(
            pushes.astype(jnp.bfloat16),
            matrix_ref[pl.ds(start, pushes.shape[1]), :],
            preferred_element_type=jnp.float32,
        )
        return [result[:, p * LANES : (p + 1) * LANES] for p in range(shell_rows)]

    def inner_totals(domain):
        pushes = side_by_side([rows_of(push_ref, at, domain) for at in range(bond_rows)])
        return product(pushes, domain, rows.inner_at[0]) + product(pushes, domain, rows.inner_at[1])

    def first_pushes(domain):
        return side_by_side([rows_of(push_ref, bond_rows + p, domain) for p in range(slot_rows)])

    def far_pushes(domain, first, count):
        return side_by_side([rows_of(far_push_ref, p, domain, first, count) for p in range(slot_rows)])

    def spread(values):
        put_pushes(values)
        for domain in range(domains):
            first = first_pushes(domain)
            far = far_pushes(domain, 0, 4 * SUBLANES)
            cross = jnp.concatenate(
                [
                    jnp.concatenate([first, jnp.zeros_like(first)], axis=1),
                    jnp.concatenate([jnp.zeros_like(far), far], axis=1),
                ],
                axis=0,
            )
            cross = product(cross, domain, rows.cross_at)
            for part, total in enumerate(inner_totals(domain)):
                if part < shell_rows:
                    total = total + cross[part][:SUBLANES, :]
                field_ref[0, part, pl.ds(domain, SUBLANES, stride=domains), :] = total
            for part, total in enumerate(cross):
                for code, stride in enumerate(strides):
                    field_ref[1 + code, part, pl.ds((domain + stride) % domains, SUBLANES, stride=domains), :] = total[
                        (1 + code) * SUBLANES : (2 + code) * SUBLANES, :
                    ]

        def field(c, part):
            pieces = [
                field_ref[source, part, pl.ds(row * domains, domains), :]
                for source in range(5 if part < shell_rows else 1)
                for row in (c, 3 + c)
            ]
            return masses[part] * functools.reduce(lambda a, b: a + b, pieces)

        return [[field(c, part) for part in range(atom_rows)] for c in range(3)]

    moves = [
        [move_rows(c * atom_rows + p) for p in range(atom_rows)]
        for c in range(3)
    ]
    push_ref[...] = jnp.zeros(push_ref.shape, jnp.float32)
    far_push_ref[...] = jnp.zeros(far_push_ref.shape, jnp.float32)
    residue = project(moves)

    def expand(_, carry):
        residue, summed = carry
        change = project(spread(residue))
        residue = [now - step for now, step in zip(residue, change)]
        return residue, [a + b for a, b in zip(summed, residue)]

    residue, summed = lax.fori_loop(0, ORDER, expand, (residue, residue))
    put_pushes(summed)
    sums = inner_totals(me)
    shares = [product(first_pushes(me), me, rows.cross_at)]
    for code, stride in enumerate(strides):
        owner = lax.rem(me + (-stride) % domains, domains)
        shares.append(product(far_pushes(owner, code * SUBLANES, SUBLANES), owner, rows.far_at))
    for part in range(shell_rows):
        for share in shares:
            sums[part] = sums[part] + share[part]
    for part in range(atom_rows):
        lanes = slice(part * LANES, (part + 1) * LANES)
        mass = around_ref[pl.ds(me * rows.count + rows.mass + part, 1), :]
        for c in range(3):
            correction = mass * (sums[part][c : c + 1, :] + sums[part][3 + c : 4 + c, :])
            move = moves_ref[pl.ds(me * rows.disp_count + c * atom_rows + part, 1), :] - correction
            start = around_ref[pl.ds(me * rows.count + rows.coords[c] + part, 1), :]
            coords_out_ref[c, 0, :, lanes] = start + move
            velocity_out_ref[c, 0, :, lanes] = move * (1.0 / time_step)


def vmem(count):
    return [pl.BlockSpec(memory_space=pltpu.VMEM)] * count


def smem(count):
    return [pl.BlockSpec(memory_space=pltpu.SMEM)] * count


def hbm(count):
    return [pl.BlockSpec(memory_space=pltpu.HBM)] * count


def in_hbm(arrays):
    return [pltpu.with_memory_space_constraint(a, pltpu.HBM) for a in arrays]


def params(mebibytes):
    return pltpu.CompilerParams(vmem_limit_bytes=mebibytes * 1024 * 1024)


def cost(flops, moved):
    return pl.CostEstimate(flops=flops, bytes_accessed=moved, transcendentals=0)


def room_for(arrays):
    return [pltpu.VMEM(a.shape, a.dtype) for a in arrays]


def shards(
    coords,
    velocity,
    charge,
    inv_mass,
    tile_block,
    tile_atoms,
    active_tile_count,
    bond_atoms,
    cross_atoms,
    cross_side,
    cross_count,
):
    atoms = coords.shape[-1]
    tiles = tile_atoms.shape[2]
    domains = lax.axis_size("dom")
    strides = strides_of(domains)
    rows = Rows(atoms, bond_atoms.shape[-1], cross_side.shape[-1])
    whole_slab = domains == SUBLANES
    copies = domains if whole_slab else 1
    f32 = jnp.float32

    sent = (coords, charge, inv_mass, bond_atoms, cross_atoms, cross_side)
    packed, rim = pl.pallas_call(
        functools.partial(pack_kernel, rows, copies),
        out_shape=(
            jax.ShapeDtypeStruct((copies * rows.count, LANES), f32),
            jax.ShapeDtypeStruct((4 * rows.shell_rows, LANES), f32),
        ),
        in_specs=hbm(len(sent)),
        out_specs=tuple(vmem(2)),
        scratch_shapes=room_for(sent) + [pltpu.SemaphoreType.DMA((len(sent),))],
        compiler_params=params(4),
        name="pack",
    )(*in_hbm(sent))

    alone = (coords, charge, velocity, inv_mass, tile_atoms)
    own = pl.pallas_call(
        functools.partial(own_kernel, rows),
        out_shape=(
            jax.ShapeDtypeStruct((4, atoms, LANES), f32),
            jax.ShapeDtypeStruct((4, tiles, TILE), f32),
            jax.ShapeDtypeStruct((tiles, TILE), jnp.int32),
            jax.ShapeDtypeStruct((4 * rows.atom_rows, LANES), f32),
        ),
        in_specs=hbm(len(alone)),
        out_specs=tuple(vmem(4)),
        scratch_shapes=room_for(alone[:4]) + [pltpu.SemaphoreType.DMA((len(alone),))],
        compiler_params=params(4),
        cost_estimate=cost(64 * atoms * LANES, 16 * atoms * LANES),
        name="own",
    )(*in_hbm(alone))

    below = passed_along(rim, "slab", 1)
    above = passed_along(rim, "slab", -1)
    if whole_slab:
        around = from_slab(packed)

        def place():
            return [place_of(stride) for stride in strides]

    else:
        around = jnp.concatenate([packed] + [passed_along(packed, "dom", -stride) for stride in strides], axis=0)

        def place():
            return [1, 2, 3, 4]


    moves = pl.pallas_call(
        functools.partial(force_kernel, rows, copies, place),
        out_shape=jax.ShapeDtypeStruct((copies * rows.disp_count, LANES), f32),
        in_specs=smem(2) + hbm(1) + vmem(7),
        out_specs=vmem(1)[0],
        scratch_shapes=[
            pltpu.VMEM((4, 6 * rows.shell_rows, SUBLANES, LANES), f32),
            pltpu.VMEM((4, tiles, LANES), f32),
            pltpu.VMEM((3, atoms, LANES), f32),
            pltpu.SMEM(tile_block.shape, jnp.int32),
            pltpu.SemaphoreType.DMA(()),
        ],
        compiler_params=params(8),
        cost_estimate=cost(30 * tiles * TILE * TILE, 4 * around.size),
        name="force",
    )(active_tile_count, cross_count, *in_hbm([tile_block]), around, below, above, *own)

    if not whole_slab:
        return by_exchange(rows, strides, around, moves, cross_count)

    constraint_rows = rows.bond_rows + rows.slot_rows
    weight, matrix = pl.pallas_call(
        functools.partial(bond_kernel, rows, domains, strides),
        out_shape=(
            jax.ShapeDtypeStruct((constraint_rows * 3 * domains, LANES), f32),
            jax.ShapeDtypeStruct((domains * rows.matrix, atoms // 2), jnp.bfloat16),
        ),
        in_specs=vmem(1),
        out_specs=tuple(vmem(2)),
        compiler_params=params(16),
        cost_estimate=cost(8 * domains * rows.matrix * atoms // 2, 4 * around.size),
        name="bonds",
    )(around)

    every_move = from_slab(moves)

    return pl.pallas_call(
        functools.partial(solve_kernel, rows, domains, strides),
        out_shape=(
            jax.ShapeDtypeStruct(coords.shape, f32),
            jax.ShapeDtypeStruct(coords.shape, f32),
        ),
        in_specs=vmem(4),
        out_specs=tuple(vmem(2)),
        scratch_shapes=[
            pltpu.VMEM((constraint_rows, SUBLANES * domains, LANES), f32),
            pltpu.VMEM((rows.slot_rows, 4 * SUBLANES * domains, LANES), f32),
            pltpu.VMEM((5, rows.atom_rows, SUBLANES * domains, LANES), f32),
        ],
        compiler_params=params(16),
        name="solve",
    )(around, every_move, weight, matrix)


def by_exchange(rows, strides, around, moves, cross_count):
    atom_count = rows.atom_rows * LANES
    shell = rows.shell_rows * LANES
    inside = around.reshape(5, rows.count, LANES)

    def flat(at, count):
        return inside[0, at : at + count].reshape(-1)

    def neighbours(at):
        return inside[1:, at : at + rows.shell_rows].reshape(-1)

    coords = jnp.stack([flat(at, rows.atom_rows) for at in rows.coords])
    inv_mass = flat(rows.mass, rows.atom_rows)
    displace = moves[: rows.live].reshape(3, atom_count)
    left = flat(rows.bond_first, rows.bond_rows).astype(jnp.int32)
    right = flat(rows.bond_second, rows.bond_rows).astype(jnp.int32)
    cross_left = flat(rows.cross_first, rows.slot_rows).astype(jnp.int32)
    cross_right = flat(rows.cross_second, rows.slot_rows).astype(jnp.int32)
    side = flat(rows.side, rows.slot_rows).astype(jnp.int32)
    flag = moves[rows.live : rows.disp_used].reshape(-1)
    cross_index = side * shell + cross_right
    far_coords = jnp.stack([neighbours(at) for at in rows.coords])
    far_mass = neighbours(rows.mass)

    def weights(first, second, mass_first, mass_second):
        gap = first - second
        length = jnp.sqrt(jnp.sum(gap * gap, axis=0) + length_floor)
        return gap / length * lax.rsqrt(mass_first + mass_second)

    inner = weights(coords[:, left], coords[:, right], inv_mass[left], inv_mass[right])
    cross = flag * weights(
        coords[:, cross_left], far_coords[:, cross_index], inv_mass[cross_left], far_mass[cross_index]
    )

    def project(field):
        rim = field[:, :shell]
        far = jnp.concatenate([passed_along(rim, "dom", -stride) for stride in strides], axis=1)
        return (
            jnp.sum(inner * (field[:, left] - field[:, right]), axis=0),
            jnp.sum(cross * (field[:, cross_left] - far[:, cross_index]), axis=0),
        )

    def spread(values):
        pushed = inner * values[0]
        pushed_cross = cross * values[1]
        totals = jnp.zeros((3, atom_count), jnp.float32).at[:, left].add(pushed).at[:, right].add(-pushed)
        totals = totals.at[:, cross_left].add(pushed_cross)
        outward = jnp.zeros((3, 4 * shell), jnp.float32).at[:, cross_index].add(-pushed_cross)
        for code, stride in enumerate(strides):
            totals = totals.at[:, :shell].add(
                passed_along(outward[:, code * shell : (code + 1) * shell], "dom", stride)
            )
        return inv_mass * totals

    residue = project(displace)
    summed = residue
    for _ in range(ORDER):
        change = project(spread(residue))
        residue = tuple(now - step for now, step in zip(residue, change))
        summed = tuple(a + b for a, b in zip(summed, residue))
    move = displace - spread(summed)
    return (
        (coords + move).reshape(3, 1, 1, atom_count),
        (move * (1.0 / time_step)).reshape(3, 1, 1, atom_count),
    )


def solution(mesh):
    return jax.shard_map(
        shards,
        mesh=mesh,
        in_specs=(
            P(None, "slab", "dom", None),
            P(None, "slab", "dom", None),
            P("slab", "dom", None),
            P("slab", "dom", None),
            P("slab", "dom", None),
            P("slab", "dom", None, None),
            P("slab", "dom"),
            P(None, "slab", "dom", None),
            P(None, "slab", "dom", None),
            P("slab", "dom", None),
            P("slab", "dom"),
        ),
        out_specs=(P(None, "slab", "dom", None), P(None, "slab", "dom", None)),
        check_vma=False,
    )
```

```python
import functools

import jax
import jax.numpy as jnp
from jax import lax
from jax.experimental import pallas as pl
from jax.experimental.pallas import tpu as pltpu
from jax.sharding import PartitionSpec as P

TILE = 128
ORDER = 4
LANES = 128
SUBLANES = 8

time_step = 0.1
cutoff_sq = 16.0
force_scale = 4.0
length_floor = 0.25


def passed_along(array, axis, by):
    length = lax.axis_size(axis)
    return lax.ppermute(array, axis, [(i, (i + by) % length) for i in range(length)])


def first_of(domains):
    return domains - 1


def from_slab(blocks):
    length = lax.axis_size("dom")
    order = [(first_of(length) + i) % length for i in range(length)]
    return lax.all_to_all(blocks, "dom", 0, 0, axis_index_groups=[order], tiled=True)


def place_of(stride=0):
    length = lax.axis_size("dom")
    return lax.rem(lax.axis_index("dom") + (stride - first_of(length)) % length, length)


def strides_of(domains):
    row_width = max(2, domains // 8)
    return (1, -1, row_width, -row_width)


def round_up(count, step):
    return -(-count // step) * step


class Rows:
    def __init__(self, atoms, bonds, slots):
        self.atom_rows = atoms // LANES
        self.shell_rows = atoms // 2 // LANES
        self.bond_rows = bonds // LANES
        self.slot_rows = slots // LANES
        at = 0
        self.coords = []
        for _ in range(3):
            self.coords.append(at)
            at += self.atom_rows
        self.charge = at
        at += self.atom_rows
        self.mass = at
        at += self.atom_rows
        self.bond_first = at
        at += self.bond_rows
        self.bond_second = at
        at += self.bond_rows
        self.cross_first = at
        at += self.slot_rows
        self.cross_second = at
        at += self.slot_rows
        self.side = at
        at += self.slot_rows
        self.used = at
        self.count = round_up(at, SUBLANES)
        self.shell_terms = (self.bond_rows + self.slot_rows) * LANES
        self.inner_at = (0, self.shell_terms)
        self.cross_at = self.bond_rows * LANES
        self.far_at = self.shell_terms + self.bond_rows * LANES
        self.matrix = self.far_at + self.slot_rows * LANES
        self.live = 3 * self.atom_rows
        self.disp_used = self.live + self.slot_rows
        self.disp_count = round_up(self.disp_used, SUBLANES)


def take_lanes(table, lanes):
    return jnp.take_along_axis(table, lanes, axis=1, mode="promise_in_bounds")


def pick(tables, index):
    lanes = index & (LANES - 1)
    chunk = index >> 7
    result = take_lanes(tables[0], lanes)
    for k in range(1, len(tables)):
        result = jnp.where(chunk == k, take_lanes(tables[k], lanes), result)
    return result


def fetched(sources, targets, sem_ref):
    copies = [pltpu.make_async_copy(s, t, sem_ref.at[n]) for n, (s, t) in enumerate(zip(sources, targets))]
    for copy in copies:
        copy.start()
    return copies


def pack_kernel(rows, copies, *refs):
    sources, (out_ref, rim_ref), targets, sem_ref = refs[:6], refs[6:8], refs[8:14], refs[14]
    for copy in fetched(sources, targets, sem_ref):
        copy.wait()
    coords_ref, charge_ref, mass_ref, bonds_ref, cross_ref, side_ref = targets

    def put(row, value):
        for part in range(value.shape[1] // LANES):
            piece = value[:, part * LANES : (part + 1) * LANES]
            for copy in range(copies):
                out_ref[pl.ds(copy * rows.count + row + part, 1), :] = piece

    shell = rows.shell_rows * LANES
    fields = [coords_ref[c, 0] for c in range(3)] + [charge_ref[0]]
    for c in range(4):
        at = rows.coords[c] if c < 3 else rows.charge
        put(at, fields[c])
        for part in range(rows.shell_rows):
            rim_ref[pl.ds(c * rows.shell_rows + part, 1), :] = fields[c][:, part * LANES : (part + 1) * LANES]
    put(rows.mass, mass_ref[0])
    put(rows.bond_first, bonds_ref[0, 0].astype(jnp.float32))
    put(rows.bond_second, bonds_ref[1, 0].astype(jnp.float32))
    put(rows.cross_first, cross_ref[0, 0].astype(jnp.float32))
    put(rows.cross_second, cross_ref[1, 0].astype(jnp.float32))
    put(rows.side, side_ref[0].astype(jnp.float32))
    if rows.count > rows.used:
        for copy in range(copies):
            out_ref[pl.ds(copy * rows.count + rows.used, rows.count - rows.used), :] = jnp.zeros(
                (rows.count - rows.used, LANES), jnp.float32
            )


SHRINK = 1.0 / 4.0
OUT_OF_REACH = 1000.0
TILES_STEP = 4
PIECE = 32


def own_kernel(
    rows,
    coords_hbm,
    charge_hbm,
    velocity_hbm,
    mass_hbm,
    atoms_hbm,
    own_ref,
    far_ref,
    index_ref,
    motion_ref,
    coords_ref,
    charge_ref,
    velocity_ref,
    mass_ref,
    sem_ref,
):
    atom_rows = rows.atom_rows
    copies = fetched(
        (coords_hbm, charge_hbm, atoms_hbm.at[0, 0], velocity_hbm, mass_hbm),
        (coords_ref, charge_ref, index_ref, velocity_ref, mass_ref),
        sem_ref,
    )
    down = lax.broadcasted_iota(jnp.int32, (SUBLANES, LANES), 0)
    copies[0].wait()
    copies[1].wait()

    def lanes_of(part):
        return slice(part * LANES, (part + 1) * LANES)

    table = []
    for c in range(4):
        field = coords_ref[c, 0] * SHRINK if c < 3 else charge_ref[0]
        table.append(
            [jnp.broadcast_to(field[:, lanes_of(part)], (SUBLANES, LANES)) for part in range(atom_rows)]
        )
    for part in range(atom_rows):
        for group in range(LANES // SUBLANES):
            at = part * LANES + group * SUBLANES
            for c in range(4):
                value = take_lanes(table[c][part], down + group * SUBLANES)
                own_ref[c, pl.ds(at, SUBLANES), :] = value if c < 3 else value * 8.0
    copies[2].wait()
    for group in range(index_ref.shape[0] // SUBLANES):
        at = pl.ds(group * SUBLANES, SUBLANES)
        index = index_ref[at, :]
        for c in range(4):
            far_ref[c, at, :] = pick(table[c], index)
    copies[3].wait()
    copies[4].wait()
    fields = [velocity_ref[c, 0] for c in range(3)] + [mass_ref[0]]
    for c, field in enumerate(fields):
        for part in range(atom_rows):
            motion_ref[pl.ds(c * atom_rows + part, 1), :] = field[:, lanes_of(part)]


def force_kernel(
    rows,
    copies,
    place,
    live_ref,
    count_ref,
    block_hbm,
    around_ref,
    below_ref,
    above_ref,
    own_ref,
    near_ref,
    index_ref,
    motion_ref,
    out_ref,
    table_ref,
    far_ref,
    sum_ref,
    block_ref,
    sem_ref,
):
    atom_rows, shell_rows = rows.atom_rows, rows.shell_rows
    tiles = index_ref.shape[0]
    block_copy = pltpu.make_async_copy(block_hbm, block_ref, sem_ref)
    block_copy.start()
    holders = place()
    starts = [rows.coords[0], rows.coords[1], rows.coords[2], rows.charge]
    entry_rows = 6 * shell_rows

    def broadcast(row):
        return jnp.broadcast_to(row, (SUBLANES, LANES))

    for c in range(4):
        factor = SHRINK if c < 3 else 1.0
        at = 0
        for neighbour in range(4):
            base = holders[neighbour] * rows.count + starts[c]
            for part in range(shell_rows):
                table_ref[c, at] = broadcast(around_ref[pl.ds(base + part, 1), :] * factor)
                at += 1
        for slab_ref in (below_ref, above_ref):
            for part in range(shell_rows):
                table_ref[c, at] = broadcast(slab_ref[pl.ds(c * shell_rows + part, 1), :] * factor)
                at += 1

    live = live_ref[0, 0]
    down = lax.broadcasted_iota(jnp.int32, (SUBLANES, LANES), 0)
    for group in range(tiles // SUBLANES):
        at = pl.ds(group * SUBLANES, SUBLANES)
        index = index_ref[at, :]
        lanes = index & (LANES - 1)
        chunk = index >> 7
        values = [near_ref[c, at, :] for c in range(4)]
        for k in range(entry_rows):
            here = chunk == atom_rows + k
            values = [jnp.where(here, take_lanes(table_ref[c, k], lanes), values[c]) for c in range(4)]
        values[0] = jnp.where(down + group * SUBLANES < live, values[0], OUT_OF_REACH)
        for c in range(4):
            far_ref[c, at, :] = values[c]

    sum_ref[...] = jnp.zeros(sum_ref.shape, jnp.float32)
    block_copy.wait()

    softening = 1.0 / cutoff_sq

    def add_tile(tile):
        base = block_ref[0, 0, tile] * TILE
        far = [jnp.broadcast_to(far_ref[c, pl.ds(tile, 1), :], (PIECE, LANES)) for c in range(4)]
        for piece in range(TILE // PIECE):
            at = pl.ds(pl.multiple_of(base + piece * PIECE, PIECE), PIECE)
            gap = [own_ref[c, at, :] - far[c] for c in range(3)]
            square = gap[0] * gap[0] + gap[1] * gap[1] + gap[2] * gap[2]
            inverse = pl.reciprocal(square + softening, approx=True)
            weight = jnp.maximum(inverse - 1.0 / (1.0 + softening), 0.0)
            strength = (inverse - own_ref[3, at, :] * far[3]) * (weight * weight)
            for c in range(3):
                sum_ref[c, at, :] = sum_ref[c, at, :] + strength * gap[c]

    def add_tiles(step, _):
        for n in range(TILES_STEP):
            add_tile(step * TILES_STEP + n)
        return 0

    lax.fori_loop(0, lax.div(live + TILES_STEP - 1, TILES_STEP), add_tiles, 0)

    scale = time_step * time_step * force_scale * 4.0 / 2048.0 * (1.0 + softening) ** 2

    def lane_sums(c, part):
        return jnp.sum(sum_ref[c, pl.ds(part * LANES, LANES), :].T, axis=0, keepdims=True)

    for part in range(atom_rows):
        mass = motion_ref[pl.ds(3 * atom_rows + part, 1), :]
        for c in range(3):
            speed = motion_ref[pl.ds(c * atom_rows + part, 1), :]
            moved = time_step * speed + scale * lane_sums(c, part) * mass
            for copy in range(copies):
                out_ref[pl.ds(copy * rows.disp_count + c * atom_rows + part, 1), :] = moved
    slot = lax.broadcasted_iota(jnp.int32, (1, LANES), 1)
    for part in range(rows.slot_rows):
        flag = jnp.where(slot + part * LANES < count_ref[0, 0], 1.0, 0.0)
        for copy in range(copies):
            out_ref[pl.ds(copy * rows.disp_count + rows.live + part, 1), :] = flag
    if rows.disp_count > rows.disp_used:
        for copy in range(copies):
            out_ref[pl.ds(copy * rows.disp_count + rows.disp_used, rows.disp_count - rows.disp_used), :] = jnp.zeros(
                (rows.disp_count - rows.disp_used, LANES), jnp.float32
            )


def bond_kernel(rows, domains, strides, around_ref, weight_ref, matrix_ref):
    atom_rows, shell_rows = rows.atom_rows, rows.shell_rows

    def load(row):
        return around_ref[pl.ds(row, domains, stride=rows.count), :]

    def index(row):
        return load(row).astype(jnp.int32)

    fields = [[load(at + part) for part in range(atom_rows)] for at in rows.coords + [rows.mass]]

    def weights(first, second, row):
        gap = [first[c] - second[c] for c in range(3)]
        length_sq = gap[0] * gap[0] + gap[1] * gap[1] + gap[2] * gap[2] + length_floor
        scale = lax.rsqrt(length_sq) * lax.rsqrt(first[3] + second[3])
        return [gap[c] * scale for c in range(3)]

    at = 0
    for part in range(rows.bond_rows):
        first = index(rows.bond_first + part)
        second = index(rows.bond_second + part)
        values = weights([pick(f, first) for f in fields], [pick(f, second) for f in fields], at)
        for c in range(3):
            weight_ref[pl.ds((at * 3 + c) * domains, domains), :] = values[c]
        at += 1
    for part in range(rows.slot_rows):
        first = index(rows.cross_first + part)
        second = index(rows.cross_second + part)
        side = load(rows.side + part)
        other = [jnp.zeros((domains, LANES), jnp.float32) for _ in range(4)]
        for code, stride in enumerate(strides):
            seen = pltpu.roll(second, stride % domains, 0)
            for f in range(4):
                value = pltpu.roll(pick(fields[f][:shell_rows], seen), -stride % domains, 0)
                other[f] = jnp.where(side == code, value, other[f])
        values = weights([pick(f[:shell_rows], first) for f in fields], other, at)
        for c in range(3):
            weight_ref[pl.ds((at * 3 + c) * domains, domains), :] = values[c]
        at += 1

    down = lax.broadcasted_iota(jnp.int32, (SUBLANES, LANES), 0)
    group_rows = 4 * SUBLANES

    kind = jnp.bfloat16 if shell_rows * LANES <= 256 else jnp.float32
    across = lax.broadcasted_iota(jnp.int32, (group_rows, LANES), 1).astype(jnp.float32)
    lanes = [(across + float(block * LANES)).astype(kind) for block in range(shell_rows)]

    def column(row, step, half=0):
        row = jnp.broadcast_to(row, (SUBLANES, LANES))
        groups = [take_lanes(row, down + at) for at in range(step * group_rows, (step + 1) * group_rows, SUBLANES)]
        return (jnp.concatenate(groups, axis=0) - float(half * shell_rows * LANES)).astype(kind)

    def put(at, ends, signs):
        for block in range(shell_rows):
            value = jnp.zeros((group_rows, LANES), kind)
            for end, sign in zip(ends, signs):
                value = jnp.where(end == lanes[block], jnp.full((group_rows, LANES), sign, kind), value)
            matrix_ref[pl.ds(at, group_rows), block * LANES : (block + 1) * LANES] = value.astype(matrix_ref.dtype)

    def build(domain, _):
        start = pl.multiple_of(domain * rows.matrix, LANES)
        for part in range(rows.bond_rows):
            first = around_ref[pl.ds(domain * rows.count + rows.bond_first + part, 1), :]
            second = around_ref[pl.ds(domain * rows.count + rows.bond_second + part, 1), :]
            for step in range(LANES // group_rows):
                for half in range(2):
                    ends = (column(first, step, half), column(second, step, half))
                    put(start + rows.inner_at[half] + part * LANES + step * group_rows, ends, (1.0, -1.0))
        for part in range(rows.slot_rows):
            for row_at, to, sign in (
                (rows.cross_first, rows.cross_at, 1.0),
                (rows.cross_second, rows.far_at, -1.0),
            ):
                row = around_ref[pl.ds(domain * rows.count + row_at + part, 1), :]
                for step in range(LANES // group_rows):
                    put(start + to + part * LANES + step * group_rows, (column(row, step),), (sign,))
        return 0

    lax.fori_loop(0, domains, build, 0)


def solve_kernel(
    rows,
    domains,
    strides,
    around_ref,
    moves_ref,
    weight_ref,
    matrix_ref,
    coords_out_ref,
    velocity_out_ref,
    push_ref,
    far_push_ref,
    field_ref,
):
    atom_rows, shell_rows = rows.atom_rows, rows.shell_rows
    bond_rows, slot_rows = rows.bond_rows, rows.slot_rows
    me = place_of()

    def load(row):
        return around_ref[pl.ds(row, domains, stride=rows.count), :]

    def index(row):
        return load(row).astype(jnp.int32)

    inner_first = [index(rows.bond_first + p) for p in range(bond_rows)]
    inner_second = [index(rows.bond_second + p) for p in range(bond_rows)]
    cross_first = [index(rows.cross_first + p) for p in range(slot_rows)]
    cross_second = [index(rows.cross_second + p) for p in range(slot_rows)]
    sides = [load(rows.side + p) for p in range(slot_rows)]
    masses = [load(rows.mass + p) for p in range(atom_rows)]

    def move_rows(row):
        return moves_ref[pl.ds(row, domains, stride=rows.disp_count), :]

    def weight(at, c):
        value = weight_ref[pl.ds((at * 3 + c) * domains, domains), :]
        return value if at < bond_rows else value * live[at - bond_rows]

    live = [move_rows(rows.live + p) for p in range(slot_rows)]

    def project(fields):
        result = []
        for part in range(bond_rows):
            total = 0.0
            for c in range(3):
                ends = pick(fields[c], inner_first[part]) - pick(fields[c], inner_second[part])
                total = total + weight(part, c) * ends
            result.append(total)
        for part in range(slot_rows):
            seen = [pltpu.roll(cross_second[part], stride % domains, 0) for stride in strides]
            total = 0.0
            for c in range(3):
                shell = fields[c][:shell_rows]
                other = 0.0
                for code, stride in enumerate(strides):
                    value = pltpu.roll(pick(shell, seen[code]), -stride % domains, 0)
                    other = jnp.where(sides[part] == code, value, other)
                total = total + weight(bond_rows + part, c) * (pick(shell, cross_first[part]) - other)
            result.append(total)
        return result

    def put_pushes(values):
        for at, value in enumerate(values):
            for c in range(3):
                pushed = weight(at, c) * value
                high = pushed.astype(jnp.bfloat16).astype(jnp.float32)
                for row, part in ((c, high), (3 + c, pushed - high)):
                    push_ref[at, pl.ds(row * domains, domains), :] = part
                    if at >= bond_rows:
                        for code in range(4):
                            far_push_ref[at - bond_rows, pl.ds((code * SUBLANES + row) * domains, domains), :] = (
                                jnp.where(sides[at - bond_rows] == code, part, 0.0)
                            )

    def pushes_of(at, domain):
        return push_ref[at, pl.ds(domain, SUBLANES, stride=domains), :].astype(jnp.bfloat16)

    def product(pushes, domain, at):
        start = domain * rows.matrix + at
        if not isinstance(start, int):
            start = pl.multiple_of(start, LANES)
        pushes = pushes[0] if len(pushes) == 1 else jnp.concatenate(pushes, axis=1)
        result = jnp.dot(
            pushes, matrix_ref[pl.ds(start, pushes.shape[1]), :], preferred_element_type=jnp.float32
        )
        return [result[:, p * LANES : (p + 1) * LANES] for p in range(shell_rows)]

    def inner_totals(domain):
        pushes = [pushes_of(at, domain) for at in range(bond_rows + slot_rows)]
        return product(pushes, domain, 0) + product(pushes[:bond_rows], domain, rows.shell_terms)

    def far_totals(domain, first_row, count):
        pushes = [
            far_push_ref[p, pl.ds(first_row * domains + domain, count, stride=domains), :].astype(jnp.bfloat16)
            for p in range(slot_rows)
        ]
        return product(pushes, domain, rows.far_at)

    def spread(values):
        put_pushes(values)
        for domain in range(domains):
            for part, total in enumerate(inner_totals(domain)):
                field_ref[0, part, pl.ds(domain, SUBLANES, stride=domains), :] = total
            for part, total in enumerate(far_totals(domain, 0, 4 * SUBLANES)):
                for code, stride in enumerate(strides):
                    field_ref[1 + code, part, pl.ds((domain + stride) % domains, SUBLANES, stride=domains), :] = total[
                        code * SUBLANES : (code + 1) * SUBLANES, :
                    ]

        def field(c, part):
            pieces = [
                field_ref[source, part, pl.ds(row * domains, domains), :]
                for source in range(5 if part < shell_rows else 1)
                for row in (c, 3 + c)
            ]
            return masses[part] * functools.reduce(lambda a, b: a + b, pieces)

        return [[field(c, part) for part in range(atom_rows)] for c in range(3)]

    moves = [
        [move_rows(c * atom_rows + p) for p in range(atom_rows)]
        for c in range(3)
    ]
    push_ref[...] = jnp.zeros(push_ref.shape, jnp.float32)
    far_push_ref[...] = jnp.zeros(far_push_ref.shape, jnp.float32)
    residue = project(moves)

    def expand(_, carry):
        residue, summed = carry
        change = project(spread(residue))
        residue = [now - step for now, step in zip(residue, change)]
        return residue, [a + b for a, b in zip(summed, residue)]

    residue, summed = lax.fori_loop(0, ORDER, expand, (residue, residue))
    put_pushes(summed)
    sums = inner_totals(me)
    for code, stride in enumerate(strides):
        owner = lax.rem(me + (-stride) % domains, domains)
        for part, total in enumerate(far_totals(owner, code * SUBLANES, SUBLANES)):
            sums[part] = sums[part] + total
    for part in range(atom_rows):
        lanes = slice(part * LANES, (part + 1) * LANES)
        mass = around_ref[pl.ds(me * rows.count + rows.mass + part, 1), :]
        for c in range(3):
            correction = mass * (sums[part][c : c + 1, :] + sums[part][3 + c : 4 + c, :])
            move = moves_ref[pl.ds(me * rows.disp_count + c * atom_rows + part, 1), :] - correction
            start = around_ref[pl.ds(me * rows.count + rows.coords[c] + part, 1), :]
            coords_out_ref[c, 0, :, lanes] = start + move
            velocity_out_ref[c, 0, :, lanes] = move * (1.0 / time_step)


def vmem(count):
    return [pl.BlockSpec(memory_space=pltpu.VMEM)] * count


def smem(count):
    return [pl.BlockSpec(memory_space=pltpu.SMEM)] * count


def hbm(count):
    return [pl.BlockSpec(memory_space=pltpu.HBM)] * count


def in_hbm(arrays):
    return [pltpu.with_memory_space_constraint(a, pltpu.HBM) for a in arrays]


def params(mebibytes):
    return pltpu.CompilerParams(vmem_limit_bytes=mebibytes * 1024 * 1024)


def cost(flops, moved):
    return pl.CostEstimate(flops=flops, bytes_accessed=moved, transcendentals=0)


def room_for(arrays):
    return [pltpu.VMEM(a.shape, a.dtype) for a in arrays]


def shards(
    coords,
    velocity,
    charge,
    inv_mass,
    tile_block,
    tile_atoms,
    active_tile_count,
    bond_atoms,
    cross_atoms,
    cross_side,
    cross_count,
):
    atoms = coords.shape[-1]
    tiles = tile_atoms.shape[2]
    domains = lax.axis_size("dom")
    strides = strides_of(domains)
    rows = Rows(atoms, bond_atoms.shape[-1], cross_side.shape[-1])
    whole_slab = domains == SUBLANES
    copies = domains if whole_slab else 1
    f32 = jnp.float32

    sent = (coords, charge, inv_mass, bond_atoms, cross_atoms, cross_side)
    packed, rim = pl.pallas_call(
        functools.partial(pack_kernel, rows, copies),
        out_shape=(
            jax.ShapeDtypeStruct((copies * rows.count, LANES), f32),
            jax.ShapeDtypeStruct((4 * rows.shell_rows, LANES), f32),
        ),
        in_specs=hbm(len(sent)),
        out_specs=tuple(vmem(2)),
        scratch_shapes=room_for(sent) + [pltpu.SemaphoreType.DMA((len(sent),))],
        compiler_params=params(4),
        name="pack",
    )(*in_hbm(sent))

    alone = (coords, charge, velocity, inv_mass, tile_atoms)
    own = pl.pallas_call(
        functools.partial(own_kernel, rows),
        out_shape=(
            jax.ShapeDtypeStruct((4, atoms, LANES), f32),
            jax.ShapeDtypeStruct((4, tiles, TILE), f32),
            jax.ShapeDtypeStruct((tiles, TILE), jnp.int32),
            jax.ShapeDtypeStruct((4 * rows.atom_rows, LANES), f32),
        ),
        in_specs=hbm(len(alone)),
        out_specs=tuple(vmem(4)),
        scratch_shapes=room_for(alone[:4]) + [pltpu.SemaphoreType.DMA((len(alone),))],
        compiler_params=params(4),
        cost_estimate=cost(64 * atoms * LANES, 16 * atoms * LANES),
        name="own",
    )(*in_hbm(alone))

    below = passed_along(rim, "slab", 1)
    above = passed_along(rim, "slab", -1)
    if whole_slab:
        around = from_slab(packed)

        def place():
            return [place_of(stride) for stride in strides]

    else:
        around = jnp.concatenate([packed] + [passed_along(packed, "dom", -stride) for stride in strides], axis=0)

        def place():
            return [1, 2, 3, 4]


    moves = pl.pallas_call(
        functools.partial(force_kernel, rows, copies, place),
        out_shape=jax.ShapeDtypeStruct((copies * rows.disp_count, LANES), f32),
        in_specs=smem(2) + hbm(1) + vmem(7),
        out_specs=vmem(1)[0],
        scratch_shapes=[
            pltpu.VMEM((4, 6 * rows.shell_rows, SUBLANES, LANES), f32),
            pltpu.VMEM((4, tiles, LANES), f32),
            pltpu.VMEM((3, atoms, LANES), f32),
            pltpu.SMEM(tile_block.shape, jnp.int32),
            pltpu.SemaphoreType.DMA(()),
        ],
        compiler_params=params(8),
        cost_estimate=cost(30 * tiles * TILE * TILE, 4 * around.size),
        name="force",
    )(active_tile_count, cross_count, *in_hbm([tile_block]), around, below, above, *own)

    if not whole_slab:
        return by_exchange(rows, strides, around, moves, cross_count)

    constraint_rows = rows.bond_rows + rows.slot_rows
    weight, matrix = pl.pallas_call(
        functools.partial(bond_kernel, rows, domains, strides),
        out_shape=(
            jax.ShapeDtypeStruct((constraint_rows * 3 * domains, LANES), f32),
            jax.ShapeDtypeStruct((domains * rows.matrix, atoms // 2), jnp.bfloat16),
        ),
        in_specs=vmem(1),
        out_specs=tuple(vmem(2)),
        compiler_params=params(16),
        cost_estimate=cost(8 * domains * rows.matrix * atoms // 2, 4 * around.size),
        name="bonds",
    )(around)

    every_move = from_slab(moves)

    return pl.pallas_call(
        functools.partial(solve_kernel, rows, domains, strides),
        out_shape=(
            jax.ShapeDtypeStruct(coords.shape, f32),
            jax.ShapeDtypeStruct(coords.shape, f32),
        ),
        in_specs=vmem(4),
        out_specs=tuple(vmem(2)),
        scratch_shapes=[
            pltpu.VMEM((constraint_rows, SUBLANES * domains, LANES), f32),
            pltpu.VMEM((rows.slot_rows, 4 * SUBLANES * domains, LANES), f32),
            pltpu.VMEM((5, rows.atom_rows, SUBLANES * domains, LANES), f32),
        ],
        compiler_params=params(16),
        name="solve",
    )(around, every_move, weight, matrix)


def by_exchange(rows, strides, around, moves, cross_count):
    atom_count = rows.atom_rows * LANES
    shell = rows.shell_rows * LANES
    inside = around.reshape(5, rows.count, LANES)

    def flat(at, count):
        return inside[0, at : at + count].reshape(-1)

    def neighbours(at):
        return inside[1:, at : at + rows.shell_rows].reshape(-1)

    coords = jnp.stack([flat(at, rows.atom_rows) for at in rows.coords])
    inv_mass = flat(rows.mass, rows.atom_rows)
    displace = moves[: rows.live].reshape(3, atom_count)
    left = flat(rows.bond_first, rows.bond_rows).astype(jnp.int32)
    right = flat(rows.bond_second, rows.bond_rows).astype(jnp.int32)
    cross_left = flat(rows.cross_first, rows.slot_rows).astype(jnp.int32)
    cross_right = flat(rows.cross_second, rows.slot_rows).astype(jnp.int32)
    side = flat(rows.side, rows.slot_rows).astype(jnp.int32)
    flag = moves[rows.live : rows.disp_used].reshape(-1)
    cross_index = side * shell + cross_right
    far_coords = jnp.stack([neighbours(at) for at in rows.coords])
    far_mass = neighbours(rows.mass)

    def weights(first, second, mass_first, mass_second):
        gap = first - second
        length = jnp.sqrt(jnp.sum(gap * gap, axis=0) + length_floor)
        return gap / length * lax.rsqrt(mass_first + mass_second)

    inner = weights(coords[:, left], coords[:, right], inv_mass[left], inv_mass[right])
    cross = flag * weights(
        coords[:, cross_left], far_coords[:, cross_index], inv_mass[cross_left], far_mass[cross_index]
    )

    def project(field):
        rim = field[:, :shell]
        far = jnp.concatenate([passed_along(rim, "dom", -stride) for stride in strides], axis=1)
        return (
            jnp.sum(inner * (field[:, left] - field[:, right]), axis=0),
            jnp.sum(cross * (field[:, cross_left] - far[:, cross_index]), axis=0),
        )

    def spread(values):
        pushed = inner * values[0]
        pushed_cross = cross * values[1]
        totals = jnp.zeros((3, atom_count), jnp.float32).at[:, left].add(pushed).at[:, right].add(-pushed)
        totals = totals.at[:, cross_left].add(pushed_cross)
        outward = jnp.zeros((3, 4 * shell), jnp.float32).at[:, cross_index].add(-pushed_cross)
        for code, stride in enumerate(strides):
            totals = totals.at[:, :shell].add(
                passed_along(outward[:, code * shell : (code + 1) * shell], "dom", stride)
            )
        return inv_mass * totals

    residue = project(displace)
    summed = residue
    for _ in range(ORDER):
        change = project(spread(residue))
        residue = tuple(now - step for now, step in zip(residue, change))
        summed = tuple(a + b for a, b in zip(summed, residue))
    move = displace - spread(summed)
    return (
        (coords + move).reshape(3, 1, 1, atom_count),
        (move * (1.0 / time_step)).reshape(3, 1, 1, atom_count),
    )


def solution(mesh):
    return jax.shard_map(
        shards,
        mesh=mesh,
        in_specs=(
            P(None, "slab", "dom", None),
            P(None, "slab", "dom", None),
            P("slab", "dom", None),
            P("slab", "dom", None),
            P("slab", "dom", None),
            P("slab", "dom", None, None),
            P("slab", "dom"),
            P(None, "slab", "dom", None),
            P(None, "slab", "dom", None),
            P("slab", "dom", None),
            P("slab", "dom"),
        ),
        out_specs=(P(None, "slab", "dom", None), P(None, "slab", "dom", None)),
        check_vma=False,
    )
```

```python
import functools

import jax
import jax.numpy as jnp
from jax import lax
from jax.experimental import pallas as pl
from jax.experimental.pallas import tpu as pltpu
from jax.sharding import PartitionSpec as P

TILE = 128
ORDER = 4
LANES = 128
SUBLANES = 8

time_step = 0.1
cutoff_sq = 16.0
force_scale = 4.0
length_floor = 0.25


def passed_along(array, axis, by):
    length = lax.axis_size(axis)
    return lax.ppermute(array, axis, [(i, (i + by) % length) for i in range(length)])


def first_of(domains):
    return domains - 1


def from_slab(blocks):
    length = lax.axis_size("dom")
    order = [(first_of(length) + i) % length for i in range(length)]
    return lax.all_to_all(blocks, "dom", 0, 0, axis_index_groups=[order], tiled=True)


def place_of(stride=0):
    length = lax.axis_size("dom")
    return lax.rem(lax.axis_index("dom") + (stride - first_of(length)) % length, length)


def strides_of(domains):
    row_width = max(2, domains // 8)
    return (1, -1, row_width, -row_width)


def round_up(count, step):
    return -(-count // step) * step


class Rows:
    def __init__(self, atoms, bonds, slots):
        self.atom_rows = atoms // LANES
        self.shell_rows = atoms // 2 // LANES
        self.bond_rows = bonds // LANES
        self.slot_rows = slots // LANES
        at = 0
        self.coords = []
        for _ in range(3):
            self.coords.append(at)
            at += self.atom_rows
        self.charge = at
        at += self.shell_rows
        self.mass = at
        at += self.atom_rows
        self.bond_first = at
        at += self.bond_rows
        self.bond_second = at
        at += self.bond_rows
        self.cross_first = at
        at += self.slot_rows
        self.cross_second = at
        at += self.slot_rows
        self.used = at
        self.count = round_up(at, SUBLANES)
        self.shell_terms = (self.bond_rows + self.slot_rows) * LANES
        self.inner_at = (0, self.shell_terms)
        self.cross_at = self.bond_rows * LANES
        self.far_at = self.shell_terms + self.bond_rows * LANES
        self.matrix = self.far_at + self.slot_rows * LANES
        self.live = 3 * self.atom_rows
        self.side = self.live + self.slot_rows
        self.disp_used = self.side + self.slot_rows
        self.disp_count = round_up(self.disp_used, SUBLANES)


def take_lanes(table, lanes):
    return jnp.take_along_axis(table, lanes, axis=1, mode="promise_in_bounds")


def pick(tables, index):
    lanes = index & (LANES - 1)
    chunk = index >> 7
    result = take_lanes(tables[0], lanes)
    for k in range(1, len(tables)):
        result = jnp.where(chunk == k, take_lanes(tables[k], lanes), result)
    return result


def fetched(sources, targets, sem_ref):
    copies = [pltpu.make_async_copy(s, t, sem_ref.at[n]) for n, (s, t) in enumerate(zip(sources, targets))]
    for copy in copies:
        copy.start()
    return copies


def pack_kernel(rows, copies, *refs):
    sources, (out_ref, rim_ref), targets, sem_ref = refs[:5], refs[5:7], refs[7:12], refs[12]
    for copy in fetched(sources, targets, sem_ref):
        copy.wait()
    coords_ref, charge_ref, mass_ref, bonds_ref, cross_ref = targets

    def put(row, value):
        for part in range(value.shape[1] // LANES):
            piece = value[:, part * LANES : (part + 1) * LANES]
            for copy in range(copies):
                out_ref[pl.ds(copy * rows.count + row + part, 1), :] = piece

    shell = rows.shell_rows * LANES
    fields = [coords_ref[c, 0] for c in range(3)] + [charge_ref[0, :, :shell]]
    for c in range(4):
        at = rows.coords[c] if c < 3 else rows.charge
        put(at, fields[c])
        for part in range(rows.shell_rows):
            rim_ref[pl.ds(c * rows.shell_rows + part, 1), :] = fields[c][:, part * LANES : (part + 1) * LANES]
    put(rows.mass, mass_ref[0])
    put(rows.bond_first, bonds_ref[0, 0].astype(jnp.float32))
    put(rows.bond_second, bonds_ref[1, 0].astype(jnp.float32))
    put(rows.cross_first, cross_ref[0, 0].astype(jnp.float32))
    put(rows.cross_second, cross_ref[1, 0].astype(jnp.float32))
    if rows.count > rows.used:
        for copy in range(copies):
            out_ref[pl.ds(copy * rows.count + rows.used, rows.count - rows.used), :] = jnp.zeros(
                (rows.count - rows.used, LANES), jnp.float32
            )


SHRINK = 1.0 / 4.0
OUT_OF_REACH = 1000.0
TILES_STEP = 4
PIECE = 32


def own_kernel(
    rows,
    coords_hbm,
    charge_hbm,
    velocity_hbm,
    mass_hbm,
    side_hbm,
    atoms_hbm,
    own_ref,
    far_ref,
    index_ref,
    motion_ref,
    coords_ref,
    charge_ref,
    velocity_ref,
    mass_ref,
    side_ref,
    sem_ref,
):
    atom_rows = rows.atom_rows
    copies = fetched(
        (coords_hbm, charge_hbm, atoms_hbm.at[0, 0], velocity_hbm, mass_hbm, side_hbm),
        (coords_ref, charge_ref, index_ref, velocity_ref, mass_ref, side_ref),
        sem_ref,
    )
    down = lax.broadcasted_iota(jnp.int32, (SUBLANES, LANES), 0)
    copies[0].wait()
    copies[1].wait()

    def lanes_of(part):
        return slice(part * LANES, (part + 1) * LANES)

    table = []
    for c in range(4):
        field = coords_ref[c, 0] * SHRINK if c < 3 else charge_ref[0]
        table.append(
            [jnp.broadcast_to(field[:, lanes_of(part)], (SUBLANES, LANES)) for part in range(atom_rows)]
        )
    for part in range(atom_rows):
        for group in range(LANES // SUBLANES):
            at = part * LANES + group * SUBLANES
            for c in range(4):
                value = take_lanes(table[c][part], down + group * SUBLANES)
                own_ref[c, pl.ds(at, SUBLANES), :] = value if c < 3 else value * 8.0
    copies[2].wait()
    for group in range(index_ref.shape[0] // SUBLANES):
        at = pl.ds(group * SUBLANES, SUBLANES)
        index = index_ref[at, :]
        for c in range(4):
            far_ref[c, at, :] = pick(table[c], index)
    for copy in copies[3:]:
        copy.wait()
    fields = [velocity_ref[c, 0] for c in range(3)] + [mass_ref[0], side_ref[0].astype(jnp.float32)]
    at = 0
    for field in fields:
        for part in range(field.shape[1] // LANES):
            motion_ref[pl.ds(at, 1), :] = field[:, lanes_of(part)]
            at += 1


def force_kernel(
    rows,
    copies,
    place,
    live_ref,
    count_ref,
    block_hbm,
    around_ref,
    below_ref,
    above_ref,
    own_ref,
    near_ref,
    index_ref,
    motion_ref,
    out_ref,
    table_ref,
    far_ref,
    sum_ref,
    block_ref,
    sem_ref,
):
    atom_rows, shell_rows = rows.atom_rows, rows.shell_rows
    tiles = index_ref.shape[0]
    block_copy = pltpu.make_async_copy(block_hbm, block_ref, sem_ref)
    block_copy.start()
    holders = place()
    starts = [rows.coords[0], rows.coords[1], rows.coords[2], rows.charge]
    entry_rows = 6 * shell_rows

    def broadcast(row):
        return jnp.broadcast_to(row, (SUBLANES, LANES))

    for c in range(4):
        factor = SHRINK if c < 3 else 1.0
        at = 0
        for neighbour in range(4):
            base = holders[neighbour] * rows.count + starts[c]
            for part in range(shell_rows):
                table_ref[c, at] = broadcast(around_ref[pl.ds(base + part, 1), :] * factor)
                at += 1
        for slab_ref in (below_ref, above_ref):
            for part in range(shell_rows):
                table_ref[c, at] = broadcast(slab_ref[pl.ds(c * shell_rows + part, 1), :] * factor)
                at += 1

    live = live_ref[0, 0]
    down = lax.broadcasted_iota(jnp.int32, (SUBLANES, LANES), 0)
    for group in range(tiles // SUBLANES):
        at = pl.ds(group * SUBLANES, SUBLANES)
        index = index_ref[at, :]
        lanes = index & (LANES - 1)
        chunk = index >> 7
        values = [near_ref[c, at, :] for c in range(4)]
        for k in range(entry_rows):
            here = chunk == atom_rows + k
            values = [jnp.where(here, take_lanes(table_ref[c, k], lanes), values[c]) for c in range(4)]
        values[0] = jnp.where(down + group * SUBLANES < live, values[0], OUT_OF_REACH)
        for c in range(4):
            far_ref[c, at, :] = values[c]

    sum_ref[...] = jnp.zeros(sum_ref.shape, jnp.float32)
    block_copy.wait()

    softening = 1.0 / cutoff_sq

    def add_tile(tile):
        base = block_ref[0, 0, tile] * TILE
        far = [jnp.broadcast_to(far_ref[c, pl.ds(tile, 1), :], (PIECE, LANES)) for c in range(4)]
        for piece in range(TILE // PIECE):
            at = pl.ds(pl.multiple_of(base + piece * PIECE, PIECE), PIECE)
            gap = [own_ref[c, at, :] - far[c] for c in range(3)]
            square = gap[0] * gap[0] + gap[1] * gap[1] + gap[2] * gap[2]
            inverse = pl.reciprocal(square + softening, approx=True)
            weight = jnp.maximum(inverse - 1.0 / (1.0 + softening), 0.0)
            strength = (inverse - own_ref[3, at, :] * far[3]) * (weight * weight)
            for c in range(3):
                sum_ref[c, at, :] = sum_ref[c, at, :] + strength * gap[c]

    def add_tiles(step, _):
        for n in range(TILES_STEP):
            add_tile(step * TILES_STEP + n)
        return 0

    lax.fori_loop(0, lax.div(live + TILES_STEP - 1, TILES_STEP), add_tiles, 0)

    scale = time_step * time_step * force_scale * 4.0 / 2048.0 * (1.0 + softening) ** 2

    lane = lax.broadcasted_iota(jnp.int32, (LANES, LANES), 1)
    columns = jnp.zeros((LANES, LANES), jnp.float32)
    for c in range(3):
        for part in range(atom_rows):
            total = jnp.sum(sum_ref[c, pl.ds(part * LANES, LANES), :], axis=1, keepdims=True)
            columns = jnp.where(lane == c * atom_rows + part, total, columns)
    totals = columns.T[: 3 * atom_rows, :]
    mass = motion_ref[pl.ds(3 * atom_rows, atom_rows), :]
    moved = time_step * motion_ref[pl.ds(0, 3 * atom_rows), :] + scale * totals * jnp.concatenate([mass] * 3, axis=0)
    for copy in range(copies):
        out_ref[pl.ds(copy * rows.disp_count, 3 * atom_rows), :] = moved
    slot = lax.broadcasted_iota(jnp.int32, (1, LANES), 1)
    for part in range(rows.slot_rows):
        flag = jnp.where(slot + part * LANES < count_ref[0, 0], 1.0, 0.0)
        side = motion_ref[pl.ds(4 * atom_rows + part, 1), :]
        for copy in range(copies):
            out_ref[pl.ds(copy * rows.disp_count + rows.live + part, 1), :] = flag
            out_ref[pl.ds(copy * rows.disp_count + rows.side + part, 1), :] = side
    if rows.disp_count > rows.disp_used:
        for copy in range(copies):
            out_ref[pl.ds(copy * rows.disp_count + rows.disp_used, rows.disp_count - rows.disp_used), :] = jnp.zeros(
                (rows.disp_count - rows.disp_used, LANES), jnp.float32
            )


def bond_kernel(rows, domains, strides, around_ref, weight_ref, matrix_ref):
    atom_rows, shell_rows = rows.atom_rows, rows.shell_rows

    def load(row):
        return around_ref[pl.ds(row, domains, stride=rows.count), :]

    def index(row):
        return load(row).astype(jnp.int32)

    fields = [[load(at + part) for part in range(atom_rows)] for at in rows.coords + [rows.mass]]

    def put_weights(first, second, at):
        gap = [first[c] - second[c] for c in range(3)]
        length_sq = gap[0] * gap[0] + gap[1] * gap[1] + gap[2] * gap[2] + length_floor
        scale = lax.rsqrt(length_sq) * lax.rsqrt(first[3] + second[3])
        for c in range(3):
            weight_ref[pl.ds((at * 3 + c) * domains, domains), :] = gap[c] * scale

    for part in range(rows.bond_rows):
        first = index(rows.bond_first + part)
        second = index(rows.bond_second + part)
        put_weights([pick(f, first) for f in fields], [pick(f, second) for f in fields], part)
    shells = [f[:shell_rows] for f in fields]
    for part in range(rows.slot_rows):
        first = index(rows.cross_first + part)
        second = index(rows.cross_second + part)
        ends = [pick(f, first) for f in shells]
        for code, stride in enumerate(strides):
            seen = pltpu.roll(second, stride % domains, 0)
            others = [pltpu.roll(pick(f, seen), -stride % domains, 0) for f in shells]
            put_weights(ends, others, rows.bond_rows + part * 4 + code)

    down = lax.broadcasted_iota(jnp.int32, (SUBLANES, LANES), 0)
    group_rows = 4 * SUBLANES

    kind = jnp.bfloat16 if shell_rows * LANES <= 256 else jnp.float32
    across = lax.broadcasted_iota(jnp.int32, (group_rows, LANES), 1).astype(jnp.float32)
    lanes = [(across + float(block * LANES)).astype(kind) for block in range(shell_rows)]

    def column(row, step, half=0):
        row = jnp.broadcast_to(row, (SUBLANES, LANES))
        groups = [take_lanes(row, down + at) for at in range(step * group_rows, (step + 1) * group_rows, SUBLANES)]
        return (jnp.concatenate(groups, axis=0) - float(half * shell_rows * LANES)).astype(kind)

    def put(at, ends, signs):
        for block in range(shell_rows):
            value = jnp.zeros((group_rows, LANES), kind)
            for end, sign in zip(ends, signs):
                value = jnp.where(end == lanes[block], jnp.full((group_rows, LANES), sign, kind), value)
            matrix_ref[pl.ds(at, group_rows), block * LANES : (block + 1) * LANES] = value.astype(matrix_ref.dtype)

    def build(domain, _):
        start = pl.multiple_of(domain * rows.matrix, LANES)
        for part in range(rows.bond_rows):
            first = around_ref[pl.ds(domain * rows.count + rows.bond_first + part, 1), :]
            second = around_ref[pl.ds(domain * rows.count + rows.bond_second + part, 1), :]
            for step in range(LANES // group_rows):
                for half in range(2):
                    ends = (column(first, step, half), column(second, step, half))
                    put(start + rows.inner_at[half] + part * LANES + step * group_rows, ends, (1.0, -1.0))
        for part in range(rows.slot_rows):
            for row_at, to, sign in (
                (rows.cross_first, rows.cross_at, 1.0),
                (rows.cross_second, rows.far_at, -1.0),
            ):
                row = around_ref[pl.ds(domain * rows.count + row_at + part, 1), :]
                for step in range(LANES // group_rows):
                    put(start + to + part * LANES + step * group_rows, (column(row, step),), (sign,))
        return 0

    lax.fori_loop(0, domains, build, 0)


def solve_kernel(
    rows,
    domains,
    strides,
    around_ref,
    moves_ref,
    weight_ref,
    matrix_ref,
    coords_out_ref,
    velocity_out_ref,
    push_ref,
    far_push_ref,
    field_ref,
):
    atom_rows, shell_rows = rows.atom_rows, rows.shell_rows
    bond_rows, slot_rows = rows.bond_rows, rows.slot_rows
    me = place_of()

    def load(row):
        return around_ref[pl.ds(row, domains, stride=rows.count), :]

    def index(row):
        return load(row).astype(jnp.int32)

    inner_first = [index(rows.bond_first + p) for p in range(bond_rows)]
    inner_second = [index(rows.bond_second + p) for p in range(bond_rows)]
    cross_first = [index(rows.cross_first + p) for p in range(slot_rows)]
    cross_second = [index(rows.cross_second + p) for p in range(slot_rows)]
    masses = [load(rows.mass + p) for p in range(atom_rows)]

    def move_rows(row):
        return moves_ref[pl.ds(row, domains, stride=rows.disp_count), :]

    def weight_rows(at, c):
        return weight_ref[pl.ds((at * 3 + c) * domains, domains), :]

    sides = [move_rows(rows.side + p) for p in range(slot_rows)]
    cross_weights = []
    for part in range(slot_rows):
        live = move_rows(rows.live + part)
        for c in range(3):
            value = 0.0
            for code in range(4):
                value = jnp.where(sides[part] == code, weight_rows(bond_rows + part * 4 + code, c), value)
            cross_weights.append(value * live)

    def weight(at, c):
        return weight_rows(at, c) if at < bond_rows else cross_weights[(at - bond_rows) * 3 + c]

    def project(fields):
        result = []
        for part in range(bond_rows):
            total = 0.0
            for c in range(3):
                ends = pick(fields[c], inner_first[part]) - pick(fields[c], inner_second[part])
                total = total + weight(part, c) * ends
            result.append(total)
        for part in range(slot_rows):
            seen = [pltpu.roll(cross_second[part], stride % domains, 0) for stride in strides]
            total = 0.0
            for c in range(3):
                shell = fields[c][:shell_rows]
                other = 0.0
                for code, stride in enumerate(strides):
                    value = pltpu.roll(pick(shell, seen[code]), -stride % domains, 0)
                    other = jnp.where(sides[part] == code, value, other)
                total = total + weight(bond_rows + part, c) * (pick(shell, cross_first[part]) - other)
            result.append(total)
        return result

    def put_pushes(values):
        for at, value in enumerate(values):
            for c in range(3):
                pushed = weight(at, c) * value
                high = pushed.astype(jnp.bfloat16).astype(jnp.float32)
                for row, part in ((c, high), (3 + c, pushed - high)):
                    push_ref[at, pl.ds(row * domains, domains), :] = part
                    if at >= bond_rows:
                        for code in range(4):
                            far_push_ref[at - bond_rows, pl.ds((code * SUBLANES + row) * domains, domains), :] = (
                                jnp.where(sides[at - bond_rows] == code, part, 0.0)
                            )

    def pushes_of(at, domain):
        return push_ref[at, pl.ds(domain, SUBLANES, stride=domains), :].astype(jnp.bfloat16)

    def product(pushes, domain, at):
        start = domain * rows.matrix + at
        if not isinstance(start, int):
            start = pl.multiple_of(start, LANES)
        pushes = pushes[0] if len(pushes) == 1 else jnp.concatenate(pushes, axis=1)
        result = jnp.dot(
            pushes, matrix_ref[pl.ds(start, pushes.shape[1]), :], preferred_element_type=jnp.float32
        )
        return [result[:, p * LANES : (p + 1) * LANES] for p in range(shell_rows)]

    def inner_totals(domain):
        pushes = [pushes_of(at, domain) for at in range(bond_rows + slot_rows)]
        return product(pushes, domain, 0) + product(pushes[:bond_rows], domain, rows.shell_terms)

    def far_totals(domain, first_row, count):
        pushes = [
            far_push_ref[p, pl.ds(first_row * domains + domain, count, stride=domains), :].astype(jnp.bfloat16)
            for p in range(slot_rows)
        ]
        return product(pushes, domain, rows.far_at)

    def spread(values):
        put_pushes(values)
        for domain in range(domains):
            for part, total in enumerate(inner_totals(domain)):
                field_ref[0, part, pl.ds(domain, SUBLANES, stride=domains), :] = total
            for part, total in enumerate(far_totals(domain, 0, 4 * SUBLANES)):
                for code, stride in enumerate(strides):
                    field_ref[1 + code, part, pl.ds((domain + stride) % domains, SUBLANES, stride=domains), :] = total[
                        code * SUBLANES : (code + 1) * SUBLANES, :
                    ]

        def field(c, part):
            pieces = [
                field_ref[source, part, pl.ds(row * domains, domains), :]
                for source in range(5 if part < shell_rows else 1)
                for row in (c, 3 + c)
            ]
            return masses[part] * functools.reduce(lambda a, b: a + b, pieces)

        return [[field(c, part) for part in range(atom_rows)] for c in range(3)]

    moves = [
        [move_rows(c * atom_rows + p) for p in range(atom_rows)]
        for c in range(3)
    ]
    push_ref[...] = jnp.zeros(push_ref.shape, jnp.float32)
    far_push_ref[...] = jnp.zeros(far_push_ref.shape, jnp.float32)
    residue = project(moves)

    def expand(_, carry):
        residue, summed = carry
        change = project(spread(residue))
        residue = [now - step for now, step in zip(residue, change)]
        return residue, [a + b for a, b in zip(summed, residue)]

    residue, summed = lax.fori_loop(0, ORDER, expand, (residue, residue))
    put_pushes(summed)
    sums = inner_totals(me)
    for code, stride in enumerate(strides):
        owner = lax.rem(me + (-stride) % domains, domains)
        for part, total in enumerate(far_totals(owner, code * SUBLANES, SUBLANES)):
            sums[part] = sums[part] + total
    for part in range(atom_rows):
        lanes = slice(part * LANES, (part + 1) * LANES)
        mass = around_ref[pl.ds(me * rows.count + rows.mass + part, 1), :]
        for c in range(3):
            correction = mass * (sums[part][c : c + 1, :] + sums[part][3 + c : 4 + c, :])
            move = moves_ref[pl.ds(me * rows.disp_count + c * atom_rows + part, 1), :] - correction
            start = around_ref[pl.ds(me * rows.count + rows.coords[c] + part, 1), :]
            coords_out_ref[c, 0, :, lanes] = start + move
            velocity_out_ref[c, 0, :, lanes] = move * (1.0 / time_step)


def vmem(count):
    return [pl.BlockSpec(memory_space=pltpu.VMEM)] * count


def smem(count):
    return [pl.BlockSpec(memory_space=pltpu.SMEM)] * count


def hbm(count):
    return [pl.BlockSpec(memory_space=pltpu.HBM)] * count


def in_hbm(arrays):
    return [pltpu.with_memory_space_constraint(a, pltpu.HBM) for a in arrays]


def params(mebibytes):
    return pltpu.CompilerParams(vmem_limit_bytes=mebibytes * 1024 * 1024)


def cost(flops, moved):
    return pl.CostEstimate(flops=flops, bytes_accessed=moved, transcendentals=0)


def room_for(arrays):
    return [pltpu.VMEM(a.shape, a.dtype) for a in arrays]


def shards(
    coords,
    velocity,
    charge,
    inv_mass,
    tile_block,
    tile_atoms,
    active_tile_count,
    bond_atoms,
    cross_atoms,
    cross_side,
    cross_count,
):
    atoms = coords.shape[-1]
    tiles = tile_atoms.shape[2]
    domains = lax.axis_size("dom")
    strides = strides_of(domains)
    rows = Rows(atoms, bond_atoms.shape[-1], cross_side.shape[-1])
    whole_slab = domains == SUBLANES
    copies = domains if whole_slab else 1
    f32 = jnp.float32

    sent = (coords, charge, inv_mass, bond_atoms, cross_atoms)
    packed, rim = pl.pallas_call(
        functools.partial(pack_kernel, rows, copies),
        out_shape=(
            jax.ShapeDtypeStruct((copies * rows.count, LANES), f32),
            jax.ShapeDtypeStruct((4 * rows.shell_rows, LANES), f32),
        ),
        in_specs=hbm(len(sent)),
        out_specs=tuple(vmem(2)),
        scratch_shapes=room_for(sent) + [pltpu.SemaphoreType.DMA((len(sent),))],
        compiler_params=params(4),
        name="pack",
    )(*in_hbm(sent))

    alone = (coords, charge, velocity, inv_mass, cross_side, tile_atoms)
    own = pl.pallas_call(
        functools.partial(own_kernel, rows),
        out_shape=(
            jax.ShapeDtypeStruct((4, atoms, LANES), f32),
            jax.ShapeDtypeStruct((4, tiles, TILE), f32),
            jax.ShapeDtypeStruct((tiles, TILE), jnp.int32),
            jax.ShapeDtypeStruct((4 * rows.atom_rows + rows.slot_rows, LANES), f32),
        ),
        in_specs=hbm(len(alone)),
        out_specs=tuple(vmem(4)),
        scratch_shapes=room_for(alone[:5]) + [pltpu.SemaphoreType.DMA((len(alone),))],
        compiler_params=params(4),
        cost_estimate=cost(64 * atoms * LANES, 16 * atoms * LANES),
        name="own",
    )(*in_hbm(alone))

    below = passed_along(rim, "slab", 1)
    above = passed_along(rim, "slab", -1)
    if whole_slab:
        around = from_slab(packed)

        def place():
            return [place_of(stride) for stride in strides]

    else:
        around = jnp.concatenate([packed] + [passed_along(packed, "dom", -stride) for stride in strides], axis=0)

        def place():
            return [1, 2, 3, 4]


    moves = pl.pallas_call(
        functools.partial(force_kernel, rows, copies, place),
        out_shape=jax.ShapeDtypeStruct((copies * rows.disp_count, LANES), f32),
        in_specs=smem(2) + hbm(1) + vmem(7),
        out_specs=vmem(1)[0],
        scratch_shapes=[
            pltpu.VMEM((4, 6 * rows.shell_rows, SUBLANES, LANES), f32),
            pltpu.VMEM((4, tiles, LANES), f32),
            pltpu.VMEM((3, atoms, LANES), f32),
            pltpu.SMEM(tile_block.shape, jnp.int32),
            pltpu.SemaphoreType.DMA(()),
        ],
        compiler_params=params(8),
        cost_estimate=cost(30 * tiles * TILE * TILE, 4 * around.size),
        name="force",
    )(active_tile_count, cross_count, *in_hbm([tile_block]), around, below, above, *own)

    if not whole_slab:
        return by_exchange(rows, strides, around, moves, cross_count)

    constraint_rows = rows.bond_rows + rows.slot_rows
    weight, matrix = pl.pallas_call(
        functools.partial(bond_kernel, rows, domains, strides),
        out_shape=(
            jax.ShapeDtypeStruct(((rows.bond_rows + 4 * rows.slot_rows) * 3 * domains, LANES), f32),
            jax.ShapeDtypeStruct((domains * rows.matrix, atoms // 2), jnp.bfloat16),
        ),
        in_specs=vmem(1),
        out_specs=tuple(vmem(2)),
        compiler_params=params(16),
        cost_estimate=cost(8 * domains * rows.matrix * atoms // 2, 4 * around.size),
        name="bonds",
    )(around)

    every_move = from_slab(moves)

    return pl.pallas_call(
        functools.partial(solve_kernel, rows, domains, strides),
        out_shape=(
            jax.ShapeDtypeStruct(coords.shape, f32),
            jax.ShapeDtypeStruct(coords.shape, f32),
        ),
        in_specs=vmem(4),
        out_specs=tuple(vmem(2)),
        scratch_shapes=[
            pltpu.VMEM((constraint_rows, SUBLANES * domains, LANES), f32),
            pltpu.VMEM((rows.slot_rows, 4 * SUBLANES * domains, LANES), f32),
            pltpu.VMEM((5, rows.atom_rows, SUBLANES * domains, LANES), f32),
        ],
        compiler_params=params(16),
        name="solve",
    )(around, every_move, weight, matrix)


def by_exchange(rows, strides, around, moves, cross_count):
    atom_count = rows.atom_rows * LANES
    shell = rows.shell_rows * LANES
    inside = around.reshape(5, rows.count, LANES)

    def flat(at, count):
        return inside[0, at : at + count].reshape(-1)

    def neighbours(at):
        return inside[1:, at : at + rows.shell_rows].reshape(-1)

    coords = jnp.stack([flat(at, rows.atom_rows) for at in rows.coords])
    inv_mass = flat(rows.mass, rows.atom_rows)
    displace = moves[: rows.live].reshape(3, atom_count)
    left = flat(rows.bond_first, rows.bond_rows).astype(jnp.int32)
    right = flat(rows.bond_second, rows.bond_rows).astype(jnp.int32)
    cross_left = flat(rows.cross_first, rows.slot_rows).astype(jnp.int32)
    cross_right = flat(rows.cross_second, rows.slot_rows).astype(jnp.int32)
    side = moves[rows.side : rows.side + rows.slot_rows].reshape(-1).astype(jnp.int32)
    flag = moves[rows.live : rows.side].reshape(-1)
    cross_index = side * shell + cross_right
    far_coords = jnp.stack([neighbours(at) for at in rows.coords])
    far_mass = neighbours(rows.mass)

    def weights(first, second, mass_first, mass_second):
        gap = first - second
        length = jnp.sqrt(jnp.sum(gap * gap, axis=0) + length_floor)
        return gap / length * lax.rsqrt(mass_first + mass_second)

    inner = weights(coords[:, left], coords[:, right], inv_mass[left], inv_mass[right])
    cross = flag * weights(
        coords[:, cross_left], far_coords[:, cross_index], inv_mass[cross_left], far_mass[cross_index]
    )

    def project(field):
        rim = field[:, :shell]
        far = jnp.concatenate([passed_along(rim, "dom", -stride) for stride in strides], axis=1)
        return (
            jnp.sum(inner * (field[:, left] - field[:, right]), axis=0),
            jnp.sum(cross * (field[:, cross_left] - far[:, cross_index]), axis=0),
        )

    def spread(values):
        pushed = inner * values[0]
        pushed_cross = cross * values[1]
        totals = jnp.zeros((3, atom_count), jnp.float32).at[:, left].add(pushed).at[:, right].add(-pushed)
        totals = totals.at[:, cross_left].add(pushed_cross)
        outward = jnp.zeros((3, 4 * shell), jnp.float32).at[:, cross_index].add(-pushed_cross)
        for code, stride in enumerate(strides):
            totals = totals.at[:, :shell].add(
                passed_along(outward[:, code * shell : (code + 1) * shell], "dom", stride)
            )
        return inv_mass * totals

    residue = project(displace)
    summed = residue
    for _ in range(ORDER):
        change = project(spread(residue))
        residue = tuple(now - step for now, step in zip(residue, change))
        summed = tuple(a + b for a, b in zip(summed, residue))
    move = displace - spread(summed)
    return (
        (coords + move).reshape(3, 1, 1, atom_count),
        (move * (1.0 / time_step)).reshape(3, 1, 1, atom_count),
    )


def solution(mesh):
    return jax.shard_map(
        shards,
        mesh=mesh,
        in_specs=(
            P(None, "slab", "dom", None),
            P(None, "slab", "dom", None),
            P("slab", "dom", None),
            P("slab", "dom", None),
            P("slab", "dom", None),
            P("slab", "dom", None, None),
            P("slab", "dom"),
            P(None, "slab", "dom", None),
            P(None, "slab", "dom", None),
            P("slab", "dom", None),
            P("slab", "dom"),
        ),
        out_specs=(P(None, "slab", "dom", None), P(None, "slab", "dom", None)),
        check_vma=False,
    )
```

```python
import functools

import jax
import jax.numpy as jnp
from jax import lax
from jax.experimental import pallas as pl
from jax.experimental.pallas import tpu as pltpu
from jax.sharding import PartitionSpec as P

TILE = 128
ORDER = 4
LANES = 128
SUBLANES = 8

time_step = 0.1
cutoff_sq = 16.0
force_scale = 4.0
length_floor = 0.25


def passed_along(array, axis, by):
    length = lax.axis_size(axis)
    return lax.ppermute(array, axis, [(i, (i + by) % length) for i in range(length)])


def first_of(domains):
    return domains - 1


def from_slab(blocks):
    length = lax.axis_size("dom")
    order = [(first_of(length) + i) % length for i in range(length)]
    return lax.all_to_all(blocks, "dom", 0, 0, axis_index_groups=[order], tiled=True)


def place_of(stride=0):
    length = lax.axis_size("dom")
    return lax.rem(lax.axis_index("dom") + (stride - first_of(length)) % length, length)


def strides_of(domains):
    row_width = max(2, domains // 8)
    return (1, -1, row_width, -row_width)


def round_up(count, step):
    return -(-count // step) * step


class Rows:
    def __init__(self, atoms, bonds, slots):
        self.atom_rows = atoms // LANES
        self.shell_rows = atoms // 2 // LANES
        self.bond_rows = bonds // LANES
        self.slot_rows = slots // LANES
        at = 0
        self.coords = []
        for _ in range(3):
            self.coords.append(at)
            at += self.atom_rows
        self.charge = at
        at += self.shell_rows
        self.mass = at
        at += self.atom_rows
        self.bond_first = at
        at += self.bond_rows
        self.bond_second = at
        at += self.bond_rows
        self.cross_first = at
        at += self.slot_rows
        self.cross_second = at
        at += self.slot_rows
        self.used = at
        self.count = round_up(at, SUBLANES)
        self.shell_terms = (self.bond_rows + self.slot_rows) * LANES
        self.inner_at = (0, self.shell_terms)
        self.cross_at = self.bond_rows * LANES
        self.far_at = self.shell_terms + self.bond_rows * LANES
        self.matrix = self.far_at + self.slot_rows * LANES
        self.live = 3 * self.atom_rows
        self.side = self.live + self.slot_rows
        self.disp_used = self.side + self.slot_rows
        self.disp_count = round_up(self.disp_used, SUBLANES)


def take_lanes(table, lanes):
    return jnp.take_along_axis(table, lanes, axis=1, mode="promise_in_bounds")


def pick(tables, index):
    lanes = index & (LANES - 1)
    chunk = index >> 7
    result = take_lanes(tables[0], lanes)
    for k in range(1, len(tables)):
        result = jnp.where(chunk == k, take_lanes(tables[k], lanes), result)
    return result


def fetched(sources, targets, sem_ref):
    copies = [pltpu.make_async_copy(s, t, sem_ref.at[n]) for n, (s, t) in enumerate(zip(sources, targets))]
    for copy in copies:
        copy.start()
    return copies


def pack_kernel(rows, copies, *refs):
    sources, (out_ref, rim_ref), targets, sem_ref = refs[:5], refs[5:7], refs[7:12], refs[12]
    block_ref = refs[13]
    for copy in fetched(sources, targets, sem_ref):
        copy.wait()
    coords_ref, charge_ref, mass_ref, bonds_ref, cross_ref = targets

    def put(row, value):
        for part in range(value.shape[1] // LANES):
            block_ref[pl.ds(row + part, 1), :] = value[:, part * LANES : (part + 1) * LANES]

    shell = rows.shell_rows * LANES
    fields = [coords_ref[c, 0] for c in range(3)] + [charge_ref[0, :, :shell]]
    for c in range(4):
        at = rows.coords[c] if c < 3 else rows.charge
        put(at, fields[c])
        for part in range(rows.shell_rows):
            rim_ref[pl.ds(c * rows.shell_rows + part, 1), :] = fields[c][:, part * LANES : (part + 1) * LANES]
    put(rows.mass, mass_ref[0])
    put(rows.bond_first, bonds_ref[0, 0].astype(jnp.float32))
    put(rows.bond_second, bonds_ref[1, 0].astype(jnp.float32))
    put(rows.cross_first, cross_ref[0, 0].astype(jnp.float32))
    put(rows.cross_second, cross_ref[1, 0].astype(jnp.float32))
    if rows.count > rows.used:
        block_ref[rows.used :, :] = jnp.zeros((rows.count - rows.used, LANES), jnp.float32)
    block = block_ref[...]
    for copy in range(copies):
        out_ref[pl.ds(copy * rows.count, rows.count), :] = block


SHRINK = 1.0 / 4.0
OUT_OF_REACH = 1000.0
TILES_STEP = 4
PIECE = 32


def own_kernel(
    rows,
    coords_hbm,
    charge_hbm,
    velocity_hbm,
    mass_hbm,
    side_hbm,
    atoms_hbm,
    own_ref,
    far_ref,
    index_ref,
    motion_ref,
    coords_ref,
    charge_ref,
    velocity_ref,
    mass_ref,
    side_ref,
    sem_ref,
):
    atom_rows = rows.atom_rows
    copies = fetched(
        (coords_hbm, charge_hbm, atoms_hbm.at[0, 0], velocity_hbm, mass_hbm, side_hbm),
        (coords_ref, charge_ref, index_ref, velocity_ref, mass_ref, side_ref),
        sem_ref,
    )
    down = lax.broadcasted_iota(jnp.int32, (SUBLANES, LANES), 0)
    copies[0].wait()
    copies[1].wait()

    def lanes_of(part):
        return slice(part * LANES, (part + 1) * LANES)

    table = []
    for c in range(4):
        field = coords_ref[c, 0] * SHRINK if c < 3 else charge_ref[0]
        table.append(
            [jnp.broadcast_to(field[:, lanes_of(part)], (SUBLANES, LANES)) for part in range(atom_rows)]
        )
    for part in range(atom_rows):
        for group in range(LANES // SUBLANES):
            at = part * LANES + group * SUBLANES
            for c in range(4):
                value = take_lanes(table[c][part], down + group * SUBLANES)
                own_ref[c, pl.ds(at, SUBLANES), :] = value if c < 3 else value * 8.0
    copies[2].wait()
    for group in range(index_ref.shape[0] // SUBLANES):
        at = pl.ds(group * SUBLANES, SUBLANES)
        index = index_ref[at, :]
        for c in range(4):
            far_ref[c, at, :] = pick(table[c], index)
    for copy in copies[3:]:
        copy.wait()
    fields = [velocity_ref[c, 0] for c in range(3)] + [mass_ref[0], side_ref[0].astype(jnp.float32)]
    at = 0
    for field in fields:
        for part in range(field.shape[1] // LANES):
            motion_ref[pl.ds(at, 1), :] = field[:, lanes_of(part)]
            at += 1


def force_kernel(
    rows,
    copies,
    place,
    live_ref,
    count_ref,
    block_hbm,
    around_ref,
    below_ref,
    above_ref,
    own_ref,
    near_ref,
    index_ref,
    motion_ref,
    out_ref,
    table_ref,
    far_ref,
    sum_ref,
    block_ref,
    sem_ref,
):
    atom_rows, shell_rows = rows.atom_rows, rows.shell_rows
    tiles = index_ref.shape[0]
    block_copy = pltpu.make_async_copy(block_hbm, block_ref, sem_ref)
    block_copy.start()
    live = live_ref[0, 0]
    holders = place()
    starts = [rows.coords[0], rows.coords[1], rows.coords[2], rows.charge]
    entry_rows = 6 * shell_rows

    def broadcast(row):
        return jnp.broadcast_to(row, (SUBLANES, LANES))

    for c in range(4):
        factor = SHRINK if c < 3 else 1.0
        at = 0
        for neighbour in range(4):
            base = holders[neighbour] * rows.count + starts[c]
            for part in range(shell_rows):
                table_ref[c, at] = broadcast(around_ref[pl.ds(base + part, 1), :] * factor)
                at += 1
        for slab_ref in (below_ref, above_ref):
            for part in range(shell_rows):
                table_ref[c, at] = broadcast(slab_ref[pl.ds(c * shell_rows + part, 1), :] * factor)
                at += 1

    for group in range(tiles // SUBLANES):
        at = pl.ds(group * SUBLANES, SUBLANES)
        index = index_ref[at, :]
        lanes = index & (LANES - 1)
        chunk = index >> 7
        values = [near_ref[c, at, :] for c in range(4)]
        for k in range(entry_rows):
            here = chunk == atom_rows + k
            values = [jnp.where(here, take_lanes(table_ref[c, k], lanes), values[c]) for c in range(4)]
        for c in range(4):
            far_ref[c, at, :] = values[c]

    sum_ref[...] = jnp.zeros(sum_ref.shape, jnp.float32)
    block_copy.wait()
    down = lax.broadcasted_iota(jnp.int32, (tiles, LANES), 0)
    far_ref[0] = jnp.where(down < live, far_ref[0], OUT_OF_REACH)

    softening = 1.0 / cutoff_sq

    def add_tile(tile):
        base = block_ref[0, 0, tile] * TILE
        far = [jnp.broadcast_to(far_ref[c, pl.ds(tile, 1), :], (PIECE, LANES)) for c in range(4)]
        for piece in range(TILE // PIECE):
            at = pl.ds(pl.multiple_of(base + piece * PIECE, PIECE), PIECE)
            gap = [own_ref[c, at, :] - far[c] for c in range(3)]
            square = gap[0] * gap[0] + gap[1] * gap[1] + gap[2] * gap[2]
            inverse = pl.reciprocal(square + softening, approx=True)
            weight = jnp.maximum(inverse - 1.0 / (1.0 + softening), 0.0)
            strength = (inverse - own_ref[3, at, :] * far[3]) * (weight * weight)
            for c in range(3):
                sum_ref[c, at, :] = sum_ref[c, at, :] + strength * gap[c]

    def add_tiles(step, _):
        for n in range(TILES_STEP):
            add_tile(step * TILES_STEP + n)
        return 0

    lax.fori_loop(0, lax.div(live + TILES_STEP - 1, TILES_STEP), add_tiles, 0)

    scale = time_step * time_step * force_scale * 4.0 / 2048.0 * (1.0 + softening) ** 2

    lane = lax.broadcasted_iota(jnp.int32, (LANES, LANES), 1)
    columns = jnp.zeros((LANES, LANES), jnp.float32)
    for c in range(3):
        for part in range(atom_rows):
            total = jnp.sum(sum_ref[c, pl.ds(part * LANES, LANES), :], axis=1, keepdims=True)
            columns = jnp.where(lane == c * atom_rows + part, total, columns)
    totals = columns.T[: 3 * atom_rows, :]
    mass = motion_ref[pl.ds(3 * atom_rows, atom_rows), :]
    moved = time_step * motion_ref[pl.ds(0, 3 * atom_rows), :] + scale * totals * jnp.concatenate([mass] * 3, axis=0)
    for copy in range(copies):
        out_ref[pl.ds(copy * rows.disp_count, 3 * atom_rows), :] = moved
    slot = lax.broadcasted_iota(jnp.int32, (1, LANES), 1)
    for part in range(rows.slot_rows):
        flag = jnp.where(slot + part * LANES < count_ref[0, 0], 1.0, 0.0)
        side = motion_ref[pl.ds(4 * atom_rows + part, 1), :]
        for copy in range(copies):
            out_ref[pl.ds(copy * rows.disp_count + rows.live + part, 1), :] = flag
            out_ref[pl.ds(copy * rows.disp_count + rows.side + part, 1), :] = side
    if rows.disp_count > rows.disp_used:
        for copy in range(copies):
            out_ref[pl.ds(copy * rows.disp_count + rows.disp_used, rows.disp_count - rows.disp_used), :] = jnp.zeros(
                (rows.disp_count - rows.disp_used, LANES), jnp.float32
            )


def bond_kernel(rows, domains, strides, around_ref, weight_ref, matrix_ref):
    atom_rows, shell_rows = rows.atom_rows, rows.shell_rows

    def load(row):
        return around_ref[pl.ds(row, domains, stride=rows.count), :]

    def index(row):
        return load(row).astype(jnp.int32)

    fields = [[load(at + part) for part in range(atom_rows)] for at in rows.coords + [rows.mass]]

    def put_weights(first, second, at):
        gap = [first[c] - second[c] for c in range(3)]
        length_sq = gap[0] * gap[0] + gap[1] * gap[1] + gap[2] * gap[2] + length_floor
        scale = lax.rsqrt(length_sq) * lax.rsqrt(first[3] + second[3])
        for c in range(3):
            weight_ref[pl.ds((at * 3 + c) * domains, domains), :] = gap[c] * scale

    for part in range(rows.bond_rows):
        first = index(rows.bond_first + part)
        second = index(rows.bond_second + part)
        put_weights([pick(f, first) for f in fields], [pick(f, second) for f in fields], part)
    shells = [f[:shell_rows] for f in fields]
    for part in range(rows.slot_rows):
        first = index(rows.cross_first + part)
        second = index(rows.cross_second + part)
        ends = [pick(f, first) for f in shells]
        for code, stride in enumerate(strides):
            seen = pltpu.roll(second, stride % domains, 0)
            others = [pltpu.roll(pick(f, seen), -stride % domains, 0) for f in shells]
            put_weights(ends, others, rows.bond_rows + part * 4 + code)

    down = lax.broadcasted_iota(jnp.int32, (SUBLANES, LANES), 0)
    group_rows = 4 * SUBLANES

    kind = jnp.bfloat16 if shell_rows * LANES <= 256 else jnp.float32
    across = lax.broadcasted_iota(jnp.int32, (group_rows, LANES), 1).astype(jnp.float32)
    lanes = [(across + float(block * LANES)).astype(kind) for block in range(shell_rows)]

    def column(row, step, half=0):
        row = jnp.broadcast_to(row, (SUBLANES, LANES))
        groups = [take_lanes(row, down + at) for at in range(step * group_rows, (step + 1) * group_rows, SUBLANES)]
        return (jnp.concatenate(groups, axis=0) - float(half * shell_rows * LANES)).astype(kind)

    def put(at, ends, signs):
        for block in range(shell_rows):
            value = jnp.zeros((group_rows, LANES), kind)
            for end, sign in zip(ends, signs):
                value = jnp.where(end == lanes[block], jnp.full((group_rows, LANES), sign, kind), value)
            matrix_ref[pl.ds(at, group_rows), block * LANES : (block + 1) * LANES] = value.astype(matrix_ref.dtype)

    def build(domain, _):
        start = pl.multiple_of(domain * rows.matrix, LANES)
        for part in range(rows.bond_rows):
            first = around_ref[pl.ds(domain * rows.count + rows.bond_first + part, 1), :]
            second = around_ref[pl.ds(domain * rows.count + rows.bond_second + part, 1), :]
            for step in range(LANES // group_rows):
                for half in range(2):
                    ends = (column(first, step, half), column(second, step, half))
                    put(start + rows.inner_at[half] + part * LANES + step * group_rows, ends, (1.0, -1.0))
        for part in range(rows.slot_rows):
            for row_at, to, sign in (
                (rows.cross_first, rows.cross_at, 1.0),
                (rows.cross_second, rows.far_at, -1.0),
            ):
                row = around_ref[pl.ds(domain * rows.count + row_at + part, 1), :]
                for step in range(LANES // group_rows):
                    put(start + to + part * LANES + step * group_rows, (column(row, step),), (sign,))
        return 0

    lax.fori_loop(0, domains, build, 0)


def solve_kernel(
    rows,
    domains,
    strides,
    around_ref,
    moves_ref,
    weight_ref,
    matrix_ref,
    coords_out_ref,
    velocity_out_ref,
    push_ref,
    field_ref,
):
    atom_rows, shell_rows = rows.atom_rows, rows.shell_rows
    bond_rows, slot_rows = rows.bond_rows, rows.slot_rows
    me = place_of()

    def load(row):
        return around_ref[pl.ds(row, domains, stride=rows.count), :]

    def index(row):
        return load(row).astype(jnp.int32)

    inner_first = [index(rows.bond_first + p) for p in range(bond_rows)]
    inner_second = [index(rows.bond_second + p) for p in range(bond_rows)]
    cross_first = [index(rows.cross_first + p) for p in range(slot_rows)]
    cross_second = [index(rows.cross_second + p) for p in range(slot_rows)]
    masses = [load(rows.mass + p) for p in range(atom_rows)]

    def move_rows(row):
        return moves_ref[pl.ds(row, domains, stride=rows.disp_count), :]

    def weight_rows(at, c):
        return weight_ref[pl.ds((at * 3 + c) * domains, domains), :]

    sides = [move_rows(rows.side + p) for p in range(slot_rows)]
    cross_weights = []
    for part in range(slot_rows):
        live = move_rows(rows.live + part)
        for c in range(3):
            value = 0.0
            for code in range(4):
                value = jnp.where(sides[part] == code, weight_rows(bond_rows + part * 4 + code, c), value)
            cross_weights.append(value * live)

    def weight(at, c):
        return weight_rows(at, c) if at < bond_rows else cross_weights[(at - bond_rows) * 3 + c]

    def project(fields):
        result = []
        for part in range(bond_rows):
            total = 0.0
            for c in range(3):
                ends = pick(fields[c], inner_first[part]) - pick(fields[c], inner_second[part])
                total = total + weight(part, c) * ends
            result.append(total)
        for part in range(slot_rows):
            seen = [pltpu.roll(cross_second[part], stride % domains, 0) for stride in strides]
            total = 0.0
            for c in range(3):
                shell = fields[c][:shell_rows]
                other = 0.0
                for code, stride in enumerate(strides):
                    value = pltpu.roll(pick(shell, seen[code]), -stride % domains, 0)
                    other = jnp.where(sides[part] == code, value, other)
                total = total + weight(bond_rows + part, c) * (pick(shell, cross_first[part]) - other)
            result.append(total)
        return result

    def put_pushes(values):
        for at, value in enumerate(values):
            for c in range(3):
                pushed = weight(at, c) * value
                high = pushed.astype(jnp.bfloat16).astype(jnp.float32)
                push_ref[at, pl.ds(c * domains, domains), :] = high
                push_ref[at, pl.ds((3 + c) * domains, domains), :] = pushed - high

    def pushes_of(at, domain):
        return push_ref[at, pl.ds(domain, SUBLANES, stride=domains), :]

    def product(pushes, domain, at):
        start = domain * rows.matrix + at
        if not isinstance(start, int):
            start = pl.multiple_of(start, LANES)
        pushes = pushes[0] if len(pushes) == 1 else jnp.concatenate(pushes, axis=1)
        result = jnp.dot(
            pushes.astype(jnp.bfloat16),
            matrix_ref[pl.ds(start, pushes.shape[1]), :],
            preferred_element_type=jnp.float32,
        )
        return [result[:, p * LANES : (p + 1) * LANES] for p in range(shell_rows)]

    def inner_totals(pushes, domain):
        return product(pushes, domain, 0) + product(pushes[:bond_rows], domain, rows.shell_terms)

    def far_totals(pushes, domain, codes):
        masked = []
        for part in range(slot_rows):
            side = moves_ref[pl.ds(domain * rows.disp_count + rows.side + part, 1), :]
            side = jnp.broadcast_to(side, (SUBLANES, LANES))
            pushed = pushes[bond_rows + part]
            masked.append(jnp.concatenate([jnp.where(side == code, pushed, 0.0) for code in codes], axis=0))
        return product(masked, domain, rows.far_at)

    def spread(values):
        put_pushes(values)
        for domain in range(domains):
            pushes = [pushes_of(at, domain) for at in range(bond_rows + slot_rows)]
            for part, total in enumerate(inner_totals(pushes, domain)):
                field_ref[0, part, pl.ds(domain, SUBLANES, stride=domains), :] = total
            for part, total in enumerate(far_totals(pushes, domain, range(4))):
                for code, stride in enumerate(strides):
                    field_ref[1 + code, part, pl.ds((domain + stride) % domains, SUBLANES, stride=domains), :] = total[
                        code * SUBLANES : (code + 1) * SUBLANES, :
                    ]

        def field(c, part):
            pieces = [
                field_ref[source, part, pl.ds(row * domains, domains), :]
                for source in range(5 if part < shell_rows else 1)
                for row in (c, 3 + c)
            ]
            return masses[part] * functools.reduce(lambda a, b: a + b, pieces)

        return [[field(c, part) for part in range(atom_rows)] for c in range(3)]

    moves = [
        [move_rows(c * atom_rows + p) for p in range(atom_rows)]
        for c in range(3)
    ]
    push_ref[...] = jnp.zeros(push_ref.shape, jnp.float32)
    residue = project(moves)

    def expand(_, carry):
        residue, summed = carry
        change = project(spread(residue))
        residue = [now - step for now, step in zip(residue, change)]
        return residue, [a + b for a, b in zip(summed, residue)]

    residue, summed = lax.fori_loop(0, ORDER, expand, (residue, residue))
    put_pushes(summed)
    sums = inner_totals([pushes_of(at, me) for at in range(bond_rows + slot_rows)], me)
    for code, stride in enumerate(strides):
        owner = lax.rem(me + (-stride) % domains, domains)
        pushes = [pushes_of(at, owner) for at in range(bond_rows + slot_rows)]
        for part, total in enumerate(far_totals(pushes, owner, [code])):
            sums[part] = sums[part] + total
    for part in range(atom_rows):
        lanes = slice(part * LANES, (part + 1) * LANES)
        mass = around_ref[pl.ds(me * rows.count + rows.mass + part, 1), :]
        for c in range(3):
            correction = mass * (sums[part][c : c + 1, :] + sums[part][3 + c : 4 + c, :])
            move = moves_ref[pl.ds(me * rows.disp_count + c * atom_rows + part, 1), :] - correction
            start = around_ref[pl.ds(me * rows.count + rows.coords[c] + part, 1), :]
            coords_out_ref[c, 0, :, lanes] = start + move
            velocity_out_ref[c, 0, :, lanes] = move * (1.0 / time_step)


def vmem(count):
    return [pl.BlockSpec(memory_space=pltpu.VMEM)] * count


def smem(count):
    return [pl.BlockSpec(memory_space=pltpu.SMEM)] * count


def hbm(count):
    return [pl.BlockSpec(memory_space=pltpu.HBM)] * count


def in_hbm(arrays):
    return [pltpu.with_memory_space_constraint(a, pltpu.HBM) for a in arrays]


def params(mebibytes):
    return pltpu.CompilerParams(vmem_limit_bytes=mebibytes * 1024 * 1024)


def cost(flops, moved):
    return pl.CostEstimate(flops=flops, bytes_accessed=moved, transcendentals=0)


def room_for(arrays):
    return [pltpu.VMEM(a.shape, a.dtype) for a in arrays]


def shards(
    coords,
    velocity,
    charge,
    inv_mass,
    tile_block,
    tile_atoms,
    active_tile_count,
    bond_atoms,
    cross_atoms,
    cross_side,
    cross_count,
):
    atoms = coords.shape[-1]
    tiles = tile_atoms.shape[2]
    domains = lax.axis_size("dom")
    strides = strides_of(domains)
    rows = Rows(atoms, bond_atoms.shape[-1], cross_side.shape[-1])
    whole_slab = domains == SUBLANES
    copies = domains if whole_slab else 1
    f32 = jnp.float32

    sent = (coords, charge, inv_mass, bond_atoms, cross_atoms)
    packed, rim = pl.pallas_call(
        functools.partial(pack_kernel, rows, copies),
        out_shape=(
            jax.ShapeDtypeStruct((copies * rows.count, LANES), f32),
            jax.ShapeDtypeStruct((4 * rows.shell_rows, LANES), f32),
        ),
        in_specs=hbm(len(sent)),
        out_specs=tuple(vmem(2)),
        scratch_shapes=room_for(sent)
        + [pltpu.SemaphoreType.DMA((len(sent),)), pltpu.VMEM((rows.count, LANES), f32)],
        compiler_params=params(4),
        name="pack",
    )(*in_hbm(sent))

    alone = (coords, charge, velocity, inv_mass, cross_side, tile_atoms)
    own = pl.pallas_call(
        functools.partial(own_kernel, rows),
        out_shape=(
            jax.ShapeDtypeStruct((4, atoms, LANES), f32),
            jax.ShapeDtypeStruct((4, tiles, TILE), f32),
            jax.ShapeDtypeStruct((tiles, TILE), jnp.int32),
            jax.ShapeDtypeStruct((4 * rows.atom_rows + rows.slot_rows, LANES), f32),
        ),
        in_specs=hbm(len(alone)),
        out_specs=tuple(vmem(4)),
        scratch_shapes=room_for(alone[:5]) + [pltpu.SemaphoreType.DMA((len(alone),))],
        compiler_params=params(4),
        cost_estimate=cost(64 * atoms * LANES, 16 * atoms * LANES),
        name="own",
    )(*in_hbm(alone))

    below = passed_along(rim, "slab", 1)
    above = passed_along(rim, "slab", -1)
    if whole_slab:
        around = from_slab(packed)

        def place():
            return [place_of(stride) for stride in strides]

    else:
        around = jnp.concatenate([packed] + [passed_along(packed, "dom", -stride) for stride in strides], axis=0)

        def place():
            return [1, 2, 3, 4]


    moves = pl.pallas_call(
        functools.partial(force_kernel, rows, copies, place),
        out_shape=jax.ShapeDtypeStruct((copies * rows.disp_count, LANES), f32),
        in_specs=smem(2) + hbm(1) + vmem(7),
        out_specs=vmem(1)[0],
        scratch_shapes=[
            pltpu.VMEM((4, 6 * rows.shell_rows, SUBLANES, LANES), f32),
            pltpu.VMEM((4, tiles, LANES), f32),
            pltpu.VMEM((3, atoms, LANES), f32),
            pltpu.SMEM(tile_block.shape, jnp.int32),
            pltpu.SemaphoreType.DMA(()),
        ],
        compiler_params=params(8),
        cost_estimate=cost(30 * tiles * TILE * TILE, 4 * around.size),
        name="force",
    )(active_tile_count, cross_count, *in_hbm([tile_block]), around, below, above, *own)

    if not whole_slab:
        return by_exchange(rows, strides, around, moves, cross_count)

    constraint_rows = rows.bond_rows + rows.slot_rows
    weight, matrix = pl.pallas_call(
        functools.partial(bond_kernel, rows, domains, strides),
        out_shape=(
            jax.ShapeDtypeStruct(((rows.bond_rows + 4 * rows.slot_rows) * 3 * domains, LANES), f32),
            jax.ShapeDtypeStruct((domains * rows.matrix, atoms // 2), jnp.bfloat16),
        ),
        in_specs=vmem(1),
        out_specs=tuple(vmem(2)),
        compiler_params=params(16),
        cost_estimate=cost(8 * domains * rows.matrix * atoms // 2, 4 * around.size),
        name="bonds",
    )(around)

    every_move = from_slab(moves)

    return pl.pallas_call(
        functools.partial(solve_kernel, rows, domains, strides),
        out_shape=(
            jax.ShapeDtypeStruct(coords.shape, f32),
            jax.ShapeDtypeStruct(coords.shape, f32),
        ),
        in_specs=vmem(4),
        out_specs=tuple(vmem(2)),
        scratch_shapes=[
            pltpu.VMEM((constraint_rows, SUBLANES * domains, LANES), f32),
            pltpu.VMEM((5, rows.atom_rows, SUBLANES * domains, LANES), f32),
        ],
        compiler_params=params(16),
        name="solve",
    )(around, every_move, weight, matrix)


def by_exchange(rows, strides, around, moves, cross_count):
    atom_count = rows.atom_rows * LANES
    shell = rows.shell_rows * LANES
    inside = around.reshape(5, rows.count, LANES)

    def flat(at, count):
        return inside[0, at : at + count].reshape(-1)

    def neighbours(at):
        return inside[1:, at : at + rows.shell_rows].reshape(-1)

    coords = jnp.stack([flat(at, rows.atom_rows) for at in rows.coords])
    inv_mass = flat(rows.mass, rows.atom_rows)
    displace = moves[: rows.live].reshape(3, atom_count)
    left = flat(rows.bond_first, rows.bond_rows).astype(jnp.int32)
    right = flat(rows.bond_second, rows.bond_rows).astype(jnp.int32)
    cross_left = flat(rows.cross_first, rows.slot_rows).astype(jnp.int32)
    cross_right = flat(rows.cross_second, rows.slot_rows).astype(jnp.int32)
    side = moves[rows.side : rows.side + rows.slot_rows].reshape(-1).astype(jnp.int32)
    flag = moves[rows.live : rows.side].reshape(-1)
    cross_index = side * shell + cross_right
    far_coords = jnp.stack([neighbours(at) for at in rows.coords])
    far_mass = neighbours(rows.mass)

    def weights(first, second, mass_first, mass_second):
        gap = first - second
        length = jnp.sqrt(jnp.sum(gap * gap, axis=0) + length_floor)
        return gap / length * lax.rsqrt(mass_first + mass_second)

    inner = weights(coords[:, left], coords[:, right], inv_mass[left], inv_mass[right])
    cross = flag * weights(
        coords[:, cross_left], far_coords[:, cross_index], inv_mass[cross_left], far_mass[cross_index]
    )

    def project(field):
        rim = field[:, :shell]
        far = jnp.concatenate([passed_along(rim, "dom", -stride) for stride in strides], axis=1)
        return (
            jnp.sum(inner * (field[:, left] - field[:, right]), axis=0),
            jnp.sum(cross * (field[:, cross_left] - far[:, cross_index]), axis=0),
        )

    def spread(values):
        pushed = inner * values[0]
        pushed_cross = cross * values[1]
        totals = jnp.zeros((3, atom_count), jnp.float32).at[:, left].add(pushed).at[:, right].add(-pushed)
        totals = totals.at[:, cross_left].add(pushed_cross)
        outward = jnp.zeros((3, 4 * shell), jnp.float32).at[:, cross_index].add(-pushed_cross)
        for code, stride in enumerate(strides):
            totals = totals.at[:, :shell].add(
                passed_along(outward[:, code * shell : (code + 1) * shell], "dom", stride)
            )
        return inv_mass * totals

    residue = project(displace)
    summed = residue
    for _ in range(ORDER):
        change = project(spread(residue))
        residue = tuple(now - step for now, step in zip(residue, change))
        summed = tuple(a + b for a, b in zip(summed, residue))
    move = displace - spread(summed)
    return (
        (coords + move).reshape(3, 1, 1, atom_count),
        (move * (1.0 / time_step)).reshape(3, 1, 1, atom_count),
    )


def solution(mesh):
    return jax.shard_map(
        shards,
        mesh=mesh,
        in_specs=(
            P(None, "slab", "dom", None),
            P(None, "slab", "dom", None),
            P("slab", "dom", None),
            P("slab", "dom", None),
            P("slab", "dom", None),
            P("slab", "dom", None, None),
            P("slab", "dom"),
            P(None, "slab", "dom", None),
            P(None, "slab", "dom", None),
            P("slab", "dom", None),
            P("slab", "dom"),
        ),
        out_specs=(P(None, "slab", "dom", None), P(None, "slab", "dom", None)),
        check_vma=False,
    )
```

```python
import functools

import jax
import jax.numpy as jnp
from jax import lax
from jax.experimental import pallas as pl
from jax.experimental.pallas import tpu as pltpu
from jax.sharding import PartitionSpec as P

TILE = 128
ORDER = 4
LANES = 128
SUBLANES = 8

time_step = 0.1
cutoff_sq = 16.0
force_scale = 4.0
length_floor = 0.25


def passed_along(array, axis, by):
    length = lax.axis_size(axis)
    return lax.ppermute(array, axis, [(i, (i + by) % length) for i in range(length)])


def first_of(domains):
    return domains - 1


def from_slab(blocks):
    length = lax.axis_size("dom")
    order = [(first_of(length) + i) % length for i in range(length)]
    return lax.all_to_all(blocks, "dom", 0, 0, axis_index_groups=[order], tiled=True)


def place_of(stride=0):
    length = lax.axis_size("dom")
    return lax.rem(lax.axis_index("dom") + (stride - first_of(length)) % length, length)


def strides_of(domains):
    row_width = max(2, domains // 8)
    return (1, -1, row_width, -row_width)


def round_up(count, step):
    return -(-count // step) * step


class Rows:
    def __init__(self, atoms, bonds, slots):
        self.atom_rows = atoms // LANES
        self.shell_rows = atoms // 2 // LANES
        self.bond_rows = bonds // LANES
        self.slot_rows = slots // LANES
        at = 0
        self.coords = []
        for _ in range(3):
            self.coords.append(at)
            at += self.atom_rows
        self.charge = at
        at += self.shell_rows
        self.mass = at
        at += self.atom_rows
        self.bond_first = at
        at += self.bond_rows
        self.bond_second = at
        at += self.bond_rows
        self.cross_first = at
        at += self.slot_rows
        self.cross_second = at
        at += self.slot_rows
        self.used = at
        self.count = round_up(at, SUBLANES)
        self.shell_terms = (self.bond_rows + self.slot_rows) * LANES
        self.inner_at = (0, self.shell_terms)
        self.cross_at = self.bond_rows * LANES
        self.far_at = self.shell_terms + self.bond_rows * LANES
        self.matrix = self.far_at + self.slot_rows * LANES
        self.live = 3 * self.atom_rows
        self.side = self.live + self.slot_rows
        self.disp_used = self.side + self.slot_rows
        self.disp_count = round_up(self.disp_used, SUBLANES)


def take_lanes(table, lanes):
    return jnp.take_along_axis(table, lanes, axis=1, mode="promise_in_bounds")


def pick(tables, index):
    lanes = index & (LANES - 1)
    chunk = index >> 7
    result = take_lanes(tables[0], lanes)
    for k in range(1, len(tables)):
        result = jnp.where(chunk == k, take_lanes(tables[k], lanes), result)
    return result


def fetched(sources, targets, sem_ref):
    copies = [pltpu.make_async_copy(s, t, sem_ref.at[n]) for n, (s, t) in enumerate(zip(sources, targets))]
    for copy in copies:
        copy.start()
    return copies


def pack_kernel(rows, copies, *refs):
    sources, (out_ref, rim_ref), targets, sem_ref = refs[:5], refs[5:7], refs[7:12], refs[12]
    block_ref = refs[13]
    for copy in fetched(sources, targets, sem_ref):
        copy.wait()
    coords_ref, charge_ref, mass_ref, bonds_ref, cross_ref = targets

    def put(row, value):
        for part in range(value.shape[1] // LANES):
            block_ref[pl.ds(row + part, 1), :] = value[:, part * LANES : (part + 1) * LANES]

    shell = rows.shell_rows * LANES
    fields = [coords_ref[c, 0] for c in range(3)] + [charge_ref[0, :, :shell]]
    for c in range(4):
        at = rows.coords[c] if c < 3 else rows.charge
        put(at, fields[c])
        for part in range(rows.shell_rows):
            rim_ref[pl.ds(c * rows.shell_rows + part, 1), :] = fields[c][:, part * LANES : (part + 1) * LANES]
    put(rows.mass, mass_ref[0])
    put(rows.bond_first, bonds_ref[0, 0].astype(jnp.float32))
    put(rows.bond_second, bonds_ref[1, 0].astype(jnp.float32))
    put(rows.cross_first, cross_ref[0, 0].astype(jnp.float32))
    put(rows.cross_second, cross_ref[1, 0].astype(jnp.float32))
    if rows.count > rows.used:
        block_ref[rows.used :, :] = jnp.zeros((rows.count - rows.used, LANES), jnp.float32)
    block = block_ref[...]
    for copy in range(copies):
        out_ref[pl.ds(copy * rows.count, rows.count), :] = block


SHRINK = 1.0 / 4.0
OUT_OF_REACH = 1000.0
PAIRS_STEP = 2
PIECE = 16


def pair_up(block_ref, live, blocks, order_ref):
    tiles = block_ref.shape[2]
    shape = (tiles, LANES)
    lane = lax.broadcasted_iota(jnp.int32, shape, 1)
    tile = lax.broadcasted_iota(jnp.int32, shape, 0)
    order_ref[...] = jnp.zeros(order_ref.shape, jnp.int32)
    order_ref[0:1, :tiles] = block_ref[0]

    def down(row):
        row = jnp.broadcast_to(row, (SUBLANES, LANES))
        start = lax.broadcasted_iota(jnp.int32, (SUBLANES, LANES), 0)
        return jnp.concatenate([take_lanes(row, start + at) for at in range(0, tiles, SUBLANES)], axis=0)

    across = jnp.where(lane[0:1] < live, order_ref[0:1, :], -1)
    along = down(across)
    rank = jnp.sum(jnp.where((along == across) & (tile < lane), 1, 0), axis=0, keepdims=True)
    start = jnp.zeros((1, LANES), jnp.int32)
    pairs = jnp.zeros((1, LANES), jnp.int32)
    for block in range(blocks):
        count = jnp.sum(jnp.where(across == block, 1.0, 0.0), axis=1, keepdims=True).astype(jnp.int32)
        start = jnp.where(across == block, 2 * pairs, start)
        pairs = pairs + ((count + 1) >> 1)
    place = down(jnp.where(across < 0, -1, start + rank))
    here = place == lane
    order_ref[0:1, :] = tiles + jnp.sum(jnp.where(here, tile - tiles, 0), axis=0, keepdims=True)
    order_ref[1:2, :] = jnp.sum(jnp.where(here, along, 0), axis=0, keepdims=True)
    order_ref[2:3, :] = pairs


def own_kernel(
    rows,
    live_ref,
    coords_hbm,
    charge_hbm,
    velocity_hbm,
    mass_hbm,
    side_hbm,
    block_hbm,
    atoms_hbm,
    own_ref,
    far_ref,
    index_ref,
    motion_ref,
    order_ref,
    coords_ref,
    charge_ref,
    velocity_ref,
    mass_ref,
    side_ref,
    block_ref,
    sem_ref,
):
    atom_rows = rows.atom_rows
    copies = fetched(
        (coords_hbm, charge_hbm, atoms_hbm.at[0, 0], velocity_hbm, mass_hbm, side_hbm, block_hbm),
        (coords_ref, charge_ref, index_ref, velocity_ref, mass_ref, side_ref, block_ref),
        sem_ref,
    )
    down = lax.broadcasted_iota(jnp.int32, (SUBLANES, LANES), 0)
    copies[0].wait()
    copies[1].wait()

    def lanes_of(part):
        return slice(part * LANES, (part + 1) * LANES)

    table = []
    for c in range(4):
        field = coords_ref[c, 0] * SHRINK if c < 3 else charge_ref[0]
        table.append(
            [jnp.broadcast_to(field[:, lanes_of(part)], (SUBLANES, LANES)) for part in range(atom_rows)]
        )
    for part in range(atom_rows):
        for group in range(LANES // SUBLANES):
            at = part * LANES + group * SUBLANES
            for c in range(4):
                value = take_lanes(table[c][part], down + group * SUBLANES)
                own_ref[c, pl.ds(at, SUBLANES), :] = value if c < 3 else value * 8.0
    copies[2].wait()
    for group in range(index_ref.shape[0] // SUBLANES):
        at = pl.ds(group * SUBLANES, SUBLANES)
        index = index_ref[at, :]
        for c in range(4):
            far_ref[c, at, :] = pick(table[c], index)
    for copy in copies[3:]:
        copy.wait()
    pair_up(block_ref, live_ref[0, 0], atom_rows * LANES // TILE, order_ref)
    fields = [velocity_ref[c, 0] for c in range(3)] + [mass_ref[0], side_ref[0].astype(jnp.float32)]
    at = 0
    for field in fields:
        for part in range(field.shape[1] // LANES):
            motion_ref[pl.ds(at, 1), :] = field[:, lanes_of(part)]
            at += 1


def force_kernel(
    rows,
    copies,
    place,
    count_ref,
    order_hbm,
    around_ref,
    below_ref,
    above_ref,
    own_ref,
    near_ref,
    index_ref,
    motion_ref,
    out_ref,
    table_ref,
    far_ref,
    sum_ref,
    order_ref,
    sem_ref,
):
    atom_rows, shell_rows = rows.atom_rows, rows.shell_rows
    tiles = index_ref.shape[0]
    order_copy = pltpu.make_async_copy(order_hbm, order_ref, sem_ref)
    order_copy.start()
    holders = place()
    starts = [rows.coords[0], rows.coords[1], rows.coords[2], rows.charge]
    entry_rows = 6 * shell_rows

    def broadcast(row):
        return jnp.broadcast_to(row, (SUBLANES, LANES))

    for c in range(4):
        factor = SHRINK if c < 3 else 1.0
        at = 0
        for neighbour in range(4):
            base = holders[neighbour] * rows.count + starts[c]
            for part in range(shell_rows):
                table_ref[c, at] = broadcast(around_ref[pl.ds(base + part, 1), :] * factor)
                at += 1
        for slab_ref in (below_ref, above_ref):
            for part in range(shell_rows):
                table_ref[c, at] = broadcast(slab_ref[pl.ds(c * shell_rows + part, 1), :] * factor)
                at += 1

    for group in range(tiles // SUBLANES):
        at = pl.ds(group * SUBLANES, SUBLANES)
        index = index_ref[at, :]
        lanes = index & (LANES - 1)
        chunk = index >> 7
        values = [near_ref[c, at, :] for c in range(4)]
        for k in range(entry_rows):
            here = chunk == atom_rows + k
            values = [jnp.where(here, take_lanes(table_ref[c, k], lanes), values[c]) for c in range(4)]
        for c in range(4):
            far_ref[c, at, :] = values[c]

    sum_ref[...] = jnp.zeros(sum_ref.shape, jnp.float32)
    far_ref[0, tiles:, :] = jnp.full((SUBLANES, LANES), OUT_OF_REACH, jnp.float32)
    for c in range(1, 4):
        far_ref[c, tiles:, :] = jnp.zeros((SUBLANES, LANES), jnp.float32)
    order_copy.wait()

    softening = 1.0 / cutoff_sq

    def add_pair(pair):
        base = order_ref[1, 2 * pair] * TILE
        fars = [
            [jnp.broadcast_to(far_ref[c, pl.ds(order_ref[0, 2 * pair + n], 1), :], (PIECE, LANES)) for c in range(4)]
            for n in range(2)
        ]
        for piece in range(TILE // PIECE):
            at = pl.ds(pl.multiple_of(base + piece * PIECE, PIECE), PIECE)
            own = [own_ref[c, at, :] for c in range(4)]
            pushes = []
            for far in fars:
                gap = [own[c] - far[c] for c in range(3)]
                square = gap[0] * gap[0] + gap[1] * gap[1] + gap[2] * gap[2]
                inverse = pl.reciprocal(square + softening, approx=True)
                weight = jnp.maximum(inverse - 1.0 / (1.0 + softening), 0.0)
                strength = (inverse - own[3] * far[3]) * (weight * weight)
                pushes.append([strength * gap[c] for c in range(3)])
            for c in range(3):
                sum_ref[c, at, :] = sum_ref[c, at, :] + (pushes[0][c] + pushes[1][c])

    def add_pairs(step, _):
        for n in range(PAIRS_STEP):
            add_pair(step * PAIRS_STEP + n)
        return 0

    lax.fori_loop(0, lax.div(order_ref[2, 0] + PAIRS_STEP - 1, PAIRS_STEP), add_pairs, 0)

    scale = time_step * time_step * force_scale * 4.0 / 2048.0 * (1.0 + softening) ** 2

    lane = lax.broadcasted_iota(jnp.int32, (LANES, LANES), 1)
    columns = jnp.zeros((LANES, LANES), jnp.float32)
    for c in range(3):
        for part in range(atom_rows):
            total = jnp.sum(sum_ref[c, pl.ds(part * LANES, LANES), :], axis=1, keepdims=True)
            columns = jnp.where(lane == c * atom_rows + part, total, columns)
    totals = columns.T[: 3 * atom_rows, :]
    mass = motion_ref[pl.ds(3 * atom_rows, atom_rows), :]
    moved = time_step * motion_ref[pl.ds(0, 3 * atom_rows), :] + scale * totals * jnp.concatenate([mass] * 3, axis=0)
    for copy in range(copies):
        out_ref[pl.ds(copy * rows.disp_count, 3 * atom_rows), :] = moved
    slot = lax.broadcasted_iota(jnp.int32, (1, LANES), 1)
    for part in range(rows.slot_rows):
        flag = jnp.where(slot + part * LANES < count_ref[0, 0], 1.0, 0.0)
        side = motion_ref[pl.ds(4 * atom_rows + part, 1), :]
        for copy in range(copies):
            out_ref[pl.ds(copy * rows.disp_count + rows.live + part, 1), :] = flag
            out_ref[pl.ds(copy * rows.disp_count + rows.side + part, 1), :] = side
    if rows.disp_count > rows.disp_used:
        for copy in range(copies):
            out_ref[pl.ds(copy * rows.disp_count + rows.disp_used, rows.disp_count - rows.disp_used), :] = jnp.zeros(
                (rows.disp_count - rows.disp_used, LANES), jnp.float32
            )


def bond_kernel(rows, domains, strides, around_ref, weight_ref, matrix_ref):
    atom_rows, shell_rows = rows.atom_rows, rows.shell_rows

    def load(row):
        return around_ref[pl.ds(row, domains, stride=rows.count), :]

    def index(row):
        return load(row).astype(jnp.int32)

    fields = [[load(at + part) for part in range(atom_rows)] for at in rows.coords + [rows.mass]]

    def put_weights(first, second, at):
        gap = [first[c] - second[c] for c in range(3)]
        length_sq = gap[0] * gap[0] + gap[1] * gap[1] + gap[2] * gap[2] + length_floor
        scale = lax.rsqrt(length_sq) * lax.rsqrt(first[3] + second[3])
        for c in range(3):
            weight_ref[pl.ds((at * 3 + c) * domains, domains), :] = gap[c] * scale

    for part in range(rows.bond_rows):
        first = index(rows.bond_first + part)
        second = index(rows.bond_second + part)
        put_weights([pick(f, first) for f in fields], [pick(f, second) for f in fields], part)
    shells = [f[:shell_rows] for f in fields]
    for part in range(rows.slot_rows):
        first = index(rows.cross_first + part)
        second = index(rows.cross_second + part)
        ends = [pick(f, first) for f in shells]
        for code, stride in enumerate(strides):
            seen = pltpu.roll(second, stride % domains, 0)
            others = [pltpu.roll(pick(f, seen), -stride % domains, 0) for f in shells]
            put_weights(ends, others, rows.bond_rows + part * 4 + code)

    down = lax.broadcasted_iota(jnp.int32, (SUBLANES, LANES), 0)
    group_rows = 4 * SUBLANES

    kind = jnp.bfloat16 if shell_rows * LANES <= 256 else jnp.float32
    across = lax.broadcasted_iota(jnp.int32, (group_rows, LANES), 1).astype(jnp.float32)
    lanes = [(across + float(block * LANES)).astype(kind) for block in range(shell_rows)]

    def column(row, step, half=0):
        row = jnp.broadcast_to(row, (SUBLANES, LANES))
        groups = [take_lanes(row, down + at) for at in range(step * group_rows, (step + 1) * group_rows, SUBLANES)]
        return (jnp.concatenate(groups, axis=0) - float(half * shell_rows * LANES)).astype(kind)

    def put(at, ends, signs):
        for block in range(shell_rows):
            value = jnp.zeros((group_rows, LANES), kind)
            for end, sign in zip(ends, signs):
                value = jnp.where(end == lanes[block], jnp.full((group_rows, LANES), sign, kind), value)
            matrix_ref[pl.ds(at, group_rows), block * LANES : (block + 1) * LANES] = value.astype(matrix_ref.dtype)

    def build(domain, _):
        start = pl.multiple_of(domain * rows.matrix, LANES)
        for part in range(rows.bond_rows):
            first = around_ref[pl.ds(domain * rows.count + rows.bond_first + part, 1), :]
            second = around_ref[pl.ds(domain * rows.count + rows.bond_second + part, 1), :]
            for step in range(LANES // group_rows):
                for half in range(2):
                    ends = (column(first, step, half), column(second, step, half))
                    put(start + rows.inner_at[half] + part * LANES + step * group_rows, ends, (1.0, -1.0))
        for part in range(rows.slot_rows):
            for row_at, to, sign in (
                (rows.cross_first, rows.cross_at, 1.0),
                (rows.cross_second, rows.far_at, -1.0),
            ):
                row = around_ref[pl.ds(domain * rows.count + row_at + part, 1), :]
                for step in range(LANES // group_rows):
                    put(start + to + part * LANES + step * group_rows, (column(row, step),), (sign,))
        return 0

    lax.fori_loop(0, domains, build, 0)


def solve_kernel(
    rows,
    domains,
    strides,
    around_ref,
    moves_ref,
    weight_ref,
    matrix_ref,
    coords_out_ref,
    velocity_out_ref,
    push_ref,
    field_ref,
):
    atom_rows, shell_rows = rows.atom_rows, rows.shell_rows
    bond_rows, slot_rows = rows.bond_rows, rows.slot_rows
    me = place_of()

    def load(row):
        return around_ref[pl.ds(row, domains, stride=rows.count), :]

    def index(row):
        return load(row).astype(jnp.int32)

    inner_first = [index(rows.bond_first + p) for p in range(bond_rows)]
    inner_second = [index(rows.bond_second + p) for p in range(bond_rows)]
    cross_first = [index(rows.cross_first + p) for p in range(slot_rows)]
    cross_second = [index(rows.cross_second + p) for p in range(slot_rows)]
    masses = [load(rows.mass + p) for p in range(atom_rows)]

    def move_rows(row):
        return moves_ref[pl.ds(row, domains, stride=rows.disp_count), :]

    def weight_rows(at, c):
        return weight_ref[pl.ds((at * 3 + c) * domains, domains), :]

    sides = [move_rows(rows.side + p) for p in range(slot_rows)]
    cross_weights = []
    for part in range(slot_rows):
        live = move_rows(rows.live + part)
        for c in range(3):
            value = 0.0
            for code in range(4):
                value = jnp.where(sides[part] == code, weight_rows(bond_rows + part * 4 + code, c), value)
            cross_weights.append(value * live)

    def weight(at, c):
        return weight_rows(at, c) if at < bond_rows else cross_weights[(at - bond_rows) * 3 + c]

    def project(fields):
        result = []
        for part in range(bond_rows):
            total = 0.0
            for c in range(3):
                ends = pick(fields[c], inner_first[part]) - pick(fields[c], inner_second[part])
                total = total + weight(part, c) * ends
            result.append(total)
        for part in range(slot_rows):
            seen = [pltpu.roll(cross_second[part], stride % domains, 0) for stride in strides]
            total = 0.0
            for c in range(3):
                shell = fields[c][:shell_rows]
                other = 0.0
                for code, stride in enumerate(strides):
                    value = pltpu.roll(pick(shell, seen[code]), -stride % domains, 0)
                    other = jnp.where(sides[part] == code, value, other)
                total = total + weight(bond_rows + part, c) * (pick(shell, cross_first[part]) - other)
            result.append(total)
        return result

    def put_pushes(values):
        for at, value in enumerate(values):
            for c in range(3):
                pushed = weight(at, c) * value
                high = pushed.astype(jnp.bfloat16).astype(jnp.float32)
                push_ref[at, pl.ds(c * domains, domains), :] = high
                push_ref[at, pl.ds((3 + c) * domains, domains), :] = pushed - high

    def pushes_of(at, domain):
        return push_ref[at, pl.ds(domain, SUBLANES, stride=domains), :]

    def product(pushes, domain, at):
        start = domain * rows.matrix + at
        if not isinstance(start, int):
            start = pl.multiple_of(start, LANES)
        pushes = pushes[0] if len(pushes) == 1 else jnp.concatenate(pushes, axis=1)
        result = jnp.dot(
            pushes.astype(jnp.bfloat16),
            matrix_ref[pl.ds(start, pushes.shape[1]), :],
            preferred_element_type=jnp.float32,
        )
        return [result[:, p * LANES : (p + 1) * LANES] for p in range(shell_rows)]

    def inner_totals(pushes, domain):
        return product(pushes, domain, 0) + product(pushes[:bond_rows], domain, rows.shell_terms)

    def far_totals(pushes, domain, codes):
        masked = []
        for part in range(slot_rows):
            side = moves_ref[pl.ds(domain * rows.disp_count + rows.side + part, 1), :]
            side = jnp.broadcast_to(side, (SUBLANES, LANES))
            pushed = pushes[bond_rows + part]
            masked.append(jnp.concatenate([jnp.where(side == code, pushed, 0.0) for code in codes], axis=0))
        return product(masked, domain, rows.far_at)

    def spread(values):
        put_pushes(values)
        for domain in range(domains):
            pushes = [pushes_of(at, domain) for at in range(bond_rows + slot_rows)]
            for part, total in enumerate(inner_totals(pushes, domain)):
                field_ref[0, part, pl.ds(domain, SUBLANES, stride=domains), :] = total
            for part, total in enumerate(far_totals(pushes, domain, range(4))):
                for code, stride in enumerate(strides):
                    field_ref[1 + code, part, pl.ds((domain + stride) % domains, SUBLANES, stride=domains), :] = total[
                        code * SUBLANES : (code + 1) * SUBLANES, :
                    ]

        def field(c, part):
            pieces = [
                field_ref[source, part, pl.ds(row * domains, domains), :]
                for source in range(5 if part < shell_rows else 1)
                for row in (c, 3 + c)
            ]
            return masses[part] * functools.reduce(lambda a, b: a + b, pieces)

        return [[field(c, part) for part in range(atom_rows)] for c in range(3)]

    moves = [
        [move_rows(c * atom_rows + p) for p in range(atom_rows)]
        for c in range(3)
    ]
    push_ref[...] = jnp.zeros(push_ref.shape, jnp.float32)
    residue = project(moves)

    def expand(_, carry):
        residue, summed = carry
        change = project(spread(residue))
        residue = [now - step for now, step in zip(residue, change)]
        return residue, [a + b for a, b in zip(summed, residue)]

    residue, summed = lax.fori_loop(0, ORDER, expand, (residue, residue))
    put_pushes(summed)
    sums = inner_totals([pushes_of(at, me) for at in range(bond_rows + slot_rows)], me)
    for code, stride in enumerate(strides):
        owner = lax.rem(me + (-stride) % domains, domains)
        pushes = [pushes_of(at, owner) for at in range(bond_rows + slot_rows)]
        for part, total in enumerate(far_totals(pushes, owner, [code])):
            sums[part] = sums[part] + total
    for part in range(atom_rows):
        lanes = slice(part * LANES, (part + 1) * LANES)
        mass = around_ref[pl.ds(me * rows.count + rows.mass + part, 1), :]
        for c in range(3):
            correction = mass * (sums[part][c : c + 1, :] + sums[part][3 + c : 4 + c, :])
            move = moves_ref[pl.ds(me * rows.disp_count + c * atom_rows + part, 1), :] - correction
            start = around_ref[pl.ds(me * rows.count + rows.coords[c] + part, 1), :]
            coords_out_ref[c, 0, :, lanes] = start + move
            velocity_out_ref[c, 0, :, lanes] = move * (1.0 / time_step)


def vmem(count):
    return [pl.BlockSpec(memory_space=pltpu.VMEM)] * count


def smem(count):
    return [pl.BlockSpec(memory_space=pltpu.SMEM)] * count


def hbm(count):
    return [pl.BlockSpec(memory_space=pltpu.HBM)] * count


def any_space(count):
    return [pl.BlockSpec(memory_space=pl.ANY)] * count


def in_hbm(arrays):
    return [pltpu.with_memory_space_constraint(a, pltpu.HBM) for a in arrays]


def params(mebibytes):
    return pltpu.CompilerParams(vmem_limit_bytes=mebibytes * 1024 * 1024)


def cost(flops, moved):
    return pl.CostEstimate(flops=flops, bytes_accessed=moved, transcendentals=0)


def room_for(arrays):
    return [pltpu.VMEM(a.shape, a.dtype) for a in arrays]


def shards(
    coords,
    velocity,
    charge,
    inv_mass,
    tile_block,
    tile_atoms,
    active_tile_count,
    bond_atoms,
    cross_atoms,
    cross_side,
    cross_count,
):
    atoms = coords.shape[-1]
    tiles = tile_atoms.shape[2]
    domains = lax.axis_size("dom")
    strides = strides_of(domains)
    rows = Rows(atoms, bond_atoms.shape[-1], cross_side.shape[-1])
    whole_slab = domains == SUBLANES
    copies = domains if whole_slab else 1
    f32 = jnp.float32

    sent = (coords, charge, inv_mass, bond_atoms, cross_atoms)
    packed, rim = pl.pallas_call(
        functools.partial(pack_kernel, rows, copies),
        out_shape=(
            jax.ShapeDtypeStruct((copies * rows.count, LANES), f32),
            jax.ShapeDtypeStruct((4 * rows.shell_rows, LANES), f32),
        ),
        in_specs=hbm(len(sent)),
        out_specs=tuple(vmem(2)),
        scratch_shapes=room_for(sent)
        + [pltpu.SemaphoreType.DMA((len(sent),)), pltpu.VMEM((rows.count, LANES), f32)],
        compiler_params=params(4),
        name="pack",
    )(*in_hbm(sent))

    alone = (coords, charge, velocity, inv_mass, cross_side, tile_block, tile_atoms)
    *own, order = pl.pallas_call(
        functools.partial(own_kernel, rows),
        out_shape=(
            jax.ShapeDtypeStruct((4, atoms, LANES), f32),
            jax.ShapeDtypeStruct((4, tiles, TILE), f32),
            jax.ShapeDtypeStruct((tiles, TILE), jnp.int32),
            jax.ShapeDtypeStruct((4 * rows.atom_rows + rows.slot_rows, LANES), f32),
            jax.ShapeDtypeStruct((SUBLANES, LANES), jnp.int32),
        ),
        in_specs=smem(1) + hbm(len(alone)),
        out_specs=tuple(vmem(5)),
        scratch_shapes=room_for(alone[:6]) + [pltpu.SemaphoreType.DMA((len(alone),))],
        compiler_params=params(4),
        cost_estimate=cost(64 * atoms * LANES, 16 * atoms * LANES),
        name="own",
    )(active_tile_count, *in_hbm(alone))

    below = passed_along(rim, "slab", 1)
    above = passed_along(rim, "slab", -1)
    if whole_slab:
        around = from_slab(packed)

        def place():
            return [place_of(stride) for stride in strides]

    else:
        around = jnp.concatenate([packed] + [passed_along(packed, "dom", -stride) for stride in strides], axis=0)

        def place():
            return [1, 2, 3, 4]


    moves = pl.pallas_call(
        functools.partial(force_kernel, rows, copies, place),
        out_shape=jax.ShapeDtypeStruct((copies * rows.disp_count, LANES), f32),
        in_specs=smem(1) + any_space(1) + vmem(7),
        out_specs=vmem(1)[0],
        scratch_shapes=[
            pltpu.VMEM((4, 6 * rows.shell_rows, SUBLANES, LANES), f32),
            pltpu.VMEM((4, tiles + SUBLANES, LANES), f32),
            pltpu.VMEM((3, atoms, LANES), f32),
            pltpu.SMEM(order.shape, jnp.int32),
            pltpu.SemaphoreType.DMA(()),
        ],
        compiler_params=params(8),
        cost_estimate=cost(30 * tiles * TILE * TILE, 4 * around.size),
        name="force",
    )(cross_count, order, around, below, above, *own)

    if not whole_slab:
        return by_exchange(rows, strides, around, moves, cross_count)

    constraint_rows = rows.bond_rows + rows.slot_rows
    weight, matrix = pl.pallas_call(
        functools.partial(bond_kernel, rows, domains, strides),
        out_shape=(
            jax.ShapeDtypeStruct(((rows.bond_rows + 4 * rows.slot_rows) * 3 * domains, LANES), f32),
            jax.ShapeDtypeStruct((domains * rows.matrix, atoms // 2), jnp.bfloat16),
        ),
        in_specs=vmem(1),
        out_specs=tuple(vmem(2)),
        compiler_params=params(16),
        cost_estimate=cost(8 * domains * rows.matrix * atoms // 2, 4 * around.size),
        name="bonds",
    )(around)

    every_move = from_slab(moves)

    return pl.pallas_call(
        functools.partial(solve_kernel, rows, domains, strides),
        out_shape=(
            jax.ShapeDtypeStruct(coords.shape, f32),
            jax.ShapeDtypeStruct(coords.shape, f32),
        ),
        in_specs=vmem(4),
        out_specs=tuple(vmem(2)),
        scratch_shapes=[
            pltpu.VMEM((constraint_rows, SUBLANES * domains, LANES), f32),
            pltpu.VMEM((5, rows.atom_rows, SUBLANES * domains, LANES), f32),
        ],
        compiler_params=params(16),
        name="solve",
    )(around, every_move, weight, matrix)


def by_exchange(rows, strides, around, moves, cross_count):
    atom_count = rows.atom_rows * LANES
    shell = rows.shell_rows * LANES
    inside = around.reshape(5, rows.count, LANES)

    def flat(at, count):
        return inside[0, at : at + count].reshape(-1)

    def neighbours(at):
        return inside[1:, at : at + rows.shell_rows].reshape(-1)

    coords = jnp.stack([flat(at, rows.atom_rows) for at in rows.coords])
    inv_mass = flat(rows.mass, rows.atom_rows)
    displace = moves[: rows.live].reshape(3, atom_count)
    left = flat(rows.bond_first, rows.bond_rows).astype(jnp.int32)
    right = flat(rows.bond_second, rows.bond_rows).astype(jnp.int32)
    cross_left = flat(rows.cross_first, rows.slot_rows).astype(jnp.int32)
    cross_right = flat(rows.cross_second, rows.slot_rows).astype(jnp.int32)
    side = moves[rows.side : rows.side + rows.slot_rows].reshape(-1).astype(jnp.int32)
    flag = moves[rows.live : rows.side].reshape(-1)
    cross_index = side * shell + cross_right
    far_coords = jnp.stack([neighbours(at) for at in rows.coords])
    far_mass = neighbours(rows.mass)

    def weights(first, second, mass_first, mass_second):
        gap = first - second
        length = jnp.sqrt(jnp.sum(gap * gap, axis=0) + length_floor)
        return gap / length * lax.rsqrt(mass_first + mass_second)

    inner = weights(coords[:, left], coords[:, right], inv_mass[left], inv_mass[right])
    cross = flag * weights(
        coords[:, cross_left], far_coords[:, cross_index], inv_mass[cross_left], far_mass[cross_index]
    )

    def project(field):
        rim = field[:, :shell]
        far = jnp.concatenate([passed_along(rim, "dom", -stride) for stride in strides], axis=1)
        return (
            jnp.sum(inner * (field[:, left] - field[:, right]), axis=0),
            jnp.sum(cross * (field[:, cross_left] - far[:, cross_index]), axis=0),
        )

    def spread(values):
        pushed = inner * values[0]
        pushed_cross = cross * values[1]
        totals = jnp.zeros((3, atom_count), jnp.float32).at[:, left].add(pushed).at[:, right].add(-pushed)
        totals = totals.at[:, cross_left].add(pushed_cross)
        outward = jnp.zeros((3, 4 * shell), jnp.float32).at[:, cross_index].add(-pushed_cross)
        for code, stride in enumerate(strides):
            totals = totals.at[:, :shell].add(
                passed_along(outward[:, code * shell : (code + 1) * shell], "dom", stride)
            )
        return inv_mass * totals

    residue = project(displace)
    summed = residue
    for _ in range(ORDER):
        change = project(spread(residue))
        residue = tuple(now - step for now, step in zip(residue, change))
        summed = tuple(a + b for a, b in zip(summed, residue))
    move = displace - spread(summed)
    return (
        (coords + move).reshape(3, 1, 1, atom_count),
        (move * (1.0 / time_step)).reshape(3, 1, 1, atom_count),
    )


def solution(mesh):
    return jax.shard_map(
        shards,
        mesh=mesh,
        in_specs=(
            P(None, "slab", "dom", None),
            P(None, "slab", "dom", None),
            P("slab", "dom", None),
            P("slab", "dom", None),
            P("slab", "dom", None),
            P("slab", "dom", None, None),
            P("slab", "dom"),
            P(None, "slab", "dom", None),
            P(None, "slab", "dom", None),
            P("slab", "dom", None),
            P("slab", "dom"),
        ),
        out_specs=(P(None, "slab", "dom", None), P(None, "slab", "dom", None)),
        check_vma=False,
    )
```

```python
import functools

import jax
import jax.numpy as jnp
from jax import lax
from jax.experimental import pallas as pl
from jax.experimental.pallas import tpu as pltpu
from jax.sharding import PartitionSpec as P

TILE = 128
ORDER = 4
LANES = 128
SUBLANES = 8

time_step = 0.1
cutoff_sq = 16.0
force_scale = 4.0
length_floor = 0.25


def passed_along(array, axis, by):
    length = lax.axis_size(axis)
    return lax.ppermute(array, axis, [(i, (i + by) % length) for i in range(length)])


def first_of(domains):
    return domains - 1


def from_slab(blocks):
    length = lax.axis_size("dom")
    order = [(first_of(length) + i) % length for i in range(length)]
    return lax.all_to_all(blocks, "dom", 0, 0, axis_index_groups=[order], tiled=True)


def place_of(stride=0):
    length = lax.axis_size("dom")
    return lax.rem(lax.axis_index("dom") + (stride - first_of(length)) % length, length)


def strides_of(domains):
    row_width = max(2, domains // 8)
    return (1, -1, row_width, -row_width)


def round_up(count, step):
    return -(-count // step) * step


class Rows:
    def __init__(self, atoms, bonds, slots):
        self.atom_rows = atoms // LANES
        self.shell_rows = atoms // 2 // LANES
        self.bond_rows = bonds // LANES
        self.slot_rows = slots // LANES
        at = 0
        self.coords = []
        for _ in range(3):
            self.coords.append(at)
            at += self.atom_rows
        self.charge = at
        at += self.shell_rows
        self.mass = at
        at += self.atom_rows
        self.bond_first = at
        at += self.bond_rows
        self.bond_second = at
        at += self.bond_rows
        self.cross_first = at
        at += self.slot_rows
        self.cross_second = at
        at += self.slot_rows
        self.used = at
        self.count = round_up(at, SUBLANES)
        self.shell_terms = (self.bond_rows + self.slot_rows) * LANES
        self.inner_at = (0, self.shell_terms)
        self.cross_at = self.bond_rows * LANES
        self.far_at = self.shell_terms + self.bond_rows * LANES
        self.matrix = self.far_at + self.slot_rows * LANES
        self.live = 3 * self.atom_rows
        self.side = self.live + self.slot_rows
        self.disp_used = self.side + self.slot_rows
        self.disp_count = round_up(self.disp_used, SUBLANES)


def take_lanes(table, lanes):
    return jnp.take_along_axis(table, lanes, axis=1, mode="promise_in_bounds")


def pick(tables, index):
    lanes = index & (LANES - 1)
    chunk = index >> 7
    result = take_lanes(tables[0], lanes)
    for k in range(1, len(tables)):
        result = jnp.where(chunk == k, take_lanes(tables[k], lanes), result)
    return result


def fetched(sources, targets, sem_ref):
    copies = [pltpu.make_async_copy(s, t, sem_ref.at[n]) for n, (s, t) in enumerate(zip(sources, targets))]
    for copy in copies:
        copy.start()
    return copies


def pack_kernel(rows, copies, *refs):
    sources, (out_ref, rim_ref), targets, sem_ref = refs[:5], refs[5:7], refs[7:12], refs[12]
    block_ref = refs[13]
    for copy in fetched(sources, targets, sem_ref):
        copy.wait()
    coords_ref, charge_ref, mass_ref, bonds_ref, cross_ref = targets

    def put(row, value):
        for part in range(value.shape[1] // LANES):
            block_ref[pl.ds(row + part, 1), :] = value[:, part * LANES : (part + 1) * LANES]

    shell = rows.shell_rows * LANES
    fields = [coords_ref[c, 0] for c in range(3)] + [charge_ref[0, :, :shell]]
    for c in range(4):
        at = rows.coords[c] if c < 3 else rows.charge
        put(at, fields[c])
        for part in range(rows.shell_rows):
            rim_ref[pl.ds(c * rows.shell_rows + part, 1), :] = fields[c][:, part * LANES : (part + 1) * LANES]
    put(rows.mass, mass_ref[0])
    put(rows.bond_first, bonds_ref[0, 0].astype(jnp.float32))
    put(rows.bond_second, bonds_ref[1, 0].astype(jnp.float32))
    put(rows.cross_first, cross_ref[0, 0].astype(jnp.float32))
    put(rows.cross_second, cross_ref[1, 0].astype(jnp.float32))
    if rows.count > rows.used:
        block_ref[rows.used :, :] = jnp.zeros((rows.count - rows.used, LANES), jnp.float32)
    block = block_ref[...]
    for copy in range(copies):
        out_ref[pl.ds(copy * rows.count, rows.count), :] = block


SHRINK = 1.0 / 4.0
OUT_OF_REACH = 1000.0
TILES_STEP = 4
PIECE = 32


def own_kernel(
    rows,
    coords_hbm,
    charge_hbm,
    velocity_hbm,
    mass_hbm,
    side_hbm,
    atoms_hbm,
    own_ref,
    far_ref,
    index_ref,
    motion_ref,
    coords_ref,
    charge_ref,
    velocity_ref,
    mass_ref,
    side_ref,
    sem_ref,
):
    atom_rows = rows.atom_rows
    copies = fetched(
        (coords_hbm, charge_hbm, atoms_hbm.at[0, 0], velocity_hbm, mass_hbm, side_hbm),
        (coords_ref, charge_ref, index_ref, velocity_ref, mass_ref, side_ref),
        sem_ref,
    )
    down = lax.broadcasted_iota(jnp.int32, (SUBLANES, LANES), 0)
    copies[0].wait()
    copies[1].wait()

    def lanes_of(part):
        return slice(part * LANES, (part + 1) * LANES)

    table = []
    for c in range(4):
        field = coords_ref[c, 0] * SHRINK if c < 3 else charge_ref[0]
        table.append(
            [jnp.broadcast_to(field[:, lanes_of(part)], (SUBLANES, LANES)) for part in range(atom_rows)]
        )
    for part in range(atom_rows):
        for group in range(LANES // SUBLANES):
            at = part * LANES + group * SUBLANES
            for c in range(4):
                value = take_lanes(table[c][part], down + group * SUBLANES)
                own_ref[c, pl.ds(at, SUBLANES), :] = value if c < 3 else value * 8.0
    copies[2].wait()
    for group in range(index_ref.shape[0] // SUBLANES):
        at = pl.ds(group * SUBLANES, SUBLANES)
        index = index_ref[at, :]
        for c in range(4):
            far_ref[c, at, :] = pick(table[c], index)
    for copy in copies[3:]:
        copy.wait()
    fields = [velocity_ref[c, 0] for c in range(3)] + [mass_ref[0], side_ref[0].astype(jnp.float32)]
    at = 0
    for field in fields:
        for part in range(field.shape[1] // LANES):
            motion_ref[pl.ds(at, 1), :] = field[:, lanes_of(part)]
            at += 1


def force_kernel(
    rows,
    copies,
    place,
    live_ref,
    count_ref,
    block_hbm,
    around_ref,
    below_ref,
    above_ref,
    own_ref,
    near_ref,
    index_ref,
    motion_ref,
    out_ref,
    table_ref,
    far_ref,
    sum_ref,
    block_ref,
    sem_ref,
):
    atom_rows, shell_rows = rows.atom_rows, rows.shell_rows
    tiles = index_ref.shape[0]
    block_copy = pltpu.make_async_copy(block_hbm, block_ref, sem_ref)
    block_copy.start()
    live = live_ref[0, 0]
    holders = place()
    starts = [rows.coords[0], rows.coords[1], rows.coords[2], rows.charge]
    entry_rows = 6 * shell_rows

    def broadcast(row):
        return jnp.broadcast_to(row, (SUBLANES, LANES))

    for c in range(4):
        factor = SHRINK if c < 3 else 1.0
        at = 0
        for neighbour in range(4):
            base = holders[neighbour] * rows.count + starts[c]
            for part in range(shell_rows):
                table_ref[c, at] = broadcast(around_ref[pl.ds(base + part, 1), :] * factor)
                at += 1
        for slab_ref in (below_ref, above_ref):
            for part in range(shell_rows):
                table_ref[c, at] = broadcast(slab_ref[pl.ds(c * shell_rows + part, 1), :] * factor)
                at += 1

    for group in range(tiles // SUBLANES):
        at = pl.ds(group * SUBLANES, SUBLANES)
        index = index_ref[at, :]
        lanes = index & (LANES - 1)
        chunk = index >> 7
        values = [near_ref[c, at, :] for c in range(4)]
        for k in range(entry_rows):
            here = chunk == atom_rows + k
            values = [jnp.where(here, take_lanes(table_ref[c, k], lanes), values[c]) for c in range(4)]
        for c in range(4):
            far_ref[c, at, :] = values[c]

    sum_ref[...] = jnp.zeros(sum_ref.shape, jnp.float32)
    block_copy.wait()
    down = lax.broadcasted_iota(jnp.int32, (tiles, LANES), 0)
    far_ref[0] = jnp.where(down < live, far_ref[0], OUT_OF_REACH)

    softening = 1.0 / cutoff_sq

    def add_tile(tile):
        base = block_ref[0, 0, tile] * TILE
        far = [jnp.broadcast_to(far_ref[c, pl.ds(tile, 1), :], (PIECE, LANES)) for c in range(4)]
        for piece in range(TILE // PIECE):
            at = pl.ds(pl.multiple_of(base + piece * PIECE, PIECE), PIECE)
            gap = [own_ref[c, at, :] - far[c] for c in range(3)]
            square = gap[0] * gap[0] + gap[1] * gap[1] + gap[2] * gap[2]
            root = lax.rsqrt(square + softening)
            inverse = root * root
            weight = jnp.maximum(inverse - 1.0 / (1.0 + softening), 0.0)
            strength = (inverse - own_ref[3, at, :] * far[3]) * (weight * weight)
            for c in range(3):
                sum_ref[c, at, :] = sum_ref[c, at, :] + strength * gap[c]

    def add_tiles(step, _):
        for n in range(TILES_STEP):
            add_tile(step * TILES_STEP + n)
        return 0

    lax.fori_loop(0, lax.div(live + TILES_STEP - 1, TILES_STEP), add_tiles, 0)

    scale = time_step * time_step * force_scale * 4.0 / 2048.0 * (1.0 + softening) ** 2

    lane = lax.broadcasted_iota(jnp.int32, (LANES, LANES), 1)
    columns = jnp.zeros((LANES, LANES), jnp.float32)
    for c in range(3):
        for part in range(atom_rows):
            total = jnp.sum(sum_ref[c, pl.ds(part * LANES, LANES), :], axis=1, keepdims=True)
            columns = jnp.where(lane == c * atom_rows + part, total, columns)
    totals = columns.T[: 3 * atom_rows, :]
    mass = motion_ref[pl.ds(3 * atom_rows, atom_rows), :]
    moved = time_step * motion_ref[pl.ds(0, 3 * atom_rows), :] + scale * totals * jnp.concatenate([mass] * 3, axis=0)
    for copy in range(copies):
        out_ref[pl.ds(copy * rows.disp_count, 3 * atom_rows), :] = moved
    slot = lax.broadcasted_iota(jnp.int32, (1, LANES), 1)
    for part in range(rows.slot_rows):
        flag = jnp.where(slot + part * LANES < count_ref[0, 0], 1.0, 0.0)
        side = motion_ref[pl.ds(4 * atom_rows + part, 1), :]
        for copy in range(copies):
            out_ref[pl.ds(copy * rows.disp_count + rows.live + part, 1), :] = flag
            out_ref[pl.ds(copy * rows.disp_count + rows.side + part, 1), :] = side
    if rows.disp_count > rows.disp_used:
        for copy in range(copies):
            out_ref[pl.ds(copy * rows.disp_count + rows.disp_used, rows.disp_count - rows.disp_used), :] = jnp.zeros(
                (rows.disp_count - rows.disp_used, LANES), jnp.float32
            )


def bond_kernel(rows, domains, strides, around_ref, weight_ref, matrix_ref):
    atom_rows, shell_rows = rows.atom_rows, rows.shell_rows

    def load(row):
        return around_ref[pl.ds(row, domains, stride=rows.count), :]

    def index(row):
        return load(row).astype(jnp.int32)

    fields = [[load(at + part) for part in range(atom_rows)] for at in rows.coords + [rows.mass]]

    def put_weights(first, second, at):
        gap = [first[c] - second[c] for c in range(3)]
        length_sq = gap[0] * gap[0] + gap[1] * gap[1] + gap[2] * gap[2] + length_floor
        scale = lax.rsqrt(length_sq) * lax.rsqrt(first[3] + second[3])
        for c in range(3):
            weight_ref[pl.ds((at * 3 + c) * domains, domains), :] = gap[c] * scale

    for part in range(rows.bond_rows):
        first = index(rows.bond_first + part)
        second = index(rows.bond_second + part)
        put_weights([pick(f, first) for f in fields], [pick(f, second) for f in fields], part)
    shells = [f[:shell_rows] for f in fields]
    for part in range(rows.slot_rows):
        first = index(rows.cross_first + part)
        second = index(rows.cross_second + part)
        ends = [pick(f, first) for f in shells]
        for code, stride in enumerate(strides):
            seen = pltpu.roll(second, stride % domains, 0)
            others = [pltpu.roll(pick(f, seen), -stride % domains, 0) for f in shells]
            put_weights(ends, others, rows.bond_rows + part * 4 + code)

    down = lax.broadcasted_iota(jnp.int32, (SUBLANES, LANES), 0)
    group_rows = 4 * SUBLANES

    kind = jnp.bfloat16 if shell_rows * LANES <= 256 else jnp.float32
    across = lax.broadcasted_iota(jnp.int32, (group_rows, LANES), 1).astype(jnp.float32)
    lanes = [(across + float(block * LANES)).astype(kind) for block in range(shell_rows)]

    def column(row, step, half=0):
        row = jnp.broadcast_to(row, (SUBLANES, LANES))
        groups = [take_lanes(row, down + at) for at in range(step * group_rows, (step + 1) * group_rows, SUBLANES)]
        return (jnp.concatenate(groups, axis=0) - float(half * shell_rows * LANES)).astype(kind)

    def put(at, ends, signs):
        for block in range(shell_rows):
            value = jnp.zeros((group_rows, LANES), kind)
            for end, sign in zip(ends, signs):
                value = jnp.where(end == lanes[block], jnp.full((group_rows, LANES), sign, kind), value)
            matrix_ref[pl.ds(at, group_rows), block * LANES : (block + 1) * LANES] = value.astype(matrix_ref.dtype)

    def build(domain, _):
        start = pl.multiple_of(domain * rows.matrix, LANES)
        for part in range(rows.bond_rows):
            first = around_ref[pl.ds(domain * rows.count + rows.bond_first + part, 1), :]
            second = around_ref[pl.ds(domain * rows.count + rows.bond_second + part, 1), :]
            for step in range(LANES // group_rows):
                for half in range(2):
                    ends = (column(first, step, half), column(second, step, half))
                    put(start + rows.inner_at[half] + part * LANES + step * group_rows, ends, (1.0, -1.0))
        for part in range(rows.slot_rows):
            for row_at, to, sign in (
                (rows.cross_first, rows.cross_at, 1.0),
                (rows.cross_second, rows.far_at, -1.0),
            ):
                row = around_ref[pl.ds(domain * rows.count + row_at + part, 1), :]
                for step in range(LANES // group_rows):
                    put(start + to + part * LANES + step * group_rows, (column(row, step),), (sign,))
        return 0

    lax.fori_loop(0, domains, build, 0)


def solve_kernel(
    rows,
    domains,
    strides,
    around_ref,
    moves_ref,
    weight_ref,
    matrix_ref,
    coords_out_ref,
    velocity_out_ref,
    push_ref,
    field_ref,
):
    atom_rows, shell_rows = rows.atom_rows, rows.shell_rows
    bond_rows, slot_rows = rows.bond_rows, rows.slot_rows
    me = place_of()

    def load(row):
        return around_ref[pl.ds(row, domains, stride=rows.count), :]

    def index(row):
        return load(row).astype(jnp.int32)

    inner_first = [index(rows.bond_first + p) for p in range(bond_rows)]
    inner_second = [index(rows.bond_second + p) for p in range(bond_rows)]
    cross_first = [index(rows.cross_first + p) for p in range(slot_rows)]
    cross_second = [index(rows.cross_second + p) for p in range(slot_rows)]
    masses = [load(rows.mass + p) for p in range(atom_rows)]

    def move_rows(row):
        return moves_ref[pl.ds(row, domains, stride=rows.disp_count), :]

    def weight_rows(at, c):
        return weight_ref[pl.ds((at * 3 + c) * domains, domains), :]

    sides = [move_rows(rows.side + p) for p in range(slot_rows)]
    cross_weights = []
    for part in range(slot_rows):
        live = move_rows(rows.live + part)
        for c in range(3):
            value = 0.0
            for code in range(4):
                value = jnp.where(sides[part] == code, weight_rows(bond_rows + part * 4 + code, c), value)
            cross_weights.append(value * live)

    def weight(at, c):
        return weight_rows(at, c) if at < bond_rows else cross_weights[(at - bond_rows) * 3 + c]

    def project(fields):
        result = []
        for part in range(bond_rows):
            total = 0.0
            for c in range(3):
                ends = pick(fields[c], inner_first[part]) - pick(fields[c], inner_second[part])
                total = total + weight(part, c) * ends
            result.append(total)
        for part in range(slot_rows):
            seen = [pltpu.roll(cross_second[part], stride % domains, 0) for stride in strides]
            total = 0.0
            for c in range(3):
                shell = fields[c][:shell_rows]
                other = 0.0
                for code, stride in enumerate(strides):
                    value = pltpu.roll(pick(shell, seen[code]), -stride % domains, 0)
                    other = jnp.where(sides[part] == code, value, other)
                total = total + weight(bond_rows + part, c) * (pick(shell, cross_first[part]) - other)
            result.append(total)
        return result

    def put_pushes(values):
        for at, value in enumerate(values):
            for c in range(3):
                pushed = weight(at, c) * value
                high = pushed.astype(jnp.bfloat16).astype(jnp.float32)
                push_ref[at, pl.ds(c * domains, domains), :] = high
                push_ref[at, pl.ds((3 + c) * domains, domains), :] = pushed - high

    def pushes_of(at, domain):
        return push_ref[at, pl.ds(domain, SUBLANES, stride=domains), :]

    def product(pushes, domain, at):
        start = domain * rows.matrix + at
        if not isinstance(start, int):
            start = pl.multiple_of(start, LANES)
        pushes = pushes[0] if len(pushes) == 1 else jnp.concatenate(pushes, axis=1)
        result = jnp.dot(
            pushes.astype(jnp.bfloat16),
            matrix_ref[pl.ds(start, pushes.shape[1]), :],
            preferred_element_type=jnp.float32,
        )
        return [result[:, p * LANES : (p + 1) * LANES] for p in range(shell_rows)]

    def inner_totals(pushes, domain):
        return product(pushes, domain, 0) + product(pushes[:bond_rows], domain, rows.shell_terms)

    def far_totals(pushes, domain, codes):
        masked = []
        for part in range(slot_rows):
            side = moves_ref[pl.ds(domain * rows.disp_count + rows.side + part, 1), :]
            side = jnp.broadcast_to(side, (SUBLANES, LANES))
            pushed = pushes[bond_rows + part]
            masked.append(jnp.concatenate([jnp.where(side == code, pushed, 0.0) for code in codes], axis=0))
        return product(masked, domain, rows.far_at)

    def spread(values):
        put_pushes(values)
        for domain in range(domains):
            pushes = [pushes_of(at, domain) for at in range(bond_rows + slot_rows)]
            for part, total in enumerate(inner_totals(pushes, domain)):
                field_ref[0, part, pl.ds(domain, SUBLANES, stride=domains), :] = total
            for part, total in enumerate(far_totals(pushes, domain, range(4))):
                for code, stride in enumerate(strides):
                    field_ref[1 + code, part, pl.ds((domain + stride) % domains, SUBLANES, stride=domains), :] = total[
                        code * SUBLANES : (code + 1) * SUBLANES, :
                    ]

        def field(c, part):
            pieces = [
                field_ref[source, part, pl.ds(row * domains, domains), :]
                for source in range(5 if part < shell_rows else 1)
                for row in (c, 3 + c)
            ]
            return masses[part] * functools.reduce(lambda a, b: a + b, pieces)

        return [[field(c, part) for part in range(atom_rows)] for c in range(3)]

    moves = [
        [move_rows(c * atom_rows + p) for p in range(atom_rows)]
        for c in range(3)
    ]
    push_ref[...] = jnp.zeros(push_ref.shape, jnp.float32)
    residue = project(moves)

    def expand(_, carry):
        residue, summed = carry
        change = project(spread(residue))
        residue = [now - step for now, step in zip(residue, change)]
        return residue, [a + b for a, b in zip(summed, residue)]

    residue, summed = lax.fori_loop(0, ORDER, expand, (residue, residue))
    put_pushes(summed)
    sums = inner_totals([pushes_of(at, me) for at in range(bond_rows + slot_rows)], me)
    for code, stride in enumerate(strides):
        owner = lax.rem(me + (-stride) % domains, domains)
        pushes = [pushes_of(at, owner) for at in range(bond_rows + slot_rows)]
        for part, total in enumerate(far_totals(pushes, owner, [code])):
            sums[part] = sums[part] + total
    for part in range(atom_rows):
        lanes = slice(part * LANES, (part + 1) * LANES)
        mass = around_ref[pl.ds(me * rows.count + rows.mass + part, 1), :]
        for c in range(3):
            correction = mass * (sums[part][c : c + 1, :] + sums[part][3 + c : 4 + c, :])
            move = moves_ref[pl.ds(me * rows.disp_count + c * atom_rows + part, 1), :] - correction
            start = around_ref[pl.ds(me * rows.count + rows.coords[c] + part, 1), :]
            coords_out_ref[c, 0, :, lanes] = start + move
            velocity_out_ref[c, 0, :, lanes] = move * (1.0 / time_step)


def vmem(count):
    return [pl.BlockSpec(memory_space=pltpu.VMEM)] * count


def smem(count):
    return [pl.BlockSpec(memory_space=pltpu.SMEM)] * count


def hbm(count):
    return [pl.BlockSpec(memory_space=pltpu.HBM)] * count


def in_hbm(arrays):
    return [pltpu.with_memory_space_constraint(a, pltpu.HBM) for a in arrays]


def params(mebibytes):
    return pltpu.CompilerParams(vmem_limit_bytes=mebibytes * 1024 * 1024)


def cost(flops, moved):
    return pl.CostEstimate(flops=flops, bytes_accessed=moved, transcendentals=0)


def room_for(arrays):
    return [pltpu.VMEM(a.shape, a.dtype) for a in arrays]


def shards(
    coords,
    velocity,
    charge,
    inv_mass,
    tile_block,
    tile_atoms,
    active_tile_count,
    bond_atoms,
    cross_atoms,
    cross_side,
    cross_count,
):
    atoms = coords.shape[-1]
    tiles = tile_atoms.shape[2]
    domains = lax.axis_size("dom")
    strides = strides_of(domains)
    rows = Rows(atoms, bond_atoms.shape[-1], cross_side.shape[-1])
    whole_slab = domains == SUBLANES
    copies = domains if whole_slab else 1
    f32 = jnp.float32

    sent = (coords, charge, inv_mass, bond_atoms, cross_atoms)
    packed, rim = pl.pallas_call(
        functools.partial(pack_kernel, rows, copies),
        out_shape=(
            jax.ShapeDtypeStruct((copies * rows.count, LANES), f32),
            jax.ShapeDtypeStruct((4 * rows.shell_rows, LANES), f32),
        ),
        in_specs=hbm(len(sent)),
        out_specs=tuple(vmem(2)),
        scratch_shapes=room_for(sent)
        + [pltpu.SemaphoreType.DMA((len(sent),)), pltpu.VMEM((rows.count, LANES), f32)],
        compiler_params=params(4),
        name="pack",
    )(*in_hbm(sent))

    alone = (coords, charge, velocity, inv_mass, cross_side, tile_atoms)
    own = pl.pallas_call(
        functools.partial(own_kernel, rows),
        out_shape=(
            jax.ShapeDtypeStruct((4, atoms, LANES), f32),
            jax.ShapeDtypeStruct((4, tiles, TILE), f32),
            jax.ShapeDtypeStruct((tiles, TILE), jnp.int32),
            jax.ShapeDtypeStruct((4 * rows.atom_rows + rows.slot_rows, LANES), f32),
        ),
        in_specs=hbm(len(alone)),
        out_specs=tuple(vmem(4)),
        scratch_shapes=room_for(alone[:5]) + [pltpu.SemaphoreType.DMA((len(alone),))],
        compiler_params=params(4),
        cost_estimate=cost(64 * atoms * LANES, 16 * atoms * LANES),
        name="own",
    )(*in_hbm(alone))

    below = passed_along(rim, "slab", 1)
    above = passed_along(rim, "slab", -1)
    if whole_slab:
        around = from_slab(packed)

        def place():
            return [place_of(stride) for stride in strides]

    else:
        around = jnp.concatenate([packed] + [passed_along(packed, "dom", -stride) for stride in strides], axis=0)

        def place():
            return [1, 2, 3, 4]


    moves = pl.pallas_call(
        functools.partial(force_kernel, rows, copies, place),
        out_shape=jax.ShapeDtypeStruct((copies * rows.disp_count, LANES), f32),
        in_specs=smem(2) + hbm(1) + vmem(7),
        out_specs=vmem(1)[0],
        scratch_shapes=[
            pltpu.VMEM((4, 6 * rows.shell_rows, SUBLANES, LANES), f32),
            pltpu.VMEM((4, tiles, LANES), f32),
            pltpu.VMEM((3, atoms, LANES), f32),
            pltpu.SMEM(tile_block.shape, jnp.int32),
            pltpu.SemaphoreType.DMA(()),
        ],
        compiler_params=params(8),
        cost_estimate=cost(30 * tiles * TILE * TILE, 4 * around.size),
        name="force",
    )(active_tile_count, cross_count, *in_hbm([tile_block]), around, below, above, *own)

    if not whole_slab:
        return by_exchange(rows, strides, around, moves, cross_count)

    constraint_rows = rows.bond_rows + rows.slot_rows
    weight, matrix = pl.pallas_call(
        functools.partial(bond_kernel, rows, domains, strides),
        out_shape=(
            jax.ShapeDtypeStruct(((rows.bond_rows + 4 * rows.slot_rows) * 3 * domains, LANES), f32),
            jax.ShapeDtypeStruct((domains * rows.matrix, atoms // 2), jnp.bfloat16),
        ),
        in_specs=vmem(1),
        out_specs=tuple(vmem(2)),
        compiler_params=params(16),
        cost_estimate=cost(8 * domains * rows.matrix * atoms // 2, 4 * around.size),
        name="bonds",
    )(around)

    every_move = from_slab(moves)

    return pl.pallas_call(
        functools.partial(solve_kernel, rows, domains, strides),
        out_shape=(
            jax.ShapeDtypeStruct(coords.shape, f32),
            jax.ShapeDtypeStruct(coords.shape, f32),
        ),
        in_specs=vmem(4),
        out_specs=tuple(vmem(2)),
        scratch_shapes=[
            pltpu.VMEM((constraint_rows, SUBLANES * domains, LANES), f32),
            pltpu.VMEM((5, rows.atom_rows, SUBLANES * domains, LANES), f32),
        ],
        compiler_params=params(16),
        name="solve",
    )(around, every_move, weight, matrix)


def by_exchange(rows, strides, around, moves, cross_count):
    atom_count = rows.atom_rows * LANES
    shell = rows.shell_rows * LANES
    inside = around.reshape(5, rows.count, LANES)

    def flat(at, count):
        return inside[0, at : at + count].reshape(-1)

    def neighbours(at):
        return inside[1:, at : at + rows.shell_rows].reshape(-1)

    coords = jnp.stack([flat(at, rows.atom_rows) for at in rows.coords])
    inv_mass = flat(rows.mass, rows.atom_rows)
    displace = moves[: rows.live].reshape(3, atom_count)
    left = flat(rows.bond_first, rows.bond_rows).astype(jnp.int32)
    right = flat(rows.bond_second, rows.bond_rows).astype(jnp.int32)
    cross_left = flat(rows.cross_first, rows.slot_rows).astype(jnp.int32)
    cross_right = flat(rows.cross_second, rows.slot_rows).astype(jnp.int32)
    side = moves[rows.side : rows.side + rows.slot_rows].reshape(-1).astype(jnp.int32)
    flag = moves[rows.live : rows.side].reshape(-1)
    cross_index = side * shell + cross_right
    far_coords = jnp.stack([neighbours(at) for at in rows.coords])
    far_mass = neighbours(rows.mass)

    def weights(first, second, mass_first, mass_second):
        gap = first - second
        length = jnp.sqrt(jnp.sum(gap * gap, axis=0) + length_floor)
        return gap / length * lax.rsqrt(mass_first + mass_second)

    inner = weights(coords[:, left], coords[:, right], inv_mass[left], inv_mass[right])
    cross = flag * weights(
        coords[:, cross_left], far_coords[:, cross_index], inv_mass[cross_left], far_mass[cross_index]
    )

    def project(field):
        rim = field[:, :shell]
        far = jnp.concatenate([passed_along(rim, "dom", -stride) for stride in strides], axis=1)
        return (
            jnp.sum(inner * (field[:, left] - field[:, right]), axis=0),
            jnp.sum(cross * (field[:, cross_left] - far[:, cross_index]), axis=0),
        )

    def spread(values):
        pushed = inner * values[0]
        pushed_cross = cross * values[1]
        totals = jnp.zeros((3, atom_count), jnp.float32).at[:, left].add(pushed).at[:, right].add(-pushed)
        totals = totals.at[:, cross_left].add(pushed_cross)
        outward = jnp.zeros((3, 4 * shell), jnp.float32).at[:, cross_index].add(-pushed_cross)
        for code, stride in enumerate(strides):
            totals = totals.at[:, :shell].add(
                passed_along(outward[:, code * shell : (code + 1) * shell], "dom", stride)
            )
        return inv_mass * totals

    residue = project(displace)
    summed = residue
    for _ in range(ORDER):
        change = project(spread(residue))
        residue = tuple(now - step for now, step in zip(residue, change))
        summed = tuple(a + b for a, b in zip(summed, residue))
    move = displace - spread(summed)
    return (
        (coords + move).reshape(3, 1, 1, atom_count),
        (move * (1.0 / time_step)).reshape(3, 1, 1, atom_count),
    )


def solution(mesh):
    return jax.shard_map(
        shards,
        mesh=mesh,
        in_specs=(
            P(None, "slab", "dom", None),
            P(None, "slab", "dom", None),
            P("slab", "dom", None),
            P("slab", "dom", None),
            P("slab", "dom", None),
            P("slab", "dom", None, None),
            P("slab", "dom"),
            P(None, "slab", "dom", None),
            P(None, "slab", "dom", None),
            P("slab", "dom", None),
            P("slab", "dom"),
        ),
        out_specs=(P(None, "slab", "dom", None), P(None, "slab", "dom", None)),
        check_vma=False,
    )
```

```python
import functools

import jax
import jax.numpy as jnp
from jax import lax
from jax.experimental import pallas as pl
from jax.experimental.pallas import tpu as pltpu
from jax.sharding import PartitionSpec as P

TILE = 128
ORDER = 4
LANES = 128
SUBLANES = 8

time_step = 0.1
cutoff_sq = 16.0
force_scale = 4.0
length_floor = 0.25


def passed_along(array, axis, by):
    length = lax.axis_size(axis)
    return lax.ppermute(array, axis, [(i, (i + by) % length) for i in range(length)])


def first_of(domains):
    return domains - 1


def from_slab(blocks):
    length = lax.axis_size("dom")
    order = [(first_of(length) + i) % length for i in range(length)]
    return lax.all_to_all(blocks, "dom", 0, 0, axis_index_groups=[order], tiled=True)


def place_of(stride=0):
    length = lax.axis_size("dom")
    return lax.rem(lax.axis_index("dom") + (stride - first_of(length)) % length, length)


def strides_of(domains):
    row_width = max(2, domains // 8)
    return (1, -1, row_width, -row_width)


def round_up(count, step):
    return -(-count // step) * step


class Rows:
    def __init__(self, atoms, bonds, slots):
        self.atom_rows = atoms // LANES
        self.shell_rows = atoms // 2 // LANES
        self.bond_rows = bonds // LANES
        self.slot_rows = slots // LANES
        at = 0
        self.coords = []
        for _ in range(3):
            self.coords.append(at)
            at += self.atom_rows
        self.charge = at
        at += self.shell_rows
        self.mass = at
        at += self.atom_rows
        self.bond_first = at
        at += self.bond_rows
        self.bond_second = at
        at += self.bond_rows
        self.cross_first = at
        at += self.slot_rows
        self.cross_second = at
        at += self.slot_rows
        self.used = at
        self.count = round_up(at, SUBLANES)
        self.shell_terms = (self.bond_rows + self.slot_rows) * LANES
        self.inner_at = (0, self.shell_terms)
        self.cross_at = self.bond_rows * LANES
        self.far_at = self.shell_terms + self.bond_rows * LANES
        self.matrix = self.far_at + self.slot_rows * LANES
        self.live = 3 * self.atom_rows
        self.side = self.live + self.slot_rows
        self.disp_used = self.side + self.slot_rows
        self.disp_count = round_up(self.disp_used, SUBLANES)


def take_lanes(table, lanes):
    return jnp.take_along_axis(table, lanes, axis=1, mode="promise_in_bounds")


def pick(tables, index):
    lanes = index & (LANES - 1)
    chunk = index >> 7
    result = take_lanes(tables[0], lanes)
    for k in range(1, len(tables)):
        result = jnp.where(chunk == k, take_lanes(tables[k], lanes), result)
    return result


def fetched(sources, targets, sem_ref):
    copies = [pltpu.make_async_copy(s, t, sem_ref.at[n]) for n, (s, t) in enumerate(zip(sources, targets))]
    for copy in copies:
        copy.start()
    return copies


def pack_kernel(rows, copies, *refs):
    sources, (out_ref, rim_ref), kept, (bonds_ref, cross_ref, block_ref, sem_ref) = refs[:8], refs[8:10], refs[10:16], refs[16:]
    coords_ref, charge_ref, mass_ref, velocity_ref, side_ref, atoms_ref = kept
    targets = (coords_ref, charge_ref, mass_ref, bonds_ref, cross_ref, velocity_ref, side_ref, atoms_ref)
    fetches = fetched(sources, targets, sem_ref)
    for copy in fetches[:5]:
        copy.wait()

    def put(row, value):
        for part in range(value.shape[1] // LANES):
            block_ref[pl.ds(row + part, 1), :] = value[:, part * LANES : (part + 1) * LANES]

    shell = rows.shell_rows * LANES
    fields = [coords_ref[c, 0] for c in range(3)] + [charge_ref[0, :, :shell]]
    for c in range(4):
        at = rows.coords[c] if c < 3 else rows.charge
        put(at, fields[c])
        for part in range(rows.shell_rows):
            rim_ref[pl.ds(c * rows.shell_rows + part, 1), :] = fields[c][:, part * LANES : (part + 1) * LANES]
    put(rows.mass, mass_ref[0])
    put(rows.bond_first, bonds_ref[0, 0].astype(jnp.float32))
    put(rows.bond_second, bonds_ref[1, 0].astype(jnp.float32))
    put(rows.cross_first, cross_ref[0, 0].astype(jnp.float32))
    put(rows.cross_second, cross_ref[1, 0].astype(jnp.float32))
    if rows.count > rows.used:
        block_ref[rows.used :, :] = jnp.zeros((rows.count - rows.used, LANES), jnp.float32)
    block = block_ref[...]
    for copy in range(copies):
        out_ref[pl.ds(copy * rows.count, rows.count), :] = block
    for copy in fetches[5:]:
        copy.wait()


SHRINK = 1.0 / 4.0
OUT_OF_REACH = 1000.0
TILES_STEP = 4
PIECE = 32


def own_kernel(
    rows, coords_ref, charge_ref, mass_ref, velocity_ref, side_ref, atoms_ref, own_ref, far_ref, motion_ref
):
    atom_rows = rows.atom_rows
    down = lax.broadcasted_iota(jnp.int32, (SUBLANES, LANES), 0)

    def lanes_of(part):
        return slice(part * LANES, (part + 1) * LANES)

    table = []
    for c in range(4):
        field = coords_ref[c, 0] * SHRINK if c < 3 else charge_ref[0]
        table.append(
            [jnp.broadcast_to(field[:, lanes_of(part)], (SUBLANES, LANES)) for part in range(atom_rows)]
        )
    for part in range(atom_rows):
        for group in range(LANES // SUBLANES):
            at = part * LANES + group * SUBLANES
            for c in range(4):
                value = take_lanes(table[c][part], down + group * SUBLANES)
                own_ref[c, pl.ds(at, SUBLANES), :] = value if c < 3 else value * 8.0
    for group in range(atoms_ref.shape[2] // SUBLANES):
        at = pl.ds(group * SUBLANES, SUBLANES)
        index = atoms_ref[0, 0, at, :]
        for c in range(4):
            far_ref[c, at, :] = pick(table[c], index)
    fields = [velocity_ref[c, 0] for c in range(3)] + [mass_ref[0], side_ref[0].astype(jnp.float32)]
    at = 0
    for field in fields:
        for part in range(field.shape[1] // LANES):
            motion_ref[pl.ds(at, 1), :] = field[:, lanes_of(part)]
            at += 1


def force_kernel(
    rows,
    copies,
    place,
    live_ref,
    count_ref,
    block_hbm,
    around_ref,
    below_ref,
    above_ref,
    own_ref,
    near_ref,
    index_ref,
    motion_ref,
    out_ref,
    table_ref,
    far_ref,
    sum_ref,
    block_ref,
    sem_ref,
):
    atom_rows, shell_rows = rows.atom_rows, rows.shell_rows
    tiles = index_ref.shape[2]
    block_copy = pltpu.make_async_copy(block_hbm, block_ref, sem_ref)
    block_copy.start()
    live = live_ref[0, 0]
    holders = place()
    starts = [rows.coords[0], rows.coords[1], rows.coords[2], rows.charge]
    entry_rows = 6 * shell_rows

    def broadcast(row):
        return jnp.broadcast_to(row, (SUBLANES, LANES))

    for c in range(4):
        factor = SHRINK if c < 3 else 1.0
        at = 0
        for neighbour in range(4):
            base = holders[neighbour] * rows.count + starts[c]
            for part in range(shell_rows):
                table_ref[c, at] = broadcast(around_ref[pl.ds(base + part, 1), :] * factor)
                at += 1
        for slab_ref in (below_ref, above_ref):
            for part in range(shell_rows):
                table_ref[c, at] = broadcast(slab_ref[pl.ds(c * shell_rows + part, 1), :] * factor)
                at += 1

    for group in range(tiles // SUBLANES):
        at = pl.ds(group * SUBLANES, SUBLANES)
        index = index_ref[0, 0, at, :]
        lanes = index & (LANES - 1)
        chunk = index >> 7
        values = [near_ref[c, at, :] for c in range(4)]
        for k in range(entry_rows):
            here = chunk == atom_rows + k
            values = [jnp.where(here, take_lanes(table_ref[c, k], lanes), values[c]) for c in range(4)]
        for c in range(4):
            far_ref[c, at, :] = values[c]

    sum_ref[...] = jnp.zeros(sum_ref.shape, jnp.float32)
    block_copy.wait()
    down = lax.broadcasted_iota(jnp.int32, (tiles, LANES), 0)
    far_ref[0] = jnp.where(down < live, far_ref[0], OUT_OF_REACH)

    softening = 1.0 / cutoff_sq

    def add_tile(tile):
        base = block_ref[0, 0, tile] * TILE
        far = [jnp.broadcast_to(far_ref[c, pl.ds(tile, 1), :], (PIECE, LANES)) for c in range(4)]
        for piece in range(TILE // PIECE):
            at = pl.ds(pl.multiple_of(base + piece * PIECE, PIECE), PIECE)
            gap = [own_ref[c, at, :] - far[c] for c in range(3)]
            square = gap[0] * gap[0] + gap[1] * gap[1] + gap[2] * gap[2]
            inverse = pl.reciprocal(square + softening, approx=True)
            weight = jnp.maximum(inverse - 1.0 / (1.0 + softening), 0.0)
            strength = (inverse - own_ref[3, at, :] * far[3]) * (weight * weight)
            for c in range(3):
                sum_ref[c, at, :] = sum_ref[c, at, :] + strength * gap[c]

    def add_tiles(step, _):
        for n in range(TILES_STEP):
            add_tile(step * TILES_STEP + n)
        return 0

    lax.fori_loop(0, lax.div(live + TILES_STEP - 1, TILES_STEP), add_tiles, 0)

    scale = time_step * time_step * force_scale * 4.0 / 2048.0 * (1.0 + softening) ** 2

    lane = lax.broadcasted_iota(jnp.int32, (LANES, LANES), 1)
    columns = jnp.zeros((LANES, LANES), jnp.float32)
    for c in range(3):
        for part in range(atom_rows):
            total = jnp.sum(sum_ref[c, pl.ds(part * LANES, LANES), :], axis=1, keepdims=True)
            columns = jnp.where(lane == c * atom_rows + part, total, columns)
    totals = columns.T[: 3 * atom_rows, :]
    mass = motion_ref[pl.ds(3 * atom_rows, atom_rows), :]
    moved = time_step * motion_ref[pl.ds(0, 3 * atom_rows), :] + scale * totals * jnp.concatenate([mass] * 3, axis=0)
    for copy in range(copies):
        out_ref[pl.ds(copy * rows.disp_count, 3 * atom_rows), :] = moved
    slot = lax.broadcasted_iota(jnp.int32, (1, LANES), 1)
    for part in range(rows.slot_rows):
        flag = jnp.where(slot + part * LANES < count_ref[0, 0], 1.0, 0.0)
        side = motion_ref[pl.ds(4 * atom_rows + part, 1), :]
        for copy in range(copies):
            out_ref[pl.ds(copy * rows.disp_count + rows.live + part, 1), :] = flag
            out_ref[pl.ds(copy * rows.disp_count + rows.side + part, 1), :] = side
    if rows.disp_count > rows.disp_used:
        for copy in range(copies):
            out_ref[pl.ds(copy * rows.disp_count + rows.disp_used, rows.disp_count - rows.disp_used), :] = jnp.zeros(
                (rows.disp_count - rows.disp_used, LANES), jnp.float32
            )


def bond_kernel(rows, domains, strides, around_ref, weight_ref, matrix_ref):
    atom_rows, shell_rows = rows.atom_rows, rows.shell_rows

    def load(row):
        return around_ref[pl.ds(row, domains, stride=rows.count), :]

    def index(row):
        return load(row).astype(jnp.int32)

    fields = [[load(at + part) for part in range(atom_rows)] for at in rows.coords + [rows.mass]]

    def put_weights(first, second, at):
        gap = [first[c] - second[c] for c in range(3)]
        length_sq = gap[0] * gap[0] + gap[1] * gap[1] + gap[2] * gap[2] + length_floor
        scale = lax.rsqrt(length_sq) * lax.rsqrt(first[3] + second[3])
        for c in range(3):
            weight_ref[pl.ds((at * 3 + c) * domains, domains), :] = gap[c] * scale

    for part in range(rows.bond_rows):
        first = index(rows.bond_first + part)
        second = index(rows.bond_second + part)
        put_weights([pick(f, first) for f in fields], [pick(f, second) for f in fields], part)
    shells = [f[:shell_rows] for f in fields]
    for part in range(rows.slot_rows):
        first = index(rows.cross_first + part)
        second = index(rows.cross_second + part)
        ends = [pick(f, first) for f in shells]
        for code, stride in enumerate(strides):
            seen = pltpu.roll(second, stride % domains, 0)
            others = [pltpu.roll(pick(f, seen), -stride % domains, 0) for f in shells]
            put_weights(ends, others, rows.bond_rows + part * 4 + code)

    down = lax.broadcasted_iota(jnp.int32, (SUBLANES, LANES), 0)
    group_rows = 4 * SUBLANES

    kind = jnp.bfloat16 if shell_rows * LANES <= 256 else jnp.float32
    across = lax.broadcasted_iota(jnp.int32, (group_rows, LANES), 1).astype(jnp.float32)
    lanes = [(across + float(block * LANES)).astype(kind) for block in range(shell_rows)]

    def column(row, step, half=0):
        row = jnp.broadcast_to(row, (SUBLANES, LANES))
        groups = [take_lanes(row, down + at) for at in range(step * group_rows, (step + 1) * group_rows, SUBLANES)]
        return (jnp.concatenate(groups, axis=0) - float(half * shell_rows * LANES)).astype(kind)

    def put(at, ends, signs):
        for block in range(shell_rows):
            value = jnp.zeros((group_rows, LANES), kind)
            for end, sign in zip(ends, signs):
                value = jnp.where(end == lanes[block], jnp.full((group_rows, LANES), sign, kind), value)
            matrix_ref[pl.ds(at, group_rows), block * LANES : (block + 1) * LANES] = value.astype(matrix_ref.dtype)

    def build(domain, _):
        start = pl.multiple_of(domain * rows.matrix, LANES)
        for part in range(rows.bond_rows):
            first = around_ref[pl.ds(domain * rows.count + rows.bond_first + part, 1), :]
            second = around_ref[pl.ds(domain * rows.count + rows.bond_second + part, 1), :]
            for step in range(LANES // group_rows):
                for half in range(2):
                    ends = (column(first, step, half), column(second, step, half))
                    put(start + rows.inner_at[half] + part * LANES + step * group_rows, ends, (1.0, -1.0))
        for part in range(rows.slot_rows):
            for row_at, to, sign in (
                (rows.cross_first, rows.cross_at, 1.0),
                (rows.cross_second, rows.far_at, -1.0),
            ):
                row = around_ref[pl.ds(domain * rows.count + row_at + part, 1), :]
                for step in range(LANES // group_rows):
                    put(start + to + part * LANES + step * group_rows, (column(row, step),), (sign,))
        return 0

    lax.fori_loop(0, domains, build, 0)


def solve_kernel(
    rows,
    domains,
    strides,
    around_ref,
    moves_ref,
    weight_ref,
    matrix_ref,
    coords_out_ref,
    velocity_out_ref,
    push_ref,
    field_ref,
):
    atom_rows, shell_rows = rows.atom_rows, rows.shell_rows
    bond_rows, slot_rows = rows.bond_rows, rows.slot_rows
    me = place_of()

    def load(row):
        return around_ref[pl.ds(row, domains, stride=rows.count), :]

    def index(row):
        return load(row).astype(jnp.int32)

    inner_first = [index(rows.bond_first + p) for p in range(bond_rows)]
    inner_second = [index(rows.bond_second + p) for p in range(bond_rows)]
    cross_first = [index(rows.cross_first + p) for p in range(slot_rows)]
    cross_second = [index(rows.cross_second + p) for p in range(slot_rows)]
    masses = [load(rows.mass + p) for p in range(atom_rows)]

    def move_rows(row):
        return moves_ref[pl.ds(row, domains, stride=rows.disp_count), :]

    def weight_rows(at, c):
        return weight_ref[pl.ds((at * 3 + c) * domains, domains), :]

    sides = [move_rows(rows.side + p) for p in range(slot_rows)]
    cross_weights = []
    for part in range(slot_rows):
        live = move_rows(rows.live + part)
        for c in range(3):
            value = 0.0
            for code in range(4):
                value = jnp.where(sides[part] == code, weight_rows(bond_rows + part * 4 + code, c), value)
            cross_weights.append(value * live)

    def weight(at, c):
        return weight_rows(at, c) if at < bond_rows else cross_weights[(at - bond_rows) * 3 + c]

    def project(fields):
        result = []
        for part in range(bond_rows):
            total = 0.0
            for c in range(3):
                ends = pick(fields[c], inner_first[part]) - pick(fields[c], inner_second[part])
                total = total + weight(part, c) * ends
            result.append(total)
        for part in range(slot_rows):
            seen = [pltpu.roll(cross_second[part], stride % domains, 0) for stride in strides]
            total = 0.0
            for c in range(3):
                shell = fields[c][:shell_rows]
                other = 0.0
                for code, stride in enumerate(strides):
                    value = pltpu.roll(pick(shell, seen[code]), -stride % domains, 0)
                    other = jnp.where(sides[part] == code, value, other)
                total = total + weight(bond_rows + part, c) * (pick(shell, cross_first[part]) - other)
            result.append(total)
        return result

    def put_pushes(values):
        for at, value in enumerate(values):
            for c in range(3):
                pushed = weight(at, c) * value
                high = pushed.astype(jnp.bfloat16).astype(jnp.float32)
                push_ref[at, pl.ds(c * domains, domains), :] = high
                push_ref[at, pl.ds((3 + c) * domains, domains), :] = pushed - high

    def pushes_of(at, domain):
        return push_ref[at, pl.ds(domain, SUBLANES, stride=domains), :]

    def product(pushes, domain, at):
        start = domain * rows.matrix + at
        if not isinstance(start, int):
            start = pl.multiple_of(start, LANES)
        pushes = pushes[0] if len(pushes) == 1 else jnp.concatenate(pushes, axis=1)
        result = jnp.dot(
            pushes.astype(jnp.bfloat16),
            matrix_ref[pl.ds(start, pushes.shape[1]), :],
            preferred_element_type=jnp.float32,
        )
        return [result[:, p * LANES : (p + 1) * LANES] for p in range(shell_rows)]

    def inner_totals(pushes, domain):
        return product(pushes, domain, 0) + product(pushes[:bond_rows], domain, rows.shell_terms)

    def far_totals(pushes, domain, codes):
        masked = []
        for part in range(slot_rows):
            side = moves_ref[pl.ds(domain * rows.disp_count + rows.side + part, 1), :]
            side = jnp.broadcast_to(side, (SUBLANES, LANES))
            pushed = pushes[bond_rows + part]
            masked.append(jnp.concatenate([jnp.where(side == code, pushed, 0.0) for code in codes], axis=0))
        return product(masked, domain, rows.far_at)

    def spread(values):
        put_pushes(values)
        for domain in range(domains):
            pushes = [pushes_of(at, domain) for at in range(bond_rows + slot_rows)]
            for part, total in enumerate(inner_totals(pushes, domain)):
                field_ref[0, part, pl.ds(domain, SUBLANES, stride=domains), :] = total
            for part, total in enumerate(far_totals(pushes, domain, range(4))):
                for code, stride in enumerate(strides):
                    field_ref[1 + code, part, pl.ds((domain + stride) % domains, SUBLANES, stride=domains), :] = total[
                        code * SUBLANES : (code + 1) * SUBLANES, :
                    ]

        def field(c, part):
            pieces = [
                field_ref[source, part, pl.ds(row * domains, domains), :]
                for source in range(5 if part < shell_rows else 1)
                for row in (c, 3 + c)
            ]
            return masses[part] * functools.reduce(lambda a, b: a + b, pieces)

        return [[field(c, part) for part in range(atom_rows)] for c in range(3)]

    moves = [
        [move_rows(c * atom_rows + p) for p in range(atom_rows)]
        for c in range(3)
    ]
    push_ref[...] = jnp.zeros(push_ref.shape, jnp.float32)
    residue = project(moves)

    def expand(_, carry):
        residue, summed = carry
        change = project(spread(residue))
        residue = [now - step for now, step in zip(residue, change)]
        return residue, [a + b for a, b in zip(summed, residue)]

    residue, summed = lax.fori_loop(0, ORDER, expand, (residue, residue))
    put_pushes(summed)
    sums = inner_totals([pushes_of(at, me) for at in range(bond_rows + slot_rows)], me)
    for code, stride in enumerate(strides):
        owner = lax.rem(me + (-stride) % domains, domains)
        pushes = [pushes_of(at, owner) for at in range(bond_rows + slot_rows)]
        for part, total in enumerate(far_totals(pushes, owner, [code])):
            sums[part] = sums[part] + total
    for part in range(atom_rows):
        lanes = slice(part * LANES, (part + 1) * LANES)
        mass = around_ref[pl.ds(me * rows.count + rows.mass + part, 1), :]
        for c in range(3):
            correction = mass * (sums[part][c : c + 1, :] + sums[part][3 + c : 4 + c, :])
            move = moves_ref[pl.ds(me * rows.disp_count + c * atom_rows + part, 1), :] - correction
            start = around_ref[pl.ds(me * rows.count + rows.coords[c] + part, 1), :]
            coords_out_ref[c, 0, :, lanes] = start + move
            velocity_out_ref[c, 0, :, lanes] = move * (1.0 / time_step)


def vmem(count):
    return [pl.BlockSpec(memory_space=pltpu.VMEM)] * count


def smem(count):
    return [pl.BlockSpec(memory_space=pltpu.SMEM)] * count


def hbm(count):
    return [pl.BlockSpec(memory_space=pltpu.HBM)] * count


def in_hbm(arrays):
    return [pltpu.with_memory_space_constraint(a, pltpu.HBM) for a in arrays]


def params(mebibytes):
    return pltpu.CompilerParams(vmem_limit_bytes=mebibytes * 1024 * 1024)


def cost(flops, moved):
    return pl.CostEstimate(flops=flops, bytes_accessed=moved, transcendentals=0)


def room_for(arrays):
    return [pltpu.VMEM(a.shape, a.dtype) for a in arrays]


def shards(
    coords,
    velocity,
    charge,
    inv_mass,
    tile_block,
    tile_atoms,
    active_tile_count,
    bond_atoms,
    cross_atoms,
    cross_side,
    cross_count,
):
    atoms = coords.shape[-1]
    tiles = tile_atoms.shape[2]
    domains = lax.axis_size("dom")
    strides = strides_of(domains)
    rows = Rows(atoms, bond_atoms.shape[-1], cross_side.shape[-1])
    whole_slab = domains == SUBLANES
    copies = domains if whole_slab else 1
    f32 = jnp.float32

    sent = (coords, charge, inv_mass, bond_atoms, cross_atoms)
    alone = (velocity, cross_side, tile_atoms)
    kept = sent[:3] + alone
    packed, rim, *kept = pl.pallas_call(
        functools.partial(pack_kernel, rows, copies),
        out_shape=(
            jax.ShapeDtypeStruct((copies * rows.count, LANES), f32),
            jax.ShapeDtypeStruct((4 * rows.shell_rows, LANES), f32),
            *(jax.ShapeDtypeStruct(a.shape, a.dtype) for a in kept),
        ),
        in_specs=hbm(len(sent + alone)),
        out_specs=tuple(vmem(2 + len(kept))),
        scratch_shapes=room_for(sent[3:])
        + [pltpu.VMEM((rows.count, LANES), f32), pltpu.SemaphoreType.DMA((len(sent + alone),))],
        compiler_params=params(4),
        name="pack",
    )(*in_hbm(sent + alone))

    own, near, motion = pl.pallas_call(
        functools.partial(own_kernel, rows),
        out_shape=(
            jax.ShapeDtypeStruct((4, atoms, LANES), f32),
            jax.ShapeDtypeStruct((4, tiles, TILE), f32),
            jax.ShapeDtypeStruct((4 * rows.atom_rows + rows.slot_rows, LANES), f32),
        ),
        in_specs=vmem(len(kept)),
        out_specs=tuple(vmem(3)),
        compiler_params=params(4),
        cost_estimate=cost(64 * atoms * LANES, 16 * atoms * LANES),
        name="own",
    )(*kept)

    below = passed_along(rim, "slab", 1)
    above = passed_along(rim, "slab", -1)
    if whole_slab:
        around = from_slab(packed)

        def place():
            return [place_of(stride) for stride in strides]

    else:
        around = jnp.concatenate([packed] + [passed_along(packed, "dom", -stride) for stride in strides], axis=0)

        def place():
            return [1, 2, 3, 4]


    moves = pl.pallas_call(
        functools.partial(force_kernel, rows, copies, place),
        out_shape=jax.ShapeDtypeStruct((copies * rows.disp_count, LANES), f32),
        in_specs=smem(2) + hbm(1) + vmem(7),
        out_specs=vmem(1)[0],
        scratch_shapes=[
            pltpu.VMEM((4, 6 * rows.shell_rows, SUBLANES, LANES), f32),
            pltpu.VMEM((4, tiles, LANES), f32),
            pltpu.VMEM((3, atoms, LANES), f32),
            pltpu.SMEM(tile_block.shape, jnp.int32),
            pltpu.SemaphoreType.DMA(()),
        ],
        compiler_params=params(8),
        cost_estimate=cost(30 * tiles * TILE * TILE, 4 * around.size),
        name="force",
    )(active_tile_count, cross_count, *in_hbm([tile_block]), around, below, above, own, near, kept[-1], motion)

    if not whole_slab:
        return by_exchange(rows, strides, around, moves, cross_count)

    constraint_rows = rows.bond_rows + rows.slot_rows
    weight, matrix = pl.pallas_call(
        functools.partial(bond_kernel, rows, domains, strides),
        out_shape=(
            jax.ShapeDtypeStruct(((rows.bond_rows + 4 * rows.slot_rows) * 3 * domains, LANES), f32),
            jax.ShapeDtypeStruct((domains * rows.matrix, atoms // 2), jnp.bfloat16),
        ),
        in_specs=vmem(1),
        out_specs=tuple(vmem(2)),
        compiler_params=params(16),
        cost_estimate=cost(8 * domains * rows.matrix * atoms // 2, 4 * around.size),
        name="bonds",
    )(around)

    every_move = from_slab(moves)

    return pl.pallas_call(
        functools.partial(solve_kernel, rows, domains, strides),
        out_shape=(
            jax.ShapeDtypeStruct(coords.shape, f32),
            jax.ShapeDtypeStruct(coords.shape, f32),
        ),
        in_specs=vmem(4),
        out_specs=tuple(vmem(2)),
        scratch_shapes=[
            pltpu.VMEM((constraint_rows, SUBLANES * domains, LANES), f32),
            pltpu.VMEM((5, rows.atom_rows, SUBLANES * domains, LANES), f32),
        ],
        compiler_params=params(16),
        name="solve",
    )(around, every_move, weight, matrix)


def by_exchange(rows, strides, around, moves, cross_count):
    atom_count = rows.atom_rows * LANES
    shell = rows.shell_rows * LANES
    inside = around.reshape(5, rows.count, LANES)

    def flat(at, count):
        return inside[0, at : at + count].reshape(-1)

    def neighbours(at):
        return inside[1:, at : at + rows.shell_rows].reshape(-1)

    coords = jnp.stack([flat(at, rows.atom_rows) for at in rows.coords])
    inv_mass = flat(rows.mass, rows.atom_rows)
    displace = moves[: rows.live].reshape(3, atom_count)
    left = flat(rows.bond_first, rows.bond_rows).astype(jnp.int32)
    right = flat(rows.bond_second, rows.bond_rows).astype(jnp.int32)
    cross_left = flat(rows.cross_first, rows.slot_rows).astype(jnp.int32)
    cross_right = flat(rows.cross_second, rows.slot_rows).astype(jnp.int32)
    side = moves[rows.side : rows.side + rows.slot_rows].reshape(-1).astype(jnp.int32)
    flag = moves[rows.live : rows.side].reshape(-1)
    cross_index = side * shell + cross_right
    far_coords = jnp.stack([neighbours(at) for at in rows.coords])
    far_mass = neighbours(rows.mass)

    def weights(first, second, mass_first, mass_second):
        gap = first - second
        length = jnp.sqrt(jnp.sum(gap * gap, axis=0) + length_floor)
        return gap / length * lax.rsqrt(mass_first + mass_second)

    inner = weights(coords[:, left], coords[:, right], inv_mass[left], inv_mass[right])
    cross = flag * weights(
        coords[:, cross_left], far_coords[:, cross_index], inv_mass[cross_left], far_mass[cross_index]
    )

    def project(field):
        rim = field[:, :shell]
        far = jnp.concatenate([passed_along(rim, "dom", -stride) for stride in strides], axis=1)
        return (
            jnp.sum(inner * (field[:, left] - field[:, right]), axis=0),
            jnp.sum(cross * (field[:, cross_left] - far[:, cross_index]), axis=0),
        )

    def spread(values):
        pushed = inner * values[0]
        pushed_cross = cross * values[1]
        totals = jnp.zeros((3, atom_count), jnp.float32).at[:, left].add(pushed).at[:, right].add(-pushed)
        totals = totals.at[:, cross_left].add(pushed_cross)
        outward = jnp.zeros((3, 4 * shell), jnp.float32).at[:, cross_index].add(-pushed_cross)
        for code, stride in enumerate(strides):
            totals = totals.at[:, :shell].add(
                passed_along(outward[:, code * shell : (code + 1) * shell], "dom", stride)
            )
        return inv_mass * totals

    residue = project(displace)
    summed = residue
    for _ in range(ORDER):
        change = project(spread(residue))
        residue = tuple(now - step for now, step in zip(residue, change))
        summed = tuple(a + b for a, b in zip(summed, residue))
    move = displace - spread(summed)
    return (
        (coords + move).reshape(3, 1, 1, atom_count),
        (move * (1.0 / time_step)).reshape(3, 1, 1, atom_count),
    )


def solution(mesh):
    return jax.shard_map(
        shards,
        mesh=mesh,
        in_specs=(
            P(None, "slab", "dom", None),
            P(None, "slab", "dom", None),
            P("slab", "dom", None),
            P("slab", "dom", None),
            P("slab", "dom", None),
            P("slab", "dom", None, None),
            P("slab", "dom"),
            P(None, "slab", "dom", None),
            P(None, "slab", "dom", None),
            P("slab", "dom", None),
            P("slab", "dom"),
        ),
        out_specs=(P(None, "slab", "dom", None), P(None, "slab", "dom", None)),
        check_vma=False,
    )
```

```python
import functools

import jax
import jax.numpy as jnp
from jax import lax
from jax.experimental import pallas as pl
from jax.experimental.pallas import tpu as pltpu
from jax.sharding import PartitionSpec as P

TILE = 128
ORDER = 4
LANES = 128
SUBLANES = 8

time_step = 0.1
cutoff_sq = 16.0
force_scale = 4.0
length_floor = 0.25


def passed_along(array, axis, by):
    length = lax.axis_size(axis)
    return lax.ppermute(array, axis, [(i, (i + by) % length) for i in range(length)])


def first_of(domains):
    return domains - 1


def from_slab(blocks):
    length = lax.axis_size("dom")
    order = [(first_of(length) + i) % length for i in range(length)]
    return lax.all_to_all(blocks, "dom", 0, 0, axis_index_groups=[order], tiled=True)


def place_of(stride=0):
    length = lax.axis_size("dom")
    return lax.rem(lax.axis_index("dom") + (stride - first_of(length)) % length, length)


def strides_of(domains):
    row_width = max(2, domains // 8)
    return (1, -1, row_width, -row_width)


def round_up(count, step):
    return -(-count // step) * step


class Rows:
    def __init__(self, atoms, bonds, slots):
        self.atom_rows = atoms // LANES
        self.shell_rows = atoms // 2 // LANES
        self.bond_rows = bonds // LANES
        self.slot_rows = slots // LANES
        at = 0
        self.coords = []
        for _ in range(3):
            self.coords.append(at)
            at += self.atom_rows
        self.charge = at
        at += self.shell_rows
        self.mass = at
        at += self.atom_rows
        self.bond_first = at
        at += self.bond_rows
        self.bond_second = at
        at += self.bond_rows
        self.cross_first = at
        at += self.slot_rows
        self.cross_second = at
        at += self.slot_rows
        self.used = at
        self.count = round_up(at, SUBLANES)
        self.shell_terms = (self.bond_rows + self.slot_rows) * LANES
        self.inner_at = (0, self.shell_terms)
        self.cross_at = self.bond_rows * LANES
        self.far_at = self.shell_terms + self.bond_rows * LANES
        self.matrix = self.far_at + self.slot_rows * LANES
        self.live = 3 * self.atom_rows
        self.side = self.live + self.slot_rows
        self.disp_used = self.side + self.slot_rows
        self.disp_count = round_up(self.disp_used, SUBLANES)


def take_lanes(table, lanes):
    return jnp.take_along_axis(table, lanes, axis=1, mode="promise_in_bounds")


def pick(tables, index):
    lanes = index & (LANES - 1)
    chunk = index >> 7
    result = take_lanes(tables[0], lanes)
    for k in range(1, len(tables)):
        result = jnp.where(chunk == k, take_lanes(tables[k], lanes), result)
    return result


def fetched(sources, targets, sem_ref):
    copies = [pltpu.make_async_copy(s, t, sem_ref.at[n]) for n, (s, t) in enumerate(zip(sources, targets))]
    for copy in copies:
        copy.start()
    return copies


def pack_kernel(rows, copies, *refs):
    sources, (out_ref, rim_ref), targets, sem_ref = refs[:5], refs[5:7], refs[7:12], refs[12]
    block_ref = refs[13]
    for copy in fetched(sources, targets, sem_ref):
        copy.wait()
    coords_ref, charge_ref, mass_ref, bonds_ref, cross_ref = targets

    def put(row, value):
        for part in range(value.shape[1] // LANES):
            block_ref[pl.ds(row + part, 1), :] = value[:, part * LANES : (part + 1) * LANES]

    shell = rows.shell_rows * LANES
    fields = [coords_ref[c, 0] for c in range(3)] + [charge_ref[0, :, :shell]]
    for c in range(4):
        at = rows.coords[c] if c < 3 else rows.charge
        put(at, fields[c])
        for part in range(rows.shell_rows):
            rim_ref[pl.ds(c * rows.shell_rows + part, 1), :] = fields[c][:, part * LANES : (part + 1) * LANES]
    put(rows.mass, mass_ref[0])
    put(rows.bond_first, bonds_ref[0, 0].astype(jnp.float32))
    put(rows.bond_second, bonds_ref[1, 0].astype(jnp.float32))
    put(rows.cross_first, cross_ref[0, 0].astype(jnp.float32))
    put(rows.cross_second, cross_ref[1, 0].astype(jnp.float32))
    if rows.count > rows.used:
        block_ref[rows.used :, :] = jnp.zeros((rows.count - rows.used, LANES), jnp.float32)
    block = block_ref[...]
    for copy in range(copies):
        out_ref[pl.ds(copy * rows.count, rows.count), :] = block


SHRINK = 1.0 / 4.0
OUT_OF_REACH = 1000.0
TILES_STEP = 4
PIECE = 32


def own_kernel(
    rows,
    coords_hbm,
    charge_hbm,
    velocity_hbm,
    mass_hbm,
    side_hbm,
    atoms_hbm,
    own_ref,
    far_ref,
    index_ref,
    motion_ref,
    coords_ref,
    charge_ref,
    velocity_ref,
    mass_ref,
    side_ref,
    sem_ref,
):
    atom_rows = rows.atom_rows
    copies = fetched(
        (coords_hbm, charge_hbm, atoms_hbm.at[0, 0], velocity_hbm, mass_hbm, side_hbm),
        (coords_ref, charge_ref, index_ref, velocity_ref, mass_ref, side_ref),
        sem_ref,
    )
    down = lax.broadcasted_iota(jnp.int32, (SUBLANES, LANES), 0)
    copies[0].wait()
    copies[1].wait()

    def lanes_of(part):
        return slice(part * LANES, (part + 1) * LANES)

    table = []
    for c in range(4):
        field = coords_ref[c, 0] * SHRINK if c < 3 else charge_ref[0]
        table.append(
            [jnp.broadcast_to(field[:, lanes_of(part)], (SUBLANES, LANES)) for part in range(atom_rows)]
        )
    for part in range(atom_rows):
        for group in range(LANES // SUBLANES):
            at = part * LANES + group * SUBLANES
            for c in range(4):
                value = take_lanes(table[c][part], down + group * SUBLANES)
                own_ref[c, pl.ds(at, SUBLANES), :] = value if c < 3 else value * 8.0
    copies[2].wait()
    for group in range(index_ref.shape[0] // SUBLANES):
        at = pl.ds(group * SUBLANES, SUBLANES)
        index = index_ref[at, :]
        for c in range(4):
            far_ref[c, at, :] = pick(table[c], index)
    for copy in copies[3:]:
        copy.wait()
    fields = [velocity_ref[c, 0] for c in range(3)] + [mass_ref[0], side_ref[0].astype(jnp.float32)]
    at = 0
    for field in fields:
        for part in range(field.shape[1] // LANES):
            motion_ref[pl.ds(at, 1), :] = field[:, lanes_of(part)]
            at += 1


def force_kernel(
    rows,
    copies,
    place,
    live_ref,
    count_ref,
    block_hbm,
    around_ref,
    below_ref,
    above_ref,
    own_ref,
    near_ref,
    index_ref,
    motion_ref,
    out_ref,
    table_ref,
    far_ref,
    sum_ref,
    block_ref,
    sem_ref,
):
    atom_rows, shell_rows = rows.atom_rows, rows.shell_rows
    tiles = index_ref.shape[0]
    block_copy = pltpu.make_async_copy(block_hbm, block_ref, sem_ref)
    block_copy.start()
    live = live_ref[0, 0]
    holders = place()
    starts = [rows.coords[0], rows.coords[1], rows.coords[2], rows.charge]
    entry_rows = 6 * shell_rows

    def broadcast(row):
        return jnp.broadcast_to(row, (SUBLANES, LANES))

    for c in range(4):
        factor = SHRINK if c < 3 else 1.0
        at = 0
        for neighbour in range(4):
            base = holders[neighbour] * rows.count + starts[c]
            for part in range(shell_rows):
                table_ref[c, at] = broadcast(around_ref[pl.ds(base + part, 1), :] * factor)
                at += 1
        for slab_ref in (below_ref, above_ref):
            for part in range(shell_rows):
                table_ref[c, at] = broadcast(slab_ref[pl.ds(c * shell_rows + part, 1), :] * factor)
                at += 1

    def gather(group):
        at = pl.ds(pl.multiple_of(group * SUBLANES, SUBLANES), SUBLANES)
        index = index_ref[at, :]
        lanes = index & (LANES - 1)
        chunk = index >> 7
        values = [near_ref[c, at, :] for c in range(4)]
        for k in range(entry_rows):
            here = chunk == atom_rows + k
            values = [jnp.where(here, take_lanes(table_ref[c, k], lanes), values[c]) for c in range(4)]
        for c in range(4):
            far_ref[c, at, :] = values[c]

    def gather_groups(step, _):
        for n in range(2):
            gather(step * 2 + n)
        return 0

    lax.fori_loop(0, tiles // SUBLANES // 2, gather_groups, 0)

    sum_ref[...] = jnp.zeros(sum_ref.shape, jnp.float32)
    block_copy.wait()
    down = lax.broadcasted_iota(jnp.int32, (tiles, LANES), 0)
    far_ref[0] = jnp.where(down < live, far_ref[0], OUT_OF_REACH)

    softening = 1.0 / cutoff_sq

    def add_tile(tile):
        base = block_ref[0, 0, tile] * TILE
        far = [jnp.broadcast_to(far_ref[c, pl.ds(tile, 1), :], (PIECE, LANES)) for c in range(4)]
        for piece in range(TILE // PIECE):
            at = pl.ds(pl.multiple_of(base + piece * PIECE, PIECE), PIECE)
            gap = [own_ref[c, at, :] - far[c] for c in range(3)]
            square = gap[0] * gap[0] + gap[1] * gap[1] + gap[2] * gap[2]
            inverse = pl.reciprocal(square + softening, approx=True)
            weight = jnp.maximum(inverse - 1.0 / (1.0 + softening), 0.0)
            strength = (inverse - own_ref[3, at, :] * far[3]) * (weight * weight)
            for c in range(3):
                sum_ref[c, at, :] = sum_ref[c, at, :] + strength * gap[c]

    def add_tiles(step, _):
        for n in range(TILES_STEP):
            add_tile(step * TILES_STEP + n)
        return 0

    lax.fori_loop(0, lax.div(live + TILES_STEP - 1, TILES_STEP), add_tiles, 0)

    scale = time_step * time_step * force_scale * 4.0 / 2048.0 * (1.0 + softening) ** 2

    lane = lax.broadcasted_iota(jnp.int32, (LANES, LANES), 1)
    columns = jnp.zeros((LANES, LANES), jnp.float32)
    for c in range(3):
        for part in range(atom_rows):
            total = jnp.sum(sum_ref[c, pl.ds(part * LANES, LANES), :], axis=1, keepdims=True)
            columns = jnp.where(lane == c * atom_rows + part, total, columns)
    totals = columns.T[: 3 * atom_rows, :]
    mass = motion_ref[pl.ds(3 * atom_rows, atom_rows), :]
    moved = time_step * motion_ref[pl.ds(0, 3 * atom_rows), :] + scale * totals * jnp.concatenate([mass] * 3, axis=0)
    for copy in range(copies):
        out_ref[pl.ds(copy * rows.disp_count, 3 * atom_rows), :] = moved
    slot = lax.broadcasted_iota(jnp.int32, (1, LANES), 1)
    for part in range(rows.slot_rows):
        flag = jnp.where(slot + part * LANES < count_ref[0, 0], 1.0, 0.0)
        side = motion_ref[pl.ds(4 * atom_rows + part, 1), :]
        for copy in range(copies):
            out_ref[pl.ds(copy * rows.disp_count + rows.live + part, 1), :] = flag
            out_ref[pl.ds(copy * rows.disp_count + rows.side + part, 1), :] = side
    if rows.disp_count > rows.disp_used:
        for copy in range(copies):
            out_ref[pl.ds(copy * rows.disp_count + rows.disp_used, rows.disp_count - rows.disp_used), :] = jnp.zeros(
                (rows.disp_count - rows.disp_used, LANES), jnp.float32
            )


def bond_kernel(rows, domains, strides, around_ref, weight_ref, matrix_ref):
    atom_rows, shell_rows = rows.atom_rows, rows.shell_rows

    def load(row):
        return around_ref[pl.ds(row, domains, stride=rows.count), :]

    def index(row):
        return load(row).astype(jnp.int32)

    fields = [[load(at + part) for part in range(atom_rows)] for at in rows.coords + [rows.mass]]

    def put_weights(first, second, at):
        gap = [first[c] - second[c] for c in range(3)]
        length_sq = gap[0] * gap[0] + gap[1] * gap[1] + gap[2] * gap[2] + length_floor
        scale = lax.rsqrt(length_sq) * lax.rsqrt(first[3] + second[3])
        for c in range(3):
            weight_ref[pl.ds((at * 3 + c) * domains, domains), :] = gap[c] * scale

    for part in range(rows.bond_rows):
        first = index(rows.bond_first + part)
        second = index(rows.bond_second + part)
        put_weights([pick(f, first) for f in fields], [pick(f, second) for f in fields], part)
    shells = [f[:shell_rows] for f in fields]
    for part in range(rows.slot_rows):
        first = index(rows.cross_first + part)
        second = index(rows.cross_second + part)
        ends = [pick(f, first) for f in shells]
        for code, stride in enumerate(strides):
            seen = pltpu.roll(second, stride % domains, 0)
            others = [pltpu.roll(pick(f, seen), -stride % domains, 0) for f in shells]
            put_weights(ends, others, rows.bond_rows + part * 4 + code)

    down = lax.broadcasted_iota(jnp.int32, (SUBLANES, LANES), 0)
    group_rows = 4 * SUBLANES

    kind = jnp.bfloat16 if shell_rows * LANES <= 256 else jnp.float32
    across = lax.broadcasted_iota(jnp.int32, (group_rows, LANES), 1).astype(jnp.float32)
    lanes = [(across + float(block * LANES)).astype(kind) for block in range(shell_rows)]

    def column(row, step, half=0):
        row = jnp.broadcast_to(row, (SUBLANES, LANES))
        groups = [take_lanes(row, down + at) for at in range(step * group_rows, (step + 1) * group_rows, SUBLANES)]
        return (jnp.concatenate(groups, axis=0) - float(half * shell_rows * LANES)).astype(kind)

    def put(at, ends, signs):
        for block in range(shell_rows):
            value = jnp.zeros((group_rows, LANES), kind)
            for end, sign in zip(ends, signs):
                value = jnp.where(end == lanes[block], jnp.full((group_rows, LANES), sign, kind), value)
            matrix_ref[pl.ds(at, group_rows), block * LANES : (block + 1) * LANES] = value.astype(matrix_ref.dtype)

    def build(domain, _):
        start = pl.multiple_of(domain * rows.matrix, LANES)
        for part in range(rows.bond_rows):
            first = around_ref[pl.ds(domain * rows.count + rows.bond_first + part, 1), :]
            second = around_ref[pl.ds(domain * rows.count + rows.bond_second + part, 1), :]
            for step in range(LANES // group_rows):
                for half in range(2):
                    ends = (column(first, step, half), column(second, step, half))
                    put(start + rows.inner_at[half] + part * LANES + step * group_rows, ends, (1.0, -1.0))
        for part in range(rows.slot_rows):
            for row_at, to, sign in (
                (rows.cross_first, rows.cross_at, 1.0),
                (rows.cross_second, rows.far_at, -1.0),
            ):
                row = around_ref[pl.ds(domain * rows.count + row_at + part, 1), :]
                for step in range(LANES // group_rows):
                    put(start + to + part * LANES + step * group_rows, (column(row, step),), (sign,))
        return 0

    lax.fori_loop(0, domains, build, 0)


def solve_kernel(
    rows,
    domains,
    strides,
    around_ref,
    moves_ref,
    weight_ref,
    matrix_ref,
    coords_out_ref,
    velocity_out_ref,
    push_ref,
    field_ref,
):
    atom_rows, shell_rows = rows.atom_rows, rows.shell_rows
    bond_rows, slot_rows = rows.bond_rows, rows.slot_rows
    me = place_of()

    def load(row):
        return around_ref[pl.ds(row, domains, stride=rows.count), :]

    def index(row):
        return load(row).astype(jnp.int32)

    inner_first = [index(rows.bond_first + p) for p in range(bond_rows)]
    inner_second = [index(rows.bond_second + p) for p in range(bond_rows)]
    cross_first = [index(rows.cross_first + p) for p in range(slot_rows)]
    cross_second = [index(rows.cross_second + p) for p in range(slot_rows)]
    masses = [load(rows.mass + p) for p in range(atom_rows)]

    def move_rows(row):
        return moves_ref[pl.ds(row, domains, stride=rows.disp_count), :]

    def weight_rows(at, c):
        return weight_ref[pl.ds((at * 3 + c) * domains, domains), :]

    sides = [move_rows(rows.side + p) for p in range(slot_rows)]
    cross_weights = []
    for part in range(slot_rows):
        live = move_rows(rows.live + part)
        for c in range(3):
            value = 0.0
            for code in range(4):
                value = jnp.where(sides[part] == code, weight_rows(bond_rows + part * 4 + code, c), value)
            cross_weights.append(value * live)

    def weight(at, c):
        return weight_rows(at, c) if at < bond_rows else cross_weights[(at - bond_rows) * 3 + c]

    def project(fields):
        result = []
        for part in range(bond_rows):
            total = 0.0
            for c in range(3):
                ends = pick(fields[c], inner_first[part]) - pick(fields[c], inner_second[part])
                total = total + weight(part, c) * ends
            result.append(total)
        for part in range(slot_rows):
            seen = [pltpu.roll(cross_second[part], stride % domains, 0) for stride in strides]
            total = 0.0
            for c in range(3):
                shell = fields[c][:shell_rows]
                other = 0.0
                for code, stride in enumerate(strides):
                    value = pltpu.roll(pick(shell, seen[code]), -stride % domains, 0)
                    other = jnp.where(sides[part] == code, value, other)
                total = total + weight(bond_rows + part, c) * (pick(shell, cross_first[part]) - other)
            result.append(total)
        return result

    def put_pushes(values):
        for at, value in enumerate(values):
            for c in range(3):
                pushed = weight(at, c) * value
                high = pushed.astype(jnp.bfloat16).astype(jnp.float32)
                push_ref[at, pl.ds(c * domains, domains), :] = high
                push_ref[at, pl.ds((3 + c) * domains, domains), :] = pushed - high

    def pushes_of(at, domain):
        return push_ref[at, pl.ds(domain, SUBLANES, stride=domains), :]

    def product(pushes, domain, at):
        start = domain * rows.matrix + at
        if not isinstance(start, int):
            start = pl.multiple_of(start, LANES)
        pushes = pushes[0] if len(pushes) == 1 else jnp.concatenate(pushes, axis=1)
        result = jnp.dot(
            pushes.astype(jnp.bfloat16),
            matrix_ref[pl.ds(start, pushes.shape[1]), :],
            preferred_element_type=jnp.float32,
        )
        return [result[:, p * LANES : (p + 1) * LANES] for p in range(shell_rows)]

    def inner_totals(pushes, domain):
        return product(pushes, domain, 0) + product(pushes[:bond_rows], domain, rows.shell_terms)

    def far_totals(pushes, domain, codes):
        masked = []
        for part in range(slot_rows):
            side = moves_ref[pl.ds(domain * rows.disp_count + rows.side + part, 1), :]
            side = jnp.broadcast_to(side, (SUBLANES, LANES))
            pushed = pushes[bond_rows + part]
            masked.append(jnp.concatenate([jnp.where(side == code, pushed, 0.0) for code in codes], axis=0))
        return product(masked, domain, rows.far_at)

    def spread(values):
        put_pushes(values)
        for domain in range(domains):
            pushes = [pushes_of(at, domain) for at in range(bond_rows + slot_rows)]
            for part, total in enumerate(inner_totals(pushes, domain)):
                field_ref[0, part, pl.ds(domain, SUBLANES, stride=domains), :] = total
            for part, total in enumerate(far_totals(pushes, domain, range(4))):
                for code, stride in enumerate(strides):
                    field_ref[1 + code, part, pl.ds((domain + stride) % domains, SUBLANES, stride=domains), :] = total[
                        code * SUBLANES : (code + 1) * SUBLANES, :
                    ]

        def field(c, part):
            pieces = [
                field_ref[source, part, pl.ds(row * domains, domains), :]
                for source in range(5 if part < shell_rows else 1)
                for row in (c, 3 + c)
            ]
            return masses[part] * functools.reduce(lambda a, b: a + b, pieces)

        return [[field(c, part) for part in range(atom_rows)] for c in range(3)]

    moves = [
        [move_rows(c * atom_rows + p) for p in range(atom_rows)]
        for c in range(3)
    ]
    push_ref[...] = jnp.zeros(push_ref.shape, jnp.float32)
    residue = project(moves)

    def expand(_, carry):
        residue, summed = carry
        change = project(spread(residue))
        residue = [now - step for now, step in zip(residue, change)]
        return residue, [a + b for a, b in zip(summed, residue)]

    residue, summed = lax.fori_loop(0, ORDER, expand, (residue, residue))
    put_pushes(summed)
    sums = inner_totals([pushes_of(at, me) for at in range(bond_rows + slot_rows)], me)
    for code, stride in enumerate(strides):
        owner = lax.rem(me + (-stride) % domains, domains)
        pushes = [pushes_of(at, owner) for at in range(bond_rows + slot_rows)]
        for part, total in enumerate(far_totals(pushes, owner, [code])):
            sums[part] = sums[part] + total
    for part in range(atom_rows):
        lanes = slice(part * LANES, (part + 1) * LANES)
        mass = around_ref[pl.ds(me * rows.count + rows.mass + part, 1), :]
        for c in range(3):
            correction = mass * (sums[part][c : c + 1, :] + sums[part][3 + c : 4 + c, :])
            move = moves_ref[pl.ds(me * rows.disp_count + c * atom_rows + part, 1), :] - correction
            start = around_ref[pl.ds(me * rows.count + rows.coords[c] + part, 1), :]
            coords_out_ref[c, 0, :, lanes] = start + move
            velocity_out_ref[c, 0, :, lanes] = move * (1.0 / time_step)


def vmem(count):
    return [pl.BlockSpec(memory_space=pltpu.VMEM)] * count


def smem(count):
    return [pl.BlockSpec(memory_space=pltpu.SMEM)] * count


def hbm(count):
    return [pl.BlockSpec(memory_space=pltpu.HBM)] * count


def in_hbm(arrays):
    return [pltpu.with_memory_space_constraint(a, pltpu.HBM) for a in arrays]


def params(mebibytes):
    return pltpu.CompilerParams(vmem_limit_bytes=mebibytes * 1024 * 1024)


def cost(flops, moved):
    return pl.CostEstimate(flops=flops, bytes_accessed=moved, transcendentals=0)


def room_for(arrays):
    return [pltpu.VMEM(a.shape, a.dtype) for a in arrays]


def shards(
    coords,
    velocity,
    charge,
    inv_mass,
    tile_block,
    tile_atoms,
    active_tile_count,
    bond_atoms,
    cross_atoms,
    cross_side,
    cross_count,
):
    atoms = coords.shape[-1]
    tiles = tile_atoms.shape[2]
    domains = lax.axis_size("dom")
    strides = strides_of(domains)
    rows = Rows(atoms, bond_atoms.shape[-1], cross_side.shape[-1])
    whole_slab = domains == SUBLANES
    copies = domains if whole_slab else 1
    f32 = jnp.float32

    sent = (coords, charge, inv_mass, bond_atoms, cross_atoms)
    packed, rim = pl.pallas_call(
        functools.partial(pack_kernel, rows, copies),
        out_shape=(
            jax.ShapeDtypeStruct((copies * rows.count, LANES), f32),
            jax.ShapeDtypeStruct((4 * rows.shell_rows, LANES), f32),
        ),
        in_specs=hbm(len(sent)),
        out_specs=tuple(vmem(2)),
        scratch_shapes=room_for(sent)
        + [pltpu.SemaphoreType.DMA((len(sent),)), pltpu.VMEM((rows.count, LANES), f32)],
        compiler_params=params(4),
        name="pack",
    )(*in_hbm(sent))

    alone = (coords, charge, velocity, inv_mass, cross_side, tile_atoms)
    own = pl.pallas_call(
        functools.partial(own_kernel, rows),
        out_shape=(
            jax.ShapeDtypeStruct((4, atoms, LANES), f32),
            jax.ShapeDtypeStruct((4, tiles, TILE), f32),
            jax.ShapeDtypeStruct((tiles, TILE), jnp.int32),
            jax.ShapeDtypeStruct((4 * rows.atom_rows + rows.slot_rows, LANES), f32),
        ),
        in_specs=hbm(len(alone)),
        out_specs=tuple(vmem(4)),
        scratch_shapes=room_for(alone[:5]) + [pltpu.SemaphoreType.DMA((len(alone),))],
        compiler_params=params(4),
        cost_estimate=cost(64 * atoms * LANES, 16 * atoms * LANES),
        name="own",
    )(*in_hbm(alone))

    below = passed_along(rim, "slab", 1)
    above = passed_along(rim, "slab", -1)
    if whole_slab:
        around = from_slab(packed)

        def place():
            return [place_of(stride) for stride in strides]

    else:
        around = jnp.concatenate([packed] + [passed_along(packed, "dom", -stride) for stride in strides], axis=0)

        def place():
            return [1, 2, 3, 4]


    moves = pl.pallas_call(
        functools.partial(force_kernel, rows, copies, place),
        out_shape=jax.ShapeDtypeStruct((copies * rows.disp_count, LANES), f32),
        in_specs=smem(2) + hbm(1) + vmem(7),
        out_specs=vmem(1)[0],
        scratch_shapes=[
            pltpu.VMEM((4, 6 * rows.shell_rows, SUBLANES, LANES), f32),
            pltpu.VMEM((4, tiles, LANES), f32),
            pltpu.VMEM((3, atoms, LANES), f32),
            pltpu.SMEM(tile_block.shape, jnp.int32),
            pltpu.SemaphoreType.DMA(()),
        ],
        compiler_params=params(8),
        cost_estimate=cost(30 * tiles * TILE * TILE, 4 * around.size),
        name="force",
    )(active_tile_count, cross_count, *in_hbm([tile_block]), around, below, above, *own)

    if not whole_slab:
        return by_exchange(rows, strides, around, moves, cross_count)

    constraint_rows = rows.bond_rows + rows.slot_rows
    weight, matrix = pl.pallas_call(
        functools.partial(bond_kernel, rows, domains, strides),
        out_shape=(
            jax.ShapeDtypeStruct(((rows.bond_rows + 4 * rows.slot_rows) * 3 * domains, LANES), f32),
            jax.ShapeDtypeStruct((domains * rows.matrix, atoms // 2), jnp.bfloat16),
        ),
        in_specs=vmem(1),
        out_specs=tuple(vmem(2)),
        compiler_params=params(16),
        cost_estimate=cost(8 * domains * rows.matrix * atoms // 2, 4 * around.size),
        name="bonds",
    )(around)

    every_move = from_slab(moves)

    return pl.pallas_call(
        functools.partial(solve_kernel, rows, domains, strides),
        out_shape=(
            jax.ShapeDtypeStruct(coords.shape, f32),
            jax.ShapeDtypeStruct(coords.shape, f32),
        ),
        in_specs=vmem(4),
        out_specs=tuple(vmem(2)),
        scratch_shapes=[
            pltpu.VMEM((constraint_rows, SUBLANES * domains, LANES), f32),
            pltpu.VMEM((5, rows.atom_rows, SUBLANES * domains, LANES), f32),
        ],
        compiler_params=params(16),
        name="solve",
    )(around, every_move, weight, matrix)


def by_exchange(rows, strides, around, moves, cross_count):
    atom_count = rows.atom_rows * LANES
    shell = rows.shell_rows * LANES
    inside = around.reshape(5, rows.count, LANES)

    def flat(at, count):
        return inside[0, at : at + count].reshape(-1)

    def neighbours(at):
        return inside[1:, at : at + rows.shell_rows].reshape(-1)

    coords = jnp.stack([flat(at, rows.atom_rows) for at in rows.coords])
    inv_mass = flat(rows.mass, rows.atom_rows)
    displace = moves[: rows.live].reshape(3, atom_count)
    left = flat(rows.bond_first, rows.bond_rows).astype(jnp.int32)
    right = flat(rows.bond_second, rows.bond_rows).astype(jnp.int32)
    cross_left = flat(rows.cross_first, rows.slot_rows).astype(jnp.int32)
    cross_right = flat(rows.cross_second, rows.slot_rows).astype(jnp.int32)
    side = moves[rows.side : rows.side + rows.slot_rows].reshape(-1).astype(jnp.int32)
    flag = moves[rows.live : rows.side].reshape(-1)
    cross_index = side * shell + cross_right
    far_coords = jnp.stack([neighbours(at) for at in rows.coords])
    far_mass = neighbours(rows.mass)

    def weights(first, second, mass_first, mass_second):
        gap = first - second
        length = jnp.sqrt(jnp.sum(gap * gap, axis=0) + length_floor)
        return gap / length * lax.rsqrt(mass_first + mass_second)

    inner = weights(coords[:, left], coords[:, right], inv_mass[left], inv_mass[right])
    cross = flag * weights(
        coords[:, cross_left], far_coords[:, cross_index], inv_mass[cross_left], far_mass[cross_index]
    )

    def project(field):
        rim = field[:, :shell]
        far = jnp.concatenate([passed_along(rim, "dom", -stride) for stride in strides], axis=1)
        return (
            jnp.sum(inner * (field[:, left] - field[:, right]), axis=0),
            jnp.sum(cross * (field[:, cross_left] - far[:, cross_index]), axis=0),
        )

    def spread(values):
        pushed = inner * values[0]
        pushed_cross = cross * values[1]
        totals = jnp.zeros((3, atom_count), jnp.float32).at[:, left].add(pushed).at[:, right].add(-pushed)
        totals = totals.at[:, cross_left].add(pushed_cross)
        outward = jnp.zeros((3, 4 * shell), jnp.float32).at[:, cross_index].add(-pushed_cross)
        for code, stride in enumerate(strides):
            totals = totals.at[:, :shell].add(
                passed_along(outward[:, code * shell : (code + 1) * shell], "dom", stride)
            )
        return inv_mass * totals

    residue = project(displace)
    summed = residue
    for _ in range(ORDER):
        change = project(spread(residue))
        residue = tuple(now - step for now, step in zip(residue, change))
        summed = tuple(a + b for a, b in zip(summed, residue))
    move = displace - spread(summed)
    return (
        (coords + move).reshape(3, 1, 1, atom_count),
        (move * (1.0 / time_step)).reshape(3, 1, 1, atom_count),
    )


def solution(mesh):
    return jax.shard_map(
        shards,
        mesh=mesh,
        in_specs=(
            P(None, "slab", "dom", None),
            P(None, "slab", "dom", None),
            P("slab", "dom", None),
            P("slab", "dom", None),
            P("slab", "dom", None),
            P("slab", "dom", None, None),
            P("slab", "dom"),
            P(None, "slab", "dom", None),
            P(None, "slab", "dom", None),
            P("slab", "dom", None),
            P("slab", "dom"),
        ),
        out_specs=(P(None, "slab", "dom", None), P(None, "slab", "dom", None)),
        check_vma=False,
    )
```

```python
import functools

import jax
import jax.numpy as jnp
from jax import lax
from jax.experimental import pallas as pl
from jax.experimental.pallas import tpu as pltpu
from jax.sharding import PartitionSpec as P

TILE = 128
ORDER = 4
LANES = 128
SUBLANES = 8

time_step = 0.1
cutoff_sq = 16.0
force_scale = 4.0
length_floor = 0.25


def passed_along(array, axis, by):
    length = lax.axis_size(axis)
    return lax.ppermute(array, axis, [(i, (i + by) % length) for i in range(length)])


def first_of(domains):
    return domains - 1


def from_slab(blocks):
    length = lax.axis_size("dom")
    order = [(first_of(length) + i) % length for i in range(length)]
    return lax.all_to_all(blocks, "dom", 0, 0, axis_index_groups=[order], tiled=True)


def place_of(stride=0):
    length = lax.axis_size("dom")
    return lax.rem(lax.axis_index("dom") + (stride - first_of(length)) % length, length)


def strides_of(domains):
    row_width = max(2, domains // 8)
    return (1, -1, row_width, -row_width)


def round_up(count, step):
    return -(-count // step) * step


class Rows:
    def __init__(self, atoms, bonds, slots):
        self.atom_rows = atoms // LANES
        self.shell_rows = atoms // 2 // LANES
        self.bond_rows = bonds // LANES
        self.slot_rows = slots // LANES
        at = 0
        self.coords = []
        for _ in range(3):
            self.coords.append(at)
            at += self.atom_rows
        self.charge = at
        at += self.shell_rows
        self.mass = at
        at += self.atom_rows
        self.bond_first = at
        at += self.bond_rows
        self.bond_second = at
        at += self.bond_rows
        self.cross_first = at
        at += self.slot_rows
        self.cross_second = at
        at += self.slot_rows
        self.used = at
        self.count = round_up(at, SUBLANES)
        self.shell_terms = (self.bond_rows + self.slot_rows) * LANES
        self.inner_at = (0, self.shell_terms)
        self.cross_at = self.bond_rows * LANES
        self.far_at = self.shell_terms + self.bond_rows * LANES
        self.matrix = self.far_at + self.slot_rows * LANES
        self.live = 3 * self.atom_rows
        self.side = self.live + self.slot_rows
        self.disp_used = self.side + self.slot_rows
        self.disp_count = round_up(self.disp_used, SUBLANES)


def take_lanes(table, lanes):
    return jnp.take_along_axis(table, lanes, axis=1, mode="promise_in_bounds")


def pick(tables, index):
    lanes = index & (LANES - 1)
    chunk = index >> 7
    result = take_lanes(tables[0], lanes)
    for k in range(1, len(tables)):
        result = jnp.where(chunk == k, take_lanes(tables[k], lanes), result)
    return result


def fetched(sources, targets, sem_ref):
    copies = [pltpu.make_async_copy(s, t, sem_ref.at[n]) for n, (s, t) in enumerate(zip(sources, targets))]
    for copy in copies:
        copy.start()
    return copies


def pack_kernel(rows, copies, *refs):
    sources, (out_ref, rim_ref), targets, sem_ref = refs[:5], refs[5:7], refs[7:12], refs[12]
    block_ref = refs[13]
    for copy in fetched(sources, targets, sem_ref):
        copy.wait()
    coords_ref, charge_ref, mass_ref, bonds_ref, cross_ref = targets

    def put(row, value):
        for part in range(value.shape[1] // LANES):
            block_ref[pl.ds(row + part, 1), :] = value[:, part * LANES : (part + 1) * LANES]

    shell = rows.shell_rows * LANES
    fields = [coords_ref[c, 0] for c in range(3)] + [charge_ref[0, :, :shell]]
    for c in range(4):
        at = rows.coords[c] if c < 3 else rows.charge
        put(at, fields[c])
        for part in range(rows.shell_rows):
            rim_ref[pl.ds(c * rows.shell_rows + part, 1), :] = fields[c][:, part * LANES : (part + 1) * LANES]
    put(rows.mass, mass_ref[0])
    put(rows.bond_first, bonds_ref[0, 0].astype(jnp.float32))
    put(rows.bond_second, bonds_ref[1, 0].astype(jnp.float32))
    put(rows.cross_first, cross_ref[0, 0].astype(jnp.float32))
    put(rows.cross_second, cross_ref[1, 0].astype(jnp.float32))
    if rows.count > rows.used:
        block_ref[rows.used :, :] = jnp.zeros((rows.count - rows.used, LANES), jnp.float32)
    block = block_ref[...]
    for copy in range(copies):
        out_ref[pl.ds(copy * rows.count, rows.count), :] = block


SHRINK = 1.0 / 4.0
OUT_OF_REACH = 1000.0
TILES_STEP = 4
PIECE = 32


def own_kernel(
    rows,
    coords_hbm,
    charge_hbm,
    velocity_hbm,
    mass_hbm,
    side_hbm,
    atoms_hbm,
    own_ref,
    far_ref,
    index_ref,
    motion_ref,
    coords_ref,
    charge_ref,
    velocity_ref,
    mass_ref,
    side_ref,
    sem_ref,
):
    atom_rows = rows.atom_rows
    copies = fetched(
        (coords_hbm, charge_hbm, atoms_hbm.at[0, 0], velocity_hbm, mass_hbm, side_hbm),
        (coords_ref, charge_ref, index_ref, velocity_ref, mass_ref, side_ref),
        sem_ref,
    )
    down = lax.broadcasted_iota(jnp.int32, (SUBLANES, LANES), 0)
    copies[0].wait()
    copies[1].wait()

    def lanes_of(part):
        return slice(part * LANES, (part + 1) * LANES)

    table = []
    for c in range(4):
        field = coords_ref[c, 0] * SHRINK if c < 3 else charge_ref[0]
        table.append(
            [jnp.broadcast_to(field[:, lanes_of(part)], (SUBLANES, LANES)) for part in range(atom_rows)]
        )
    for part in range(atom_rows):
        for group in range(LANES // SUBLANES):
            at = part * LANES + group * SUBLANES
            for c in range(4):
                value = take_lanes(table[c][part], down + group * SUBLANES)
                own_ref[c, pl.ds(at, SUBLANES), :] = value if c < 3 else value * 8.0
    copies[2].wait()
    for group in range(index_ref.shape[0] // SUBLANES):
        at = pl.ds(group * SUBLANES, SUBLANES)
        index = index_ref[at, :]
        for c in range(4):
            far_ref[c, at, :] = pick(table[c], index)
    for copy in copies[3:]:
        copy.wait()
    fields = [velocity_ref[c, 0] for c in range(3)] + [mass_ref[0], side_ref[0].astype(jnp.float32)]
    at = 0
    for field in fields:
        for part in range(field.shape[1] // LANES):
            motion_ref[pl.ds(at, 1), :] = field[:, lanes_of(part)]
            at += 1


def force_kernel(
    rows,
    copies,
    place,
    live_ref,
    count_ref,
    block_hbm,
    around_ref,
    below_ref,
    above_ref,
    own_ref,
    near_ref,
    index_ref,
    motion_ref,
    out_ref,
    table_ref,
    far_ref,
    sum_ref,
    block_ref,
    sem_ref,
):
    atom_rows, shell_rows = rows.atom_rows, rows.shell_rows
    tiles = index_ref.shape[0]
    block_copy = pltpu.make_async_copy(block_hbm, block_ref, sem_ref)
    block_copy.start()
    live = live_ref[0, 0]
    holders = place()
    starts = [rows.coords[0], rows.coords[1], rows.coords[2], rows.charge]
    entry_rows = 6 * shell_rows

    def broadcast(row):
        return jnp.broadcast_to(row, (SUBLANES, LANES))

    for c in range(4):
        factor = SHRINK if c < 3 else 1.0
        at = 0
        for neighbour in range(4):
            base = holders[neighbour] * rows.count + starts[c]
            for part in range(shell_rows):
                table_ref[c, at] = broadcast(around_ref[pl.ds(base + part, 1), :] * factor)
                at += 1
        for slab_ref in (below_ref, above_ref):
            for part in range(shell_rows):
                table_ref[c, at] = broadcast(slab_ref[pl.ds(c * shell_rows + part, 1), :] * factor)
                at += 1

    for group in range(tiles // SUBLANES):
        at = pl.ds(group * SUBLANES, SUBLANES)
        index = index_ref[at, :]
        lanes = index & (LANES - 1)
        chunk = index >> 7
        values = [near_ref[c, at, :] for c in range(4)]
        for k in range(entry_rows):
            here = chunk == atom_rows + k
            values = [jnp.where(here, take_lanes(table_ref[c, k], lanes), values[c]) for c in range(4)]
        for c in range(4):
            far_ref[c, at, :] = values[c]

    sum_ref[...] = jnp.zeros(sum_ref.shape, jnp.float32)
    block_copy.wait()
    down = lax.broadcasted_iota(jnp.int32, (tiles, LANES), 0)
    far_ref[0] = jnp.where(down < live, far_ref[0], OUT_OF_REACH)

    softening = 1.0 / cutoff_sq

    def add_tile(tile):
        base = block_ref[0, 0, tile] * TILE
        far = [jnp.broadcast_to(far_ref[c, pl.ds(tile, 1), :], (PIECE, LANES)) for c in range(4)]
        for piece in range(TILE // PIECE):
            at = pl.ds(pl.multiple_of(base + piece * PIECE, PIECE), PIECE)
            gap = [own_ref[c, at, :] - far[c] for c in range(3)]
            square = gap[0] * gap[0] + gap[1] * gap[1] + gap[2] * gap[2]
            inverse = pl.reciprocal(square + softening, approx=True)
            weight = jnp.maximum(inverse - 1.0 / (1.0 + softening), 0.0)
            strength = (inverse - own_ref[3, at, :] * far[3]) * (weight * weight)
            for c in range(3):
                sum_ref[c, at, :] = sum_ref[c, at, :] + strength * gap[c]

    def add_tiles(step, _):
        for n in range(TILES_STEP):
            add_tile(step * TILES_STEP + n)
        return 0

    lax.fori_loop(0, lax.div(live + TILES_STEP - 1, TILES_STEP), add_tiles, 0)

    scale = time_step * time_step * force_scale * 4.0 / 2048.0 * (1.0 + softening) ** 2

    lane = lax.broadcasted_iota(jnp.int32, (LANES, LANES), 1)
    columns = jnp.zeros((LANES, LANES), jnp.float32)
    for c in range(3):
        for part in range(atom_rows):
            total = jnp.sum(sum_ref[c, pl.ds(part * LANES, LANES), :], axis=1, keepdims=True)
            columns = jnp.where(lane == c * atom_rows + part, total, columns)
    totals = columns.T[: 3 * atom_rows, :]
    mass = motion_ref[pl.ds(3 * atom_rows, atom_rows), :]
    moved = time_step * motion_ref[pl.ds(0, 3 * atom_rows), :] + scale * totals * jnp.concatenate([mass] * 3, axis=0)
    for copy in range(copies):
        out_ref[pl.ds(copy * rows.disp_count, 3 * atom_rows), :] = moved
    slot = lax.broadcasted_iota(jnp.int32, (1, LANES), 1)
    for part in range(rows.slot_rows):
        flag = jnp.where(slot + part * LANES < count_ref[0, 0], 1.0, 0.0)
        side = motion_ref[pl.ds(4 * atom_rows + part, 1), :]
        for copy in range(copies):
            out_ref[pl.ds(copy * rows.disp_count + rows.live + part, 1), :] = flag
            out_ref[pl.ds(copy * rows.disp_count + rows.side + part, 1), :] = side
    if rows.disp_count > rows.disp_used:
        for copy in range(copies):
            out_ref[pl.ds(copy * rows.disp_count + rows.disp_used, rows.disp_count - rows.disp_used), :] = jnp.zeros(
                (rows.disp_count - rows.disp_used, LANES), jnp.float32
            )


def bond_kernel(rows, domains, strides, around_ref, weight_ref, matrix_ref):
    atom_rows, shell_rows = rows.atom_rows, rows.shell_rows

    def load(row):
        return around_ref[pl.ds(row, domains, stride=rows.count), :]

    def index(row):
        return load(row).astype(jnp.int32)

    fields = [[load(at + part) for part in range(atom_rows)] for at in rows.coords + [rows.mass]]

    def put_weights(first, second, at):
        gap = [first[c] - second[c] for c in range(3)]
        length_sq = gap[0] * gap[0] + gap[1] * gap[1] + gap[2] * gap[2] + length_floor
        scale = lax.rsqrt(length_sq) * lax.rsqrt(first[3] + second[3])
        for c in range(3):
            weight_ref[pl.ds((at * 3 + c) * domains, domains), :] = gap[c] * scale

    for part in range(rows.bond_rows):
        first = index(rows.bond_first + part)
        second = index(rows.bond_second + part)
        put_weights([pick(f, first) for f in fields], [pick(f, second) for f in fields], part)
    shells = [f[:shell_rows] for f in fields]
    for part in range(rows.slot_rows):
        first = index(rows.cross_first + part)
        second = index(rows.cross_second + part)
        ends = [pick(f, first) for f in shells]
        for code, stride in enumerate(strides):
            seen = pltpu.roll(second, stride % domains, 0)
            others = [pltpu.roll(pick(f, seen), -stride % domains, 0) for f in shells]
            put_weights(ends, others, rows.bond_rows + part * 4 + code)

    down = lax.broadcasted_iota(jnp.int32, (SUBLANES, LANES), 0)
    group_rows = 4 * SUBLANES

    kind = jnp.bfloat16 if shell_rows * LANES <= 256 else jnp.float32
    across = lax.broadcasted_iota(jnp.int32, (group_rows, LANES), 1).astype(jnp.float32)
    lanes = [(across + float(block * LANES)).astype(kind) for block in range(shell_rows)]

    def column(row, step, half=0):
        row = jnp.broadcast_to(row, (SUBLANES, LANES))
        groups = [take_lanes(row, down + at) for at in range(step * group_rows, (step + 1) * group_rows, SUBLANES)]
        return (jnp.concatenate(groups, axis=0) - float(half * shell_rows * LANES)).astype(kind)

    def put(at, ends, signs):
        for block in range(shell_rows):
            value = jnp.zeros((group_rows, LANES), kind)
            for end, sign in zip(ends, signs):
                value = jnp.where(end == lanes[block], jnp.full((group_rows, LANES), sign, kind), value)
            matrix_ref[pl.ds(at, group_rows), block * LANES : (block + 1) * LANES] = value.astype(matrix_ref.dtype)

    def build(domain, _):
        start = pl.multiple_of(domain * rows.matrix, LANES)
        for part in range(rows.bond_rows):
            first = around_ref[pl.ds(domain * rows.count + rows.bond_first + part, 1), :]
            second = around_ref[pl.ds(domain * rows.count + rows.bond_second + part, 1), :]
            for step in range(LANES // group_rows):
                for half in range(2):
                    ends = (column(first, step, half), column(second, step, half))
                    put(start + rows.inner_at[half] + part * LANES + step * group_rows, ends, (1.0, -1.0))
        for part in range(rows.slot_rows):
            for row_at, to, sign in (
                (rows.cross_first, rows.cross_at, 1.0),
                (rows.cross_second, rows.far_at, -1.0),
            ):
                row = around_ref[pl.ds(domain * rows.count + row_at + part, 1), :]
                for step in range(LANES // group_rows):
                    put(start + to + part * LANES + step * group_rows, (column(row, step),), (sign,))
        return 0

    lax.fori_loop(0, domains, build, 0)


def solve_kernel(
    rows,
    domains,
    strides,
    around_ref,
    moves_ref,
    weight_ref,
    matrix_ref,
    coords_out_ref,
    velocity_out_ref,
    push_ref,
    field_ref,
):
    atom_rows, shell_rows = rows.atom_rows, rows.shell_rows
    bond_rows, slot_rows = rows.bond_rows, rows.slot_rows
    me = place_of()

    def load(row):
        return around_ref[pl.ds(row, domains, stride=rows.count), :]

    def index(row):
        return load(row).astype(jnp.int32)

    inner_first = [index(rows.bond_first + p) for p in range(bond_rows)]
    inner_second = [index(rows.bond_second + p) for p in range(bond_rows)]
    cross_first = [index(rows.cross_first + p) for p in range(slot_rows)]
    cross_second = [index(rows.cross_second + p) for p in range(slot_rows)]
    masses = [load(rows.mass + p) for p in range(atom_rows)]

    def move_rows(row):
        return moves_ref[pl.ds(row, domains, stride=rows.disp_count), :]

    def weight_rows(at, c):
        return weight_ref[pl.ds((at * 3 + c) * domains, domains), :]

    sides = [move_rows(rows.side + p) for p in range(slot_rows)]
    cross_weights = []
    for part in range(slot_rows):
        live = move_rows(rows.live + part)
        for c in range(3):
            value = 0.0
            for code in range(4):
                value = jnp.where(sides[part] == code, weight_rows(bond_rows + part * 4 + code, c), value)
            cross_weights.append(value * live)

    def weight(at, c):
        return weight_rows(at, c) if at < bond_rows else cross_weights[(at - bond_rows) * 3 + c]

    def project(fields):
        result = []
        for part in range(bond_rows):
            total = 0.0
            for c in range(3):
                ends = pick(fields[c], inner_first[part]) - pick(fields[c], inner_second[part])
                total = total + weight(part, c) * ends
            result.append(total)
        for part in range(slot_rows):
            seen = [pltpu.roll(cross_second[part], stride % domains, 0) for stride in strides]
            total = 0.0
            for c in range(3):
                shell = fields[c][:shell_rows]
                other = 0.0
                for code, stride in enumerate(strides):
                    value = pltpu.roll(pick(shell, seen[code]), -stride % domains, 0)
                    other = jnp.where(sides[part] == code, value, other)
                total = total + weight(bond_rows + part, c) * (pick(shell, cross_first[part]) - other)
            result.append(total)
        return result

    def put_pushes(values):
        for at, value in enumerate(values):
            for c in range(3):
                pushed = weight(at, c) * value
                high = pushed.astype(jnp.bfloat16).astype(jnp.float32)
                push_ref[at, pl.ds(c * domains, domains), :] = high
                push_ref[at, pl.ds((3 + c) * domains, domains), :] = pushed - high

    def pushes_of(at, domain):
        return push_ref[at, pl.ds(domain, SUBLANES, stride=domains), :]

    def product(pushes, domain, at):
        start = domain * rows.matrix + at
        if not isinstance(start, int):
            start = pl.multiple_of(start, LANES)
        pushes = pushes[0] if len(pushes) == 1 else jnp.concatenate(pushes, axis=1)
        result = jnp.dot(
            pushes.astype(jnp.bfloat16),
            matrix_ref[pl.ds(start, pushes.shape[1]), :],
            preferred_element_type=jnp.float32,
        )
        return [result[:, p * LANES : (p + 1) * LANES] for p in range(shell_rows)]

    def inner_totals(pushes, domain):
        return product(pushes, domain, 0) + product(pushes[:bond_rows], domain, rows.shell_terms)

    def far_totals(pushes, domain, codes):
        masked = []
        for part in range(slot_rows):
            side = moves_ref[pl.ds(domain * rows.disp_count + rows.side + part, 1), :]
            side = jnp.broadcast_to(side, (SUBLANES, LANES))
            pushed = pushes[bond_rows + part]
            masked.append(jnp.concatenate([jnp.where(side == code, pushed, 0.0) for code in codes], axis=0))
        return product(masked, domain, rows.far_at)

    def spread(values):
        put_pushes(values)
        for domain in range(domains):
            pushes = [pushes_of(at, domain) for at in range(bond_rows + slot_rows)]
            for part, total in enumerate(inner_totals(pushes, domain)):
                field_ref[0, part, pl.ds(domain, SUBLANES, stride=domains), :] = total
            for part, total in enumerate(far_totals(pushes, domain, range(4))):
                for code, stride in enumerate(strides):
                    field_ref[1 + code, part, pl.ds((domain + stride) % domains, SUBLANES, stride=domains), :] = total[
                        code * SUBLANES : (code + 1) * SUBLANES, :
                    ]

        def field(c, part):
            pieces = [
                field_ref[source, part, pl.ds(row * domains, domains), :]
                for source in range(5 if part < shell_rows else 1)
                for row in (c, 3 + c)
            ]
            return masses[part] * functools.reduce(lambda a, b: a + b, pieces)

        return [[field(c, part) for part in range(atom_rows)] for c in range(3)]

    moves = [
        [move_rows(c * atom_rows + p) for p in range(atom_rows)]
        for c in range(3)
    ]
    push_ref[...] = jnp.zeros(push_ref.shape, jnp.float32)
    residue = project(moves)

    def expand(_, carry):
        residue, summed = carry
        change = project(spread(residue))
        residue = [now - step for now, step in zip(residue, change)]
        return residue, [a + b for a, b in zip(summed, residue)]

    summed = residue
    for step in range(ORDER):
        residue, summed = expand(step, (residue, summed))
    put_pushes(summed)
    sums = inner_totals([pushes_of(at, me) for at in range(bond_rows + slot_rows)], me)
    for code, stride in enumerate(strides):
        owner = lax.rem(me + (-stride) % domains, domains)
        pushes = [pushes_of(at, owner) for at in range(bond_rows + slot_rows)]
        for part, total in enumerate(far_totals(pushes, owner, [code])):
            sums[part] = sums[part] + total
    for part in range(atom_rows):
        lanes = slice(part * LANES, (part + 1) * LANES)
        mass = around_ref[pl.ds(me * rows.count + rows.mass + part, 1), :]
        for c in range(3):
            correction = mass * (sums[part][c : c + 1, :] + sums[part][3 + c : 4 + c, :])
            move = moves_ref[pl.ds(me * rows.disp_count + c * atom_rows + part, 1), :] - correction
            start = around_ref[pl.ds(me * rows.count + rows.coords[c] + part, 1), :]
            coords_out_ref[c, 0, :, lanes] = start + move
            velocity_out_ref[c, 0, :, lanes] = move * (1.0 / time_step)


def vmem(count):
    return [pl.BlockSpec(memory_space=pltpu.VMEM)] * count


def smem(count):
    return [pl.BlockSpec(memory_space=pltpu.SMEM)] * count


def hbm(count):
    return [pl.BlockSpec(memory_space=pltpu.HBM)] * count


def in_hbm(arrays):
    return [pltpu.with_memory_space_constraint(a, pltpu.HBM) for a in arrays]


def params(mebibytes):
    return pltpu.CompilerParams(vmem_limit_bytes=mebibytes * 1024 * 1024)


def cost(flops, moved):
    return pl.CostEstimate(flops=flops, bytes_accessed=moved, transcendentals=0)


def room_for(arrays):
    return [pltpu.VMEM(a.shape, a.dtype) for a in arrays]


def shards(
    coords,
    velocity,
    charge,
    inv_mass,
    tile_block,
    tile_atoms,
    active_tile_count,
    bond_atoms,
    cross_atoms,
    cross_side,
    cross_count,
):
    atoms = coords.shape[-1]
    tiles = tile_atoms.shape[2]
    domains = lax.axis_size("dom")
    strides = strides_of(domains)
    rows = Rows(atoms, bond_atoms.shape[-1], cross_side.shape[-1])
    whole_slab = domains == SUBLANES
    copies = domains if whole_slab else 1
    f32 = jnp.float32

    sent = (coords, charge, inv_mass, bond_atoms, cross_atoms)
    packed, rim = pl.pallas_call(
        functools.partial(pack_kernel, rows, copies),
        out_shape=(
            jax.ShapeDtypeStruct((copies * rows.count, LANES), f32),
            jax.ShapeDtypeStruct((4 * rows.shell_rows, LANES), f32),
        ),
        in_specs=hbm(len(sent)),
        out_specs=tuple(vmem(2)),
        scratch_shapes=room_for(sent)
        + [pltpu.SemaphoreType.DMA((len(sent),)), pltpu.VMEM((rows.count, LANES), f32)],
        compiler_params=params(4),
        name="pack",
    )(*in_hbm(sent))

    alone = (coords, charge, velocity, inv_mass, cross_side, tile_atoms)
    own = pl.pallas_call(
        functools.partial(own_kernel, rows),
        out_shape=(
            jax.ShapeDtypeStruct((4, atoms, LANES), f32),
            jax.ShapeDtypeStruct((4, tiles, TILE), f32),
            jax.ShapeDtypeStruct((tiles, TILE), jnp.int32),
            jax.ShapeDtypeStruct((4 * rows.atom_rows + rows.slot_rows, LANES), f32),
        ),
        in_specs=hbm(len(alone)),
        out_specs=tuple(vmem(4)),
        scratch_shapes=room_for(alone[:5]) + [pltpu.SemaphoreType.DMA((len(alone),))],
        compiler_params=params(4),
        cost_estimate=cost(64 * atoms * LANES, 16 * atoms * LANES),
        name="own",
    )(*in_hbm(alone))

    below = passed_along(rim, "slab", 1)
    above = passed_along(rim, "slab", -1)
    if whole_slab:
        around = from_slab(packed)

        def place():
            return [place_of(stride) for stride in strides]

    else:
        around = jnp.concatenate([packed] + [passed_along(packed, "dom", -stride) for stride in strides], axis=0)

        def place():
            return [1, 2, 3, 4]


    moves = pl.pallas_call(
        functools.partial(force_kernel, rows, copies, place),
        out_shape=jax.ShapeDtypeStruct((copies * rows.disp_count, LANES), f32),
        in_specs=smem(2) + hbm(1) + vmem(7),
        out_specs=vmem(1)[0],
        scratch_shapes=[
            pltpu.VMEM((4, 6 * rows.shell_rows, SUBLANES, LANES), f32),
            pltpu.VMEM((4, tiles, LANES), f32),
            pltpu.VMEM((3, atoms, LANES), f32),
            pltpu.SMEM(tile_block.shape, jnp.int32),
            pltpu.SemaphoreType.DMA(()),
        ],
        compiler_params=params(8),
        cost_estimate=cost(30 * tiles * TILE * TILE, 4 * around.size),
        name="force",
    )(active_tile_count, cross_count, *in_hbm([tile_block]), around, below, above, *own)

    if not whole_slab:
        return by_exchange(rows, strides, around, moves, cross_count)

    constraint_rows = rows.bond_rows + rows.slot_rows
    weight, matrix = pl.pallas_call(
        functools.partial(bond_kernel, rows, domains, strides),
        out_shape=(
            jax.ShapeDtypeStruct(((rows.bond_rows + 4 * rows.slot_rows) * 3 * domains, LANES), f32),
            jax.ShapeDtypeStruct((domains * rows.matrix, atoms // 2), jnp.bfloat16),
        ),
        in_specs=vmem(1),
        out_specs=tuple(vmem(2)),
        compiler_params=params(16),
        cost_estimate=cost(8 * domains * rows.matrix * atoms // 2, 4 * around.size),
        name="bonds",
    )(around)

    every_move = from_slab(moves)

    return pl.pallas_call(
        functools.partial(solve_kernel, rows, domains, strides),
        out_shape=(
            jax.ShapeDtypeStruct(coords.shape, f32),
            jax.ShapeDtypeStruct(coords.shape, f32),
        ),
        in_specs=vmem(4),
        out_specs=tuple(vmem(2)),
        scratch_shapes=[
            pltpu.VMEM((constraint_rows, SUBLANES * domains, LANES), f32),
            pltpu.VMEM((5, rows.atom_rows, SUBLANES * domains, LANES), f32),
        ],
        compiler_params=params(16),
        name="solve",
    )(around, every_move, weight, matrix)


def by_exchange(rows, strides, around, moves, cross_count):
    atom_count = rows.atom_rows * LANES
    shell = rows.shell_rows * LANES
    inside = around.reshape(5, rows.count, LANES)

    def flat(at, count):
        return inside[0, at : at + count].reshape(-1)

    def neighbours(at):
        return inside[1:, at : at + rows.shell_rows].reshape(-1)

    coords = jnp.stack([flat(at, rows.atom_rows) for at in rows.coords])
    inv_mass = flat(rows.mass, rows.atom_rows)
    displace = moves[: rows.live].reshape(3, atom_count)
    left = flat(rows.bond_first, rows.bond_rows).astype(jnp.int32)
    right = flat(rows.bond_second, rows.bond_rows).astype(jnp.int32)
    cross_left = flat(rows.cross_first, rows.slot_rows).astype(jnp.int32)
    cross_right = flat(rows.cross_second, rows.slot_rows).astype(jnp.int32)
    side = moves[rows.side : rows.side + rows.slot_rows].reshape(-1).astype(jnp.int32)
    flag = moves[rows.live : rows.side].reshape(-1)
    cross_index = side * shell + cross_right
    far_coords = jnp.stack([neighbours(at) for at in rows.coords])
    far_mass = neighbours(rows.mass)

    def weights(first, second, mass_first, mass_second):
        gap = first - second
        length = jnp.sqrt(jnp.sum(gap * gap, axis=0) + length_floor)
        return gap / length * lax.rsqrt(mass_first + mass_second)

    inner = weights(coords[:, left], coords[:, right], inv_mass[left], inv_mass[right])
    cross = flag * weights(
        coords[:, cross_left], far_coords[:, cross_index], inv_mass[cross_left], far_mass[cross_index]
    )

    def project(field):
        rim = field[:, :shell]
        far = jnp.concatenate([passed_along(rim, "dom", -stride) for stride in strides], axis=1)
        return (
            jnp.sum(inner * (field[:, left] - field[:, right]), axis=0),
            jnp.sum(cross * (field[:, cross_left] - far[:, cross_index]), axis=0),
        )

    def spread(values):
        pushed = inner * values[0]
        pushed_cross = cross * values[1]
        totals = jnp.zeros((3, atom_count), jnp.float32).at[:, left].add(pushed).at[:, right].add(-pushed)
        totals = totals.at[:, cross_left].add(pushed_cross)
        outward = jnp.zeros((3, 4 * shell), jnp.float32).at[:, cross_index].add(-pushed_cross)
        for code, stride in enumerate(strides):
            totals = totals.at[:, :shell].add(
                passed_along(outward[:, code * shell : (code + 1) * shell], "dom", stride)
            )
        return inv_mass * totals

    residue = project(displace)
    summed = residue
    for _ in range(ORDER):
        change = project(spread(residue))
        residue = tuple(now - step for now, step in zip(residue, change))
        summed = tuple(a + b for a, b in zip(summed, residue))
    move = displace - spread(summed)
    return (
        (coords + move).reshape(3, 1, 1, atom_count),
        (move * (1.0 / time_step)).reshape(3, 1, 1, atom_count),
    )


def solution(mesh):
    return jax.shard_map(
        shards,
        mesh=mesh,
        in_specs=(
            P(None, "slab", "dom", None),
            P(None, "slab", "dom", None),
            P("slab", "dom", None),
            P("slab", "dom", None),
            P("slab", "dom", None),
            P("slab", "dom", None, None),
            P("slab", "dom"),
            P(None, "slab", "dom", None),
            P(None, "slab", "dom", None),
            P("slab", "dom", None),
            P("slab", "dom"),
        ),
        out_specs=(P(None, "slab", "dom", None), P(None, "slab", "dom", None)),
        check_vma=False,
    )
```

```python
import functools

import jax
import jax.numpy as jnp
from jax import lax
from jax.experimental import pallas as pl
from jax.experimental.pallas import tpu as pltpu
from jax.sharding import PartitionSpec as P

TILE = 128
ORDER = 4
LANES = 128
SUBLANES = 8

time_step = 0.1
cutoff_sq = 16.0
force_scale = 4.0
length_floor = 0.25


def passed_along(array, axis, by):
    length = lax.axis_size(axis)
    return lax.ppermute(array, axis, [(i, (i + by) % length) for i in range(length)])


def first_of(domains):
    return domains - 1


def from_slab(blocks):
    length = lax.axis_size("dom")
    order = [(first_of(length) + i) % length for i in range(length)]
    return lax.all_to_all(blocks, "dom", 0, 0, axis_index_groups=[order], tiled=True)


def place_of(stride=0):
    length = lax.axis_size("dom")
    return lax.rem(lax.axis_index("dom") + (stride - first_of(length)) % length, length)


def strides_of(domains):
    row_width = max(2, domains // 8)
    return (1, -1, row_width, -row_width)


def round_up(count, step):
    return -(-count // step) * step


class Rows:
    def __init__(self, atoms, bonds, slots):
        self.atom_rows = atoms // LANES
        self.shell_rows = atoms // 2 // LANES
        self.bond_rows = bonds // LANES
        self.slot_rows = slots // LANES
        at = 0
        self.coords = []
        for _ in range(3):
            self.coords.append(at)
            at += self.atom_rows
        self.charge = at
        at += self.shell_rows
        self.mass = at
        at += self.atom_rows
        self.bond_first = at
        at += self.bond_rows
        self.bond_second = at
        at += self.bond_rows
        self.cross_first = at
        at += self.slot_rows
        self.cross_second = at
        at += self.slot_rows
        self.used = at
        self.count = round_up(at, SUBLANES)
        self.shell_terms = (self.bond_rows + self.slot_rows) * LANES
        self.inner_at = (0, self.shell_terms)
        self.cross_at = self.bond_rows * LANES
        self.far_at = self.shell_terms + self.bond_rows * LANES
        self.matrix = self.far_at + self.slot_rows * LANES
        self.live = 3 * self.atom_rows
        self.side = self.live + self.slot_rows
        self.disp_used = self.side + self.slot_rows
        self.disp_count = round_up(self.disp_used, SUBLANES)


def take_lanes(table, lanes):
    return jnp.take_along_axis(table, lanes, axis=1, mode="promise_in_bounds")


def pick(tables, index):
    lanes = index & (LANES - 1)
    chunk = index >> 7
    result = take_lanes(tables[0], lanes)
    for k in range(1, len(tables)):
        result = jnp.where(chunk == k, take_lanes(tables[k], lanes), result)
    return result


def fetched(sources, targets, sem_ref):
    copies = [pltpu.make_async_copy(s, t, sem_ref.at[n]) for n, (s, t) in enumerate(zip(sources, targets))]
    for copy in copies:
        copy.start()
    return copies


def pack_kernel(rows, copies, *refs):
    sources, (out_ref, rim_ref), targets, sem_ref = refs[:5], refs[5:7], refs[7:12], refs[12]
    block_ref = refs[13]
    for copy in fetched(sources, targets, sem_ref):
        copy.wait()
    coords_ref, charge_ref, mass_ref, bonds_ref, cross_ref = targets

    def put(row, value):
        for part in range(value.shape[1] // LANES):
            block_ref[pl.ds(row + part, 1), :] = value[:, part * LANES : (part + 1) * LANES]

    shell = rows.shell_rows * LANES
    fields = [coords_ref[c, 0] for c in range(3)] + [charge_ref[0, :, :shell]]
    for c in range(4):
        at = rows.coords[c] if c < 3 else rows.charge
        put(at, fields[c])
        for part in range(rows.shell_rows):
            rim_ref[pl.ds(c * rows.shell_rows + part, 1), :] = fields[c][:, part * LANES : (part + 1) * LANES]
    put(rows.mass, mass_ref[0])
    put(rows.bond_first, bonds_ref[0, 0].astype(jnp.float32))
    put(rows.bond_second, bonds_ref[1, 0].astype(jnp.float32))
    put(rows.cross_first, cross_ref[0, 0].astype(jnp.float32))
    put(rows.cross_second, cross_ref[1, 0].astype(jnp.float32))
    if rows.count > rows.used:
        block_ref[rows.used :, :] = jnp.zeros((rows.count - rows.used, LANES), jnp.float32)
    block = block_ref[...]
    for copy in range(copies):
        out_ref[pl.ds(copy * rows.count, rows.count), :] = block


SHRINK = 1.0 / 4.0
OUT_OF_REACH = 1000.0
TILES_STEP = 4
PIECE = 32


def own_kernel(
    rows,
    coords_hbm,
    charge_hbm,
    velocity_hbm,
    mass_hbm,
    side_hbm,
    atoms_hbm,
    own_ref,
    far_ref,
    index_ref,
    motion_ref,
    coords_ref,
    charge_ref,
    velocity_ref,
    mass_ref,
    side_ref,
    sem_ref,
):
    atom_rows = rows.atom_rows
    copies = fetched(
        (coords_hbm, charge_hbm, atoms_hbm.at[0, 0], velocity_hbm, mass_hbm, side_hbm),
        (coords_ref, charge_ref, index_ref, velocity_ref, mass_ref, side_ref),
        sem_ref,
    )
    down = lax.broadcasted_iota(jnp.int32, (SUBLANES, LANES), 0)
    copies[0].wait()
    copies[1].wait()

    def lanes_of(part):
        return slice(part * LANES, (part + 1) * LANES)

    table = []
    for c in range(4):
        field = coords_ref[c, 0] * SHRINK if c < 3 else charge_ref[0]
        table.append(
            [jnp.broadcast_to(field[:, lanes_of(part)], (SUBLANES, LANES)) for part in range(atom_rows)]
        )
    for part in range(atom_rows):
        for group in range(LANES // SUBLANES):
            at = part * LANES + group * SUBLANES
            for c in range(4):
                value = take_lanes(table[c][part], down + group * SUBLANES)
                own_ref[c, pl.ds(at, SUBLANES), :] = value if c < 3 else value * 8.0
    copies[2].wait()
    for group in range(index_ref.shape[0] // SUBLANES):
        at = pl.ds(group * SUBLANES, SUBLANES)
        index = index_ref[at, :]
        for c in range(4):
            far_ref[c, at, :] = pick(table[c], index)
    for copy in copies[3:]:
        copy.wait()
    fields = [velocity_ref[c, 0] for c in range(3)] + [mass_ref[0], side_ref[0].astype(jnp.float32)]
    at = 0
    for field in fields:
        for part in range(field.shape[1] // LANES):
            motion_ref[pl.ds(at, 1), :] = field[:, lanes_of(part)]
            at += 1


def force_kernel(
    rows,
    copies,
    place,
    live_ref,
    count_ref,
    block_hbm,
    around_ref,
    below_ref,
    above_ref,
    own_ref,
    near_ref,
    index_ref,
    motion_ref,
    out_ref,
    table_ref,
    far_ref,
    sum_ref,
    block_ref,
    sem_ref,
):
    atom_rows, shell_rows = rows.atom_rows, rows.shell_rows
    tiles = index_ref.shape[0]
    block_copy = pltpu.make_async_copy(block_hbm, block_ref, sem_ref)
    block_copy.start()
    live = live_ref[0, 0]
    holders = place()
    starts = [rows.coords[0], rows.coords[1], rows.coords[2], rows.charge]
    entry_rows = 6 * shell_rows

    def broadcast(row):
        return jnp.broadcast_to(row, (SUBLANES, LANES))

    for c in range(4):
        factor = SHRINK if c < 3 else 1.0
        at = 0
        for neighbour in range(4):
            base = holders[neighbour] * rows.count + starts[c]
            for part in range(shell_rows):
                table_ref[c, at] = broadcast(around_ref[pl.ds(base + part, 1), :] * factor)
                at += 1
        for slab_ref in (below_ref, above_ref):
            for part in range(shell_rows):
                table_ref[c, at] = broadcast(slab_ref[pl.ds(c * shell_rows + part, 1), :] * factor)
                at += 1

    for group in range(tiles // SUBLANES):
        at = pl.ds(group * SUBLANES, SUBLANES)
        index = index_ref[at, :]
        lanes = index & (LANES - 1)
        chunk = index >> 7
        values = [near_ref[c, at, :] for c in range(4)]
        for k in range(entry_rows):
            here = chunk == atom_rows + k
            values = [jnp.where(here, take_lanes(table_ref[c, k], lanes), values[c]) for c in range(4)]
        for c in range(4):
            far_ref[c, at, :] = values[c]

    sum_ref[...] = jnp.zeros(sum_ref.shape, jnp.float32)
    block_copy.wait()
    down = lax.broadcasted_iota(jnp.int32, (tiles, LANES), 0)
    far_ref[0] = jnp.where(down < live, far_ref[0], OUT_OF_REACH)

    softening = 1.0 / cutoff_sq

    def add_tile(tile):
        base = block_ref[0, 0, tile] * TILE
        far = [jnp.broadcast_to(far_ref[c, pl.ds(tile, 1), :], (PIECE, LANES)) for c in range(4)]
        for piece in range(TILE // PIECE):
            at = pl.ds(pl.multiple_of(base + piece * PIECE, PIECE), PIECE)
            gap = [own_ref[c, at, :] - far[c] for c in range(3)]
            square = gap[0] * gap[0] + gap[1] * gap[1] + gap[2] * gap[2]
            inverse = pl.reciprocal(square + softening, approx=True)
            weight = jnp.maximum(inverse - 1.0 / (1.0 + softening), 0.0)
            strength = (inverse - own_ref[3, at, :] * far[3]) * (weight * weight)
            for c in range(3):
                sum_ref[c, at, :] = sum_ref[c, at, :] + strength * gap[c]

    def add_tiles(step, _):
        for n in range(TILES_STEP):
            add_tile(step * TILES_STEP + n)
        return 0

    lax.fori_loop(0, lax.div(live + TILES_STEP - 1, TILES_STEP), add_tiles, 0)

    scale = time_step * time_step * force_scale * 4.0 / 2048.0 * (1.0 + softening) ** 2

    lane = lax.broadcasted_iota(jnp.int32, (LANES, LANES), 1)
    columns = jnp.zeros((LANES, LANES), jnp.float32)
    for c in range(3):
        for part in range(atom_rows):
            total = jnp.sum(sum_ref[c, pl.ds(part * LANES, LANES), :], axis=1, keepdims=True)
            columns = jnp.where(lane == c * atom_rows + part, total, columns)
    totals = columns.T[: 3 * atom_rows, :]
    mass = motion_ref[pl.ds(3 * atom_rows, atom_rows), :]
    moved = time_step * motion_ref[pl.ds(0, 3 * atom_rows), :] + scale * totals * jnp.concatenate([mass] * 3, axis=0)
    for copy in range(copies):
        out_ref[pl.ds(copy * rows.disp_count, 3 * atom_rows), :] = moved
    slot = lax.broadcasted_iota(jnp.int32, (1, LANES), 1)
    for part in range(rows.slot_rows):
        flag = jnp.where(slot + part * LANES < count_ref[0, 0], 1.0, 0.0)
        side = motion_ref[pl.ds(4 * atom_rows + part, 1), :]
        for copy in range(copies):
            out_ref[pl.ds(copy * rows.disp_count + rows.live + part, 1), :] = flag
            out_ref[pl.ds(copy * rows.disp_count + rows.side + part, 1), :] = side
    if rows.disp_count > rows.disp_used:
        for copy in range(copies):
            out_ref[pl.ds(copy * rows.disp_count + rows.disp_used, rows.disp_count - rows.disp_used), :] = jnp.zeros(
                (rows.disp_count - rows.disp_used, LANES), jnp.float32
            )


def bond_kernel(rows, domains, strides, around_ref, weight_ref, matrix_ref):
    atom_rows, shell_rows = rows.atom_rows, rows.shell_rows

    def load(row):
        return around_ref[pl.ds(row, domains, stride=rows.count), :]

    def index(row):
        return load(row).astype(jnp.int32)

    fields = [[load(at + part) for part in range(atom_rows)] for at in rows.coords + [rows.mass]]

    def put_weights(first, second, at):
        gap = [first[c] - second[c] for c in range(3)]
        length_sq = gap[0] * gap[0] + gap[1] * gap[1] + gap[2] * gap[2] + length_floor
        scale = lax.rsqrt(length_sq) * lax.rsqrt(first[3] + second[3])
        for c in range(3):
            weight_ref[pl.ds((at * 3 + c) * domains, domains), :] = gap[c] * scale

    for part in range(rows.bond_rows):
        first = index(rows.bond_first + part)
        second = index(rows.bond_second + part)
        put_weights([pick(f, first) for f in fields], [pick(f, second) for f in fields], part)
    shells = [f[:shell_rows] for f in fields]
    for part in range(rows.slot_rows):
        first = index(rows.cross_first + part)
        second = index(rows.cross_second + part)
        ends = [pick(f, first) for f in shells]
        for code, stride in enumerate(strides):
            seen = pltpu.roll(second, stride % domains, 0)
            others = [pltpu.roll(pick(f, seen), -stride % domains, 0) for f in shells]
            put_weights(ends, others, rows.bond_rows + part * 4 + code)

    down = lax.broadcasted_iota(jnp.int32, (SUBLANES, LANES), 0)
    group_rows = 4 * SUBLANES

    kind = jnp.bfloat16 if shell_rows * LANES <= 256 else jnp.float32
    across = lax.broadcasted_iota(jnp.int32, (group_rows, LANES), 1).astype(jnp.float32)
    lanes = [(across + float(block * LANES)).astype(kind) for block in range(shell_rows)]

    def column(row, step, half=0):
        row = jnp.broadcast_to(row, (SUBLANES, LANES))
        groups = [take_lanes(row, down + at) for at in range(step * group_rows, (step + 1) * group_rows, SUBLANES)]
        return (jnp.concatenate(groups, axis=0) - float(half * shell_rows * LANES)).astype(kind)

    def put(at, ends, signs):
        for block in range(shell_rows):
            value = jnp.zeros((group_rows, LANES), kind)
            for end, sign in zip(ends, signs):
                value = jnp.where(end == lanes[block], jnp.full((group_rows, LANES), sign, kind), value)
            matrix_ref[pl.ds(at, group_rows), block * LANES : (block + 1) * LANES] = value.astype(matrix_ref.dtype)

    def build(domain, _):
        start = pl.multiple_of(domain * rows.matrix, LANES)
        for part in range(rows.bond_rows):
            first = around_ref[pl.ds(domain * rows.count + rows.bond_first + part, 1), :]
            second = around_ref[pl.ds(domain * rows.count + rows.bond_second + part, 1), :]
            for step in range(LANES // group_rows):
                for half in range(2):
                    ends = (column(first, step, half), column(second, step, half))
                    put(start + rows.inner_at[half] + part * LANES + step * group_rows, ends, (1.0, -1.0))
        for part in range(rows.slot_rows):
            for row_at, to, sign in (
                (rows.cross_first, rows.cross_at, 1.0),
                (rows.cross_second, rows.far_at, -1.0),
            ):
                row = around_ref[pl.ds(domain * rows.count + row_at + part, 1), :]
                for step in range(LANES // group_rows):
                    put(start + to + part * LANES + step * group_rows, (column(row, step),), (sign,))
        return 0

    lax.fori_loop(0, domains, build, 0)


def solve_kernel(
    rows,
    domains,
    strides,
    around_ref,
    moves_ref,
    weight_ref,
    matrix_ref,
    coords_out_ref,
    velocity_out_ref,
    push_ref,
    field_ref,
):
    atom_rows, shell_rows = rows.atom_rows, rows.shell_rows
    bond_rows, slot_rows = rows.bond_rows, rows.slot_rows
    me = place_of()

    def load(row):
        return around_ref[pl.ds(row, domains, stride=rows.count), :]

    def index(row):
        return load(row).astype(jnp.int32)

    inner_first = [index(rows.bond_first + p) for p in range(bond_rows)]
    inner_second = [index(rows.bond_second + p) for p in range(bond_rows)]
    cross_first = [index(rows.cross_first + p) for p in range(slot_rows)]
    cross_second = [index(rows.cross_second + p) for p in range(slot_rows)]
    masses = [load(rows.mass + p) for p in range(atom_rows)]

    def move_rows(row):
        return moves_ref[pl.ds(row, domains, stride=rows.disp_count), :]

    def weight_rows(at, c):
        return weight_ref[pl.ds((at * 3 + c) * domains, domains), :]

    sides = [move_rows(rows.side + p) for p in range(slot_rows)]
    cross_weights = []
    for part in range(slot_rows):
        live = move_rows(rows.live + part)
        for c in range(3):
            value = 0.0
            for code in range(4):
                value = jnp.where(sides[part] == code, weight_rows(bond_rows + part * 4 + code, c), value)
            cross_weights.append(value * live)

    def weight(at, c):
        return weight_rows(at, c) if at < bond_rows else cross_weights[(at - bond_rows) * 3 + c]

    def project(fields):
        result = []
        for part in range(bond_rows):
            total = 0.0
            for c in range(3):
                ends = pick(fields[c], inner_first[part]) - pick(fields[c], inner_second[part])
                total = total + weight(part, c) * ends
            result.append(total)
        for part in range(slot_rows):
            seen = [pltpu.roll(cross_second[part], stride % domains, 0) for stride in strides]
            total = 0.0
            for c in range(3):
                shell = fields[c][:shell_rows]
                other = 0.0
                for code, stride in enumerate(strides):
                    value = pltpu.roll(pick(shell, seen[code]), -stride % domains, 0)
                    other = jnp.where(sides[part] == code, value, other)
                total = total + weight(bond_rows + part, c) * (pick(shell, cross_first[part]) - other)
            result.append(total)
        return result

    def put_pushes(values):
        for at, value in enumerate(values):
            for c in range(3):
                pushed = weight(at, c) * value
                high = pushed.astype(jnp.bfloat16).astype(jnp.float32)
                push_ref[at, pl.ds(c * domains, domains), :] = high
                push_ref[at, pl.ds((3 + c) * domains, domains), :] = pushed - high

    def pushes_of(at, domain):
        return push_ref[at, pl.ds(domain, SUBLANES, stride=domains), :]

    def product(pushes, domain, at):
        start = domain * rows.matrix + at
        if not isinstance(start, int):
            start = pl.multiple_of(start, LANES)
        pushes = pushes[0] if len(pushes) == 1 else jnp.concatenate(pushes, axis=1)
        result = jnp.dot(
            pushes.astype(jnp.bfloat16),
            matrix_ref[pl.ds(start, pushes.shape[1]), :],
            preferred_element_type=jnp.float32,
        )
        return [result[:, p * LANES : (p + 1) * LANES] for p in range(shell_rows)]

    def inner_totals(pushes, domain):
        return product(pushes, domain, 0) + product(pushes[:bond_rows], domain, rows.shell_terms)

    def far_totals(pushes, domain, codes):
        masked = []
        for part in range(slot_rows):
            side = moves_ref[pl.ds(domain * rows.disp_count + rows.side + part, 1), :]
            side = jnp.broadcast_to(side, (SUBLANES, LANES))
            pushed = pushes[bond_rows + part]
            masked.append(jnp.concatenate([jnp.where(side == code, pushed, 0.0) for code in codes], axis=0))
        return product(masked, domain, rows.far_at)

    def spread(values):
        put_pushes(values)
        for domain in range(domains):
            pushes = [pushes_of(at, domain) for at in range(bond_rows + slot_rows)]
            for part, total in enumerate(inner_totals(pushes, domain)):
                field_ref[0, part, pl.ds(domain, SUBLANES, stride=domains), :] = total
            for part, total in enumerate(far_totals(pushes, domain, range(4))):
                for code, stride in enumerate(strides):
                    field_ref[1 + code, part, pl.ds((domain + stride) % domains, SUBLANES, stride=domains), :] = total[
                        code * SUBLANES : (code + 1) * SUBLANES, :
                    ]

        def field(c, part):
            pieces = [
                field_ref[source, part, pl.ds(row * domains, domains), :]
                for source in range(5 if part < shell_rows else 1)
                for row in (c, 3 + c)
            ]
            return masses[part] * functools.reduce(lambda a, b: a + b, pieces)

        return [[field(c, part) for part in range(atom_rows)] for c in range(3)]

    moves = [
        [move_rows(c * atom_rows + p) for p in range(atom_rows)]
        for c in range(3)
    ]
    push_ref[...] = jnp.zeros(push_ref.shape, jnp.float32)
    residue = project(moves)

    def expand(_, carry):
        residue, summed = carry
        change = project(spread(residue))
        residue = [now - step for now, step in zip(residue, change)]
        return residue, [a + b for a, b in zip(summed, residue)]

    summed = residue
    for step in range(ORDER):
        residue, summed = expand(step, (residue, summed))
    put_pushes(summed)
    sums = inner_totals([pushes_of(at, me) for at in range(bond_rows + slot_rows)], me)
    for code, stride in enumerate(strides):
        owner = lax.rem(me + (-stride) % domains, domains)
        pushes = [pushes_of(at, owner) for at in range(bond_rows + slot_rows)]
        for part, total in enumerate(far_totals(pushes, owner, [code])):
            sums[part] = sums[part] + total
    for part in range(atom_rows):
        lanes = slice(part * LANES, (part + 1) * LANES)
        mass = around_ref[pl.ds(me * rows.count + rows.mass + part, 1), :]
        for c in range(3):
            correction = mass * (sums[part][c : c + 1, :] + sums[part][3 + c : 4 + c, :])
            move = moves_ref[pl.ds(me * rows.disp_count + c * atom_rows + part, 1), :] - correction
            start = around_ref[pl.ds(me * rows.count + rows.coords[c] + part, 1), :]
            coords_out_ref[c, 0, :, lanes] = start + move
            velocity_out_ref[c, 0, :, lanes] = move * (1.0 / time_step)


def vmem(count):
    return [pl.BlockSpec(memory_space=pltpu.VMEM)] * count


def smem(count):
    return [pl.BlockSpec(memory_space=pltpu.SMEM)] * count


def hbm(count):
    return [pl.BlockSpec(memory_space=pltpu.HBM)] * count


def in_hbm(arrays):
    return [pltpu.with_memory_space_constraint(a, pltpu.HBM) for a in arrays]


def params(mebibytes):
    return pltpu.CompilerParams(vmem_limit_bytes=mebibytes * 1024 * 1024)


def cost(flops, moved):
    return pl.CostEstimate(flops=flops, bytes_accessed=moved, transcendentals=0)


def room_for(arrays):
    return [pltpu.VMEM(a.shape, a.dtype) for a in arrays]


def shards(
    coords,
    velocity,
    charge,
    inv_mass,
    tile_block,
    tile_atoms,
    active_tile_count,
    bond_atoms,
    cross_atoms,
    cross_side,
    cross_count,
):
    atoms = coords.shape[-1]
    tiles = tile_atoms.shape[2]
    domains = lax.axis_size("dom")
    strides = strides_of(domains)
    rows = Rows(atoms, bond_atoms.shape[-1], cross_side.shape[-1])
    whole_slab = domains == SUBLANES
    copies = domains if whole_slab else 1
    f32 = jnp.float32

    sent = (coords, charge, inv_mass, bond_atoms, cross_atoms)
    packed, rim = pl.pallas_call(
        functools.partial(pack_kernel, rows, copies),
        out_shape=(
            jax.ShapeDtypeStruct((copies * rows.count, LANES), f32),
            jax.ShapeDtypeStruct((4 * rows.shell_rows, LANES), f32),
        ),
        in_specs=hbm(len(sent)),
        out_specs=tuple(vmem(2)),
        scratch_shapes=room_for(sent)
        + [pltpu.SemaphoreType.DMA((len(sent),)), pltpu.VMEM((rows.count, LANES), f32)],
        compiler_params=params(4),
        name="pack",
    )(*in_hbm(sent))

    alone = (coords, charge, velocity, inv_mass, cross_side, tile_atoms)
    own = pl.pallas_call(
        functools.partial(own_kernel, rows),
        out_shape=(
            jax.ShapeDtypeStruct((4, atoms, LANES), f32),
            jax.ShapeDtypeStruct((4, tiles, TILE), f32),
            jax.ShapeDtypeStruct((tiles, TILE), jnp.int32),
            jax.ShapeDtypeStruct((4 * rows.atom_rows + rows.slot_rows, LANES), f32),
        ),
        in_specs=hbm(len(alone)),
        out_specs=tuple(vmem(4)),
        scratch_shapes=room_for(alone[:5]) + [pltpu.SemaphoreType.DMA((len(alone),))],
        compiler_params=params(4),
        cost_estimate=cost(64 * atoms * LANES, 16 * atoms * LANES),
        name="own",
    )(*in_hbm(alone))

    below = passed_along(rim, "slab", 1)
    above = passed_along(rim, "slab", -1)
    if whole_slab:
        around = from_slab(packed)

        def place():
            return [place_of(stride) for stride in strides]

    else:
        around = jnp.concatenate([packed] + [passed_along(packed, "dom", -stride) for stride in strides], axis=0)

        def place():
            return [1, 2, 3, 4]


    moves = pl.pallas_call(
        functools.partial(force_kernel, rows, copies, place),
        out_shape=jax.ShapeDtypeStruct((copies * rows.disp_count, LANES), f32),
        in_specs=smem(2) + hbm(1) + vmem(7),
        out_specs=vmem(1)[0],
        scratch_shapes=[
            pltpu.VMEM((4, 6 * rows.shell_rows, SUBLANES, LANES), f32),
            pltpu.VMEM((4, tiles, LANES), f32),
            pltpu.VMEM((3, atoms, LANES), f32),
            pltpu.SMEM(tile_block.shape, jnp.int32),
            pltpu.SemaphoreType.DMA(()),
        ],
        compiler_params=params(8),
        cost_estimate=cost(30 * tiles * TILE * TILE, 4 * around.size),
        name="force",
    )(active_tile_count, cross_count, *in_hbm([tile_block]), around, below, above, *own)

    if not whole_slab:
        return by_exchange(rows, strides, around, moves, cross_count)

    constraint_rows = rows.bond_rows + rows.slot_rows
    weight, matrix = pl.pallas_call(
        functools.partial(bond_kernel, rows, domains, strides),
        out_shape=(
            jax.ShapeDtypeStruct(((rows.bond_rows + 4 * rows.slot_rows) * 3 * domains, LANES), f32),
            jax.ShapeDtypeStruct((domains * rows.matrix, atoms // 2), jnp.bfloat16),
        ),
        in_specs=vmem(1),
        out_specs=tuple(vmem(2)),
        compiler_params=params(16),
        cost_estimate=cost(8 * domains * rows.matrix * atoms // 2, 4 * around.size),
        name="bonds",
    )(around)

    every_move = from_slab(moves)

    return pl.pallas_call(
        functools.partial(solve_kernel, rows, domains, strides),
        out_shape=(
            jax.ShapeDtypeStruct(coords.shape, f32),
            jax.ShapeDtypeStruct(coords.shape, f32),
        ),
        in_specs=vmem(4),
        out_specs=tuple(vmem(2)),
        scratch_shapes=[
            pltpu.VMEM((constraint_rows, SUBLANES * domains + SUBLANES, LANES), f32),
            pltpu.VMEM((5, rows.atom_rows, SUBLANES * domains, LANES), f32),
        ],
        compiler_params=params(16),
        name="solve",
    )(around, every_move, weight, matrix)


def by_exchange(rows, strides, around, moves, cross_count):
    atom_count = rows.atom_rows * LANES
    shell = rows.shell_rows * LANES
    inside = around.reshape(5, rows.count, LANES)

    def flat(at, count):
        return inside[0, at : at + count].reshape(-1)

    def neighbours(at):
        return inside[1:, at : at + rows.shell_rows].reshape(-1)

    coords = jnp.stack([flat(at, rows.atom_rows) for at in rows.coords])
    inv_mass = flat(rows.mass, rows.atom_rows)
    displace = moves[: rows.live].reshape(3, atom_count)
    left = flat(rows.bond_first, rows.bond_rows).astype(jnp.int32)
    right = flat(rows.bond_second, rows.bond_rows).astype(jnp.int32)
    cross_left = flat(rows.cross_first, rows.slot_rows).astype(jnp.int32)
    cross_right = flat(rows.cross_second, rows.slot_rows).astype(jnp.int32)
    side = moves[rows.side : rows.side + rows.slot_rows].reshape(-1).astype(jnp.int32)
    flag = moves[rows.live : rows.side].reshape(-1)
    cross_index = side * shell + cross_right
    far_coords = jnp.stack([neighbours(at) for at in rows.coords])
    far_mass = neighbours(rows.mass)

    def weights(first, second, mass_first, mass_second):
        gap = first - second
        length = jnp.sqrt(jnp.sum(gap * gap, axis=0) + length_floor)
        return gap / length * lax.rsqrt(mass_first + mass_second)

    inner = weights(coords[:, left], coords[:, right], inv_mass[left], inv_mass[right])
    cross = flag * weights(
        coords[:, cross_left], far_coords[:, cross_index], inv_mass[cross_left], far_mass[cross_index]
    )

    def project(field):
        rim = field[:, :shell]
        far = jnp.concatenate([passed_along(rim, "dom", -stride) for stride in strides], axis=1)
        return (
            jnp.sum(inner * (field[:, left] - field[:, right]), axis=0),
            jnp.sum(cross * (field[:, cross_left] - far[:, cross_index]), axis=0),
        )

    def spread(values):
        pushed = inner * values[0]
        pushed_cross = cross * values[1]
        totals = jnp.zeros((3, atom_count), jnp.float32).at[:, left].add(pushed).at[:, right].add(-pushed)
        totals = totals.at[:, cross_left].add(pushed_cross)
        outward = jnp.zeros((3, 4 * shell), jnp.float32).at[:, cross_index].add(-pushed_cross)
        for code, stride in enumerate(strides):
            totals = totals.at[:, :shell].add(
                passed_along(outward[:, code * shell : (code + 1) * shell], "dom", stride)
            )
        return inv_mass * totals

    residue = project(displace)
    summed = residue
    for _ in range(ORDER):
        change = project(spread(residue))
        residue = tuple(now - step for now, step in zip(residue, change))
        summed = tuple(a + b for a, b in zip(summed, residue))
    move = displace - spread(summed)
    return (
        (coords + move).reshape(3, 1, 1, atom_count),
        (move * (1.0 / time_step)).reshape(3, 1, 1, atom_count),
    )


def solution(mesh):
    return jax.shard_map(
        shards,
        mesh=mesh,
        in_specs=(
            P(None, "slab", "dom", None),
            P(None, "slab", "dom", None),
            P("slab", "dom", None),
            P("slab", "dom", None),
            P("slab", "dom", None),
            P("slab", "dom", None, None),
            P("slab", "dom"),
            P(None, "slab", "dom", None),
            P(None, "slab", "dom", None),
            P("slab", "dom", None),
            P("slab", "dom"),
        ),
        out_specs=(P(None, "slab", "dom", None), P(None, "slab", "dom", None)),
        check_vma=False,
    )
```

```python
import functools

import jax
import jax.numpy as jnp
from jax import lax
from jax.experimental import pallas as pl
from jax.experimental.pallas import tpu as pltpu
from jax.sharding import PartitionSpec as P

TILE = 128
ORDER = 4
LANES = 128
SUBLANES = 8

time_step = 0.1
cutoff_sq = 16.0
force_scale = 4.0
length_floor = 0.25


def passed_along(array, axis, by):
    length = lax.axis_size(axis)
    return lax.ppermute(array, axis, [(i, (i + by) % length) for i in range(length)])


def first_of(domains):
    return domains - 1


def from_slab(blocks):
    length = lax.axis_size("dom")
    order = [(first_of(length) + i) % length for i in range(length)]
    return lax.all_to_all(blocks, "dom", 0, 0, axis_index_groups=[order], tiled=True)


def place_of(stride=0):
    length = lax.axis_size("dom")
    return lax.rem(lax.axis_index("dom") + (stride - first_of(length)) % length, length)


def strides_of(domains):
    row_width = max(2, domains // 8)
    return (1, -1, row_width, -row_width)


def round_up(count, step):
    return -(-count // step) * step


class Rows:
    def __init__(self, atoms, bonds, slots):
        self.atom_rows = atoms // LANES
        self.shell_rows = atoms // 2 // LANES
        self.bond_rows = bonds // LANES
        self.slot_rows = slots // LANES
        at = 0
        self.coords = []
        for _ in range(3):
            self.coords.append(at)
            at += self.atom_rows
        self.charge = at
        at += self.shell_rows
        self.mass = at
        at += self.atom_rows
        self.bond_first = at
        at += self.bond_rows
        self.bond_second = at
        at += self.bond_rows
        self.cross_first = at
        at += self.slot_rows
        self.cross_second = at
        at += self.slot_rows
        self.used = at
        self.count = round_up(at, SUBLANES)
        self.shell_terms = (self.bond_rows + self.slot_rows) * LANES
        self.inner_at = (0, self.shell_terms)
        self.cross_at = self.bond_rows * LANES
        self.far_at = self.shell_terms + self.bond_rows * LANES
        self.matrix = self.far_at + self.slot_rows * LANES
        self.live = 3 * self.atom_rows
        self.side = self.live + self.slot_rows
        self.disp_used = self.side + self.slot_rows
        self.disp_count = round_up(self.disp_used, SUBLANES)


def take_lanes(table, lanes):
    return jnp.take_along_axis(table, lanes, axis=1, mode="promise_in_bounds")


def pick(tables, index):
    lanes = index & (LANES - 1)
    chunk = index >> 7
    result = take_lanes(tables[0], lanes)
    for k in range(1, len(tables)):
        result = jnp.where(chunk == k, take_lanes(tables[k], lanes), result)
    return result


def fetched(sources, targets, sem_ref):
    copies = [pltpu.make_async_copy(s, t, sem_ref.at[n]) for n, (s, t) in enumerate(zip(sources, targets))]
    for copy in copies:
        copy.start()
    return copies


def pack_kernel(rows, copies, *refs):
    sources, (out_ref, rim_ref), targets, sem_ref = refs[:5], refs[5:7], refs[7:12], refs[12]
    block_ref = refs[13]
    for copy in fetched(sources, targets, sem_ref):
        copy.wait()
    coords_ref, charge_ref, mass_ref, bonds_ref, cross_ref = targets

    def put(row, value):
        for part in range(value.shape[1] // LANES):
            block_ref[pl.ds(row + part, 1), :] = value[:, part * LANES : (part + 1) * LANES]

    shell = rows.shell_rows * LANES
    fields = [coords_ref[c, 0] for c in range(3)] + [charge_ref[0, :, :shell]]
    for c in range(4):
        at = rows.coords[c] if c < 3 else rows.charge
        put(at, fields[c])
        for part in range(rows.shell_rows):
            rim_ref[pl.ds(c * rows.shell_rows + part, 1), :] = fields[c][:, part * LANES : (part + 1) * LANES]
    put(rows.mass, mass_ref[0])
    put(rows.bond_first, bonds_ref[0, 0].astype(jnp.float32))
    put(rows.bond_second, bonds_ref[1, 0].astype(jnp.float32))
    put(rows.cross_first, cross_ref[0, 0].astype(jnp.float32))
    put(rows.cross_second, cross_ref[1, 0].astype(jnp.float32))
    if rows.count > rows.used:
        block_ref[rows.used :, :] = jnp.zeros((rows.count - rows.used, LANES), jnp.float32)
    block = block_ref[...]
    for copy in range(copies):
        out_ref[pl.ds(copy * rows.count, rows.count), :] = block


SHRINK = 1.0 / 4.0
OUT_OF_REACH = 1000.0
TILES_STEP = 4
PIECE = 16


def own_kernel(
    rows,
    coords_hbm,
    charge_hbm,
    velocity_hbm,
    mass_hbm,
    side_hbm,
    atoms_hbm,
    own_ref,
    far_ref,
    index_ref,
    motion_ref,
    coords_ref,
    charge_ref,
    velocity_ref,
    mass_ref,
    side_ref,
    sem_ref,
):
    atom_rows = rows.atom_rows
    copies = fetched(
        (coords_hbm, charge_hbm, atoms_hbm.at[0, 0], velocity_hbm, mass_hbm, side_hbm),
        (coords_ref, charge_ref, index_ref, velocity_ref, mass_ref, side_ref),
        sem_ref,
    )
    down = lax.broadcasted_iota(jnp.int32, (SUBLANES, LANES), 0)
    copies[0].wait()
    copies[1].wait()

    def lanes_of(part):
        return slice(part * LANES, (part + 1) * LANES)

    table = []
    for c in range(4):
        field = coords_ref[c, 0] * SHRINK if c < 3 else charge_ref[0]
        table.append(
            [jnp.broadcast_to(field[:, lanes_of(part)], (SUBLANES, LANES)) for part in range(atom_rows)]
        )
    for part in range(atom_rows):
        for group in range(LANES // SUBLANES):
            at = part * LANES + group * SUBLANES
            for c in range(4):
                value = take_lanes(table[c][part], down + group * SUBLANES)
                own_ref[c, pl.ds(at, SUBLANES), :] = value if c < 3 else value * 8.0
    copies[2].wait()
    for group in range(index_ref.shape[0] // SUBLANES):
        at = pl.ds(group * SUBLANES, SUBLANES)
        index = index_ref[at, :]
        for c in range(4):
            far_ref[c, at, :] = pick(table[c], index)
    for copy in copies[3:]:
        copy.wait()
    fields = [velocity_ref[c, 0] for c in range(3)] + [mass_ref[0], side_ref[0].astype(jnp.float32)]
    at = 0
    for field in fields:
        for part in range(field.shape[1] // LANES):
            motion_ref[pl.ds(at, 1), :] = field[:, lanes_of(part)]
            at += 1


def force_kernel(
    rows,
    copies,
    place,
    live_ref,
    count_ref,
    block_hbm,
    around_ref,
    below_ref,
    above_ref,
    own_ref,
    near_ref,
    index_ref,
    motion_ref,
    out_ref,
    table_ref,
    far_ref,
    sum_ref,
    block_ref,
    sem_ref,
):
    atom_rows, shell_rows = rows.atom_rows, rows.shell_rows
    tiles = index_ref.shape[0]
    block_copy = pltpu.make_async_copy(block_hbm, block_ref, sem_ref)
    block_copy.start()
    live = live_ref[0, 0]
    holders = place()
    starts = [rows.coords[0], rows.coords[1], rows.coords[2], rows.charge]
    entry_rows = 6 * shell_rows

    def broadcast(row):
        return jnp.broadcast_to(row, (SUBLANES, LANES))

    for c in range(4):
        factor = SHRINK if c < 3 else 1.0
        at = 0
        for neighbour in range(4):
            base = holders[neighbour] * rows.count + starts[c]
            for part in range(shell_rows):
                table_ref[c, at] = broadcast(around_ref[pl.ds(base + part, 1), :] * factor)
                at += 1
        for slab_ref in (below_ref, above_ref):
            for part in range(shell_rows):
                table_ref[c, at] = broadcast(slab_ref[pl.ds(c * shell_rows + part, 1), :] * factor)
                at += 1

    for group in range(tiles // SUBLANES):
        at = pl.ds(group * SUBLANES, SUBLANES)
        index = index_ref[at, :]
        lanes = index & (LANES - 1)
        chunk = index >> 7
        values = [near_ref[c, at, :] for c in range(4)]
        for k in range(entry_rows):
            here = chunk == atom_rows + k
            values = [jnp.where(here, take_lanes(table_ref[c, k], lanes), values[c]) for c in range(4)]
        for c in range(4):
            far_ref[c, at, :] = values[c]

    sum_ref[...] = jnp.zeros(sum_ref.shape, jnp.float32)
    block_copy.wait()
    down = lax.broadcasted_iota(jnp.int32, (tiles, LANES), 0)
    far_ref[0] = jnp.where(down < live, far_ref[0], OUT_OF_REACH)

    softening = 1.0 / cutoff_sq

    def add_tile(tile):
        base = block_ref[0, 0, tile] * TILE
        far = [jnp.broadcast_to(far_ref[c, pl.ds(tile, 1), :], (PIECE, LANES)) for c in range(4)]
        for piece in range(TILE // PIECE):
            at = pl.ds(pl.multiple_of(base + piece * PIECE, PIECE), PIECE)
            gap = [own_ref[c, at, :] - far[c] for c in range(3)]
            square = gap[0] * gap[0] + gap[1] * gap[1] + gap[2] * gap[2]
            inverse = pl.reciprocal(square + softening, approx=True)
            weight = jnp.maximum(inverse - 1.0 / (1.0 + softening), 0.0)
            strength = (inverse - own_ref[3, at, :] * far[3]) * (weight * weight)
            for c in range(3):
                sum_ref[c, at, :] = sum_ref[c, at, :] + strength * gap[c]

    def add_tiles(step, _):
        for n in range(TILES_STEP):
            add_tile(step * TILES_STEP + n)
        return 0

    lax.fori_loop(0, lax.div(live + TILES_STEP - 1, TILES_STEP), add_tiles, 0)

    scale = time_step * time_step * force_scale * 4.0 / 2048.0 * (1.0 + softening) ** 2

    lane = lax.broadcasted_iota(jnp.int32, (LANES, LANES), 1)
    columns = jnp.zeros((LANES, LANES), jnp.float32)
    for c in range(3):
        for part in range(atom_rows):
            total = jnp.sum(sum_ref[c, pl.ds(part * LANES, LANES), :], axis=1, keepdims=True)
            columns = jnp.where(lane == c * atom_rows + part, total, columns)
    totals = columns.T[: 3 * atom_rows, :]
    mass = motion_ref[pl.ds(3 * atom_rows, atom_rows), :]
    moved = time_step * motion_ref[pl.ds(0, 3 * atom_rows), :] + scale * totals * jnp.concatenate([mass] * 3, axis=0)
    for copy in range(copies):
        out_ref[pl.ds(copy * rows.disp_count, 3 * atom_rows), :] = moved
    slot = lax.broadcasted_iota(jnp.int32, (1, LANES), 1)
    for part in range(rows.slot_rows):
        flag = jnp.where(slot + part * LANES < count_ref[0, 0], 1.0, 0.0)
        side = motion_ref[pl.ds(4 * atom_rows + part, 1), :]
        for copy in range(copies):
            out_ref[pl.ds(copy * rows.disp_count + rows.live + part, 1), :] = flag
            out_ref[pl.ds(copy * rows.disp_count + rows.side + part, 1), :] = side
    if rows.disp_count > rows.disp_used:
        for copy in range(copies):
            out_ref[pl.ds(copy * rows.disp_count + rows.disp_used, rows.disp_count - rows.disp_used), :] = jnp.zeros(
                (rows.disp_count - rows.disp_used, LANES), jnp.float32
            )


def bond_kernel(rows, domains, strides, around_ref, weight_ref, matrix_ref):
    atom_rows, shell_rows = rows.atom_rows, rows.shell_rows

    def load(row):
        return around_ref[pl.ds(row, domains, stride=rows.count), :]

    def index(row):
        return load(row).astype(jnp.int32)

    fields = [[load(at + part) for part in range(atom_rows)] for at in rows.coords + [rows.mass]]

    def put_weights(first, second, at):
        gap = [first[c] - second[c] for c in range(3)]
        length_sq = gap[0] * gap[0] + gap[1] * gap[1] + gap[2] * gap[2] + length_floor
        scale = lax.rsqrt(length_sq) * lax.rsqrt(first[3] + second[3])
        for c in range(3):
            weight_ref[pl.ds((at * 3 + c) * domains, domains), :] = gap[c] * scale

    for part in range(rows.bond_rows):
        first = index(rows.bond_first + part)
        second = index(rows.bond_second + part)
        put_weights([pick(f, first) for f in fields], [pick(f, second) for f in fields], part)
    shells = [f[:shell_rows] for f in fields]
    for part in range(rows.slot_rows):
        first = index(rows.cross_first + part)
        second = index(rows.cross_second + part)
        ends = [pick(f, first) for f in shells]
        for code, stride in enumerate(strides):
            seen = pltpu.roll(second, stride % domains, 0)
            others = [pltpu.roll(pick(f, seen), -stride % domains, 0) for f in shells]
            put_weights(ends, others, rows.bond_rows + part * 4 + code)

    down = lax.broadcasted_iota(jnp.int32, (SUBLANES, LANES), 0)
    group_rows = 4 * SUBLANES

    kind = jnp.bfloat16 if shell_rows * LANES <= 256 else jnp.float32
    across = lax.broadcasted_iota(jnp.int32, (group_rows, LANES), 1).astype(jnp.float32)
    lanes = [(across + float(block * LANES)).astype(kind) for block in range(shell_rows)]

    def column(row, step, half=0):
        row = jnp.broadcast_to(row, (SUBLANES, LANES))
        groups = [take_lanes(row, down + at) for at in range(step * group_rows, (step + 1) * group_rows, SUBLANES)]
        return (jnp.concatenate(groups, axis=0) - float(half * shell_rows * LANES)).astype(kind)

    def put(at, ends, signs):
        for block in range(shell_rows):
            value = jnp.zeros((group_rows, LANES), kind)
            for end, sign in zip(ends, signs):
                value = jnp.where(end == lanes[block], jnp.full((group_rows, LANES), sign, kind), value)
            matrix_ref[pl.ds(at, group_rows), block * LANES : (block + 1) * LANES] = value.astype(matrix_ref.dtype)

    def build(domain, _):
        start = pl.multiple_of(domain * rows.matrix, LANES)
        for part in range(rows.bond_rows):
            first = around_ref[pl.ds(domain * rows.count + rows.bond_first + part, 1), :]
            second = around_ref[pl.ds(domain * rows.count + rows.bond_second + part, 1), :]
            for step in range(LANES // group_rows):
                for half in range(2):
                    ends = (column(first, step, half), column(second, step, half))
                    put(start + rows.inner_at[half] + part * LANES + step * group_rows, ends, (1.0, -1.0))
        for part in range(rows.slot_rows):
            for row_at, to, sign in (
                (rows.cross_first, rows.cross_at, 1.0),
                (rows.cross_second, rows.far_at, -1.0),
            ):
                row = around_ref[pl.ds(domain * rows.count + row_at + part, 1), :]
                for step in range(LANES // group_rows):
                    put(start + to + part * LANES + step * group_rows, (column(row, step),), (sign,))
        return 0

    lax.fori_loop(0, domains, build, 0)


def solve_kernel(
    rows,
    domains,
    strides,
    around_ref,
    moves_ref,
    weight_ref,
    matrix_ref,
    coords_out_ref,
    velocity_out_ref,
    push_ref,
    field_ref,
):
    atom_rows, shell_rows = rows.atom_rows, rows.shell_rows
    bond_rows, slot_rows = rows.bond_rows, rows.slot_rows
    me = place_of()

    def load(row):
        return around_ref[pl.ds(row, domains, stride=rows.count), :]

    def index(row):
        return load(row).astype(jnp.int32)

    inner_first = [index(rows.bond_first + p) for p in range(bond_rows)]
    inner_second = [index(rows.bond_second + p) for p in range(bond_rows)]
    cross_first = [index(rows.cross_first + p) for p in range(slot_rows)]
    cross_second = [index(rows.cross_second + p) for p in range(slot_rows)]
    masses = [load(rows.mass + p) for p in range(atom_rows)]

    def move_rows(row):
        return moves_ref[pl.ds(row, domains, stride=rows.disp_count), :]

    def weight_rows(at, c):
        return weight_ref[pl.ds((at * 3 + c) * domains, domains), :]

    sides = [move_rows(rows.side + p) for p in range(slot_rows)]
    cross_weights = []
    for part in range(slot_rows):
        live = move_rows(rows.live + part)
        for c in range(3):
            value = 0.0
            for code in range(4):
                value = jnp.where(sides[part] == code, weight_rows(bond_rows + part * 4 + code, c), value)
            cross_weights.append(value * live)

    def weight(at, c):
        return weight_rows(at, c) if at < bond_rows else cross_weights[(at - bond_rows) * 3 + c]

    def project(fields):
        result = []
        for part in range(bond_rows):
            total = 0.0
            for c in range(3):
                ends = pick(fields[c], inner_first[part]) - pick(fields[c], inner_second[part])
                total = total + weight(part, c) * ends
            result.append(total)
        for part in range(slot_rows):
            seen = [pltpu.roll(cross_second[part], stride % domains, 0) for stride in strides]
            total = 0.0
            for c in range(3):
                shell = fields[c][:shell_rows]
                other = 0.0
                for code, stride in enumerate(strides):
                    value = pltpu.roll(pick(shell, seen[code]), -stride % domains, 0)
                    other = jnp.where(sides[part] == code, value, other)
                total = total + weight(bond_rows + part, c) * (pick(shell, cross_first[part]) - other)
            result.append(total)
        return result

    def put_pushes(values):
        for at, value in enumerate(values):
            for c in range(3):
                pushed = weight(at, c) * value
                high = pushed.astype(jnp.bfloat16).astype(jnp.float32)
                push_ref[at, pl.ds(c * domains, domains), :] = high
                push_ref[at, pl.ds((3 + c) * domains, domains), :] = pushed - high

    def pushes_of(at, domain):
        return push_ref[at, pl.ds(domain, SUBLANES, stride=domains), :]

    def product(pushes, domain, at):
        start = domain * rows.matrix + at
        if not isinstance(start, int):
            start = pl.multiple_of(start, LANES)
        pushes = pushes[0] if len(pushes) == 1 else jnp.concatenate(pushes, axis=1)
        result = jnp.dot(
            pushes.astype(jnp.bfloat16),
            matrix_ref[pl.ds(start, pushes.shape[1]), :],
            preferred_element_type=jnp.float32,
        )
        return [result[:, p * LANES : (p + 1) * LANES] for p in range(shell_rows)]

    def inner_totals(pushes, domain):
        return product(pushes, domain, 0) + product(pushes[:bond_rows], domain, rows.shell_terms)

    def far_totals(pushes, domain, codes):
        masked = []
        for part in range(slot_rows):
            side = moves_ref[pl.ds(domain * rows.disp_count + rows.side + part, 1), :]
            side = jnp.broadcast_to(side, (SUBLANES, LANES))
            pushed = pushes[bond_rows + part]
            masked.append(jnp.concatenate([jnp.where(side == code, pushed, 0.0) for code in codes], axis=0))
        return product(masked, domain, rows.far_at)

    def spread(values):
        put_pushes(values)
        for domain in range(domains):
            pushes = [pushes_of(at, domain) for at in range(bond_rows + slot_rows)]
            for part, total in enumerate(inner_totals(pushes, domain)):
                field_ref[0, part, pl.ds(domain, SUBLANES, stride=domains), :] = total
            for part, total in enumerate(far_totals(pushes, domain, range(4))):
                for code, stride in enumerate(strides):
                    field_ref[1 + code, part, pl.ds((domain + stride) % domains, SUBLANES, stride=domains), :] = total[
                        code * SUBLANES : (code + 1) * SUBLANES, :
                    ]

        def field(c, part):
            pieces = [
                field_ref[source, part, pl.ds(row * domains, domains), :]
                for source in range(5 if part < shell_rows else 1)
                for row in (c, 3 + c)
            ]
            return masses[part] * functools.reduce(lambda a, b: a + b, pieces)

        return [[field(c, part) for part in range(atom_rows)] for c in range(3)]

    moves = [
        [move_rows(c * atom_rows + p) for p in range(atom_rows)]
        for c in range(3)
    ]
    push_ref[...] = jnp.zeros(push_ref.shape, jnp.float32)
    residue = project(moves)

    def expand(_, carry):
        residue, summed = carry
        change = project(spread(residue))
        residue = [now - step for now, step in zip(residue, change)]
        return residue, [a + b for a, b in zip(summed, residue)]

    summed = residue
    for step in range(ORDER):
        residue, summed = expand(step, (residue, summed))
    put_pushes(summed)
    sums = inner_totals([pushes_of(at, me) for at in range(bond_rows + slot_rows)], me)
    for code, stride in enumerate(strides):
        owner = lax.rem(me + (-stride) % domains, domains)
        pushes = [pushes_of(at, owner) for at in range(bond_rows + slot_rows)]
        for part, total in enumerate(far_totals(pushes, owner, [code])):
            sums[part] = sums[part] + total
    for part in range(atom_rows):
        lanes = slice(part * LANES, (part + 1) * LANES)
        mass = around_ref[pl.ds(me * rows.count + rows.mass + part, 1), :]
        for c in range(3):
            correction = mass * (sums[part][c : c + 1, :] + sums[part][3 + c : 4 + c, :])
            move = moves_ref[pl.ds(me * rows.disp_count + c * atom_rows + part, 1), :] - correction
            start = around_ref[pl.ds(me * rows.count + rows.coords[c] + part, 1), :]
            coords_out_ref[c, 0, :, lanes] = start + move
            velocity_out_ref[c, 0, :, lanes] = move * (1.0 / time_step)


def vmem(count):
    return [pl.BlockSpec(memory_space=pltpu.VMEM)] * count


def smem(count):
    return [pl.BlockSpec(memory_space=pltpu.SMEM)] * count


def hbm(count):
    return [pl.BlockSpec(memory_space=pltpu.HBM)] * count


def in_hbm(arrays):
    return [pltpu.with_memory_space_constraint(a, pltpu.HBM) for a in arrays]


def params(mebibytes):
    return pltpu.CompilerParams(vmem_limit_bytes=mebibytes * 1024 * 1024)


def cost(flops, moved):
    return pl.CostEstimate(flops=flops, bytes_accessed=moved, transcendentals=0)


def room_for(arrays):
    return [pltpu.VMEM(a.shape, a.dtype) for a in arrays]


def shards(
    coords,
    velocity,
    charge,
    inv_mass,
    tile_block,
    tile_atoms,
    active_tile_count,
    bond_atoms,
    cross_atoms,
    cross_side,
    cross_count,
):
    atoms = coords.shape[-1]
    tiles = tile_atoms.shape[2]
    domains = lax.axis_size("dom")
    strides = strides_of(domains)
    rows = Rows(atoms, bond_atoms.shape[-1], cross_side.shape[-1])
    whole_slab = domains == SUBLANES
    copies = domains if whole_slab else 1
    f32 = jnp.float32

    sent = (coords, charge, inv_mass, bond_atoms, cross_atoms)
    packed, rim = pl.pallas_call(
        functools.partial(pack_kernel, rows, copies),
        out_shape=(
            jax.ShapeDtypeStruct((copies * rows.count, LANES), f32),
            jax.ShapeDtypeStruct((4 * rows.shell_rows, LANES), f32),
        ),
        in_specs=hbm(len(sent)),
        out_specs=tuple(vmem(2)),
        scratch_shapes=room_for(sent)
        + [pltpu.SemaphoreType.DMA((len(sent),)), pltpu.VMEM((rows.count, LANES), f32)],
        compiler_params=params(4),
        name="pack",
    )(*in_hbm(sent))

    alone = (coords, charge, velocity, inv_mass, cross_side, tile_atoms)
    own = pl.pallas_call(
        functools.partial(own_kernel, rows),
        out_shape=(
            jax.ShapeDtypeStruct((4, atoms, LANES), f32),
            jax.ShapeDtypeStruct((4, tiles, TILE), f32),
            jax.ShapeDtypeStruct((tiles, TILE), jnp.int32),
            jax.ShapeDtypeStruct((4 * rows.atom_rows + rows.slot_rows, LANES), f32),
        ),
        in_specs=hbm(len(alone)),
        out_specs=tuple(vmem(4)),
        scratch_shapes=room_for(alone[:5]) + [pltpu.SemaphoreType.DMA((len(alone),))],
        compiler_params=params(4),
        cost_estimate=cost(64 * atoms * LANES, 16 * atoms * LANES),
        name="own",
    )(*in_hbm(alone))

    below = passed_along(rim, "slab", 1)
    above = passed_along(rim, "slab", -1)
    if whole_slab:
        around = from_slab(packed)

        def place():
            return [place_of(stride) for stride in strides]

    else:
        around = jnp.concatenate([packed] + [passed_along(packed, "dom", -stride) for stride in strides], axis=0)

        def place():
            return [1, 2, 3, 4]


    moves = pl.pallas_call(
        functools.partial(force_kernel, rows, copies, place),
        out_shape=jax.ShapeDtypeStruct((copies * rows.disp_count, LANES), f32),
        in_specs=smem(2) + hbm(1) + vmem(7),
        out_specs=vmem(1)[0],
        scratch_shapes=[
            pltpu.VMEM((4, 6 * rows.shell_rows, SUBLANES, LANES), f32),
            pltpu.VMEM((4, tiles, LANES), f32),
            pltpu.VMEM((3, atoms, LANES), f32),
            pltpu.SMEM(tile_block.shape, jnp.int32),
            pltpu.SemaphoreType.DMA(()),
        ],
        compiler_params=params(8),
        cost_estimate=cost(30 * tiles * TILE * TILE, 4 * around.size),
        name="force",
    )(active_tile_count, cross_count, *in_hbm([tile_block]), around, below, above, *own)

    if not whole_slab:
        return by_exchange(rows, strides, around, moves, cross_count)

    constraint_rows = rows.bond_rows + rows.slot_rows
    weight, matrix = pl.pallas_call(
        functools.partial(bond_kernel, rows, domains, strides),
        out_shape=(
            jax.ShapeDtypeStruct(((rows.bond_rows + 4 * rows.slot_rows) * 3 * domains, LANES), f32),
            jax.ShapeDtypeStruct((domains * rows.matrix, atoms // 2), jnp.bfloat16),
        ),
        in_specs=vmem(1),
        out_specs=tuple(vmem(2)),
        compiler_params=params(16),
        cost_estimate=cost(8 * domains * rows.matrix * atoms // 2, 4 * around.size),
        name="bonds",
    )(around)

    every_move = from_slab(moves)

    return pl.pallas_call(
        functools.partial(solve_kernel, rows, domains, strides),
        out_shape=(
            jax.ShapeDtypeStruct(coords.shape, f32),
            jax.ShapeDtypeStruct(coords.shape, f32),
        ),
        in_specs=vmem(4),
        out_specs=tuple(vmem(2)),
        scratch_shapes=[
            pltpu.VMEM((constraint_rows, SUBLANES * domains + SUBLANES, LANES), f32),
            pltpu.VMEM((5, rows.atom_rows, SUBLANES * domains, LANES), f32),
        ],
        compiler_params=params(16),
        name="solve",
    )(around, every_move, weight, matrix)


def by_exchange(rows, strides, around, moves, cross_count):
    atom_count = rows.atom_rows * LANES
    shell = rows.shell_rows * LANES
    inside = around.reshape(5, rows.count, LANES)

    def flat(at, count):
        return inside[0, at : at + count].reshape(-1)

    def neighbours(at):
        return inside[1:, at : at + rows.shell_rows].reshape(-1)

    coords = jnp.stack([flat(at, rows.atom_rows) for at in rows.coords])
    inv_mass = flat(rows.mass, rows.atom_rows)
    displace = moves[: rows.live].reshape(3, atom_count)
    left = flat(rows.bond_first, rows.bond_rows).astype(jnp.int32)
    right = flat(rows.bond_second, rows.bond_rows).astype(jnp.int32)
    cross_left = flat(rows.cross_first, rows.slot_rows).astype(jnp.int32)
    cross_right = flat(rows.cross_second, rows.slot_rows).astype(jnp.int32)
    side = moves[rows.side : rows.side + rows.slot_rows].reshape(-1).astype(jnp.int32)
    flag = moves[rows.live : rows.side].reshape(-1)
    cross_index = side * shell + cross_right
    far_coords = jnp.stack([neighbours(at) for at in rows.coords])
    far_mass = neighbours(rows.mass)

    def weights(first, second, mass_first, mass_second):
        gap = first - second
        length = jnp.sqrt(jnp.sum(gap * gap, axis=0) + length_floor)
        return gap / length * lax.rsqrt(mass_first + mass_second)

    inner = weights(coords[:, left], coords[:, right], inv_mass[left], inv_mass[right])
    cross = flag * weights(
        coords[:, cross_left], far_coords[:, cross_index], inv_mass[cross_left], far_mass[cross_index]
    )

    def project(field):
        rim = field[:, :shell]
        far = jnp.concatenate([passed_along(rim, "dom", -stride) for stride in strides], axis=1)
        return (
            jnp.sum(inner * (field[:, left] - field[:, right]), axis=0),
            jnp.sum(cross * (field[:, cross_left] - far[:, cross_index]), axis=0),
        )

    def spread(values):
        pushed = inner * values[0]
        pushed_cross = cross * values[1]
        totals = jnp.zeros((3, atom_count), jnp.float32).at[:, left].add(pushed).at[:, right].add(-pushed)
        totals = totals.at[:, cross_left].add(pushed_cross)
        outward = jnp.zeros((3, 4 * shell), jnp.float32).at[:, cross_index].add(-pushed_cross)
        for code, stride in enumerate(strides):
            totals = totals.at[:, :shell].add(
                passed_along(outward[:, code * shell : (code + 1) * shell], "dom", stride)
            )
        return inv_mass * totals

    residue = project(displace)
    summed = residue
    for _ in range(ORDER):
        change = project(spread(residue))
        residue = tuple(now - step for now, step in zip(residue, change))
        summed = tuple(a + b for a, b in zip(summed, residue))
    move = displace - spread(summed)
    return (
        (coords + move).reshape(3, 1, 1, atom_count),
        (move * (1.0 / time_step)).reshape(3, 1, 1, atom_count),
    )


def solution(mesh):
    return jax.shard_map(
        shards,
        mesh=mesh,
        in_specs=(
            P(None, "slab", "dom", None),
            P(None, "slab", "dom", None),
            P("slab", "dom", None),
            P("slab", "dom", None),
            P("slab", "dom", None),
            P("slab", "dom", None, None),
            P("slab", "dom"),
            P(None, "slab", "dom", None),
            P(None, "slab", "dom", None),
            P("slab", "dom", None),
            P("slab", "dom"),
        ),
        out_specs=(P(None, "slab", "dom", None), P(None, "slab", "dom", None)),
        check_vma=False,
    )
```
